32 devices in a mesh: dp: 4 (over z), mp: 8 (over y, x, core).
Axes of the slice: x: 2, y: 2, z: 4, core: 2. Of those that a mesh axis runs over, the one named last changes fastest.
Arguments:
- h_first: bfloat16 [512, 8192], P('dp', 'mp'), may hold values from -8 to 8
- h_second: bfloat16 [512, 8192], P('dp', 'mp'), may hold values from -8 to 8
- weight: bfloat16 [8192, 8192], P('dp', 'mp'), may hold values from -0.0625 to 0.0625
Outputs:
- grad_first: bfloat16 [512, 8192], P('dp', 'mp')
- grad_second: bfloat16 [512, 8192], P('dp', 'mp')
- loss: float32 [], replicated
The draws below stay inside these ranges and needn't reach their ends.
All inputs are finite; a program needn't handle non-finite values.
Results may differ from the reference program's by a relative error of at most 0.0016.
Values may be sent and summed in bfloat16 or wider, within the bound.
No kernel may reach another device: no remote copies, remote signals or barrier semaphores. Data moves between devices by JAX's collectives and lax.ppermute only.
A program may use at most 64 MiB of HBM per device.

```python
import jax
import jax.numpy as jnp
from jax import lax

D = 8192
BATCH = 512


def draw_parts(key, which):
    shape = (BATCH, D)
    shared = jax.random.normal(jax.random.fold_in(key, 11), shape, jnp.float32)
    own = jax.random.normal(jax.random.fold_in(key, 20 + which), shape, jnp.float32)
    factor = jax.random.normal(jax.random.fold_in(key, 12), (BATCH, 1), jnp.float32)
    loading = jax.random.normal(jax.random.fold_in(key, 13), (1, D), jnp.float32)
    values = 0.7 * shared + 0.7 * own + 0.3 * factor * loading
    return jnp.clip(values, -8.0, 8.0).astype(jnp.bfloat16)


def draw_h_first(key, part):
    return draw_parts(key, 1)


def draw_h_second(key, part):
    return draw_parts(key, 2)


def block_scale(stream_key, extent, shards, smallest, high):
    def one(axis_at, shards_of):
        heights = jax.random.uniform(jax.random.fold_in(jax.random.fold_in(stream_key, 6), axis_at), (shards_of,), jnp.float32, smallest / len(shards), high / len(shards))
        return jnp.repeat(jnp.exp(heights), extent[axis_at] // shards_of).reshape((-1,) + (1,) * (len(extent) - axis_at - 1))

    gain = one(*shards[0])
    for cut in shards[1:]:
        gain = gain * one(*cut)
    return gain


def centred(key, shape, width, bound, pieces=(), dtype=jnp.bfloat16):
    result = jax.random.normal(key, shape, jnp.float32) * width
    if len(pieces) > 0:
        result = block_scale(key, shape, pieces, -0.22, 0.18) * result
    return jnp.clip(result, min=-bound, max=bound).astype(dtype)


def setup_inputs(seed: int = 0) -> dict:
    key_list = jax.random.split(jax.random.key(seed), 4)
    h_first = draw_h_first(jax.random.fold_in(key_list[3], 71), 0)
    h_second = draw_h_second(jax.random.fold_in(key_list[3], 71), 0)
    weight = centred(key_list[2], (D, D), D ** -0.5, 0.0625, ((0, 4), (1, 8)))
    return {"h_first": h_first, "h_second": h_second, "weight": weight}


off_weight = 0.0051
bn_eps = 1e-05

def normalize(values):
    mean_col = lax.optimization_barrier(jnp.sum(values, 0)) / BATCH
    variance = lax.optimization_barrier(jnp.sum(values * values, 0)) / BATCH - mean_col * mean_col
    scale = lax.rsqrt(variance + bn_eps)
    return ((values - mean_col) * scale, scale)

def backward(grad, normed, scale):
    first_mean = lax.optimization_barrier(jnp.sum(grad, 0)) / BATCH
    second_mean = lax.optimization_barrier(jnp.sum(grad * normed, 0)) / BATCH
    return (scale * (grad - first_mean - normed * second_mean)).astype(jnp.bfloat16)

def reference(h_first, h_second, weight):
    z_first = jnp.dot(h_first, weight, preferred_element_type=jnp.float32)
    z_second = jnp.dot(h_second, weight, preferred_element_type=jnp.float32)
    norm_first, scale_first = normalize(z_first)
    norm_second, scale_second = normalize(z_second)
    diag = lax.optimization_barrier(jnp.sum(norm_first * norm_second, 0)) / BATCH
    packed_first = norm_first.astype(jnp.bfloat16)
    packed_second = norm_second.astype(jnp.bfloat16)
    dims = (((1,), (1,)), ((), ()))
    gram_first = lax.dot_general(packed_first, packed_first, dims, preferred_element_type=jnp.float32)
    gram_second = lax.dot_general(packed_second, packed_second, dims, preferred_element_type=jnp.float32)
    frob = jnp.sum(gram_first * gram_second) / (BATCH * BATCH)
    loss = (jnp.sum((1.0 - diag) ** 2) + off_weight * (frob - jnp.sum(diag * diag))) / D
    coeff = 2.0 * ((1.0 - off_weight) * diag - 1.0)
    factor = 2.0 * off_weight / BATCH
    grad_n_first = factor * jnp.dot(gram_second.astype(jnp.bfloat16), packed_first, preferred_element_type=jnp.float32) + coeff * norm_second
    grad_n_second = factor * jnp.dot(gram_first.astype(jnp.bfloat16), packed_second, preferred_element_type=jnp.float32) + coeff * norm_first
    return (backward(grad_n_first, norm_first, scale_first), backward(grad_n_second, norm_second, scale_second), loss)
```

```python
import jax
import jax.numpy as jnp
from jax import lax
from jax.sharding import PartitionSpec as P

D = 8192


off_weight = 0.0051
bn_eps = 1e-05


class Place:
    def __init__(self):
        self.n = lax.axis_size("dp")
        self.k = lax.axis_size("mp") // self.n
        self.z = lax.axis_index("dp")
        self.a = lax.axis_index("mp") // self.k
        self.b = lax.axis_index("mp") % self.k

    def send(self, value, target):
        n, k = self.n, self.k
        pairs = []
        for z in range(n):
            for a in range(n):
                for b in range(k):
                    to_z, to_a, to_b = target(z, a, b)
                    pairs.append(((z * n + a) * k + b, (to_z * n + to_a) * k + to_b))
        return lax.ppermute(value, ("dp", "mp"), pairs)

    def along(self, axis):
        if axis == "z":
            return self.n, self.z, lambda step: lambda z, a, b: (z ^ step, a, b)
        if axis == "a":
            return self.n, self.a, lambda step: lambda z, a, b: (z, a ^ step, b)
        return self.k, self.b, lambda step: lambda z, a, b: (z, a, b ^ step)


def ordered(parts, place):
    bit = 1
    while bit < len(parts):
        odd = (place & bit) != 0
        parts = [jnp.where(odd, parts[i ^ bit], parts[i]) for i in range(len(parts))]
        bit *= 2
    return parts


def tree_sum(parts):
    while len(parts) > 1:
        parts = [parts[i] + parts[i + 1] for i in range(0, len(parts), 2)]
    return parts[0]


def pick(value, index):
    return lax.dynamic_index_in_dim(value, index, 0, keepdims=False)


def exchange(place, axis, value):
    size, here, toward = place.along(axis)
    return [pick(value, here)] + [
        place.send(pick(value, here ^ step), toward(step)) for step in range(1, size)
    ]


def reduce_scatter(place, axis, value, travel):
    size, here, toward = place.along(axis)
    value = value.reshape((size, value.shape[0] // size) + value.shape[1:])
    parts = exchange(place, axis, value.astype(travel))
    return tree_sum([part.astype(jnp.float32) for part in parts])


def gather(place, axis, value):
    size, here, toward = place.along(axis)
    parts = [value] + [place.send(value, toward(step)) for step in range(1, size)]
    return jnp.concatenate(ordered(parts, here), 0)


def all_reduce_rounded(place, gram):
    part = gram
    for axis in ("b", "a", "z"):
        part = reduce_scatter(place, axis, part, jnp.float32)
    part = part.astype(jnp.bfloat16)
    for axis in ("z", "a", "b"):
        part = gather(place, axis, part)
    return part


def per_device(h_first, h_second, weight):
    place = Place()
    n, k, z, a, b = place.n, place.k, place.z, place.a, place.b
    rows, width = h_first.shape
    batch = rows * n
    columns = weight.shape[1] // n
    weight_parts = weight.reshape(k, width, n * columns)

    turns = ((0, n - 1), (1 % n, (n - 2) % n))
    zs = []
    for values, turn in ((h_first, turns[0]), (h_second, turns[1])):
        halves = values.reshape(2, rows // 2, width)
        moved = jnp.stack(
            [
                place.send(halves[i], lambda z, a, b, t=turn[i]: (a, z ^ t, b))
                for i in range(2)
            ]
        )
        size, here, toward = place.along("a")
        met = [moved] + [place.send(moved, toward(step)) for step in range(1, n)]
        own = jnp.concatenate(met, 0).reshape(batch, width)
        total = jnp.dot(own, pick(weight_parts, b), preferred_element_type=jnp.float32)
        for step in range(1, k):
            other = place.send(own, lambda z, a, b, s=step: (z, a, b ^ s))
            total += jnp.dot(
                other, pick(weight_parts, b ^ step), preferred_element_type=jnp.float32
            )
        cut = total.reshape(batch, n, columns).transpose(1, 0, 2)
        mine = pick(cut, z)
        coarse = cut
        met = [mine] + [
            place.send(pick(coarse, z ^ step), lambda z, a, b, s=step: (z ^ s, a, b)).astype(
                jnp.float32
            )
            for step in range(1, n)
        ]
        whole = tree_sum(met).reshape(n, 2, rows // 2, columns)
        whole = [
            jnp.stack(ordered([whole[i, half] for i in range(n)], a ^ turn[half]))
            for half in range(2)
        ]
        zs.append(jnp.stack(whole, 1).reshape(batch, columns))

    normed, scales = [], []
    for values in zs:
        mean = jnp.sum(values, 0) / batch
        scale = lax.rsqrt(jnp.sum(values * values, 0) / batch - mean * mean + bn_eps)
        normed.append((values - mean) * scale)
        scales.append(scale)
    diag = jnp.sum(normed[0] * normed[1], 0) / batch
    packed = [values.astype(jnp.bfloat16) for values in normed]
    dims = (((1,), (1,)), ((), ()))
    rounded = [
        all_reduce_rounded(
            place, lax.dot_general(values, values, dims, preferred_element_type=jnp.float32)
        )
        for values in packed
    ]
    frob = jnp.sum(rounded[0].astype(jnp.float32) * rounded[1].astype(jnp.float32))
    frob = frob / (batch * batch)
    coeff = 2.0 * ((1.0 - off_weight) * diag - 1.0)
    factor = 2.0 * off_weight / batch
    outs = []
    for view in range(2):
        grad = (
            factor * jnp.dot(rounded[1 - view], packed[view], preferred_element_type=jnp.float32)
            + coeff * normed[1 - view]
        )
        first = jnp.sum(grad, 0) / batch
        second = jnp.sum(grad * normed[view], 0) / batch
        out = (scales[view] * (grad - first - normed[view] * second)).astype(jnp.bfloat16)
        parts = exchange(place, "z", out.reshape(n, rows, columns))
        outs.append(jnp.concatenate(ordered(parts, z), 1))
    share = jnp.sum((1.0 - diag) ** 2) - off_weight * jnp.sum(diag * diag)
    loss = (lax.psum(share, ("dp", "mp")) + off_weight * frob) / D
    return (outs[0], outs[1], loss)


def solution(mesh):
    in_specs = (P("dp", "mp"), P("dp", "mp"), P("dp", "mp"))
    out_specs = (P("dp", "mp"), P("dp", "mp"), P())
    return jax.shard_map(
        per_device, mesh=mesh, in_specs=in_specs, out_specs=out_specs, check_vma=False
    )
```

```python
import functools

import jax
import jax.numpy as jnp
from jax import lax
from jax.experimental import pallas as pl
from jax.experimental.pallas import tpu as pltpu
from jax.sharding import PartitionSpec as P

D = 8192


off_weight = 0.0051
bn_eps = 1e-05

F32 = jnp.float32
BF16 = jnp.bfloat16
VMEM_BYTES = 40 * 1024 * 1024
SHARED = 8
LEVELS = 8


class Place:
    def __init__(self):
        self.n = lax.axis_size("dp")
        self.k = lax.axis_size("mp") // self.n
        self.z = lax.axis_index("dp")
        self.a = lax.axis_index("mp") // self.k
        self.b = lax.axis_index("mp") % self.k

    def send(self, value, target):
        n, k = self.n, self.k
        pairs = []
        for z in range(n):
            for a in range(n):
                for b in range(k):
                    to_z, to_a, to_b = target(z, a, b)
                    pairs.append(((z * n + a) * k + b, (to_z * n + to_a) * k + to_b))
        return lax.ppermute(value, ("dp", "mp"), pairs)

    def along(self, axis):
        if axis == "z":
            return self.n, self.z, lambda step: lambda z, a, b: (z ^ step, a, b)
        if axis == "a":
            return self.n, self.a, lambda step: lambda z, a, b: (z, a ^ step, b)
        return self.k, self.b, lambda step: lambda z, a, b: (z, a, b ^ step)


def ordered(parts, place):
    bit = 1
    while bit < len(parts):
        odd = (place & bit) != 0
        parts = [jnp.where(odd, parts[i ^ bit], parts[i]) for i in range(len(parts))]
        bit *= 2
    return parts


def tree_sum(parts):
    while len(parts) > 1:
        parts = [parts[i] + parts[i + 1] for i in range(0, len(parts), 2)]
    return parts[0]


def pick(value, index):
    return lax.dynamic_index_in_dim(value, index, 0, keepdims=False)


def exchange(place, axis, value):
    size, here, toward = place.along(axis)
    return [pick(value, here)] + [
        place.send(pick(value, here ^ step), toward(step)) for step in range(1, size)
    ]


def reduce_scatter(place, axis, value):
    size, here, toward = place.along(axis)
    value = value.reshape((size, value.shape[0] // size) + value.shape[1:])
    return tree_sum(exchange(place, axis, value))


def gather(place, axis, value):
    size, here, toward = place.along(axis)
    parts = [value] + [place.send(value, toward(step)) for step in range(1, size)]
    return jnp.concatenate(ordered(parts, here), 0)


def rounded_gram(place, part, share):
    for axis in ("a", "z"):
        part = reduce_scatter(place, axis, part)
    if share:
        last = (place.z == place.n - 1) & (place.a == place.n - 1) & (place.b == place.k - 1)
        total = part[-1:, :1]
        high = lax.reduce_precision(total, 8, 7)
        middle = lax.reduce_precision(total - high, 8, 7)
        three = jnp.concatenate([high, middle, total - high - middle], 1)
        three = jnp.where(last, three, part[-1:, :3])
        part = lax.dynamic_update_slice(part, three, (part.shape[0] - 1, 0))
    part = part.astype(BF16)
    for axis in ("z", "a", "b"):
        part = gather(place, axis, part)
    return part


def met_rows(place, values, turn):
    rows, width = values.shape
    halves = values.reshape(2, rows // 2, width)
    moved = jnp.stack(
        [place.send(halves[i], lambda z, a, b, t=turn[i]: (a, z ^ t, b)) for i in range(2)]
    ).reshape(rows, width)
    size, here, toward = place.along("a")
    return [moved] + [place.send(moved, toward(step)) for step in range(1, size)]


def project_kernel(place_ref, *refs, n, k):
    met, others = refs[:n], refs[n : n + k - 1]
    weights = refs[n + k - 1 : n + 2 * k - 1]
    own_ref, coarse, fine = refs[n + 2 * k - 1], refs[n + 2 * k : 3 * n + 2 * k - 2 : 2], refs[n + 2 * k + 1 : 3 * n + 2 * k - 2 : 2]
    step = pl.program_id(0)
    total = jnp.dot(
        jnp.concatenate([ref[...] for ref in met], 0), weights[0][...], preferred_element_type=F32
    )
    for ref, part in zip(others, weights[1:]):
        total += jnp.dot(ref[...], part[...], preferred_element_type=F32)

    @pl.when(step == 0)
    def _():
        own_ref[...] = total

    for other in range(1, n):

        @pl.when(step == other)
        def _():
            encode(total, coarse[other - 1], fine[other - 1])


def encode(total, coarse_ref, fine_ref):
    coarse = total.astype(BF16)
    coarse_ref[...] = coarse
    near = coarse.astype(F32)
    ratio = jnp.where(near == 0.0, 0.0, (total - near) / jnp.where(near == 0.0, 1.0, near))
    level = jnp.floor((ratio * 256.0 + 1.0) * (LEVELS / 2))
    level = jnp.clip(level, 0.0, LEVELS - 1.0)
    height = total.shape[0] // SHARED
    word = level[:height]
    for i in range(1, SHARED):
        word = word * float(LEVELS) + level[i * height : (i + 1) * height]
    fine_ref[...] = word


def decode(coarse, fine):
    height = fine.shape[0]
    blocks = []
    for i in reversed(range(SHARED)):
        rest = jnp.floor(fine * (1.0 / LEVELS))
        level = fine - rest * float(LEVELS)
        fine = rest
        near = coarse[i * height : (i + 1) * height].astype(F32)
        blocks.append(near + near * ((level + (0.5 - LEVELS / 2)) * (2.0 / LEVELS / 256.0)))
    return blocks[::-1]


def project(place, place_array, met, others, weight):
    n, k = place.n, place.k
    rows, width = met[0].shape
    batch, columns = rows * n, weight.shape[1] // n
    whole = lambda step, at: (0, 0)

    def weight_map(i):
        return lambda step, at: (at[2] ^ i, at[0] ^ step)

    out_shape = [jax.ShapeDtypeStruct((batch, columns), F32)]
    out_specs = [pl.BlockSpec((batch, columns), whole)]
    for _ in range(1, n):
        out_shape.append(jax.ShapeDtypeStruct((batch, columns), BF16))
        out_specs.append(pl.BlockSpec((batch, columns), whole))
        out_shape.append(jax.ShapeDtypeStruct((batch // SHARED, columns), F32))
        out_specs.append(pl.BlockSpec((batch // SHARED, columns), whole))
    outs = pl.pallas_call(
        functools.partial(project_kernel, n=n, k=k),
        grid_spec=pltpu.PrefetchScalarGridSpec(
            num_scalar_prefetch=1,
            grid=(n,),
            in_specs=[pl.BlockSpec((rows, width), whole)] * n
            + [pl.BlockSpec((batch, width), whole)] * (k - 1)
            + [pl.BlockSpec((width, columns), weight_map(i)) for i in range(k)],
            out_specs=out_specs,
        ),
        out_shape=out_shape,
        compiler_params=pltpu.CompilerParams(vmem_limit_bytes=VMEM_BYTES),
        cost_estimate=pl.CostEstimate(
            flops=2 * batch * k * width * n * columns,
            bytes_accessed=2 * k * width * (batch + n * columns) + 3 * n * batch * columns,
            transcendentals=0,
        ),
        name="project",
    )(place_array, *met, *others, *([weight] * k))
    return outs[0], list(zip(outs[1::2], outs[2::2]))


def normalize_kernel(place_ref, *refs, n, k, turn, second):
    own_ref, parts = refs[0], refs[1 : 2 * n - 1]
    refs = refs[2 * n - 1 :]
    if second:
        other_ref, refs = refs[0], refs[1:]
    norm_ref, packed_ref, scale_ref = refs[:3]
    grams = refs[3 : 3 + k]
    batch, columns = own_ref.shape
    height = batch // SHARED
    met = [[own_ref[i * height : (i + 1) * height] for i in range(SHARED)]]
    for step in range(1, n):
        met.append(decode(parts[2 * step - 2][...], parts[2 * step - 1][...]))
    blocks = [tree_sum([met[step][i] for step in range(n)]) for i in range(SHARED)]
    total = tree_sum([jnp.sum(block, 0, keepdims=True) for block in blocks])
    squares = tree_sum([jnp.sum(block * block, 0, keepdims=True) for block in blocks])
    mean = total / batch
    scale = lax.rsqrt(squares / batch - mean * mean + bn_eps)
    scale_ref[...] = scale
    rows = batch // n
    per_row = SHARED // n
    for i, block in enumerate(blocks):
        step, part = i // per_row, i % per_row
        at = (place_ref[1] ^ step ^ turn[part * 2 // per_row]) * rows + part * height
        at = pl.multiple_of(at, height)
        normed = (block - mean) * scale
        norm_ref[pl.ds(at, height), :] = normed
        packed_ref[pl.ds(at, height), :] = normed.astype(BF16)
    dims = (((1,), (1,)), ((), ()))
    packed = packed_ref[...]
    size = batch // k
    for i in range(k):
        at = pl.multiple_of((place_ref[2] ^ i) * size, size)
        gram = lax.dot_general(packed_ref[pl.ds(at, size), :], packed, dims, preferred_element_type=F32)
        grams[i][...] = gram
    if second:
        coeff_ref = refs[3 + k]
        diag = jnp.sum(norm_ref[...] * other_ref[...], 0, keepdims=True) / batch
        coeff_ref[...] = 2.0 * ((1.0 - off_weight) * diag - 1.0)
        share = jnp.sum((1.0 - diag) ** 2 - off_weight * diag * diag, 1, keepdims=True)
        for i in range(k):

            @pl.when((place_ref[2] ^ i) == k - 1)
            def _():
                row = grams[i][size - 8 :, :128]
                first = (lax.broadcasted_iota(jnp.int32, row.shape, 0) == 7) & (
                    lax.broadcasted_iota(jnp.int32, row.shape, 1) == 0
                )
                grams[i][size - 8 :, :128] = jnp.where(first, share, row)


def vector(dims):
    return pl.BlockSpec(memory_space=pltpu.VMEM)


def normalize_parts(place, place_array, own, parts, turn, other=None):
    n, k = place.n, place.k
    batch, columns = own.shape
    second = other is not None
    out_shape = [
        jax.ShapeDtypeStruct((batch, columns), F32),
        jax.ShapeDtypeStruct((batch, columns), BF16),
        jax.ShapeDtypeStruct((1, columns), F32),
    ] + [jax.ShapeDtypeStruct((batch // k, batch), F32)] * k
    if second:
        out_shape.append(jax.ShapeDtypeStruct((1, columns), F32))
    args = [own] + [ref for pair in parts for ref in pair] + ([other] if second else [])
    space = pl.BlockSpec(memory_space=pltpu.VMEM)
    return pl.pallas_call(
        functools.partial(normalize_kernel, n=n, k=k, turn=turn, second=second),
        in_specs=[pl.BlockSpec(memory_space=pltpu.SMEM)] + [space] * len(args),
        out_specs=[space] * len(out_shape),
        out_shape=out_shape,
        compiler_params=pltpu.CompilerParams(vmem_limit_bytes=VMEM_BYTES),
        cost_estimate=pl.CostEstimate(
            flops=2 * batch * batch * columns,
            bytes_accessed=16 * batch * columns + 4 * batch * batch,
            transcendentals=0,
        ),
        name="normalize",
    )(place_array, *args)


def gradient_kernel(place_ref, *refs, n, last, squares):
    gram_ref, packed_ref, norm_ref, other_ref, scale_ref, coeff_ref = refs[:6]
    refs = refs[6:]
    if last:
        first_ref, refs = refs[0], refs[1:]
    outs, whole_ref = refs[:n], refs[-1]
    batch, columns = norm_ref.shape
    gram = gram_ref[...]
    if last:
        edge = batch - 128
        tail = gram[edge:, :128]
        row = lax.broadcasted_iota(jnp.int32, tail.shape, 0)
        column = lax.broadcasted_iota(jnp.int32, tail.shape, 1)
        taken = (row == 127) & (column < 3)
        mirror = gram[:128, edge:].astype(F32).T
        share = jnp.sum(jnp.where(taken, tail.astype(F32), 0.0), keepdims=True)
        fixed = jnp.where(taken, mirror, tail.astype(F32)).astype(BF16)
        gram = jnp.concatenate(
            [gram[:edge], jnp.concatenate([fixed, gram[edge:, 128:]], 1)], 0
        )
        frob = jnp.sum(gram.astype(F32) * first_ref[...].astype(F32), keepdims=True)
        refs[n][...] = (share + off_weight * (frob / (batch * batch))) / D
    factor = 2.0 * off_weight / batch
    norm = norm_ref[...]
    grad = (
        factor * jnp.dot(gram, packed_ref[...], preferred_element_type=F32)
        + coeff_ref[...] * other_ref[...]
    )
    first = jnp.sum(grad, 0, keepdims=True) / batch
    second = jnp.sum(grad * norm, 0, keepdims=True) / batch
    whole_ref[...] = (scale_ref[...] * (grad - first - norm * second)).astype(BF16)
    rows = batch // n
    for step in range(n):
        at = pl.multiple_of((place_ref[0] ^ step) * rows, rows)
        outs[step][...] = whole_ref[pl.ds(at, rows), :]


def gradient(place, place_array, gram, packed, norm, other, scale, coeff, first=None):
    n = place.n
    batch, columns = norm.shape
    last = first is not None
    out_shape = [jax.ShapeDtypeStruct((batch // n, columns), BF16)] * n
    if last:
        out_shape.append(jax.ShapeDtypeStruct((1, 1), F32))
    args = [gram, packed, norm, other, scale, coeff] + ([first] if last else [])
    space = pl.BlockSpec(memory_space=pltpu.VMEM)
    return pl.pallas_call(
        functools.partial(gradient_kernel, n=n, last=last, squares=0),
        in_specs=[pl.BlockSpec(memory_space=pltpu.SMEM)] + [space] * len(args),
        out_specs=[space] * len(out_shape),
        out_shape=out_shape,
        scratch_shapes=[pltpu.VMEM((batch, columns), BF16)],
        compiler_params=pltpu.CompilerParams(vmem_limit_bytes=VMEM_BYTES),
        cost_estimate=pl.CostEstimate(
            flops=2 * batch * batch * columns,
            bytes_accessed=14 * batch * columns + 2 * batch * batch,
            transcendentals=0,
        ),
        name="gradient",
    )(place_array, *args)


def with_kernels(place, h_first, h_second, weight):
    n, k, z, a, b = place.n, place.k, place.z, place.a, place.b
    place_array = jnp.stack([z, a, b]).astype(jnp.int32)
    turns = ((0, n - 1), (1, n - 2))
    sent = []
    for values, turn in ((h_first, turns[0]), (h_second, turns[1])):
        met = met_rows(place, values, turn)
        own = jnp.concatenate(met, 0)
        others = [
            place.send(own, lambda z, a, b, s=step: (z, a, b ^ s)) for step in range(1, k)
        ]
        total, pairs = project(place, place_array, met, others, weight)
        pairs = [
            tuple(
                place.send(part, lambda z, a, b, s=step + 1: (z ^ s, a, b)) for part in pair
            )
            for step, pair in enumerate(pairs)
        ]
        sent.append((total, pairs))

    def halves(grams):
        part = grams[0]
        for step in range(1, k):
            part = part + place.send(grams[step], lambda z, a, b, s=step: (z, a, b ^ s))
        return part

    norm_1, packed_1, scale_1, *grams = normalize_parts(
        place, place_array, *sent[0], turns[0]
    )
    gram_1 = rounded_gram(place, halves(grams), False)
    (total, pairs), gram_1 = lax.optimization_barrier((sent[1], gram_1))
    norm_2, packed_2, scale_2, *grams, coeff = normalize_parts(
        place, place_array, total, pairs, turns[1], norm_1
    )
    gram_2 = rounded_gram(place, halves(grams), True)
    parts_2 = gradient(place, place_array, gram_1, packed_2, norm_2, norm_1, scale_2, coeff)
    *parts_1, loss = gradient(
        place, place_array, gram_2, packed_1, norm_1, norm_2, scale_1, coeff, gram_1
    )
    outs = []
    for parts in (parts_1, parts_2):
        met = [parts[0]] + [
            place.send(parts[step], lambda z, a, b, s=step: (z ^ s, a, b)) for step in range(1, n)
        ]
        outs.append(jnp.concatenate(ordered(met, z), 1))
    return (outs[0], outs[1], loss.reshape(()))


def plain(place, h_first, h_second, weight):
    n, k, z, a, b = place.n, place.k, place.z, place.a, place.b
    rows, width = h_first.shape
    batch = rows * n
    columns = weight.shape[1] // n
    weight_parts = weight.reshape(k, width, n * columns)
    zs = []
    for values in (h_first, h_second):
        own = jnp.concatenate(met_rows(place, values, (0, 0)), 0)
        total = jnp.dot(own, pick(weight_parts, b), preferred_element_type=F32)
        for step in range(1, k):
            other = place.send(own, lambda z, a, b, s=step: (z, a, b ^ s))
            total += jnp.dot(other, pick(weight_parts, b ^ step), preferred_element_type=F32)
        cut = total.reshape(batch, n, columns).transpose(1, 0, 2)
        whole = tree_sum(exchange(place, "z", cut)).reshape(n, rows, columns)
        zs.append(jnp.concatenate(ordered([whole[i] for i in range(n)], a), 0))
    normed, scales = [], []
    for values in zs:
        mean = jnp.sum(values, 0) / batch
        scale = lax.rsqrt(jnp.sum(values * values, 0) / batch - mean * mean + bn_eps)
        normed.append((values - mean) * scale)
        scales.append(scale)
    diag = jnp.sum(normed[0] * normed[1], 0) / batch
    packed = [values.astype(BF16) for values in normed]
    dims = (((1,), (1,)), ((), ()))
    grams = []
    for values in packed:
        gram = lax.dot_general(values, values, dims, preferred_element_type=F32)
        grams.append(rounded_gram(place, reduce_scatter(place, "b", gram), False))
    frob = jnp.sum(grams[0].astype(F32) * grams[1].astype(F32)) / (batch * batch)
    coeff = 2.0 * ((1.0 - off_weight) * diag - 1.0)
    factor = 2.0 * off_weight / batch
    outs = []
    for view in range(2):
        grad = (
            factor * jnp.dot(grams[1 - view], packed[view], preferred_element_type=F32)
            + coeff * normed[1 - view]
        )
        first = jnp.sum(grad, 0) / batch
        second = jnp.sum(grad * normed[view], 0) / batch
        out = (scales[view] * (grad - first - normed[view] * second)).astype(BF16)
        parts = exchange(place, "z", out.reshape(n, rows, columns))
        outs.append(jnp.concatenate(ordered(parts, z), 1))
    share = jnp.sum((1.0 - diag) ** 2) - off_weight * jnp.sum(diag * diag)
    loss = (lax.psum(share, ("dp", "mp")) + off_weight * frob) / D
    return (outs[0], outs[1], loss)


def per_device(h_first, h_second, weight):
    place = Place()
    columns = weight.shape[1] // place.n
    fits = columns % 128 == 0 and 1 < place.n <= SHARED // 2
    return (with_kernels if fits else plain)(place, h_first, h_second, weight)


def solution(mesh):
    in_specs = (P("dp", "mp"), P("dp", "mp"), P("dp", "mp"))
    out_specs = (P("dp", "mp"), P("dp", "mp"), P())
    return jax.shard_map(
        per_device, mesh=mesh, in_specs=in_specs, out_specs=out_specs, check_vma=False
    )
```

```python
import functools

import jax
import jax.numpy as jnp
from jax import lax
from jax.experimental import pallas as pl
from jax.experimental.pallas import tpu as pltpu
from jax.sharding import PartitionSpec as P

D = 8192


off_weight = 0.0051
bn_eps = 1e-05

F32 = jnp.float32
BF16 = jnp.bfloat16
VMEM_BYTES = 40 * 1024 * 1024
SHARED = 8
LEVELS = 8


class Place:
    def __init__(self):
        self.n = lax.axis_size("dp")
        self.k = lax.axis_size("mp") // self.n
        self.z = lax.axis_index("dp")
        self.a = lax.axis_index("mp") // self.k
        self.b = lax.axis_index("mp") % self.k

    def send(self, value, target):
        n, k = self.n, self.k
        pairs = []
        for z in range(n):
            for a in range(n):
                for b in range(k):
                    to_z, to_a, to_b = target(z, a, b)
                    pairs.append(((z * n + a) * k + b, (to_z * n + to_a) * k + to_b))
        return lax.ppermute(value, ("dp", "mp"), pairs)

    def along(self, axis):
        if axis == "z":
            return self.n, self.z, lambda step: lambda z, a, b: (z ^ step, a, b)
        if axis == "a":
            return self.n, self.a, lambda step: lambda z, a, b: (z, a ^ step, b)
        return self.k, self.b, lambda step: lambda z, a, b: (z, a, b ^ step)


def ordered(parts, place):
    bit = 1
    while bit < len(parts):
        odd = (place & bit) != 0
        parts = [jnp.where(odd, parts[i ^ bit], parts[i]) for i in range(len(parts))]
        bit *= 2
    return parts


def tree_sum(parts):
    while len(parts) > 1:
        parts = [parts[i] + parts[i + 1] for i in range(0, len(parts), 2)]
    return parts[0]


def pick(value, index):
    return lax.dynamic_index_in_dim(value, index, 0, keepdims=False)


def exchange(place, axis, value):
    size, here, toward = place.along(axis)
    return [pick(value, here)] + [
        place.send(pick(value, here ^ step), toward(step)) for step in range(1, size)
    ]


def reduce_scatter(place, axis, value):
    size, here, toward = place.along(axis)
    value = value.reshape((size, value.shape[0] // size) + value.shape[1:])
    return tree_sum(exchange(place, axis, value))


def gather(place, axis, value):
    size, here, toward = place.along(axis)
    parts = [value] + [place.send(value, toward(step)) for step in range(1, size)]
    return jnp.concatenate(ordered(parts, here), 0)


def swap(place, value, split, join):
    return lax.all_to_all(value, "dp", split, join, tiled=True)


def finish_kernel(place_ref, part_ref, out_ref, *, n, k, share):
    total = tree_sum([part_ref[i] for i in range(n)])
    if share:
        last = (place_ref[0] == n - 1) & (place_ref[1] == n - 1) & (place_ref[2] == k - 1)
        row = lax.broadcasted_iota(jnp.int32, total.shape, 0)
        column = lax.broadcasted_iota(jnp.int32, total.shape, 1)
        taken = (row == total.shape[0] - 1) & last
        whole = jnp.sum(jnp.where(taken & (column == 0), total, 0.0), keepdims=True)
        high = whole.astype(BF16).astype(F32)
        middle = (whole - high).astype(BF16).astype(F32)
        three = jnp.where(column == 0, high, jnp.where(column == 1, middle, whole - high - middle))
        total = jnp.where(taken & (column < 3), three, total)
    total = total.astype(BF16)
    for i in range(n):
        out_ref[i] = total


def finish(place, place_array, parts, share):
    space = pl.BlockSpec(memory_space=pltpu.VMEM)
    return pl.pallas_call(
        functools.partial(finish_kernel, n=place.n, k=place.k, share=share),
        in_specs=[pl.BlockSpec(memory_space=pltpu.SMEM), space],
        out_specs=space,
        out_shape=jax.ShapeDtypeStruct(parts.shape, BF16),
        name="finish",
    )(place_array, parts)


def rounded_gram(place, place_array, part, share):
    part = reduce_scatter(place, "a", part)
    height, width = part.shape
    part = part.reshape(place.n, height // place.n, width)
    part = swap(place, finish(place, place_array, swap(place, part, 0, 0), share), 0, 0)
    part = part.reshape(height, width)
    for axis in ("a", "b"):
        part = gather(place, axis, part)
    return part


def plain_gram(place, part):
    for axis in ("b", "a", "z"):
        part = reduce_scatter(place, axis, part)
    part = part.astype(BF16)
    for axis in ("z", "a", "b"):
        part = gather(place, axis, part)
    return part


def spread(place, views):
    n = place.n
    groups = [[a * place.k + b for a in range(n)] for b in range(place.k)]
    rows, width = views[0].shape
    few = rows // n
    values = jnp.stack([view.reshape(n, few, width) for view in views], 1)
    values = values.reshape(n, len(views) * few, width)
    values = lax.all_to_all(values, "mp", 0, 0, axis_index_groups=groups, tiled=True)
    values = swap(place, values, 0, 0).reshape(n, len(views), few, width)
    return [values[:, view].reshape(rows, width) for view in range(len(views))]


def met_rows(place, values):
    size, here, toward = place.along("a")
    return [values] + [place.send(values, toward(step)) for step in range(1, size)]


def project_kernel(place_ref, *refs, n, k):
    met, others = refs[:n], refs[n : n + k - 1]
    weights = refs[n + k - 1 : n + 2 * k - 1]
    own_ref, coarse, fine = refs[n + 2 * k - 1], refs[n + 2 * k : 3 * n + 2 * k - 2 : 2], refs[n + 2 * k + 1 : 3 * n + 2 * k - 2 : 2]
    step = pl.program_id(0)
    total = jnp.dot(
        jnp.concatenate([ref[...] for ref in met], 0), weights[0][...], preferred_element_type=F32
    )
    for ref, part in zip(others, weights[1:]):
        total += jnp.dot(ref[...], part[...], preferred_element_type=F32)

    @pl.when(step == 0)
    def _():
        own_ref[...] = total

    for other in range(1, n):

        @pl.when(step == other)
        def _():
            encode(total, coarse[other - 1], fine[other - 1])


def encode(total, coarse_ref, fine_ref):
    coarse = total.astype(BF16)
    coarse_ref[...] = coarse
    near = coarse.astype(F32)
    ratio = jnp.where(near == 0.0, 0.0, (total - near) / jnp.where(near == 0.0, 1.0, near))
    level = jnp.floor((ratio * 256.0 + 1.0) * (LEVELS / 2))
    level = jnp.clip(level, 0.0, LEVELS - 1.0)
    height = total.shape[0] // SHARED
    word = level[:height]
    for i in range(1, SHARED):
        word = word * float(LEVELS) + level[i * height : (i + 1) * height]
    fine_ref[...] = word


def decode(coarse, fine):
    height = fine.shape[0]
    blocks = []
    for i in reversed(range(SHARED)):
        rest = jnp.floor(fine * (1.0 / LEVELS))
        level = fine - rest * float(LEVELS)
        fine = rest
        near = coarse[i * height : (i + 1) * height].astype(F32)
        blocks.append(near + near * ((level + (0.5 - LEVELS / 2)) * (2.0 / LEVELS / 256.0)))
    return blocks[::-1]


def project(place, place_array, met, others, weight):
    n, k = place.n, place.k
    rows, width = met[0].shape
    batch, columns = rows * n, weight.shape[1] // n
    whole = lambda step, at: (0, 0)

    def weight_map(i):
        return lambda step, at: (at[2] ^ i, at[0] ^ step)

    out_shape = [jax.ShapeDtypeStruct((batch, columns), F32)]
    out_specs = [pl.BlockSpec((batch, columns), whole)]
    for _ in range(1, n):
        out_shape.append(jax.ShapeDtypeStruct((batch, columns), BF16))
        out_specs.append(pl.BlockSpec((batch, columns), whole))
        out_shape.append(jax.ShapeDtypeStruct((batch // SHARED, columns), F32))
        out_specs.append(pl.BlockSpec((batch // SHARED, columns), whole))
    outs = pl.pallas_call(
        functools.partial(project_kernel, n=n, k=k),
        grid_spec=pltpu.PrefetchScalarGridSpec(
            num_scalar_prefetch=1,
            grid=(n,),
            in_specs=[pl.BlockSpec((rows, width), whole)] * n
            + [pl.BlockSpec((batch, width), whole)] * (k - 1)
            + [pl.BlockSpec((width, columns), weight_map(i)) for i in range(k)],
            out_specs=out_specs,
        ),
        out_shape=out_shape,
        compiler_params=pltpu.CompilerParams(vmem_limit_bytes=VMEM_BYTES),
        cost_estimate=pl.CostEstimate(
            flops=2 * batch * k * width * n * columns,
            bytes_accessed=2 * k * width * (batch + n * columns) + 3 * n * batch * columns,
            transcendentals=0,
        ),
        name="project",
    )(place_array, *met, *others, *([weight] * k))
    return outs[0], list(zip(outs[1::2], outs[2::2]))


def normalize_kernel(place_ref, *refs, n, k, second):
    own_ref, parts = refs[0], refs[1 : 2 * n - 1]
    refs = refs[2 * n - 1 :]
    if second:
        other_ref, refs = refs[0], refs[1:]
    norm_ref, packed_ref, scale_ref = refs[:3]
    grams = refs[3 : 3 + k]
    batch, columns = own_ref.shape
    height = batch // SHARED
    met = [[own_ref[i * height : (i + 1) * height] for i in range(SHARED)]]
    for step in range(1, n):
        met.append(decode(parts[2 * step - 2][...], parts[2 * step - 1][...]))
    blocks = [tree_sum([met[step][i] for step in range(n)]) for i in range(SHARED)]
    total = tree_sum([jnp.sum(block, 0, keepdims=True) for block in blocks])
    squares = tree_sum([jnp.sum(block * block, 0, keepdims=True) for block in blocks])
    mean = total / batch
    scale = lax.rsqrt(squares / batch - mean * mean + bn_eps)
    scale_ref[...] = scale
    rows, few = batch // n, batch // (n * n)
    for i, block in enumerate(blocks):
        normed = (block - mean) * scale
        for first in range(0, height, few):
            step, plane = divmod((i * height + first) // few, n)
            at = pl.multiple_of(plane * rows + (place_ref[1] ^ step) * few, few)
            norm_ref[pl.ds(at, few), :] = normed[first : first + few]
            packed_ref[pl.ds(at, few), :] = normed[first : first + few].astype(BF16)
    dims = (((1,), (1,)), ((), ()))
    packed = packed_ref[...]
    size = batch // k
    for i in range(k):
        at = pl.multiple_of((place_ref[2] ^ i) * size, size)
        gram = lax.dot_general(packed_ref[pl.ds(at, size), :], packed, dims, preferred_element_type=F32)
        grams[i][...] = gram
    if second:
        coeff_ref = refs[3 + k]
        diag = jnp.sum(norm_ref[...] * other_ref[...], 0, keepdims=True) / batch
        coeff_ref[...] = 2.0 * ((1.0 - off_weight) * diag - 1.0)
        share = jnp.sum((1.0 - diag) ** 2 - off_weight * diag * diag, 1, keepdims=True)
        for i in range(k):

            @pl.when((place_ref[2] ^ i) == k - 1)
            def _():
                row = grams[i][size - 8 :, :128]
                first = (lax.broadcasted_iota(jnp.int32, row.shape, 0) == 7) & (
                    lax.broadcasted_iota(jnp.int32, row.shape, 1) == 0
                )
                grams[i][size - 8 :, :128] = jnp.where(first, share, row)


def normalize_parts(place, place_array, own, parts, other=None):
    n, k = place.n, place.k
    batch, columns = own.shape
    second = other is not None
    out_shape = [
        jax.ShapeDtypeStruct((batch, columns), F32),
        jax.ShapeDtypeStruct((batch, columns), BF16),
        jax.ShapeDtypeStruct((1, columns), F32),
    ] + [jax.ShapeDtypeStruct((batch // k, batch), F32)] * k
    if second:
        out_shape.append(jax.ShapeDtypeStruct((1, columns), F32))
    args = [own] + [ref for pair in parts for ref in pair] + ([other] if second else [])
    space = pl.BlockSpec(memory_space=pltpu.VMEM)
    return pl.pallas_call(
        functools.partial(normalize_kernel, n=n, k=k, second=second),
        in_specs=[pl.BlockSpec(memory_space=pltpu.SMEM)] + [space] * len(args),
        out_specs=[space] * len(out_shape),
        out_shape=out_shape,
        compiler_params=pltpu.CompilerParams(vmem_limit_bytes=VMEM_BYTES),
        cost_estimate=pl.CostEstimate(
            flops=2 * batch * batch * columns,
            bytes_accessed=16 * batch * columns + 4 * batch * batch,
            transcendentals=0,
        ),
        name="normalize",
    )(place_array, *args)


def gradient_kernel(*refs, n, last):
    gram_ref, packed_ref, norm_ref, other_ref, scale_ref, coeff_ref = refs[:6]
    refs = refs[6:]
    if last:
        first_ref, refs = refs[0], refs[1:]
    out_ref = refs[0]
    batch, columns = norm_ref.shape
    gram = gram_ref[...]
    if last:
        edge = batch - 128
        tail = gram[edge:, :128]
        row = lax.broadcasted_iota(jnp.int32, tail.shape, 0)
        column = lax.broadcasted_iota(jnp.int32, tail.shape, 1)
        taken = (row == 127) & (column < 3)
        mirror = gram[:128, edge:].astype(F32).T
        share = jnp.sum(jnp.where(taken, tail.astype(F32), 0.0), keepdims=True)
        fixed = jnp.where(taken, mirror, tail.astype(F32)).astype(BF16)
        gram = jnp.concatenate(
            [gram[:edge], jnp.concatenate([fixed, gram[edge:, 128:]], 1)], 0
        )
        frob = jnp.sum(gram.astype(F32) * first_ref[...].astype(F32), keepdims=True)
        refs[1][...] = (share + off_weight * (frob / (batch * batch))) / D
    factor = 2.0 * off_weight / batch
    norm = norm_ref[...]
    grad = (
        factor * jnp.dot(gram, packed_ref[...], preferred_element_type=F32)
        + coeff_ref[...] * other_ref[...]
    )
    first = jnp.sum(grad, 0, keepdims=True) / batch
    second = jnp.sum(grad * norm, 0, keepdims=True) / batch
    out_ref[...] = (scale_ref[...] * (grad - first - norm * second)).astype(BF16)


def gradient(place, gram, packed, norm, other, scale, coeff, first=None):
    n = place.n
    batch, columns = norm.shape
    last = first is not None
    out_shape = [jax.ShapeDtypeStruct((batch, columns), BF16)]
    if last:
        out_shape.append(jax.ShapeDtypeStruct((1, 1), F32))
    args = [gram, packed, norm, other, scale, coeff] + ([first] if last else [])
    space = pl.BlockSpec(memory_space=pltpu.VMEM)
    return pl.pallas_call(
        functools.partial(gradient_kernel, n=n, last=last),
        in_specs=[space] * len(args),
        out_specs=[space] * len(out_shape),
        out_shape=out_shape,
        compiler_params=pltpu.CompilerParams(vmem_limit_bytes=VMEM_BYTES),
        cost_estimate=pl.CostEstimate(
            flops=2 * batch * batch * columns,
            bytes_accessed=14 * batch * columns + 2 * batch * batch,
            transcendentals=0,
        ),
        name="gradient",
    )(*args)


def with_kernels(place, h_first, h_second, weight):
    n, k, z, a, b = place.n, place.k, place.z, place.a, place.b
    place_array = jnp.stack([z, a, b]).astype(jnp.int32)
    both = spread(place, (h_first, h_second))

    def projected(values):
        met = met_rows(place, values)
        own = jnp.concatenate(met, 0)
        others = [
            place.send(own, lambda z, a, b, s=step: (z, a, b ^ s)) for step in range(1, k)
        ]
        return project(place, place_array, met, others, weight)

    def sent(pairs):
        return [
            tuple(
                place.send(part, lambda z, a, b, s=step + 1: (z ^ s, a, b)) for part in pair
            )
            for step, pair in enumerate(pairs)
        ]

    def halves(grams):
        part = grams[0]
        for step in range(1, k):
            part = part + place.send(grams[step], lambda z, a, b, s=step: (z, a, b ^ s))
        return part

    own_1, pairs_1 = projected(both[0])
    pairs_1 = sent(pairs_1)
    own_2, pairs_2 = projected(both[1])
    own_1, pairs_1, own_2, pairs_2 = lax.optimization_barrier((own_1, pairs_1, own_2, pairs_2))
    pairs_2 = sent(pairs_2)
    norm_1, packed_1, scale_1, *grams = normalize_parts(place, place_array, own_1, pairs_1)
    gram_1 = rounded_gram(place, place_array, halves(grams), False)
    own_2, pairs_2, gram_1 = lax.optimization_barrier((own_2, pairs_2, gram_1))
    norm_2, packed_2, scale_2, *grams, coeff = normalize_parts(
        place, place_array, own_2, pairs_2, norm_1
    )
    gram_2 = rounded_gram(place, place_array, halves(grams), True)
    (out_2,) = gradient(place, gram_1, packed_2, norm_2, norm_1, scale_2, coeff)
    out_1, loss = gradient(place, gram_2, packed_1, norm_1, norm_2, scale_1, coeff, gram_1)
    return (swap(place, out_1, 0, 1), swap(place, out_2, 0, 1), loss.reshape(()))


def plain(place, h_first, h_second, weight):
    n, k, z, a, b = place.n, place.k, place.z, place.a, place.b
    rows, width = h_first.shape
    batch = rows * n
    columns = weight.shape[1] // n
    weight_parts = weight.reshape(k, width, n * columns)
    zs = []
    for values in (h_first, h_second):
        moved = place.send(values, lambda z, a, b: (a, z, b))
        own = jnp.concatenate(met_rows(place, moved), 0)
        total = jnp.dot(own, pick(weight_parts, b), preferred_element_type=F32)
        for step in range(1, k):
            other = place.send(own, lambda z, a, b, s=step: (z, a, b ^ s))
            total += jnp.dot(other, pick(weight_parts, b ^ step), preferred_element_type=F32)
        cut = total.reshape(batch, n, columns).transpose(1, 0, 2)
        whole = tree_sum(exchange(place, "z", cut)).reshape(n, rows, columns)
        zs.append(jnp.concatenate(ordered([whole[i] for i in range(n)], a), 0))
    normed, scales = [], []
    for values in zs:
        mean = jnp.sum(values, 0) / batch
        scale = lax.rsqrt(jnp.sum(values * values, 0) / batch - mean * mean + bn_eps)
        normed.append((values - mean) * scale)
        scales.append(scale)
    diag = jnp.sum(normed[0] * normed[1], 0) / batch
    packed = [values.astype(BF16) for values in normed]
    dims = (((1,), (1,)), ((), ()))
    grams = []
    for values in packed:
        gram = lax.dot_general(values, values, dims, preferred_element_type=F32)
        grams.append(plain_gram(place, gram))
    frob = jnp.sum(grams[0].astype(F32) * grams[1].astype(F32)) / (batch * batch)
    coeff = 2.0 * ((1.0 - off_weight) * diag - 1.0)
    factor = 2.0 * off_weight / batch
    outs = []
    for view in range(2):
        grad = (
            factor * jnp.dot(grams[1 - view], packed[view], preferred_element_type=F32)
            + coeff * normed[1 - view]
        )
        first = jnp.sum(grad, 0) / batch
        second = jnp.sum(grad * normed[view], 0) / batch
        out = (scales[view] * (grad - first - normed[view] * second)).astype(BF16)
        parts = exchange(place, "z", out.reshape(n, rows, columns))
        outs.append(jnp.concatenate(ordered(parts, z), 1))
    share = jnp.sum((1.0 - diag) ** 2) - off_weight * jnp.sum(diag * diag)
    loss = (lax.psum(share, ("dp", "mp")) + off_weight * frob) / D
    return (outs[0], outs[1], loss)


def per_device(h_first, h_second, weight):
    place = Place()
    columns = weight.shape[1] // place.n
    fits = columns % 128 == 0 and 1 < place.n <= SHARED // 2
    return (with_kernels if fits else plain)(place, h_first, h_second, weight)


def solution(mesh):
    in_specs = (P("dp", "mp"), P("dp", "mp"), P("dp", "mp"))
    out_specs = (P("dp", "mp"), P("dp", "mp"), P())
    return jax.shard_map(
        per_device, mesh=mesh, in_specs=in_specs, out_specs=out_specs, check_vma=False
    )
```

```python
import functools

import jax
import jax.numpy as jnp
from jax import lax
from jax.experimental import pallas as pl
from jax.experimental.pallas import tpu as pltpu
from jax.sharding import PartitionSpec as P

D = 8192


off_weight = 0.0051
bn_eps = 1e-05

F32 = jnp.float32
BF16 = jnp.bfloat16
VMEM_BYTES = 24 * 1024 * 1024
SHARED = 4
BITS = 3
LEVELS = 1 << BITS


class Place:
    def __init__(self):
        self.n = lax.axis_size("dp")
        self.k = lax.axis_size("mp") // self.n
        self.z = lax.axis_index("dp")
        self.a = lax.axis_index("mp") // self.k
        self.b = lax.axis_index("mp") % self.k

    def send(self, value, target):
        n, k = self.n, self.k
        pairs = []
        for z in range(n):
            for a in range(n):
                for b in range(k):
                    to_z, to_a, to_b = target(z, a, b)
                    pairs.append(((z * n + a) * k + b, (to_z * n + to_a) * k + to_b))
        return lax.ppermute(value, ("dp", "mp"), pairs)

    def along(self, axis):
        if axis == "z":
            return self.n, self.z, lambda step: lambda z, a, b: (z ^ step, a, b)
        if axis == "a":
            return self.n, self.a, lambda step: lambda z, a, b: (z, a ^ step, b)
        return self.k, self.b, lambda step: lambda z, a, b: (z, a, b ^ step)


def ordered(parts, place):
    bit = 1
    while bit < len(parts):
        odd = (place & bit) != 0
        parts = [jnp.where(odd, parts[i ^ bit], parts[i]) for i in range(len(parts))]
        bit *= 2
    return parts


def tree_sum(parts):
    while len(parts) > 1:
        parts = [parts[i] + parts[i + 1] for i in range(0, len(parts), 2)]
    return parts[0]


def pick(value, index):
    return lax.dynamic_index_in_dim(value, index, 0, keepdims=False)


def exchange(place, axis, value, few=False):
    size, here, toward = place.along(axis)
    return sends(place, axis, [pick(value, here ^ step) for step in range(size)], few)


def sends(place, axis, parts, few=False):
    size, here, toward = place.along(axis)
    met = [parts[0]]
    for step in range(1, size):
        part = parts[step]
        if few and step > 2:
            met[step - 2], part = lax.optimization_barrier((met[step - 2], part))
        met.append(place.send(part, toward(step)))
    return met


def reduce_scatter(place, axis, value, few=False):
    size, here, toward = place.along(axis)
    value = value.reshape((size, value.shape[0] // size) + value.shape[1:])
    return tree_sum(exchange(place, axis, value, few))


def gather(place, axis, value, few=False):
    size, here, toward = place.along(axis)
    parts = sends(place, axis, [value] * size, few)
    return jnp.concatenate(ordered(parts, here), 0)


def finish_kernel(place_ref, *refs, n, k, share):
    out_ref = refs[n]
    total = tree_sum([ref[...] for ref in refs[:n]])
    if share:
        last = (place_ref[0] == n - 1) & (place_ref[1] == n - 1) & (place_ref[2] == k - 1)
        edge = total[-8:, :128]
        row = lax.broadcasted_iota(jnp.int32, edge.shape, 0)
        column = lax.broadcasted_iota(jnp.int32, edge.shape, 1)
        taken = (row == 7) & last
        whole = jnp.sum(jnp.where(taken & (column == 0), edge, 0.0), keepdims=True)
        high = whole.astype(BF16).astype(F32)
        middle = (whole - high).astype(BF16).astype(F32)
        three = jnp.where(column == 0, high, jnp.where(column == 1, middle, whole - high - middle))
        edge = jnp.where(taken & (column < 3), three, edge)
        edge = jnp.concatenate([edge, total[-8:, 128:]], 1)
        total = jnp.concatenate([total[:-8], edge], 0)
    out_ref[...] = total.astype(BF16)


def finish(place, place_array, parts, share):
    space = pl.BlockSpec(memory_space=pltpu.VMEM)
    return pl.pallas_call(
        functools.partial(finish_kernel, n=place.n, k=place.k, share=share),
        in_specs=[pl.BlockSpec(memory_space=pltpu.SMEM)] + [space] * place.n,
        out_specs=space,
        out_shape=jax.ShapeDtypeStruct(parts[0].shape, BF16),
        name="finish",
    )(place_array, *parts)


def rounded_gram(place, place_array, part, last):
    few = not last
    part = reduce_scatter(place, "a", part, few)
    height, width = part.shape
    part = part.reshape(place.n, height // place.n, width)
    part = finish(place, place_array, exchange(place, "z", part, few), last)
    for axis in ("z", "a", "b"):
        part = gather(place, axis, part, few)
    return part


def plain_gram(place, part):
    for axis in ("b", "a", "z"):
        part = reduce_scatter(place, axis, part)
    part = part.astype(BF16)
    for axis in ("z", "a", "b"):
        part = gather(place, axis, part)
    return part


def spread(place, views):
    n = place.n
    rows, width = views[0].shape
    few = rows // n
    values = jnp.stack([view.reshape(n, few, width) for view in views], 1)
    values = values.reshape(n, len(views) * few, width)
    parts = ordered(exchange(place, "a", values), place.a ^ place.z)
    parts = ordered(sends(place, "z", parts), place.z)
    return [
        jnp.concatenate([part[view * few : (view + 1) * few] for part in parts], 0)
        for view in range(len(views))
    ]


def met_rows(place, values):
    return sends(place, "a", [values] * place.n)


def project_kernel(place_ref, *refs, n, k):
    met, others = refs[:n], refs[n : n + k - 1]
    weight_ref = refs[n + k - 1]
    own_ref, coded = refs[n + k], refs[n + k + 1 :]
    width = met[0].shape[1]
    columns = own_ref.shape[1]
    own = jnp.concatenate([ref[...] for ref in met], 0)
    for step in [*range(1, n), 0]:
        at = pl.ds(pl.multiple_of((place_ref[0] ^ step) * columns, columns), columns)
        total = 0.0
        for i in range(k):
            rows = pl.ds(pl.multiple_of((place_ref[2] ^ i) * width, width), width)
            values = own if i == 0 else others[i - 1][...]
            total += jnp.dot(values, weight_ref[rows, at], preferred_element_type=F32)
        if step == 0:
            own_ref[...] = total
        else:
            encode(total, coded[step - 1])


def unit(near):
    near = jnp.abs(near)
    return (near * (1.0 + 1.01 / 256.0)).astype(BF16).astype(F32) - near


def encode(total, coded_ref):
    coarse = total.astype(BF16)
    batch = total.shape[0]
    coded_ref[:batch] = coarse
    near = coarse.astype(F32)
    step = unit(near)
    level = (total - near) / jnp.where(step > 0.0, step, 1.0)
    level = jnp.clip(jnp.floor((level + 0.5) * LEVELS), 0.0, LEVELS - 1.0).astype(jnp.int32)
    height = batch // SHARED
    first, second, third, fourth = [level[i * height : (i + 1) * height] for i in range(SHARED)]
    word = 128 + (first << BITS) + second + ((fourth & 1) << 6)
    word = word << (third + ((fourth & 4) << 1))
    word = jnp.where((fourth & 2) != 0, -word, word)
    coded_ref[batch:] = word.astype(F32).astype(BF16)


def decode(coded_ref):
    height = coded_ref.shape[0] // (SHARED + 1)
    word = coded_ref[SHARED * height :].astype(F32).astype(jnp.int32)
    negative = word < 0
    word = jnp.abs(word)
    power = jnp.zeros_like(word)
    for shift in (8, 4, 2, 1):
        large = word >= (128 << shift)
        word = jnp.where(large, word >> shift, word)
        power = power + jnp.where(large, shift, 0)
    levels = [
        (word >> BITS) & (LEVELS - 1),
        word & (LEVELS - 1),
        power & (LEVELS - 1),
        ((word >> 6) & 1) + jnp.where(negative, 2, 0) + ((power >> 3) << 2),
    ]
    blocks = []
    for i, level in enumerate(levels):
        near = coded_ref[i * height : (i + 1) * height].astype(F32)
        offset = (level.astype(F32) + (0.5 - LEVELS / 2)) * (1.0 / LEVELS)
        blocks.append(near + unit(near) * offset)
    return blocks


def project(place, place_array, met, others, weight):
    n, k = place.n, place.k
    rows, width = met[0].shape
    batch, columns = rows * n, weight.shape[1] // n
    coded = batch + batch // SHARED
    out_shape = [jax.ShapeDtypeStruct((batch, columns), F32)]
    out_shape += [jax.ShapeDtypeStruct((coded, columns), BF16)] * (n - 1)
    args = [*met, *others, weight]
    space = pl.BlockSpec(memory_space=pltpu.VMEM)
    own, *parts = pl.pallas_call(
        functools.partial(project_kernel, n=n, k=k),
        in_specs=[pl.BlockSpec(memory_space=pltpu.SMEM)] + [space] * len(args),
        out_specs=[space] * n,
        out_shape=out_shape,
        compiler_params=pltpu.CompilerParams(vmem_limit_bytes=VMEM_BYTES),
        cost_estimate=pl.CostEstimate(
            flops=2 * batch * k * width * n * columns,
            bytes_accessed=2 * k * width * (batch + n * columns) + 3 * n * batch * columns,
            transcendentals=0,
        ),
        name="project",
    )(place_array, *args)
    return own, parts


def normalize_kernel(place_ref, *refs, n, k, second):
    own_ref, parts = refs[0], refs[1:n]
    refs = refs[n:]
    if second:
        other_ref, refs = refs[0], refs[1:]
    norm_ref, packed_ref, scale_ref = refs[:3]
    grams = refs[3 : 3 + k]
    batch, columns = own_ref.shape
    height = batch // SHARED
    met = [[own_ref[i * height : (i + 1) * height] for i in range(SHARED)]]
    for step in range(1, n):
        met.append(decode(parts[step - 1]))
    blocks = [tree_sum([met[step][i] for step in range(n)]) for i in range(SHARED)]
    total = tree_sum([jnp.sum(block, 0, keepdims=True) for block in blocks])
    squares = tree_sum([jnp.sum(block * block, 0, keepdims=True) for block in blocks])
    mean = total / batch
    scale = lax.rsqrt(squares / batch - mean * mean + bn_eps)
    scale_ref[...] = scale
    rows, few = batch // n, batch // (n * n)
    for i, block in enumerate(blocks):
        normed = (block - mean) * scale
        for first in range(0, height, few):
            step, plane = divmod((i * height + first) // few, n)
            at = pl.multiple_of(plane * rows + (place_ref[1] ^ step) * few, few)
            norm_ref[pl.ds(at, few), :] = normed[first : first + few]
            packed_ref[pl.ds(at, few), :] = normed[first : first + few].astype(BF16)
    dims = (((1,), (1,)), ((), ()))
    packed = packed_ref[...]
    size = batch // k
    for i in range(k):
        at = pl.multiple_of((place_ref[2] ^ i) * size, size)
        gram = lax.dot_general(packed_ref[pl.ds(at, size), :], packed, dims, preferred_element_type=F32)
        grams[i][...] = gram
    if second:
        coeff_ref = refs[3 + k]
        diag = jnp.sum(norm_ref[...] * other_ref[...], 0, keepdims=True) / batch
        coeff_ref[...] = 2.0 * ((1.0 - off_weight) * diag - 1.0)
        share = jnp.sum((1.0 - diag) ** 2 - off_weight * diag * diag, 1, keepdims=True)
        for i in range(k):

            @pl.when((place_ref[2] ^ i) == k - 1)
            def _():
                row = grams[i][size - 8 :, :128]
                first = (lax.broadcasted_iota(jnp.int32, row.shape, 0) == 7) & (
                    lax.broadcasted_iota(jnp.int32, row.shape, 1) == 0
                )
                grams[i][size - 8 :, :128] = jnp.where(first, share, row)


def normalize_parts(place, place_array, own, parts, other=None):
    n, k = place.n, place.k
    batch, columns = own.shape
    second = other is not None
    out_shape = [
        jax.ShapeDtypeStruct((batch, columns), F32),
        jax.ShapeDtypeStruct((batch, columns), BF16),
        jax.ShapeDtypeStruct((1, columns), F32),
    ] + [jax.ShapeDtypeStruct((batch // k, batch), F32)] * k
    if second:
        out_shape.append(jax.ShapeDtypeStruct((1, columns), F32))
    args = [own, *parts] + ([other] if second else [])
    space = pl.BlockSpec(memory_space=pltpu.VMEM)
    return pl.pallas_call(
        functools.partial(normalize_kernel, n=n, k=k, second=second),
        in_specs=[pl.BlockSpec(memory_space=pltpu.SMEM)] + [space] * len(args),
        out_specs=[space] * len(out_shape),
        out_shape=out_shape,
        compiler_params=pltpu.CompilerParams(vmem_limit_bytes=VMEM_BYTES),
        cost_estimate=pl.CostEstimate(
            flops=2 * batch * batch * columns,
            bytes_accessed=16 * batch * columns + 4 * batch * batch,
            transcendentals=0,
        ),
        name="normalize",
    )(place_array, *args)


def gradient_kernel(place_ref, *refs, n, last):
    gram_ref, packed_ref, norm_ref, other_ref, scale_ref, coeff_ref = refs[:6]
    refs = refs[6:]
    if last:
        first_ref, refs = refs[0], refs[1:]
    outs, whole_ref = refs[:n], refs[-1]
    batch, columns = norm_ref.shape
    gram = gram_ref[...]
    if last:
        edge = batch - 128
        tail = gram[edge:, :128]
        row = lax.broadcasted_iota(jnp.int32, tail.shape, 0)
        column = lax.broadcasted_iota(jnp.int32, tail.shape, 1)
        taken = (row == 127) & (column < 3)
        mirror = gram[:128, edge:].astype(F32).T
        share = jnp.sum(jnp.where(taken, tail.astype(F32), 0.0), keepdims=True)
        fixed = jnp.where(taken, mirror, tail.astype(F32)).astype(BF16)
        gram = jnp.concatenate(
            [gram[:edge], jnp.concatenate([fixed, gram[edge:, 128:]], 1)], 0
        )
        frob = jnp.sum(gram.astype(F32) * first_ref[...].astype(F32), keepdims=True)
        refs[n][...] = (share + off_weight * (frob / (batch * batch))) / D
    factor = 2.0 * off_weight / batch
    norm = norm_ref[...]
    grad = (
        factor * jnp.dot(gram, packed_ref[...], preferred_element_type=F32)
        + coeff_ref[...] * other_ref[...]
    )
    first = jnp.sum(grad, 0, keepdims=True) / batch
    second = jnp.sum(grad * norm, 0, keepdims=True) / batch
    whole_ref[...] = (scale_ref[...] * (grad - first - norm * second)).astype(BF16)
    rows = batch // n
    for step in range(n):
        at = pl.multiple_of((place_ref[0] ^ step) * rows, rows)
        outs[step][...] = whole_ref[pl.ds(at, rows), :]


def gradient(place, place_array, gram, packed, norm, other, scale, coeff, first=None):
    n = place.n
    batch, columns = norm.shape
    last = first is not None
    out_shape = [jax.ShapeDtypeStruct((batch // n, columns), BF16)] * n
    if last:
        out_shape.append(jax.ShapeDtypeStruct((1, 1), F32))
    args = [gram, packed, norm, other, scale, coeff] + ([first] if last else [])
    space = pl.BlockSpec(memory_space=pltpu.VMEM)
    return pl.pallas_call(
        functools.partial(gradient_kernel, n=n, last=last),
        in_specs=[pl.BlockSpec(memory_space=pltpu.SMEM)] + [space] * len(args),
        out_specs=[space] * len(out_shape),
        out_shape=out_shape,
        scratch_shapes=[pltpu.VMEM((batch, columns), BF16)],
        compiler_params=pltpu.CompilerParams(vmem_limit_bytes=VMEM_BYTES),
        cost_estimate=pl.CostEstimate(
            flops=2 * batch * batch * columns,
            bytes_accessed=14 * batch * columns + 2 * batch * batch,
            transcendentals=0,
        ),
        name="gradient",
    )(place_array, *args)


def joined(place, parts):
    return jnp.concatenate(ordered(sends(place, "z", parts), place.z), 1)


def with_kernels(place, h_first, h_second, weight):
    n, k, z, a, b = place.n, place.k, place.z, place.a, place.b
    place_array = jnp.stack([z, a, b]).astype(jnp.int32)
    both = spread(place, (h_first, h_second))

    def projected(values):
        met = met_rows(place, values)
        own = jnp.concatenate(met, 0)
        others = [
            place.send(own, lambda z, a, b, s=step: (z, a, b ^ s)) for step in range(1, k)
        ]
        return project(place, place_array, met, others, weight)

    def halves(grams):
        part = grams[0]
        for step in range(1, k):
            part = part + place.send(grams[step], lambda z, a, b, s=step: (z, a, b ^ s))
        return part

    def sent(parts):
        return sends(place, "z", [parts[0], *parts])[1:]

    own_1, parts_1 = projected(both[0])
    parts_1 = sent(parts_1)
    own_2, parts_2 = projected(both[1])
    own_1, parts_1, own_2, parts_2 = lax.optimization_barrier((own_1, parts_1, own_2, parts_2))
    parts_2 = sent(parts_2)
    norm_1, packed_1, scale_1, *grams = normalize_parts(place, place_array, own_1, parts_1)
    gram_1 = rounded_gram(place, place_array, halves(grams), False)
    own_2, parts_2, gram_1 = lax.optimization_barrier((own_2, parts_2, gram_1))
    norm_2, packed_2, scale_2, *grams, coeff = normalize_parts(
        place, place_array, own_2, parts_2, norm_1
    )
    grads_2 = gradient(
        place, place_array, gram_1, packed_2, norm_2, norm_1, scale_2, coeff
    )
    out_2 = joined(place, grads_2)
    gram_2 = rounded_gram(place, place_array, halves(grams), True)
    *grads_1, loss = gradient(
        place, place_array, gram_2, packed_1, norm_1, norm_2, scale_1, coeff, gram_1
    )
    return (joined(place, grads_1), out_2, loss.reshape(()))


def plain(place, h_first, h_second, weight):
    n, k, z, a, b = place.n, place.k, place.z, place.a, place.b
    rows, width = h_first.shape
    batch = rows * n
    columns = weight.shape[1] // n
    weight_parts = weight.reshape(k, width, n * columns)
    zs = []
    for values in (h_first, h_second):
        moved = place.send(values, lambda z, a, b: (a, z, b))
        own = jnp.concatenate(met_rows(place, moved), 0)
        total = jnp.dot(own, pick(weight_parts, b), preferred_element_type=F32)
        for step in range(1, k):
            other = place.send(own, lambda z, a, b, s=step: (z, a, b ^ s))
            total += jnp.dot(other, pick(weight_parts, b ^ step), preferred_element_type=F32)
        cut = total.reshape(batch, n, columns).transpose(1, 0, 2)
        whole = tree_sum(exchange(place, "z", cut)).reshape(n, rows, columns)
        zs.append(jnp.concatenate(ordered([whole[i] for i in range(n)], a), 0))
    normed, scales = [], []
    for values in zs:
        mean = jnp.sum(values, 0) / batch
        scale = lax.rsqrt(jnp.sum(values * values, 0) / batch - mean * mean + bn_eps)
        normed.append((values - mean) * scale)
        scales.append(scale)
    diag = jnp.sum(normed[0] * normed[1], 0) / batch
    packed = [values.astype(BF16) for values in normed]
    dims = (((1,), (1,)), ((), ()))
    grams = []
    for values in packed:
        gram = lax.dot_general(values, values, dims, preferred_element_type=F32)
        grams.append(plain_gram(place, gram))
    frob = jnp.sum(grams[0].astype(F32) * grams[1].astype(F32)) / (batch * batch)
    coeff = 2.0 * ((1.0 - off_weight) * diag - 1.0)
    factor = 2.0 * off_weight / batch
    outs = []
    for view in range(2):
        grad = (
            factor * jnp.dot(grams[1 - view], packed[view], preferred_element_type=F32)
            + coeff * normed[1 - view]
        )
        first = jnp.sum(grad, 0) / batch
        second = jnp.sum(grad * normed[view], 0) / batch
        out = (scales[view] * (grad - first - normed[view] * second)).astype(BF16)
        parts = exchange(place, "z", out.reshape(n, rows, columns))
        outs.append(jnp.concatenate(ordered(parts, z), 1))
    share = jnp.sum((1.0 - diag) ** 2) - off_weight * jnp.sum(diag * diag)
    loss = (lax.psum(share, ("dp", "mp")) + off_weight * frob) / D
    return (outs[0], outs[1], loss)


def per_device(h_first, h_second, weight):
    place = Place()
    columns = weight.shape[1] // place.n
    fits = columns % 128 == 0 and place.n == SHARED
    return (with_kernels if fits else plain)(place, h_first, h_second, weight)


def solution(mesh):
    in_specs = (P("dp", "mp"), P("dp", "mp"), P("dp", "mp"))
    out_specs = (P("dp", "mp"), P("dp", "mp"), P())
    return jax.shard_map(
        per_device, mesh=mesh, in_specs=in_specs, out_specs=out_specs, check_vma=False
    )
```

```python
import functools

import jax
import jax.numpy as jnp
from jax import lax
from jax.experimental import pallas as pl
from jax.experimental.pallas import tpu as pltpu
from jax.sharding import PartitionSpec as P

D = 8192


off_weight = 0.0051
bn_eps = 1e-05

F32 = jnp.float32
BF16 = jnp.bfloat16
VMEM_BYTES = 16 * 1024 * 1024
SHARED = 4
BITS = 3
LEVELS = 1 << BITS


class Place:
    def __init__(self):
        self.n = lax.axis_size("dp")
        self.k = lax.axis_size("mp") // self.n
        self.z = lax.axis_index("dp")
        self.a = lax.axis_index("mp") // self.k
        self.b = lax.axis_index("mp") % self.k

    def send(self, value, target):
        n, k = self.n, self.k
        pairs = []
        for z in range(n):
            for a in range(n):
                for b in range(k):
                    to_z, to_a, to_b = target(z, a, b)
                    pairs.append(((z * n + a) * k + b, (to_z * n + to_a) * k + to_b))
        return lax.ppermute(value, ("dp", "mp"), pairs)

    def along(self, axis):
        if axis == "z":
            return self.n, self.z, lambda step: lambda z, a, b: (z ^ step, a, b)
        if axis == "a":
            return self.n, self.a, lambda step: lambda z, a, b: (z, a ^ step, b)
        return self.k, self.b, lambda step: lambda z, a, b: (z, a, b ^ step)


def ordered(parts, place):
    bit = 1
    while bit < len(parts):
        odd = (place & bit) != 0
        parts = [jnp.where(odd, parts[i ^ bit], parts[i]) for i in range(len(parts))]
        bit *= 2
    return parts


def tree_sum(parts):
    while len(parts) > 1:
        parts = [parts[i] + parts[i + 1] for i in range(0, len(parts), 2)]
    return parts[0]


def pick(value, index):
    return lax.dynamic_index_in_dim(value, index, 0, keepdims=False)


def exchange(place, axis, value, few=False):
    size, here, toward = place.along(axis)
    return sends(place, axis, [pick(value, here ^ step) for step in range(size)], few)


def sends(place, axis, parts, few=False):
    size, here, toward = place.along(axis)
    met = [parts[0]]
    for step in range(1, size):
        part = parts[step]
        if few and step > 2:
            met[step - 2], part = lax.optimization_barrier((met[step - 2], part))
        met.append(place.send(part, toward(step)))
    return met


def reduce_scatter(place, axis, value, few=False):
    size, here, toward = place.along(axis)
    value = value.reshape((size, value.shape[0] // size) + value.shape[1:])
    return tree_sum(exchange(place, axis, value, few))


def gather(place, axis, value, few=False):
    size, here, toward = place.along(axis)
    parts = sends(place, axis, [value] * size, few)
    return jnp.concatenate(ordered(parts, here), 0)


def finish_kernel(place_ref, *refs, n, k, share):
    out_ref = refs[n]
    total = tree_sum([ref[...] for ref in refs[:n]])
    if share:
        last = (place_ref[0] == n - 1) & (place_ref[1] == n - 1) & (place_ref[2] == k - 1)
        edge = total[-8:, :128]
        row = lax.broadcasted_iota(jnp.int32, edge.shape, 0)
        column = lax.broadcasted_iota(jnp.int32, edge.shape, 1)
        taken = (row == 7) & last
        whole = jnp.sum(jnp.where(taken & (column == 0), edge, 0.0), keepdims=True)
        high = whole.astype(BF16).astype(F32)
        middle = (whole - high).astype(BF16).astype(F32)
        three = jnp.where(column == 0, high, jnp.where(column == 1, middle, whole - high - middle))
        edge = jnp.where(taken & (column < 3), three, edge)
        edge = jnp.concatenate([edge, total[-8:, 128:]], 1)
        total = jnp.concatenate([total[:-8], edge], 0)
    out_ref[...] = total.astype(BF16)


def finish(place, place_array, parts, share):
    space = pl.BlockSpec(memory_space=pltpu.VMEM)
    return pl.pallas_call(
        functools.partial(finish_kernel, n=place.n, k=place.k, share=share),
        in_specs=[pl.BlockSpec(memory_space=pltpu.SMEM)] + [space] * place.n,
        out_specs=space,
        out_shape=jax.ShapeDtypeStruct(parts[0].shape, BF16),
        compiler_params=pltpu.CompilerParams(vmem_limit_bytes=VMEM_BYTES // 4),
        name="finish",
    )(place_array, *parts)


def gram_rows(place, place_array, grams, last):
    few = not last
    part = grams[0]
    for step in range(1, place.k):
        part = part + place.send(grams[step], lambda z, a, b, s=step: (z, a, b ^ s))
    part = reduce_scatter(place, "a", part, few)
    height, width = part.shape
    part = part.reshape(place.n, height // place.n, width)
    return finish(place, place_array, exchange(place, "z", part, few), last)


def whole_gram(place, part):
    for axis in ("z", "a", "b"):
        part = gather(place, axis, part)
    return part


def in_one(place, run, args):
    shapes = jax.eval_shape(run, *args)
    return lax.cond(
        place.z < place.n,
        run,
        lambda *args: jax.tree.map(lambda leaf: jnp.zeros(leaf.shape, leaf.dtype), shapes),
        *args,
    )


def plain_gram(place, part):
    for axis in ("b", "a", "z"):
        part = reduce_scatter(place, axis, part)
    part = part.astype(BF16)
    for axis in ("z", "a", "b"):
        part = gather(place, axis, part)
    return part


def spread(place, views):
    n = place.n
    rows, width = views[0].shape
    few = rows // n
    values = jnp.stack([view.reshape(n, few, width) for view in views], 1)
    values = values.reshape(n, len(views) * few, width)
    parts = ordered(exchange(place, "a", values), place.a ^ place.z)
    parts = ordered(sends(place, "z", parts), place.z)
    return [
        jnp.concatenate([part[view * few : (view + 1) * few] for part in parts], 0)
        for view in range(len(views))
    ]


def met_rows(place, values, few=False):
    return sends(place, "a", [values] * place.n, few)


def project_kernel(place_ref, *refs, n, k):
    met, others = refs[:n], refs[n : n + k - 1]
    weight_ref = refs[n + k - 1]
    own_ref, coded = refs[n + k], refs[n + k + 1 : 2 * n + k]
    held_ref, arrived = refs[2 * n + k :]
    width = met[0].shape[1]
    columns = own_ref.shape[1]
    copies = {}
    for step in [*range(1, n), 0]:
        at = pl.ds(pl.multiple_of((place_ref[0] ^ step) * columns, columns), columns)
        copies[step] = pltpu.make_async_copy(
            weight_ref.at[:, at], held_ref.at[step], arrived.at[step]
        )
        copies[step].start()
    own = jnp.concatenate([ref[...] for ref in met], 0)
    for step in [*range(1, n), 0]:
        copies[step].wait()
        total = 0.0
        for i in range(k):
            rows = pl.ds(pl.multiple_of((place_ref[2] ^ i) * width, width), width)
            values = own if i == 0 else others[i - 1][...]
            total += jnp.dot(values, held_ref[step, rows, :], preferred_element_type=F32)
        if step == 0:
            own_ref[...] = total
        else:
            encode(total, coded[step - 1])


def unit(near):
    near = jnp.abs(near)
    return (near * (1.0 + 1.01 / 256.0)).astype(BF16).astype(F32) - near


def encode(total, coded_ref):
    coarse = total.astype(BF16)
    batch = total.shape[0]
    coded_ref[:batch] = coarse
    near = coarse.astype(F32)
    step = unit(near)
    level = (total - near) / jnp.where(step > 0.0, step, 1.0)
    level = jnp.clip(jnp.floor((level + 0.5) * LEVELS), 0.0, LEVELS - 1.0).astype(jnp.int32)
    height = batch // SHARED
    first, second, third, fourth = [level[i * height : (i + 1) * height] for i in range(SHARED)]
    word = 128 + (first << BITS) + second + ((fourth & 1) << 6)
    word = word << (third + ((fourth & 4) << 1))
    word = jnp.where((fourth & 2) != 0, -word, word)
    coded_ref[batch:] = word.astype(F32).astype(BF16)


def decode(coded_ref):
    height = coded_ref.shape[0] // (SHARED + 1)
    word = coded_ref[SHARED * height :].astype(F32).astype(jnp.int32)
    negative = word < 0
    word = jnp.abs(word)
    power = jnp.zeros_like(word)
    for shift in (8, 4, 2, 1):
        large = word >= (128 << shift)
        word = jnp.where(large, word >> shift, word)
        power = power + jnp.where(large, shift, 0)
    levels = [
        (word >> BITS) & (LEVELS - 1),
        word & (LEVELS - 1),
        power & (LEVELS - 1),
        ((word >> 6) & 1) + jnp.where(negative, 2, 0) + ((power >> 3) << 2),
    ]
    blocks = []
    for i, level in enumerate(levels):
        near = coded_ref[i * height : (i + 1) * height].astype(F32)
        offset = (level.astype(F32) + (0.5 - LEVELS / 2)) * (1.0 / LEVELS)
        blocks.append(near + unit(near) * offset)
    return blocks


def project(place, place_array, met, others, weight):
    n, k = place.n, place.k
    rows, width = met[0].shape
    batch, columns = rows * n, weight.shape[1] // n
    coded = batch + batch // SHARED
    out_shape = [jax.ShapeDtypeStruct((batch, columns), F32)]
    out_shape += [jax.ShapeDtypeStruct((coded, columns), BF16)] * (n - 1)
    args = [*met, *others, weight]
    space = pl.BlockSpec(memory_space=pltpu.VMEM)
    own, *parts = pl.pallas_call(
        functools.partial(project_kernel, n=n, k=k),
        in_specs=[pl.BlockSpec(memory_space=pltpu.SMEM)]
        + [space] * (len(args) - 1)
        + [pl.BlockSpec(memory_space=pl.ANY)],
        out_specs=[space] * n,
        out_shape=out_shape,
        scratch_shapes=[
            pltpu.VMEM((n, k * width, columns), BF16),
            pltpu.SemaphoreType.DMA((n,)),
        ],
        compiler_params=pltpu.CompilerParams(vmem_limit_bytes=VMEM_BYTES),
        cost_estimate=pl.CostEstimate(
            flops=2 * batch * k * width * n * columns,
            bytes_accessed=2 * k * width * (batch + n * columns) + 3 * n * batch * columns,
            transcendentals=0,
        ),
        name="project",
    )(place_array, *args)
    return own, parts


def normalize_kernel(place_ref, *refs, n, k, second):
    own_ref, parts = refs[0], refs[1:n]
    refs = refs[n:]
    if second:
        other_ref, refs = refs[0], refs[1:]
    norm_ref, packed_ref, scale_ref = refs[:3]
    grams = refs[3 : 3 + k]
    batch, columns = own_ref.shape
    height = batch // SHARED
    met = [[own_ref[i * height : (i + 1) * height] for i in range(SHARED)]]
    for step in range(1, n):
        met.append(decode(parts[step - 1]))
    blocks = [tree_sum([met[step][i] for step in range(n)]) for i in range(SHARED)]
    total = tree_sum([jnp.sum(block, 0, keepdims=True) for block in blocks])
    squares = tree_sum([jnp.sum(block * block, 0, keepdims=True) for block in blocks])
    mean = total / batch
    scale = lax.rsqrt(squares / batch - mean * mean + bn_eps)
    scale_ref[...] = scale
    rows, few = batch // n, batch // (n * n)
    for i, block in enumerate(blocks):
        normed = (block - mean) * scale
        for first in range(0, height, few):
            step, plane = divmod((i * height + first) // few, n)
            at = pl.multiple_of(plane * rows + (place_ref[1] ^ step) * few, few)
            norm_ref[pl.ds(at, few), :] = normed[first : first + few]
            packed_ref[pl.ds(at, few), :] = normed[first : first + few].astype(BF16)
    dims = (((1,), (1,)), ((), ()))
    packed = packed_ref[...]
    size = batch // k
    for i in range(k):
        at = pl.multiple_of((place_ref[2] ^ i) * size, size)
        gram = lax.dot_general(packed_ref[pl.ds(at, size), :], packed, dims, preferred_element_type=F32)
        grams[i][...] = gram
    if second:
        coeff_ref = refs[3 + k]
        diag = jnp.sum(norm_ref[...] * other_ref[...], 0, keepdims=True) / batch
        coeff_ref[...] = 2.0 * ((1.0 - off_weight) * diag - 1.0)
        share = jnp.sum((1.0 - diag) ** 2 - off_weight * diag * diag, 1, keepdims=True)
        for i in range(k):

            @pl.when((place_ref[2] ^ i) == k - 1)
            def _():
                row = grams[i][size - 8 :, :128]
                first = (lax.broadcasted_iota(jnp.int32, row.shape, 0) == 7) & (
                    lax.broadcasted_iota(jnp.int32, row.shape, 1) == 0
                )
                grams[i][size - 8 :, :128] = jnp.where(first, share, row)


def normalize_parts(place, place_array, own, parts, other=None):
    n, k = place.n, place.k
    batch, columns = own.shape
    second = other is not None
    out_shape = [
        jax.ShapeDtypeStruct((batch, columns), F32),
        jax.ShapeDtypeStruct((batch, columns), BF16),
        jax.ShapeDtypeStruct((1, columns), F32),
    ] + [jax.ShapeDtypeStruct((batch // k, batch), F32)] * k
    if second:
        out_shape.append(jax.ShapeDtypeStruct((1, columns), F32))
    args = [own, *parts] + ([other] if second else [])
    space = pl.BlockSpec(memory_space=pltpu.VMEM)
    return pl.pallas_call(
        functools.partial(normalize_kernel, n=n, k=k, second=second),
        in_specs=[pl.BlockSpec(memory_space=pltpu.SMEM)] + [space] * len(args),
        out_specs=[space] * len(out_shape),
        out_shape=out_shape,
        compiler_params=pltpu.CompilerParams(vmem_limit_bytes=VMEM_BYTES),
        cost_estimate=pl.CostEstimate(
            flops=2 * batch * batch * columns,
            bytes_accessed=16 * batch * columns + 4 * batch * batch,
            transcendentals=0,
        ),
        name="normalize",
    )(place_array, *args)


def gradient_kernel(place_ref, *refs, n, last):
    gram_ref, packed_ref, norm_ref, other_ref, scale_ref, coeff_ref = refs[:6]
    refs = refs[6:]
    if last:
        first_ref, refs = refs[0], refs[1:]
    outs, whole_ref = refs[:n], refs[-1]
    batch, columns = norm_ref.shape
    gram = gram_ref[...]
    if last:
        edge = batch - 128
        tail = gram[edge:, :128]
        row = lax.broadcasted_iota(jnp.int32, tail.shape, 0)
        column = lax.broadcasted_iota(jnp.int32, tail.shape, 1)
        taken = (row == 127) & (column < 3)
        mirror = gram[:128, edge:].astype(F32).T
        share = jnp.sum(jnp.where(taken, tail.astype(F32), 0.0), keepdims=True)
        fixed = jnp.where(taken, mirror, tail.astype(F32)).astype(BF16)
        gram = jnp.concatenate(
            [gram[:edge], jnp.concatenate([fixed, gram[edge:, 128:]], 1)], 0
        )
        frob = jnp.sum(gram.astype(F32) * first_ref[...].astype(F32), keepdims=True)
        refs[n][...] = (share + off_weight * (frob / (batch * batch))) / D
    factor = 2.0 * off_weight / batch
    norm = norm_ref[...]
    grad = (
        factor * jnp.dot(gram, packed_ref[...], preferred_element_type=F32)
        + coeff_ref[...] * other_ref[...]
    )
    first = jnp.sum(grad, 0, keepdims=True) / batch
    second = jnp.sum(grad * norm, 0, keepdims=True) / batch
    whole_ref[...] = (scale_ref[...] * (grad - first - norm * second)).astype(BF16)
    rows = batch // n
    for step in range(n):
        at = pl.multiple_of((place_ref[0] ^ step) * rows, rows)
        outs[step][...] = whole_ref[pl.ds(at, rows), :]


def gradient(place, place_array, gram, packed, norm, other, scale, coeff, first=None):
    n = place.n
    batch, columns = norm.shape
    last = first is not None
    out_shape = [jax.ShapeDtypeStruct((batch // n, columns), BF16)] * n
    if last:
        out_shape.append(jax.ShapeDtypeStruct((1, 1), F32))
    args = [gram, packed, norm, other, scale, coeff] + ([first] if last else [])
    space = pl.BlockSpec(memory_space=pltpu.VMEM)
    return pl.pallas_call(
        functools.partial(gradient_kernel, n=n, last=last),
        in_specs=[pl.BlockSpec(memory_space=pltpu.SMEM)] + [space] * len(args),
        out_specs=[space] * len(out_shape),
        out_shape=out_shape,
        scratch_shapes=[pltpu.VMEM((batch, columns), BF16)],
        compiler_params=pltpu.CompilerParams(vmem_limit_bytes=VMEM_BYTES),
        cost_estimate=pl.CostEstimate(
            flops=2 * batch * batch * columns,
            bytes_accessed=14 * batch * columns + 2 * batch * batch,
            transcendentals=0,
        ),
        name="gradient",
    )(place_array, *args)


def joined(place, parts):
    return jnp.concatenate(ordered(sends(place, "z", parts), place.z), 1)


def with_kernels(place, h_first, h_second, weight):
    n, k, z, a, b = place.n, place.k, place.z, place.a, place.b
    place_array = jnp.stack([z, a, b]).astype(jnp.int32)
    first, second = spread(place, (h_first, h_second))

    def projected(values, weight, few):
        met = met_rows(place, values, few)
        own = jnp.concatenate(met, 0)
        others = [
            place.send(own, lambda z, a, b, s=step: (z, a, b ^ s)) for step in range(1, k)
        ]
        return project(place, place_array, met, others, weight)

    def sent(parts):
        return sends(place, "z", [parts[0], *parts])[1:]

    own_1, parts_1 = projected(first, weight, False)
    second, own_1 = lax.optimization_barrier((second, own_1))
    parts_1 = sent(parts_1)
    own_2, parts_2 = in_one(
        place, lambda values, weight: projected(values, weight, True), (second, weight)
    )
    own_1, own_2 = lax.optimization_barrier((own_1, own_2))
    parts_2 = sent(parts_2)
    norm_1, packed_1, scale_1, *grams = normalize_parts(place, place_array, own_1, parts_1)
    rows_1 = in_one(place, lambda *grams: gram_rows(place, place_array, grams, False), grams)
    own_2, parts_2, rows_1 = lax.optimization_barrier((own_2, parts_2, rows_1))
    norm_2, packed_2, scale_2, *grams, coeff = normalize_parts(
        place, place_array, own_2, parts_2, norm_1
    )
    gram_1 = whole_gram(place, rows_1)
    grads_2 = gradient(
        place, place_array, gram_1, packed_2, norm_2, norm_1, scale_2, coeff
    )
    rows_2 = gram_rows(place, place_array, grams, True)
    grads_2, rows_2 = lax.optimization_barrier((grads_2, rows_2))
    out_2 = joined(place, grads_2)
    gram_2 = whole_gram(place, rows_2)
    out_2, gram_2 = lax.optimization_barrier((out_2, gram_2))
    *grads_1, loss = gradient(
        place, place_array, gram_2, packed_1, norm_1, norm_2, scale_1, coeff, gram_1
    )
    return (joined(place, grads_1), out_2, loss.reshape(()))


def plain(place, h_first, h_second, weight):
    n, k, z, a, b = place.n, place.k, place.z, place.a, place.b
    rows, width = h_first.shape
    batch = rows * n
    columns = weight.shape[1] // n
    weight_parts = weight.reshape(k, width, n * columns)
    zs = []
    for values in (h_first, h_second):
        moved = place.send(values, lambda z, a, b: (a, z, b))
        own = jnp.concatenate(met_rows(place, moved), 0)
        total = jnp.dot(own, pick(weight_parts, b), preferred_element_type=F32)
        for step in range(1, k):
            other = place.send(own, lambda z, a, b, s=step: (z, a, b ^ s))
            total += jnp.dot(other, pick(weight_parts, b ^ step), preferred_element_type=F32)
        cut = total.reshape(batch, n, columns).transpose(1, 0, 2)
        whole = tree_sum(exchange(place, "z", cut)).reshape(n, rows, columns)
        zs.append(jnp.concatenate(ordered([whole[i] for i in range(n)], a), 0))
    normed, scales = [], []
    for values in zs:
        mean = jnp.sum(values, 0) / batch
        scale = lax.rsqrt(jnp.sum(values * values, 0) / batch - mean * mean + bn_eps)
        normed.append((values - mean) * scale)
        scales.append(scale)
    diag = jnp.sum(normed[0] * normed[1], 0) / batch
    packed = [values.astype(BF16) for values in normed]
    dims = (((1,), (1,)), ((), ()))
    grams = []
    for values in packed:
        gram = lax.dot_general(values, values, dims, preferred_element_type=F32)
        grams.append(plain_gram(place, gram))
    frob = jnp.sum(grams[0].astype(F32) * grams[1].astype(F32)) / (batch * batch)
    coeff = 2.0 * ((1.0 - off_weight) * diag - 1.0)
    factor = 2.0 * off_weight / batch
    outs = []
    for view in range(2):
        grad = (
            factor * jnp.dot(grams[1 - view], packed[view], preferred_element_type=F32)
            + coeff * normed[1 - view]
        )
        first = jnp.sum(grad, 0) / batch
        second = jnp.sum(grad * normed[view], 0) / batch
        out = (scales[view] * (grad - first - normed[view] * second)).astype(BF16)
        parts = exchange(place, "z", out.reshape(n, rows, columns))
        outs.append(jnp.concatenate(ordered(parts, z), 1))
    share = jnp.sum((1.0 - diag) ** 2) - off_weight * jnp.sum(diag * diag)
    loss = (lax.psum(share, ("dp", "mp")) + off_weight * frob) / D
    return (outs[0], outs[1], loss)


def per_device(h_first, h_second, weight):
    place = Place()
    columns = weight.shape[1] // place.n
    fits = columns % 128 == 0 and place.n == SHARED
    return (with_kernels if fits else plain)(place, h_first, h_second, weight)


def solution(mesh):
    in_specs = (P("dp", "mp"), P("dp", "mp"), P("dp", "mp"))
    out_specs = (P("dp", "mp"), P("dp", "mp"), P())
    return jax.shard_map(
        per_device, mesh=mesh, in_specs=in_specs, out_specs=out_specs, check_vma=False
    )
```

```python
import functools

import jax
import jax.numpy as jnp
from jax import lax
from jax.experimental import pallas as pl
from jax.experimental.pallas import tpu as pltpu
from jax.sharding import PartitionSpec as P

D = 8192


off_weight = 0.0051
bn_eps = 1e-05

F32 = jnp.float32
BF16 = jnp.bfloat16
VMEM_BYTES = 16 * 1024 * 1024
SHARED = 4
BITS = 3
LEVELS = 1 << BITS


class Place:
    def __init__(self):
        self.n = lax.axis_size("dp")
        self.k = lax.axis_size("mp") // self.n
        self.z = lax.axis_index("dp")
        self.a = lax.axis_index("mp") // self.k
        self.b = lax.axis_index("mp") % self.k

    def send(self, value, target):
        n, k = self.n, self.k
        pairs = []
        for z in range(n):
            for a in range(n):
                for b in range(k):
                    to_z, to_a, to_b = target(z, a, b)
                    pairs.append(((z * n + a) * k + b, (to_z * n + to_a) * k + to_b))
        return lax.ppermute(value, ("dp", "mp"), pairs)

    def along(self, axis):
        if axis == "z":
            return self.n, self.z, lambda step: lambda z, a, b: (z ^ step, a, b)
        if axis == "a":
            return self.n, self.a, lambda step: lambda z, a, b: (z, a ^ step, b)
        return self.k, self.b, lambda step: lambda z, a, b: (z, a, b ^ step)


def ordered(parts, place):
    bit = 1
    while bit < len(parts):
        odd = (place & bit) != 0
        parts = [jnp.where(odd, parts[i ^ bit], parts[i]) for i in range(len(parts))]
        bit *= 2
    return parts


def tree_sum(parts):
    while len(parts) > 1:
        parts = [parts[i] + parts[i + 1] for i in range(0, len(parts), 2)]
    return parts[0]


def pick(value, index):
    return lax.dynamic_index_in_dim(value, index, 0, keepdims=False)


def exchange(place, axis, value, few=False):
    size, here, toward = place.along(axis)
    return sends(place, axis, [pick(value, here ^ step) for step in range(size)], few)


def sends(place, axis, parts, few=False):
    size, here, toward = place.along(axis)
    met = [parts[0]]
    for step in range(1, size):
        part = parts[step]
        if few and step > 2:
            met[step - 2], part = lax.optimization_barrier((met[step - 2], part))
        met.append(place.send(part, toward(step)))
    return met


def reduce_scatter(place, axis, value, few=False):
    size, here, toward = place.along(axis)
    value = value.reshape((size, value.shape[0] // size) + value.shape[1:])
    return tree_sum(exchange(place, axis, value, few))


def gather(place, axis, value, few=False):
    size, here, toward = place.along(axis)
    parts = sends(place, axis, [value] * size, few)
    return jnp.concatenate(ordered(parts, here), 0)


def finish_kernel(place_ref, *refs, n, k, share):
    out_ref = refs[n]
    total = tree_sum([ref[...] for ref in refs[:n]])
    if share:
        last = (place_ref[0] == n - 1) & (place_ref[1] == n - 1) & (place_ref[2] == k - 1)
        edge = total[-8:, :128]
        row = lax.broadcasted_iota(jnp.int32, edge.shape, 0)
        column = lax.broadcasted_iota(jnp.int32, edge.shape, 1)
        taken = (row == 7) & last
        whole = jnp.sum(jnp.where(taken & (column == 0), edge, 0.0), keepdims=True)
        high = whole.astype(BF16).astype(F32)
        middle = (whole - high).astype(BF16).astype(F32)
        three = jnp.where(column == 0, high, jnp.where(column == 1, middle, whole - high - middle))
        edge = jnp.where(taken & (column < 3), three, edge)
        edge = jnp.concatenate([edge, total[-8:, 128:]], 1)
        total = jnp.concatenate([total[:-8], edge], 0)
    out_ref[...] = total.astype(BF16)


def finish(place, place_array, parts, share):
    space = pl.BlockSpec(memory_space=pltpu.VMEM)
    return pl.pallas_call(
        functools.partial(finish_kernel, n=place.n, k=place.k, share=share),
        in_specs=[pl.BlockSpec(memory_space=pltpu.SMEM)] + [space] * place.n,
        out_specs=space,
        out_shape=jax.ShapeDtypeStruct(parts[0].shape, BF16),
        compiler_params=pltpu.CompilerParams(vmem_limit_bytes=VMEM_BYTES // 4),
        name="finish",
    )(place_array, *parts)


def plane_rows(place, grams, few=False):
    part = grams[0]
    for step in range(1, place.k):
        part = part + place.send(grams[step], lambda z, a, b, s=step: (z, a, b ^ s))
    return reduce_scatter(place, "a", part, few)


def plane_parts(place, part):
    height, width = part.shape
    return exchange(place, "z", part.reshape(place.n, height // place.n, width))


def in_one(place, run, args):
    shapes = jax.eval_shape(run, *args)
    return lax.cond(
        place.z < place.n,
        run,
        lambda *args: jax.tree.map(lambda leaf: jnp.zeros(leaf.shape, leaf.dtype), shapes),
        *args,
    )


def plain_gram(place, part):
    for axis in ("b", "a", "z"):
        part = reduce_scatter(place, axis, part)
    part = part.astype(BF16)
    for axis in ("z", "a", "b"):
        part = gather(place, axis, part)
    return part


def cut_kernel(place_ref, *refs, n):
    views, outs = refs[:-n], refs[-n:]
    few = outs[0].shape[0] // len(views)
    for step in range(n):
        at = pl.ds(pl.multiple_of((place_ref[1] ^ step) * few, few), few)
        for i, view in enumerate(views):
            outs[step][i * few : (i + 1) * few, :] = view[at, :]


def lay_kernel(place_ref, *refs, n):
    parts, outs = refs[:n], refs[n:]
    few = parts[0].shape[0] // len(outs)
    for step in range(n):
        at = pl.ds(pl.multiple_of((place_ref[0] ^ step) * few, few), few)
        for i, out in enumerate(outs):
            out[at, :] = parts[step][i * few : (i + 1) * few, :]


def fetch_kernel(place_ref, weight_ref, held_ref, arrived, *, n, k):
    width, columns = held_ref.shape[1] // k, held_ref.shape[2]
    copies = []
    for step in [*range(1, n), 0]:
        at = pl.ds(pl.multiple_of((place_ref[0] ^ step) * columns, columns), columns)
        for i in range(k):
            rows = pl.ds(pl.multiple_of((place_ref[2] ^ i) * width, width), width)
            copies.append(
                pltpu.make_async_copy(
                    weight_ref.at[rows, at],
                    held_ref.at[step, i * width : (i + 1) * width],
                    arrived.at[step, i],
                )
            )
            copies[-1].start()
    for copy in copies:
        copy.wait()


def local(kernel, place_array, args, shapes, name, spaces=None, **more):
    space = pl.BlockSpec(memory_space=pltpu.VMEM)
    spaces = [space] * len(args) if spaces is None else spaces
    return pl.pallas_call(
        kernel,
        in_specs=[pl.BlockSpec(memory_space=pltpu.SMEM)] + spaces,
        out_specs=[space] * len(shapes),
        out_shape=[jax.ShapeDtypeStruct(shape, dtype) for shape, dtype in shapes],
        name=name,
        **more,
    )(place_array, *args)


def spread(place, place_array, views, weight):
    n, k = place.n, place.k
    rows, width = views[0].shape
    few = rows // n
    limit = pltpu.CompilerParams(vmem_limit_bytes=VMEM_BYTES // 2)
    parts = local(
        functools.partial(cut_kernel, n=n),
        place_array,
        views,
        [((len(views) * few, width), BF16)] * n,
        "cut",
        compiler_params=limit,
    )
    parts = sends(place, "a", parts)
    (held,) = local(
        functools.partial(fetch_kernel, n=n, k=k),
        place_array,
        (weight,),
        [((n, weight.shape[0], weight.shape[1] // n), BF16)],
        "fetch",
        [pl.BlockSpec(memory_space=pl.ANY)],
        scratch_shapes=[pltpu.SemaphoreType.DMA((n, k))],
        compiler_params=limit,
    )
    parts, held = lax.optimization_barrier((parts, held))
    parts = sends(place, "z", ordered(parts, place.a ^ place.z))
    laid = local(
        functools.partial(lay_kernel, n=n),
        place_array,
        parts,
        [((rows, width), BF16)] * len(views),
        "lay",
        compiler_params=limit,
    )
    return laid, held


def met_rows(place, values, few=False):
    return sends(place, "a", [values] * place.n, few)


def project_kernel(*refs, counts, n, k):
    met = refs[: sum(counts)]
    weight_ref, own_ref, *coded = refs[sum(counts) :]
    width = met[0].shape[1]
    values = []
    for count in counts:
        values.append(jnp.concatenate([ref[...] for ref in met[:count]], 0))
        met = met[count:]
    for step in [*range(1, n), 0]:
        total = 0.0
        for i in range(k):
            part = weight_ref[step, i * width : (i + 1) * width, :]
            total += jnp.dot(values[i], part, preferred_element_type=F32)
        if step == 0:
            own_ref[...] = total
        else:
            encode(total, coded[step - 1])


def unit(near):
    near = jnp.abs(near)
    return (near * (1.0 + 1.01 / 256.0)).astype(BF16).astype(F32) - near


def encode(total, coded_ref):
    coarse = total.astype(BF16)
    batch = total.shape[0]
    coded_ref[:batch] = coarse
    near = coarse.astype(F32)
    step = unit(near)
    level = (total - near) / jnp.where(step > 0.0, step, 1.0)
    level = jnp.clip(jnp.floor((level + 0.5) * LEVELS), 0.0, LEVELS - 1.0).astype(jnp.int32)
    height = batch // SHARED
    first, second, third, fourth = [level[i * height : (i + 1) * height] for i in range(SHARED)]
    word = 128 + (first << BITS) + second + ((fourth & 1) << 6)
    word = word << (third + ((fourth & 4) << 1))
    word = jnp.where((fourth & 2) != 0, -word, word)
    coded_ref[batch:] = word.astype(F32).astype(BF16)


def decode(coded_ref):
    height = coded_ref.shape[0] // (SHARED + 1)
    word = coded_ref[SHARED * height :].astype(F32).astype(jnp.int32)
    negative = word < 0
    word = jnp.abs(word)
    power = jnp.zeros_like(word)
    for shift in (8, 4, 2, 1):
        large = word >= (128 << shift)
        word = jnp.where(large, word >> shift, word)
        power = power + jnp.where(large, shift, 0)
    levels = [
        (word >> BITS) & (LEVELS - 1),
        word & (LEVELS - 1),
        power & (LEVELS - 1),
        ((word >> 6) & 1) + jnp.where(negative, 2, 0) + ((power >> 3) << 2),
    ]
    blocks = []
    for i, level in enumerate(levels):
        near = coded_ref[i * height : (i + 1) * height].astype(F32)
        offset = (level.astype(F32) + (0.5 - LEVELS / 2)) * (1.0 / LEVELS)
        blocks.append(near + unit(near) * offset)
    return blocks


def project(place, met, held):
    n, k = place.n, place.k
    rows, width = met[0][0].shape
    batch, columns = rows * n, held.shape[2]
    counts = [len(parts) for parts in met]
    met = [part for parts in met for part in parts]
    coded = batch + batch // SHARED
    out_shape = [jax.ShapeDtypeStruct((batch, columns), F32)]
    out_shape += [jax.ShapeDtypeStruct((coded, columns), BF16)] * (n - 1)
    space = pl.BlockSpec(memory_space=pltpu.VMEM)
    own, *parts = pl.pallas_call(
        functools.partial(project_kernel, counts=counts, n=n, k=k),
        in_specs=[space] * (len(met) + 1),
        out_specs=[space] * n,
        out_shape=out_shape,
        compiler_params=pltpu.CompilerParams(vmem_limit_bytes=VMEM_BYTES),
        cost_estimate=pl.CostEstimate(
            flops=2 * batch * k * width * n * columns,
            bytes_accessed=2 * k * width * (batch + n * columns) + 3 * n * batch * columns,
            transcendentals=0,
        ),
        name="project",
    )(*met, held)
    return own, parts


def normalize_kernel(place_ref, *refs, n, k, second):
    own_ref, parts = refs[0], refs[1:n]
    refs = refs[n:]
    if second:
        other_ref, refs = refs[0], refs[1:]
    norm_ref, packed_ref, scale_ref = refs[:3]
    grams = refs[3 : 3 + k]
    batch, columns = own_ref.shape
    height = batch // SHARED
    met = [[own_ref[i * height : (i + 1) * height] for i in range(SHARED)]]
    for step in range(1, n):
        met.append(decode(parts[step - 1]))
    blocks = [tree_sum([met[step][i] for step in range(n)]) for i in range(SHARED)]
    total = tree_sum([jnp.sum(block, 0, keepdims=True) for block in blocks])
    squares = tree_sum([jnp.sum(block * block, 0, keepdims=True) for block in blocks])
    mean = total / batch
    scale = lax.rsqrt(squares / batch - mean * mean + bn_eps)
    scale_ref[...] = scale
    rows, few = batch // n, batch // (n * n)
    for i, block in enumerate(blocks):
        normed = (block - mean) * scale
        for first in range(0, height, few):
            step, plane = divmod((i * height + first) // few, n)
            at = pl.multiple_of(plane * rows + (place_ref[1] ^ step) * few, few)
            norm_ref[pl.ds(at, few), :] = normed[first : first + few]
            packed_ref[pl.ds(at, few), :] = normed[first : first + few].astype(BF16)
    dims = (((1,), (1,)), ((), ()))
    packed = packed_ref[...]
    size = batch // k
    for i in range(k):
        at = pl.multiple_of((place_ref[2] ^ i) * size, size)
        gram = lax.dot_general(packed_ref[pl.ds(at, size), :], packed, dims, preferred_element_type=F32)
        grams[i][...] = gram
    if second:
        coeff_ref = refs[3 + k]
        diag = jnp.sum(norm_ref[...] * other_ref[...], 0, keepdims=True) / batch
        coeff_ref[...] = 2.0 * ((1.0 - off_weight) * diag - 1.0)
        share = jnp.sum((1.0 - diag) ** 2 - off_weight * diag * diag, 1, keepdims=True)
        for i in range(k):

            @pl.when((place_ref[2] ^ i) == k - 1)
            def _():
                row = grams[i][size - 8 :, :128]
                first = (lax.broadcasted_iota(jnp.int32, row.shape, 0) == 7) & (
                    lax.broadcasted_iota(jnp.int32, row.shape, 1) == 0
                )
                grams[i][size - 8 :, :128] = jnp.where(first, share, row)


def normalize_parts(place, place_array, own, parts, other=None):
    n, k = place.n, place.k
    batch, columns = own.shape
    second = other is not None
    out_shape = [
        jax.ShapeDtypeStruct((batch, columns), F32),
        jax.ShapeDtypeStruct((batch, columns), BF16),
        jax.ShapeDtypeStruct((1, columns), F32),
    ] + [jax.ShapeDtypeStruct((batch // k, batch), F32)] * k
    if second:
        out_shape.append(jax.ShapeDtypeStruct((1, columns), F32))
    args = [own, *parts] + ([other] if second else [])
    space = pl.BlockSpec(memory_space=pltpu.VMEM)
    return pl.pallas_call(
        functools.partial(normalize_kernel, n=n, k=k, second=second),
        in_specs=[pl.BlockSpec(memory_space=pltpu.SMEM)] + [space] * len(args),
        out_specs=[space] * len(out_shape),
        out_shape=out_shape,
        compiler_params=pltpu.CompilerParams(vmem_limit_bytes=VMEM_BYTES // 2),
        cost_estimate=pl.CostEstimate(
            flops=2 * batch * batch * columns,
            bytes_accessed=16 * batch * columns + 4 * batch * batch,
            transcendentals=0,
        ),
        name="normalize",
    )(place_array, *args)


def gradient_kernel(place_ref, *refs, n, last):
    gram_ref, packed_ref, norm_ref, other_ref, scale_ref, coeff_ref = refs[:6]
    refs = refs[6:]
    if last:
        first_ref, refs = refs[0], refs[1:]
    outs, whole_ref = refs[:n], refs[-1]
    batch, columns = norm_ref.shape
    gram = gram_ref[...]
    if last:
        edge = batch - 128
        tail = gram[edge:, :128]
        row = lax.broadcasted_iota(jnp.int32, tail.shape, 0)
        column = lax.broadcasted_iota(jnp.int32, tail.shape, 1)
        taken = (row == 127) & (column < 3)
        mirror = gram[:128, edge:].astype(F32).T
        share = jnp.sum(jnp.where(taken, tail.astype(F32), 0.0), keepdims=True)
        fixed = jnp.where(taken, mirror, tail.astype(F32)).astype(BF16)
        gram = jnp.concatenate(
            [gram[:edge], jnp.concatenate([fixed, gram[edge:, 128:]], 1)], 0
        )
        frob = jnp.sum(gram.astype(F32) * first_ref[...].astype(F32), keepdims=True)
        refs[n][...] = (share + off_weight * (frob / (batch * batch))) / D
    factor = 2.0 * off_weight / batch
    norm = norm_ref[...]
    grad = (
        factor * jnp.dot(gram, packed_ref[...], preferred_element_type=F32)
        + coeff_ref[...] * other_ref[...]
    )
    first = jnp.sum(grad, 0, keepdims=True) / batch
    second = jnp.sum(grad * norm, 0, keepdims=True) / batch
    whole_ref[...] = (scale_ref[...] * (grad - first - norm * second)).astype(BF16)
    rows = batch // n
    for step in range(n):
        at = pl.multiple_of((place_ref[0] ^ step) * rows, rows)
        outs[step][...] = whole_ref[pl.ds(at, rows), :]


def gradient(place, place_array, gram, packed, norm, other, scale, coeff, first=None):
    n = place.n
    batch, columns = norm.shape
    last = first is not None
    out_shape = [jax.ShapeDtypeStruct((batch // n, columns), BF16)] * n
    if last:
        out_shape.append(jax.ShapeDtypeStruct((1, 1), F32))
    args = [gram, packed, norm, other, scale, coeff] + ([first] if last else [])
    space = pl.BlockSpec(memory_space=pltpu.VMEM)
    return pl.pallas_call(
        functools.partial(gradient_kernel, n=n, last=last),
        in_specs=[pl.BlockSpec(memory_space=pltpu.SMEM)] + [space] * len(args),
        out_specs=[space] * len(out_shape),
        out_shape=out_shape,
        scratch_shapes=[pltpu.VMEM((batch, columns), BF16)],
        compiler_params=pltpu.CompilerParams(vmem_limit_bytes=VMEM_BYTES // 2),
        cost_estimate=pl.CostEstimate(
            flops=2 * batch * batch * columns,
            bytes_accessed=14 * batch * columns + 2 * batch * batch,
            transcendentals=0,
        ),
        name="gradient",
    )(place_array, *args)


def with_kernels(place, h_first, h_second, weight):
    n, k, z, a, b = place.n, place.k, place.z, place.a, place.b
    batch = h_first.shape[0] * n
    place_array = jnp.stack([z, a, b]).astype(jnp.int32)
    (first, second), held = spread(place, place_array, (h_first, h_second), weight)

    def projected(values, held, few):
        met = met_rows(place, values, few)
        own = [jnp.concatenate(met, 0)] if few else met
        others = [
            [place.send(part, lambda z, a, b, s=step: (z, a, b ^ s)) for part in own]
            for step in range(1, k)
        ]
        return project(place, [met, *others], held)

    def sent(parts):
        return sends(place, "z", [parts[0], *parts])[1:]

    own_1, parts_1 = projected(first, held, False)
    second, own_1 = lax.optimization_barrier((second, own_1))
    parts_1 = sent(parts_1)
    own_2, parts_2 = in_one(
        place, lambda values, held: projected(values, held, True), (second, held)
    )
    own_1, own_2 = lax.optimization_barrier((own_1, own_2))
    parts_2 = sent(parts_2)
    norm_1, packed_1, scale_1, *grams = normalize_parts(place, place_array, own_1, parts_1)
    rows_1 = in_one(place, lambda *grams: plane_rows(place, grams, True), grams)
    met_1 = plane_parts(place, rows_1)
    own_2, parts_2, met_1 = lax.optimization_barrier((own_2, parts_2, met_1))
    norm_2, packed_2, scale_2, *grams, coeff = normalize_parts(
        place, place_array, own_2, parts_2, norm_1
    )
    met_1, norm_2 = lax.optimization_barrier((met_1, norm_2))
    rows_1 = finish(place, place_array, met_1, False)
    part_2 = grams[0]
    for step in range(1, k):
        part_2 = part_2 + place.send(grams[step], lambda z, a, b, s=step: (z, a, b ^ s))
    height = part_2.shape[0] // n
    met_2 = exchange(place, "a", part_2.reshape(n, height, batch))
    met_1 = sends(place, "z", [rows_1] * n)
    met_1, met_2 = lax.optimization_barrier((met_1, met_2))
    met_2 = plane_parts(place, tree_sum(met_2))
    met_1 = sends(place, "a", [jnp.concatenate(ordered(met_1, z), 0)] * n)
    met_1, met_2 = lax.optimization_barrier((met_1, met_2))
    met_2 = sends(place, "z", [finish(place, place_array, met_2, True)] * n)
    met_1 = sends(place, "b", [jnp.concatenate(ordered(met_1, a), 0)] * k)
    met_1, met_2 = lax.optimization_barrier((met_1, met_2))
    gram_1 = jnp.concatenate(ordered(met_1, b), 0)
    met_2 = sends(place, "a", [jnp.concatenate(ordered(met_2, z), 0)] * n)
    met_1 = gradient(place, place_array, gram_1, packed_2, norm_2, norm_1, scale_2, coeff)
    met_1 = sends(place, "z", met_1)
    met_1, met_2 = lax.optimization_barrier((met_1, met_2))
    met_2 = sends(place, "b", [jnp.concatenate(ordered(met_2, a), 0)] * k)
    out_2 = jnp.concatenate(ordered(met_1, z), 1)
    gram_2 = jnp.concatenate(ordered(met_2, b), 0)
    *met_1, loss = gradient(
        place, place_array, gram_2, packed_1, norm_1, norm_2, scale_1, coeff, gram_1
    )
    out_1 = jnp.concatenate(ordered(sends(place, "z", met_1), z), 1)
    return (out_1, out_2, loss.reshape(()))


def plain(place, h_first, h_second, weight):
    n, k, z, a, b = place.n, place.k, place.z, place.a, place.b
    rows, width = h_first.shape
    batch = rows * n
    columns = weight.shape[1] // n
    weight_parts = weight.reshape(k, width, n * columns)
    zs = []
    for values in (h_first, h_second):
        moved = place.send(values, lambda z, a, b: (a, z, b))
        own = jnp.concatenate(met_rows(place, moved), 0)
        total = jnp.dot(own, pick(weight_parts, b), preferred_element_type=F32)
        for step in range(1, k):
            other = place.send(own, lambda z, a, b, s=step: (z, a, b ^ s))
            total += jnp.dot(other, pick(weight_parts, b ^ step), preferred_element_type=F32)
        cut = total.reshape(batch, n, columns).transpose(1, 0, 2)
        whole = tree_sum(exchange(place, "z", cut)).reshape(n, rows, columns)
        zs.append(jnp.concatenate(ordered([whole[i] for i in range(n)], a), 0))
    normed, scales = [], []
    for values in zs:
        mean = jnp.sum(values, 0) / batch
        scale = lax.rsqrt(jnp.sum(values * values, 0) / batch - mean * mean + bn_eps)
        normed.append((values - mean) * scale)
        scales.append(scale)
    diag = jnp.sum(normed[0] * normed[1], 0) / batch
    packed = [values.astype(BF16) for values in normed]
    dims = (((1,), (1,)), ((), ()))
    grams = []
    for values in packed:
        gram = lax.dot_general(values, values, dims, preferred_element_type=F32)
        grams.append(plain_gram(place, gram))
    frob = jnp.sum(grams[0].astype(F32) * grams[1].astype(F32)) / (batch * batch)
    coeff = 2.0 * ((1.0 - off_weight) * diag - 1.0)
    factor = 2.0 * off_weight / batch
    outs = []
    for view in range(2):
        grad = (
            factor * jnp.dot(grams[1 - view], packed[view], preferred_element_type=F32)
            + coeff * normed[1 - view]
        )
        first = jnp.sum(grad, 0) / batch
        second = jnp.sum(grad * normed[view], 0) / batch
        out = (scales[view] * (grad - first - normed[view] * second)).astype(BF16)
        parts = exchange(place, "z", out.reshape(n, rows, columns))
        outs.append(jnp.concatenate(ordered(parts, z), 1))
    share = jnp.sum((1.0 - diag) ** 2) - off_weight * jnp.sum(diag * diag)
    loss = (lax.psum(share, ("dp", "mp")) + off_weight * frob) / D
    return (outs[0], outs[1], loss)


def per_device(h_first, h_second, weight):
    place = Place()
    columns = weight.shape[1] // place.n
    fits = columns % 128 == 0 and place.n == SHARED
    return (with_kernels if fits else plain)(place, h_first, h_second, weight)


def solution(mesh):
    in_specs = (P("dp", "mp"), P("dp", "mp"), P("dp", "mp"))
    out_specs = (P("dp", "mp"), P("dp", "mp"), P())
    return jax.shard_map(
        per_device, mesh=mesh, in_specs=in_specs, out_specs=out_specs, check_vma=False
    )
```

```python
import functools

import jax
import jax.numpy as jnp
from jax import lax
from jax.experimental import pallas as pl
from jax.experimental.pallas import tpu as pltpu
from jax.sharding import PartitionSpec as P

D = 8192


off_weight = 0.0051
bn_eps = 1e-05

F32 = jnp.float32
BF16 = jnp.bfloat16
VMEM_BYTES = 16 * 1024 * 1024
SHARED = 4
BITS = 3
LEVELS = 1 << BITS


class Place:
    def __init__(self):
        self.n = lax.axis_size("dp")
        self.k = lax.axis_size("mp") // self.n
        self.z = lax.axis_index("dp")
        self.a = lax.axis_index("mp") // self.k
        self.b = lax.axis_index("mp") % self.k

    def send(self, value, target):
        n, k = self.n, self.k
        pairs = []
        for z in range(n):
            for a in range(n):
                for b in range(k):
                    to_z, to_a, to_b = target(z, a, b)
                    pairs.append(((z * n + a) * k + b, (to_z * n + to_a) * k + to_b))
        return lax.ppermute(value, ("dp", "mp"), pairs)

    def along(self, axis):
        if axis == "z":
            return self.n, self.z, lambda step: lambda z, a, b: (z ^ step, a, b)
        if axis == "a":
            return self.n, self.a, lambda step: lambda z, a, b: (z, a ^ step, b)
        return self.k, self.b, lambda step: lambda z, a, b: (z, a, b ^ step)


def ordered(parts, place):
    bit = 1
    while bit < len(parts):
        odd = (place & bit) != 0
        parts = [jnp.where(odd, parts[i ^ bit], parts[i]) for i in range(len(parts))]
        bit *= 2
    return parts


def tree_sum(parts):
    while len(parts) > 1:
        parts = [parts[i] + parts[i + 1] for i in range(0, len(parts), 2)]
    return parts[0]


def pick(value, index):
    return lax.dynamic_index_in_dim(value, index, 0, keepdims=False)


def exchange(place, axis, value, few=False):
    size, here, toward = place.along(axis)
    return sends(place, axis, [pick(value, here ^ step) for step in range(size)], few)


def sends(place, axis, parts, few=False):
    size, here, toward = place.along(axis)
    met = [parts[0]]
    for step in range(1, size):
        part = parts[step]
        if few and step > 2:
            met[step - 2], part = lax.optimization_barrier((met[step - 2], part))
        met.append(place.send(part, toward(step)))
    return met


def reduce_scatter(place, axis, value, few=False):
    size, here, toward = place.along(axis)
    value = value.reshape((size, value.shape[0] // size) + value.shape[1:])
    return tree_sum(exchange(place, axis, value, few))


def gather(place, axis, value, few=False):
    size, here, toward = place.along(axis)
    parts = sends(place, axis, [value] * size, few)
    return jnp.concatenate(ordered(parts, here), 0)


def halve_kernel(place_ref, kept_ref, met_ref, *outs, axis):
    height = outs[0].shape[0]
    for step, out in enumerate(outs):
        at = pl.ds(pl.multiple_of((place_ref[axis] ^ step) * height, height), height)
        out[...] = kept_ref[at, :] + met_ref[at, :]


def plane_kernel(place_ref, *refs, n):
    met, outs, whole_ref = refs[:n], refs[n:-1], refs[-1]
    whole_ref[...] = tree_sum([ref[...] for ref in met])
    height = outs[0].shape[0]
    for step, out in enumerate(outs):
        at = pl.ds(pl.multiple_of((place_ref[0] ^ step) * height, height), height)
        out[...] = whole_ref[at, :]


def finish_kernel(place_ref, *refs, n, k):
    out_ref = refs[-1]
    height = refs[0].shape[0]
    out_ref[:height] = tree_sum([ref[...] for ref in refs[:n]]).astype(BF16)
    total = tree_sum([ref[...] for ref in refs[n : 2 * n]])
    last = (place_ref[0] == n - 1) & (place_ref[1] == n - 1) & (place_ref[2] == k - 1)
    edge = total[-8:, :128]
    row = lax.broadcasted_iota(jnp.int32, edge.shape, 0)
    column = lax.broadcasted_iota(jnp.int32, edge.shape, 1)
    taken = (row == 7) & last
    whole = jnp.sum(jnp.where(taken & (column == 0), edge, 0.0), keepdims=True)
    high = whole.astype(BF16).astype(F32)
    middle = (whole - high).astype(BF16).astype(F32)
    three = jnp.where(column == 0, high, jnp.where(column == 1, middle, whole - high - middle))
    edge = jnp.where(taken & (column < 3), three, edge)
    edge = jnp.concatenate([edge, total[-8:, 128:]], 1)
    out_ref[height:] = jnp.concatenate([total[:-8], edge], 0).astype(BF16)


def local(kernel, place_array, args, shapes, name, **more):
    space = pl.BlockSpec(memory_space=pltpu.VMEM)
    return pl.pallas_call(
        kernel,
        in_specs=[pl.BlockSpec(memory_space=pltpu.SMEM)] + [space] * len(args),
        out_specs=[space] * len(shapes),
        out_shape=[jax.ShapeDtypeStruct(shape, dtype) for shape, dtype in shapes],
        compiler_params=pltpu.CompilerParams(vmem_limit_bytes=VMEM_BYTES // 2),
        name=name,
        **more,
    )(place_array, *args)


def plane_rows(place, place_array, grams, few=False):
    n = place.n
    half, batch = grams[0].shape
    kept, other = grams
    other = place.send(other, lambda z, a, b: (z, a, b ^ 1))
    parts = local(
        functools.partial(halve_kernel, axis=1),
        place_array,
        (kept, other),
        [((half // n, batch), F32)] * n,
        "halve",
    )
    return local(
        functools.partial(plane_kernel, n=n),
        place_array,
        sends(place, "a", parts, few),
        [((half // (n * n), batch), F32)] * n,
        "plane",
        scratch_shapes=[pltpu.VMEM((half // n, batch), F32)],
    )


def in_one(place, run, args):
    shapes = jax.eval_shape(run, *args)
    return lax.cond(
        place.z < place.n,
        run,
        lambda *args: jax.tree.map(lambda leaf: jnp.zeros(leaf.shape, leaf.dtype), shapes),
        *args,
    )


def plain_gram(place, part):
    for axis in ("b", "a", "z"):
        part = reduce_scatter(place, axis, part)
    part = part.astype(BF16)
    for axis in ("z", "a", "b"):
        part = gather(place, axis, part)
    return part


def cut_kernel(place_ref, *refs, views, n):
    inputs, outs, done = refs[:views], refs[views:-1], refs[-1]
    few = outs[0].shape[0] // views
    copies = []
    for step in range(n):
        at = pl.ds(pl.multiple_of((place_ref[1] ^ step) * few, few), few)
        for i, view in enumerate(inputs):
            part = outs[step].at[i * few : (i + 1) * few]
            copies.append(pltpu.make_async_copy(view.at[at], part, done.at[step, i]))
            copies[-1].start()
    for copy in copies:
        copy.wait()


def lay_kernel(place_ref, *refs, n):
    parts, outs = refs[:n], refs[n:]
    few = parts[0].shape[0] // len(outs)
    for step in range(n):
        at = pl.ds(pl.multiple_of((place_ref[0] ^ step) * few, few), few)
        for i, out in enumerate(outs):
            out[at, :] = parts[step][i * few : (i + 1) * few, :]


def spread(place, place_array, views):
    n = place.n
    rows, width = views[0].shape
    few = rows // n
    parts = pl.pallas_call(
        functools.partial(cut_kernel, views=len(views), n=n),
        in_specs=[pl.BlockSpec(memory_space=pltpu.SMEM)]
        + [pl.BlockSpec(memory_space=pl.ANY)] * len(views),
        out_specs=[pl.BlockSpec(memory_space=pltpu.VMEM)] * n,
        out_shape=[jax.ShapeDtypeStruct((len(views) * few, width), BF16)] * n,
        scratch_shapes=[pltpu.SemaphoreType.DMA((n, len(views)))],
        compiler_params=pltpu.CompilerParams(vmem_limit_bytes=VMEM_BYTES // 2),
        name="cut",
    )(place_array, *views)
    parts = sends(place, "a", parts)
    parts = sends(place, "z", ordered(parts, place.a ^ place.z))
    return local(
        functools.partial(lay_kernel, n=n),
        place_array,
        parts,
        [((rows, width), BF16)] * len(views),
        "lay",
    )


def met_rows(place, values, few=False):
    return sends(place, "a", [values] * place.n, few)


def project_kernel(place_ref, *refs, counts, n, k):
    met = refs[: sum(counts)]
    weight_ref, own_ref, *coded = refs[sum(counts) : -2]
    held_ref, arrived = refs[-2:]
    width = met[0].shape[1]
    columns = own_ref.shape[1]
    order = [*range(1, n), 0]
    copies = []
    for slot, step in enumerate(order):
        at = pl.ds(pl.multiple_of((place_ref[0] ^ step) * columns, columns), columns)
        copies.append([])
        for i in range(k):
            rows = pl.ds(pl.multiple_of((place_ref[2] ^ i) * width, width), width)
            part = held_ref.at[slot, i * width : (i + 1) * width]
            copies[slot].append(
                pltpu.make_async_copy(weight_ref.at[rows, at], part, arrived.at[slot, i])
            )
    for copy in copies[0]:
        copy.start()
    values = []
    for count in counts:
        values.append(jnp.concatenate([ref[...] for ref in met[:count]], 0))
        met = met[count:]
    for slot, step in enumerate(order):
        for copy in copies[slot]:
            copy.wait()
        if slot + 1 < n:
            for copy in copies[slot + 1]:
                copy.start()
        total = 0.0
        for i in range(k):
            part = held_ref[slot, i * width : (i + 1) * width, :]
            total += jnp.dot(values[i], part, preferred_element_type=F32)
        if step == 0:
            own_ref[...] = total
        else:
            encode(total, coded[step - 1])


def unit(near):
    near = jnp.abs(near)
    return (near * (1.0 + 1.01 / 256.0)).astype(BF16).astype(F32) - near


def encode(total, coded_ref):
    coarse = total.astype(BF16)
    batch = total.shape[0]
    coded_ref[:batch] = coarse
    near = coarse.astype(F32)
    step = unit(near)
    level = (total - near) * pl.reciprocal(jnp.where(step > 0.0, step, 1.0), approx=True)
    level = jnp.clip(jnp.floor((level + 0.5) * LEVELS), 0.0, LEVELS - 1.0).astype(jnp.int32)
    height = batch // SHARED
    first, second, third, fourth = [level[i * height : (i + 1) * height] for i in range(SHARED)]
    word = 128 + (first << BITS) + second + ((fourth & 1) << 6)
    word = word << (third + ((fourth & 4) << 1))
    word = jnp.where((fourth & 2) != 0, -word, word)
    coded_ref[batch:] = word.astype(F32).astype(BF16)


def decode(coded_ref):
    height = coded_ref.shape[0] // (SHARED + 1)
    word = coded_ref[SHARED * height :].astype(F32).astype(jnp.int32)
    negative = word < 0
    word = jnp.abs(word)
    power = jnp.zeros_like(word)
    for shift in (8, 4, 2, 1):
        large = word >= (128 << shift)
        word = jnp.where(large, word >> shift, word)
        power = power + jnp.where(large, shift, 0)
    levels = [
        (word >> BITS) & (LEVELS - 1),
        word & (LEVELS - 1),
        power & (LEVELS - 1),
        ((word >> 6) & 1) + jnp.where(negative, 2, 0) + ((power >> 3) << 2),
    ]
    blocks = []
    for i, level in enumerate(levels):
        near = coded_ref[i * height : (i + 1) * height].astype(F32)
        offset = (level.astype(F32) + (0.5 - LEVELS / 2)) * (1.0 / LEVELS)
        blocks.append(near + unit(near) * offset)
    return blocks


def project(place, place_array, met, weight):
    n, k = place.n, place.k
    rows, width = met[0][0].shape
    batch, columns = rows * n, weight.shape[1] // n
    counts = [len(parts) for parts in met]
    met = [part for parts in met for part in parts]
    coded = batch + batch // SHARED
    out_shape = [jax.ShapeDtypeStruct((batch, columns), F32)]
    out_shape += [jax.ShapeDtypeStruct((coded, columns), BF16)] * (n - 1)
    space = pl.BlockSpec(memory_space=pltpu.VMEM)
    own, *parts = pl.pallas_call(
        functools.partial(project_kernel, counts=counts, n=n, k=k),
        in_specs=[pl.BlockSpec(memory_space=pltpu.SMEM)]
        + [space] * len(met)
        + [pl.BlockSpec(memory_space=pl.ANY)],
        out_specs=[space] * n,
        out_shape=out_shape,
        scratch_shapes=[
            pltpu.VMEM((n, k * width, columns), BF16),
            pltpu.SemaphoreType.DMA((n, k)),
        ],
        compiler_params=pltpu.CompilerParams(vmem_limit_bytes=VMEM_BYTES),
        cost_estimate=pl.CostEstimate(
            flops=2 * batch * k * width * n * columns,
            bytes_accessed=2 * k * width * (batch + n * columns) + 3 * n * batch * columns,
            transcendentals=0,
        ),
        name="project",
    )(place_array, *met, weight)
    return own, parts


def normalize_kernel(place_ref, *refs, n, k, second):
    own_ref, parts = refs[0], refs[1:n]
    refs = refs[n:]
    if second:
        other_ref, refs = refs[0], refs[1:]
    norm_ref, packed_ref, scale_ref = refs[:3]
    grams = refs[3 : 3 + k]
    batch, columns = own_ref.shape
    height = batch // SHARED
    met = [[own_ref[i * height : (i + 1) * height] for i in range(SHARED)]]
    for step in range(1, n):
        met.append(decode(parts[step - 1]))
    blocks = [tree_sum([met[step][i] for step in range(n)]) for i in range(SHARED)]
    total = tree_sum([jnp.sum(block, 0, keepdims=True) for block in blocks])
    squares = tree_sum([jnp.sum(block * block, 0, keepdims=True) for block in blocks])
    mean = total / batch
    scale = lax.rsqrt(squares / batch - mean * mean + bn_eps)
    scale_ref[...] = scale
    rows, few = batch // n, batch // (n * n)
    for i, block in enumerate(blocks):
        normed = (block - mean) * scale
        for first in range(0, height, few):
            step, plane = divmod((i * height + first) // few, n)
            at = pl.multiple_of(plane * rows + (place_ref[1] ^ step) * few, few)
            norm_ref[pl.ds(at, few), :] = normed[first : first + few]
            packed_ref[pl.ds(at, few), :] = normed[first : first + few].astype(BF16)
    dims = (((1,), (1,)), ((), ()))
    packed = packed_ref[...]
    size = batch // k
    for i in range(k):
        at = pl.multiple_of((place_ref[2] ^ i) * size, size)
        gram = lax.dot_general(packed_ref[pl.ds(at, size), :], packed, dims, preferred_element_type=F32)
        grams[i][...] = gram
    if second:
        coeff_ref = refs[3 + k]
        diag = jnp.sum(norm_ref[...] * other_ref[...], 0, keepdims=True) / batch
        coeff_ref[...] = 2.0 * ((1.0 - off_weight) * diag - 1.0)
        share = jnp.sum((1.0 - diag) ** 2 - off_weight * diag * diag, 1, keepdims=True)
        for i in range(k):

            @pl.when((place_ref[2] ^ i) == k - 1)
            def _():
                row = grams[i][size - 8 :, :128]
                first = (lax.broadcasted_iota(jnp.int32, row.shape, 0) == 7) & (
                    lax.broadcasted_iota(jnp.int32, row.shape, 1) == 0
                )
                grams[i][size - 8 :, :128] = jnp.where(first, share, row)


def normalize_parts(place, place_array, own, parts, other=None):
    n, k = place.n, place.k
    batch, columns = own.shape
    second = other is not None
    out_shape = [
        jax.ShapeDtypeStruct((batch, columns), F32),
        jax.ShapeDtypeStruct((batch, columns), BF16),
        jax.ShapeDtypeStruct((1, columns), F32),
    ] + [jax.ShapeDtypeStruct((batch // k, batch), F32)] * k
    if second:
        out_shape.append(jax.ShapeDtypeStruct((1, columns), F32))
    args = [own, *parts] + ([other] if second else [])
    space = pl.BlockSpec(memory_space=pltpu.VMEM)
    return pl.pallas_call(
        functools.partial(normalize_kernel, n=n, k=k, second=second),
        in_specs=[pl.BlockSpec(memory_space=pltpu.SMEM)] + [space] * len(args),
        out_specs=[space] * len(out_shape),
        out_shape=out_shape,
        compiler_params=pltpu.CompilerParams(vmem_limit_bytes=VMEM_BYTES // 2),
        cost_estimate=pl.CostEstimate(
            flops=2 * batch * batch * columns,
            bytes_accessed=16 * batch * columns + 4 * batch * batch,
            transcendentals=0,
        ),
        name="normalize",
    )(place_array, *args)


def gradient_kernel(place_ref, *refs, n, k):
    grams, refs = refs[: n * k], refs[n * k :]
    packed, norms, scales, coeff_ref, refs = refs[0:2], refs[2:4], refs[4:6], refs[6], refs[7:]
    outs, loss_ref = refs[:n], refs[n]
    gram_ref, whole_ref = refs[n + 1 :]
    batch, columns = norms[0].shape
    height = grams[0].shape[0] // 2
    few = height // n
    for i in range(k):
        for step in range(n):
            at = ((place_ref[2] ^ i) * n + (place_ref[1] ^ step)) * height
            for plane in range(n):
                for view in range(2):
                    to = pl.ds(pl.multiple_of(at + plane * few, few), few)
                    first = (plane * 2 + view) * few
                    gram_ref[view, to, :] = grams[i * n + step][first : first + few, :]
    edge = batch - 128
    tail = gram_ref[1, edge:, :128].astype(F32)
    row = lax.broadcasted_iota(jnp.int32, tail.shape, 0)
    column = lax.broadcasted_iota(jnp.int32, tail.shape, 1)
    taken = (row == 127) & (column < 3)
    mirror = gram_ref[1, :128, edge:].astype(F32).T
    share = jnp.sum(jnp.where(taken, tail, 0.0), keepdims=True)
    gram_ref[1, edge:, :128] = jnp.where(taken, mirror, tail).astype(BF16)
    factor = 2.0 * off_weight / batch
    rows = batch // n
    for view in (1, 0):
        norm = norms[view][...]
        grad = (
            factor * jnp.dot(gram_ref[1 - view], packed[view][...], preferred_element_type=F32)
            + coeff_ref[...] * norms[1 - view][...]
        )
        first = jnp.sum(grad, 0, keepdims=True) / batch
        second = jnp.sum(grad * norm, 0, keepdims=True) / batch
        whole_ref[view] = (scales[view][...] * (grad - first - norm * second)).astype(BF16)
        for step in range(n):
            at = pl.multiple_of((place_ref[0] ^ step) * rows, rows)
            outs[step][view * rows : (view + 1) * rows, :] = whole_ref[view, pl.ds(at, rows), :]
    frob = jnp.sum(gram_ref[0].astype(F32) * gram_ref[1].astype(F32), keepdims=True)
    loss_ref[...] = (share + off_weight * (frob / (batch * batch))) / D


def gradient(place, place_array, grams, packed, norms, scales, coeff):
    batch, columns = norms[0].shape
    return local(
        functools.partial(gradient_kernel, n=place.n, k=place.k),
        place_array,
        (*grams, *packed, *norms, *scales, coeff),
        [((2 * batch // place.n, columns), BF16)] * place.n + [((1, 1), F32)],
        "gradient",
        scratch_shapes=[
            pltpu.VMEM((2, batch, batch), BF16),
            pltpu.VMEM((2, batch, columns), BF16),
        ],
    )


def place_kernel(place_ref, *refs, n):
    parts, outs = refs[:n], refs[n:]
    rows, columns = parts[0].shape[0] // len(outs), parts[0].shape[1]
    for step in range(n):
        at = pl.ds(pl.multiple_of((place_ref[0] ^ step) * columns, columns), columns)
        for i, out in enumerate(outs):
            out[:, at] = parts[step][i * rows : (i + 1) * rows, :]


def with_kernels(place, h_first, h_second, weight):
    n, k, z, a, b = place.n, place.k, place.z, place.a, place.b
    place_array = jnp.stack([z, a, b]).astype(jnp.int32)
    first, second = spread(place, place_array, (h_first, h_second))

    def projected(values, weight, few):
        met = met_rows(place, values, few)
        own = [jnp.concatenate(met, 0)] if few else met
        others = [place.send(part, lambda z, a, b: (z, a, b ^ 1)) for part in own]
        return project(place, place_array, [met, others], weight)

    def sent(parts):
        return sends(place, "z", [parts[0], *parts])[1:]

    own_1, parts_1 = projected(first, weight, False)
    second, own_1 = lax.optimization_barrier((second, own_1))
    parts_1 = sent(parts_1)
    own_2, parts_2 = in_one(
        place, lambda values, weight: projected(values, weight, True), (second, weight)
    )
    own_1, own_2 = lax.optimization_barrier((own_1, own_2))
    parts_2 = sent(parts_2)
    norm_1, packed_1, scale_1, *grams = normalize_parts(place, place_array, own_1, parts_1)
    met_1 = in_one(place, lambda *grams: plane_rows(place, place_array, grams, True), grams)
    met_1 = sends(place, "z", met_1)
    own_2, parts_2, met_1 = lax.optimization_barrier((own_2, parts_2, met_1))
    norm_2, packed_2, scale_2, *grams, coeff = normalize_parts(
        place, place_array, own_2, parts_2, norm_1
    )
    met_2 = sends(place, "z", plane_rows(place, place_array, grams))
    rows, batch = 2 * met_2[0].shape[0], h_first.shape[0] * n
    (part,) = local(
        functools.partial(finish_kernel, n=n, k=k),
        place_array,
        (*met_1, *met_2),
        [((rows, batch), BF16)],
        "finish",
    )
    part = jnp.concatenate(ordered(sends(place, "z", [part] * n), z), 0)
    grams = sends(place, "a", [part] * n)
    grams += [place.send(part, lambda z, a, b: (z, a, b ^ 1)) for part in grams]
    *parts, loss = gradient(
        place,
        place_array,
        grams,
        (packed_1, packed_2),
        (norm_1, norm_2),
        (scale_1, scale_2),
        coeff,
    )
    out_1, out_2 = local(
        functools.partial(place_kernel, n=n),
        place_array,
        sends(place, "z", parts),
        [(h_first.shape, BF16)] * 2,
        "place",
    )
    return (out_1, out_2, loss.reshape(()))


def plain(place, h_first, h_second, weight):
    n, k, z, a, b = place.n, place.k, place.z, place.a, place.b
    rows, width = h_first.shape
    batch = rows * n
    columns = weight.shape[1] // n
    weight_parts = weight.reshape(k, width, n * columns)
    zs = []
    for values in (h_first, h_second):
        moved = place.send(values, lambda z, a, b: (a, z, b))
        own = jnp.concatenate(met_rows(place, moved), 0)
        total = jnp.dot(own, pick(weight_parts, b), preferred_element_type=F32)
        for step in range(1, k):
            other = place.send(own, lambda z, a, b, s=step: (z, a, b ^ s))
            total += jnp.dot(other, pick(weight_parts, b ^ step), preferred_element_type=F32)
        cut = total.reshape(batch, n, columns).transpose(1, 0, 2)
        whole = tree_sum(exchange(place, "z", cut)).reshape(n, rows, columns)
        zs.append(jnp.concatenate(ordered([whole[i] for i in range(n)], a), 0))
    normed, scales = [], []
    for values in zs:
        mean = jnp.sum(values, 0) / batch
        scale = lax.rsqrt(jnp.sum(values * values, 0) / batch - mean * mean + bn_eps)
        normed.append((values - mean) * scale)
        scales.append(scale)
    diag = jnp.sum(normed[0] * normed[1], 0) / batch
    packed = [values.astype(BF16) for values in normed]
    dims = (((1,), (1,)), ((), ()))
    grams = []
    for values in packed:
        gram = lax.dot_general(values, values, dims, preferred_element_type=F32)
        grams.append(plain_gram(place, gram))
    frob = jnp.sum(grams[0].astype(F32) * grams[1].astype(F32)) / (batch * batch)
    coeff = 2.0 * ((1.0 - off_weight) * diag - 1.0)
    factor = 2.0 * off_weight / batch
    outs = []
    for view in range(2):
        grad = (
            factor * jnp.dot(grams[1 - view], packed[view], preferred_element_type=F32)
            + coeff * normed[1 - view]
        )
        first = jnp.sum(grad, 0) / batch
        second = jnp.sum(grad * normed[view], 0) / batch
        out = (scales[view] * (grad - first - normed[view] * second)).astype(BF16)
        parts = exchange(place, "z", out.reshape(n, rows, columns))
        outs.append(jnp.concatenate(ordered(parts, z), 1))
    share = jnp.sum((1.0 - diag) ** 2) - off_weight * jnp.sum(diag * diag)
    loss = (lax.psum(share, ("dp", "mp")) + off_weight * frob) / D
    return (outs[0], outs[1], loss)


def per_device(h_first, h_second, weight):
    place = Place()
    columns = weight.shape[1] // place.n
    fits = columns % 128 == 0 and place.n == SHARED and place.k == 2
    return (with_kernels if fits else plain)(place, h_first, h_second, weight)


def solution(mesh):
    in_specs = (P("dp", "mp"), P("dp", "mp"), P("dp", "mp"))
    out_specs = (P("dp", "mp"), P("dp", "mp"), P())
    return jax.shard_map(
        per_device, mesh=mesh, in_specs=in_specs, out_specs=out_specs, check_vma=False
    )
```

```python
import functools

import jax
import jax.numpy as jnp
from jax import lax
from jax.experimental import pallas as pl
from jax.experimental.pallas import tpu as pltpu
from jax.sharding import PartitionSpec as P

D = 8192


off_weight = 0.0051
bn_eps = 1e-05

F32 = jnp.float32
BF16 = jnp.bfloat16
VMEM_BYTES = 16 * 1024 * 1024
SHARED = 4
BITS = 3
LEVELS = 1 << BITS


class Place:
    def __init__(self):
        self.n = lax.axis_size("dp")
        self.k = lax.axis_size("mp") // self.n
        self.z = lax.axis_index("dp")
        self.a = lax.axis_index("mp") // self.k
        self.b = lax.axis_index("mp") % self.k

    def send(self, value, target):
        n, k = self.n, self.k
        pairs = []
        for z in range(n):
            for a in range(n):
                for b in range(k):
                    to_z, to_a, to_b = target(z, a, b)
                    pairs.append(((z * n + a) * k + b, (to_z * n + to_a) * k + to_b))
        return lax.ppermute(value, ("dp", "mp"), pairs)

    def along(self, axis):
        if axis == "z":
            return self.n, self.z, lambda step: lambda z, a, b: (z ^ step, a, b)
        if axis == "a":
            return self.n, self.a, lambda step: lambda z, a, b: (z, a ^ step, b)
        return self.k, self.b, lambda step: lambda z, a, b: (z, a, b ^ step)


def ordered(parts, place):
    bit = 1
    while bit < len(parts):
        odd = (place & bit) != 0
        parts = [jnp.where(odd, parts[i ^ bit], parts[i]) for i in range(len(parts))]
        bit *= 2
    return parts


def tree_sum(parts):
    while len(parts) > 1:
        parts = [parts[i] + parts[i + 1] for i in range(0, len(parts), 2)]
    return parts[0]


def pick(value, index):
    return lax.dynamic_index_in_dim(value, index, 0, keepdims=False)


def exchange(place, axis, value, few=False):
    size, here, toward = place.along(axis)
    return sends(place, axis, [pick(value, here ^ step) for step in range(size)], few)


def sends(place, axis, parts, few=False):
    size, here, toward = place.along(axis)
    met = [parts[0]]
    for step in range(1, size):
        part = parts[step]
        if few and step > 2:
            met[step - 2], part = lax.optimization_barrier((met[step - 2], part))
        met.append(place.send(part, toward(step)))
    return met


def reduce_scatter(place, axis, value, few=False):
    size, here, toward = place.along(axis)
    value = value.reshape((size, value.shape[0] // size) + value.shape[1:])
    return tree_sum(exchange(place, axis, value, few))


def gather(place, axis, value, few=False):
    size, here, toward = place.along(axis)
    parts = sends(place, axis, [value] * size, few)
    return jnp.concatenate(ordered(parts, here), 0)


def halve_kernel(place_ref, kept_ref, met_ref, *outs, axis):
    height = outs[0].shape[0]
    for step, out in enumerate(outs):
        at = pl.ds(pl.multiple_of((place_ref[axis] ^ step) * height, height), height)
        out[...] = kept_ref[at, :] + met_ref[at, :]


def plane_kernel(place_ref, *refs, n):
    met, outs, whole_ref = refs[:n], refs[n:-1], refs[-1]
    whole_ref[...] = tree_sum([ref[...] for ref in met])
    height = outs[0].shape[0]
    for step, out in enumerate(outs):
        at = pl.ds(pl.multiple_of((place_ref[0] ^ step) * height, height), height)
        out[...] = whole_ref[at, :]


def rows_kernel(place_ref, *refs):
    refs[-1][...] = tree_sum([ref[...] for ref in refs[:-1]]).astype(BF16)


def code_kernel(place_ref, *refs, n):
    met, rows_ref, out_ref = refs[:n], refs[n], refs[n + 1]
    total = tree_sum([ref[...] for ref in met])
    coded = total.shape[0] + total.shape[0] // SHARED
    encode(total, out_ref.at[:coded])
    out_ref[coded:] = rows_ref[...]


def finish_kernel(place_ref, *refs, n, k):
    out_ref = refs[-1]
    height = out_ref.shape[0] // 2
    coded, few = height + height // SHARED, height // n
    met = []
    for step in range(n):
        at = pl.ds(pl.multiple_of((place_ref[0] ^ step) * few, few), few)
        out_ref[at, :] = refs[step][coded:]
        met.append(jnp.concatenate(decode(refs[step].at[:coded]), 0))
    total = tree_sum(met)
    last = (place_ref[1] == n - 1) & (place_ref[2] == k - 1)
    edge = total[-8:, :128]
    row = lax.broadcasted_iota(jnp.int32, edge.shape, 0)
    column = lax.broadcasted_iota(jnp.int32, edge.shape, 1)
    taken = (row == 7) & last
    whole = jnp.sum(jnp.where(taken & (column == 0), edge, 0.0), keepdims=True)
    high = whole.astype(BF16).astype(F32)
    middle = (whole - high).astype(BF16).astype(F32)
    three = jnp.where(column == 0, high, jnp.where(column == 1, middle, whole - high - middle))
    edge = jnp.where(taken & (column < 3), three, edge)
    edge = jnp.concatenate([edge, total[-8:, 128:]], 1)
    out_ref[height:] = jnp.concatenate([total[:-8], edge], 0).astype(BF16)


def local(kernel, place_array, args, shapes, name, **more):
    space = pl.BlockSpec(memory_space=pltpu.VMEM)
    return pl.pallas_call(
        kernel,
        in_specs=[pl.BlockSpec(memory_space=pltpu.SMEM)] + [space] * len(args),
        out_specs=[space] * len(shapes),
        out_shape=[jax.ShapeDtypeStruct(shape, dtype) for shape, dtype in shapes],
        compiler_params=pltpu.CompilerParams(vmem_limit_bytes=VMEM_BYTES // 2),
        name=name,
        **more,
    )(place_array, *args)


def plane_rows(place, place_array, grams, few=False):
    half, batch = grams[0].shape
    kept, other = grams
    other = place.send(other, lambda z, a, b: (z, a, b ^ 1))
    parts = local(
        functools.partial(halve_kernel, axis=1),
        place_array,
        (kept, other),
        [((half // place.n, batch), F32)] * place.n,
        "halve",
    )
    return sends(place, "a", parts, few)


def first_rows(place, place_array, grams):
    parts = plane_rows(place, place_array, grams, True)
    height, batch = parts[0].shape
    return local(
        functools.partial(plane_kernel, n=place.n),
        place_array,
        parts,
        [((height // place.n, batch), F32)] * place.n,
        "plane",
        scratch_shapes=[pltpu.VMEM((height, batch), F32)],
    )


def in_one(place, run, args):
    shapes = jax.eval_shape(run, *args)
    return lax.cond(
        place.z < place.n,
        run,
        lambda *args: jax.tree.map(lambda leaf: jnp.zeros(leaf.shape, leaf.dtype), shapes),
        *args,
    )


def plain_gram(place, part):
    for axis in ("b", "a", "z"):
        part = reduce_scatter(place, axis, part)
    part = part.astype(BF16)
    for axis in ("z", "a", "b"):
        part = gather(place, axis, part)
    return part


def lay_kernel(place_ref, *refs, n):
    parts, outs = refs[:n], refs[n:]
    few = parts[0].shape[0] // len(outs)
    for step in range(n):
        at = pl.ds(pl.multiple_of((place_ref[0] ^ step) * few, few), few)
        for i, out in enumerate(outs):
            out[at, :] = parts[step][i * few : (i + 1) * few, :]


def fetch_kernel(weight_ref, held_ref, arrived):
    copy = pltpu.make_async_copy(weight_ref, held_ref, arrived)
    copy.start()
    copy.wait()


def fetch(weight):
    return pl.pallas_call(
        fetch_kernel,
        in_specs=[pl.BlockSpec(memory_space=pl.ANY)],
        out_specs=pl.BlockSpec(memory_space=pltpu.VMEM),
        out_shape=jax.ShapeDtypeStruct(weight.shape, BF16),
        scratch_shapes=[pltpu.SemaphoreType.DMA],
        compiler_params=pltpu.CompilerParams(vmem_limit_bytes=VMEM_BYTES // 2),
        cost_estimate=pl.CostEstimate(flops=0, bytes_accessed=4 * weight.size, transcendentals=0),
        name="fetch",
    )(weight)


def to_columns(place, view):
    rows, width = view.shape
    return exchange(place, "a", view.reshape(place.n, rows // place.n, width))


def to_planes(place, parts):
    return sends(place, "z", ordered(parts, place.a ^ place.z))


def lay(place, place_array, parts):
    rows, width = parts[0].shape
    (laid,) = local(
        functools.partial(lay_kernel, n=place.n),
        place_array,
        parts,
        [((rows * place.n, width), BF16)],
        "lay",
    )
    return laid


def met_rows(place, values, few=False):
    return sends(place, "a", [values] * place.n, few)


def project_kernel(place_ref, *refs, counts, n, k):
    met = refs[: sum(counts)]
    weight_ref, own_ref, *coded = refs[sum(counts) :]
    width = met[0].shape[1]
    columns = own_ref.shape[1]
    values = []
    for count in counts:
        values.append(jnp.concatenate([ref[...] for ref in met[:count]], 0))
        met = met[count:]
    for step in [*range(1, n), 0]:
        at = pl.ds(pl.multiple_of((place_ref[0] ^ step) * columns, columns), columns)
        total = 0.0
        for i in range(k):
            rows = pl.ds(pl.multiple_of((place_ref[2] ^ i) * width, width), width)
            total += jnp.dot(values[i], weight_ref[rows, at], preferred_element_type=F32)
        if step == 0:
            own_ref[...] = total
        else:
            encode(total, coded[step - 1])


def unit(near):
    near = jnp.abs(near)
    return (near * (1.0 + 1.01 / 256.0)).astype(BF16).astype(F32) - near


def encode(total, coded_ref):
    coarse = total.astype(BF16)
    batch = total.shape[0]
    coded_ref[:batch] = coarse
    near = coarse.astype(F32)
    step = unit(near)
    level = (total - near) * pl.reciprocal(jnp.where(step > 0.0, step, 1.0), approx=True)
    level = jnp.clip(jnp.floor((level + 0.5) * LEVELS), 0.0, LEVELS - 1.0).astype(jnp.int32)
    height = batch // SHARED
    first, second, third, fourth = [level[i * height : (i + 1) * height] for i in range(SHARED)]
    word = 128 + (first << BITS) + second + ((fourth & 1) << 6)
    word = word << (third + ((fourth & 4) << 1))
    word = jnp.where((fourth & 2) != 0, -word, word)
    coded_ref[batch:] = word.astype(F32).astype(BF16)


def decode(coded_ref):
    height = coded_ref.shape[0] // (SHARED + 1)
    word = coded_ref[SHARED * height :].astype(F32).astype(jnp.int32)
    negative = word < 0
    word = jnp.abs(word)
    power = jnp.zeros_like(word)
    for shift in (8, 4, 2, 1):
        large = word >= (128 << shift)
        word = jnp.where(large, word >> shift, word)
        power = power + jnp.where(large, shift, 0)
    levels = [
        (word >> BITS) & (LEVELS - 1),
        word & (LEVELS - 1),
        power & (LEVELS - 1),
        ((word >> 6) & 1) + jnp.where(negative, 2, 0) + ((power >> 3) << 2),
    ]
    blocks = []
    for i, level in enumerate(levels):
        near = coded_ref[i * height : (i + 1) * height].astype(F32)
        offset = (level.astype(F32) + (0.5 - LEVELS / 2)) * (1.0 / LEVELS)
        blocks.append(near + unit(near) * offset)
    return blocks


def project(place, place_array, met, weight):
    n, k = place.n, place.k
    rows, width = met[0][0].shape
    batch, columns = rows * n, weight.shape[1] // n
    counts = [len(parts) for parts in met]
    met = [part for parts in met for part in parts]
    coded = batch + batch // SHARED
    out_shape = [jax.ShapeDtypeStruct((batch, columns), F32)]
    out_shape += [jax.ShapeDtypeStruct((coded, columns), BF16)] * (n - 1)
    space = pl.BlockSpec(memory_space=pltpu.VMEM)
    own, *parts = pl.pallas_call(
        functools.partial(project_kernel, counts=counts, n=n, k=k),
        in_specs=[pl.BlockSpec(memory_space=pltpu.SMEM)]
        + [space] * (len(met) + 1),
        out_specs=[space] * n,
        out_shape=out_shape,
        compiler_params=pltpu.CompilerParams(vmem_limit_bytes=VMEM_BYTES),
        cost_estimate=pl.CostEstimate(
            flops=2 * batch * k * width * n * columns,
            bytes_accessed=2 * k * width * (batch + n * columns) + 3 * n * batch * columns,
            transcendentals=0,
        ),
        name="project",
    )(place_array, *met, weight)
    return own, parts


def normalize_kernel(place_ref, *refs, n, k, second):
    own_ref, parts = refs[0], refs[1:n]
    refs = refs[n:]
    if second:
        other_ref, refs = refs[0], refs[1:]
    norm_ref, packed_ref, scale_ref = refs[:3]
    grams = refs[3 : 3 + k]
    batch, columns = own_ref.shape
    height = batch // SHARED
    met = [[own_ref[i * height : (i + 1) * height] for i in range(SHARED)]]
    for step in range(1, n):
        met.append(decode(parts[step - 1]))
    blocks = [tree_sum([met[step][i] for step in range(n)]) for i in range(SHARED)]
    total = tree_sum([jnp.sum(block, 0, keepdims=True) for block in blocks])
    squares = tree_sum([jnp.sum(block * block, 0, keepdims=True) for block in blocks])
    mean = total / batch
    scale = lax.rsqrt(squares / batch - mean * mean + bn_eps)
    scale_ref[...] = scale
    rows, few = batch // n, batch // (n * n)
    for i, block in enumerate(blocks):
        normed = (block - mean) * scale
        for first in range(0, height, few):
            step, plane = divmod((i * height + first) // few, n)
            at = pl.multiple_of(plane * rows + (place_ref[1] ^ step) * few, few)
            norm_ref[pl.ds(at, few), :] = normed[first : first + few]
            packed_ref[pl.ds(at, few), :] = normed[first : first + few].astype(BF16)
    dims = (((1,), (1,)), ((), ()))
    packed = packed_ref[...]
    size = batch // k
    for i in range(k):
        at = pl.multiple_of((place_ref[2] ^ i) * size, size)
        gram = lax.dot_general(packed_ref[pl.ds(at, size), :], packed, dims, preferred_element_type=F32)
        grams[i][...] = gram
    if second:
        coeff_ref = refs[3 + k]
        diag = jnp.sum(norm_ref[...] * other_ref[...], 0, keepdims=True) / batch
        coeff_ref[...] = 2.0 * ((1.0 - off_weight) * diag - 1.0)
        share = jnp.sum((1.0 - diag) ** 2 - off_weight * diag * diag, 1, keepdims=True)
        for i in range(k):

            @pl.when((place_ref[2] ^ i) == k - 1)
            def _():
                row = grams[i][size - 8 :, :128]
                first = (lax.broadcasted_iota(jnp.int32, row.shape, 0) == 7) & (
                    lax.broadcasted_iota(jnp.int32, row.shape, 1) == 0
                )
                grams[i][size - 8 :, :128] = jnp.where(first, share, row)


def normalize_parts(place, place_array, own, parts, other=None):
    n, k = place.n, place.k
    batch, columns = own.shape
    second = other is not None
    out_shape = [
        jax.ShapeDtypeStruct((batch, columns), F32),
        jax.ShapeDtypeStruct((batch, columns), BF16),
        jax.ShapeDtypeStruct((1, columns), F32),
    ] + [jax.ShapeDtypeStruct((batch // k, batch), F32)] * k
    if second:
        out_shape.append(jax.ShapeDtypeStruct((1, columns), F32))
    args = [own, *parts] + ([other] if second else [])
    space = pl.BlockSpec(memory_space=pltpu.VMEM)
    return pl.pallas_call(
        functools.partial(normalize_kernel, n=n, k=k, second=second),
        in_specs=[pl.BlockSpec(memory_space=pltpu.SMEM)] + [space] * len(args),
        out_specs=[space] * len(out_shape),
        out_shape=out_shape,
        compiler_params=pltpu.CompilerParams(vmem_limit_bytes=VMEM_BYTES // 2),
        cost_estimate=pl.CostEstimate(
            flops=2 * batch * batch * columns,
            bytes_accessed=16 * batch * columns + 4 * batch * batch,
            transcendentals=0,
        ),
        name="normalize",
    )(place_array, *args)


def gradient_kernel(place_ref, *refs, n, k):
    grams, refs = refs[: n * k], refs[n * k :]
    packed, norms, scales, coeff_ref, refs = refs[0:2], refs[2:4], refs[4:6], refs[6], refs[7:]
    outs, loss_ref = refs[:n], refs[n]
    gram_ref, whole_ref = refs[n + 1 :]
    batch, columns = norms[0].shape
    height = grams[0].shape[0] // 2
    for i in range(k):
        for step in range(n):
            at = ((place_ref[2] ^ i) * n + (place_ref[1] ^ step)) * height
            to = pl.ds(pl.multiple_of(at, height), height)
            for view in range(2):
                gram_ref[view, to, :] = grams[i * n + step][view * height : (view + 1) * height, :]
    edge = batch - 128
    tail = gram_ref[1, edge:, :128].astype(F32)
    row = lax.broadcasted_iota(jnp.int32, tail.shape, 0)
    column = lax.broadcasted_iota(jnp.int32, tail.shape, 1)
    taken = (row == 127) & (column < 3)
    mirror = gram_ref[1, :128, edge:].astype(F32).T
    share = jnp.sum(jnp.where(taken, tail, 0.0), keepdims=True)
    gram_ref[1, edge:, :128] = jnp.where(taken, mirror, tail).astype(BF16)
    factor = 2.0 * off_weight / batch
    rows = batch // n
    for view in (1, 0):
        norm = norms[view][...]
        grad = (
            factor * jnp.dot(gram_ref[1 - view], packed[view][...], preferred_element_type=F32)
            + coeff_ref[...] * norms[1 - view][...]
        )
        first = jnp.sum(grad, 0, keepdims=True) / batch
        second = jnp.sum(grad * norm, 0, keepdims=True) / batch
        whole_ref[view] = (scales[view][...] * (grad - first - norm * second)).astype(BF16)
        for step in range(n):
            at = pl.multiple_of((place_ref[0] ^ step) * rows, rows)
            outs[step][view * rows : (view + 1) * rows, :] = whole_ref[view, pl.ds(at, rows), :]
    frob = jnp.sum(gram_ref[0].astype(F32) * gram_ref[1].astype(F32), keepdims=True)
    loss_ref[...] = (share + off_weight * (frob / (batch * batch))) / D


def gradient(place, place_array, grams, packed, norms, scales, coeff):
    batch, columns = norms[0].shape
    return local(
        functools.partial(gradient_kernel, n=place.n, k=place.k),
        place_array,
        (*grams, *packed, *norms, *scales, coeff),
        [((2 * batch // place.n, columns), BF16)] * place.n + [((1, 1), F32)],
        "gradient",
        scratch_shapes=[
            pltpu.VMEM((2, batch, batch), BF16),
            pltpu.VMEM((2, batch, columns), BF16),
        ],
    )


def place_kernel(place_ref, *refs, n):
    parts, outs = refs[:n], refs[n:]
    rows, columns = parts[0].shape[0] // len(outs), parts[0].shape[1]
    for step in range(n):
        at = pl.ds(pl.multiple_of((place_ref[0] ^ step) * columns, columns), columns)
        for i, out in enumerate(outs):
            out[:, at] = parts[step][i * rows : (i + 1) * rows, :]


def with_kernels(place, h_first, h_second, weight):
    n, k, z, a, b = place.n, place.k, place.z, place.a, place.b
    place_array = jnp.stack([z, a, b]).astype(jnp.int32)
    first = to_columns(place, h_first)
    first, held = lax.optimization_barrier((first, fetch(weight)))
    first, second = lax.optimization_barrier((to_planes(place, first), to_columns(place, h_second)))
    met, second = lax.optimization_barrier(
        (met_rows(place, lay(place, place_array, first)), to_planes(place, second))
    )

    def projected(met, held, whole):
        own = [jnp.concatenate(met, 0)] if whole else met
        others = [place.send(part, lambda z, a, b: (z, a, b ^ 1)) for part in own]
        return project(place, place_array, [met, others], held)

    def second_projected(weight, *parts):
        return projected(met_rows(place, lay(place, place_array, parts), True), fetch(weight), True)

    def sent(parts):
        return sends(place, "z", [parts[0], *parts])[1:]

    own_1, parts_1 = projected(met, held, False)
    second, own_1 = lax.optimization_barrier((second, own_1))
    parts_1 = sent(parts_1)
    own_2, parts_2 = in_one(place, second_projected, (weight, *second))
    own_1, own_2 = lax.optimization_barrier((own_1, own_2))
    parts_2 = sent(parts_2)
    norm_1, packed_1, scale_1, *grams = normalize_parts(place, place_array, own_1, parts_1)
    met_1 = in_one(place, lambda *grams: first_rows(place, place_array, grams), grams)
    met_1 = sends(place, "z", met_1)
    own_2, parts_2, met_1 = lax.optimization_barrier((own_2, parts_2, met_1))
    norm_2, packed_2, scale_2, *grams, coeff = normalize_parts(
        place, place_array, own_2, parts_2, norm_1
    )
    height, batch = met_1[0].shape
    (rows_1,) = local(rows_kernel, place_array, met_1, [((height, batch), BF16)], "rows")
    met_2 = plane_rows(place, place_array, grams)
    rows = met_2[0].shape[0]
    (part,) = local(
        functools.partial(code_kernel, n=n),
        place_array,
        (*met_2, rows_1),
        [((rows + rows // SHARED + height, batch), BF16)],
        "code",
    )
    (part,) = local(
        functools.partial(finish_kernel, n=n, k=k),
        place_array,
        sends(place, "z", [part] * n),
        [((2 * rows, batch), BF16)],
        "finish",
    )
    grams = sends(place, "a", [part] * n)
    grams += [place.send(part, lambda z, a, b: (z, a, b ^ 1)) for part in grams]
    *parts, loss = gradient(
        place,
        place_array,
        grams,
        (packed_1, packed_2),
        (norm_1, norm_2),
        (scale_1, scale_2),
        coeff,
    )
    out_1, out_2 = local(
        functools.partial(place_kernel, n=n),
        place_array,
        sends(place, "z", parts),
        [(h_first.shape, BF16)] * 2,
        "place",
    )
    return (out_1, out_2, loss.reshape(()))


def plain(place, h_first, h_second, weight):
    n, k, z, a, b = place.n, place.k, place.z, place.a, place.b
    rows, width = h_first.shape
    batch = rows * n
    columns = weight.shape[1] // n
    weight_parts = weight.reshape(k, width, n * columns)
    zs = []
    for values in (h_first, h_second):
        moved = place.send(values, lambda z, a, b: (a, z, b))
        own = jnp.concatenate(met_rows(place, moved), 0)
        total = jnp.dot(own, pick(weight_parts, b), preferred_element_type=F32)
        for step in range(1, k):
            other = place.send(own, lambda z, a, b, s=step: (z, a, b ^ s))
            total += jnp.dot(other, pick(weight_parts, b ^ step), preferred_element_type=F32)
        cut = total.reshape(batch, n, columns).transpose(1, 0, 2)
        whole = tree_sum(exchange(place, "z", cut)).reshape(n, rows, columns)
        zs.append(jnp.concatenate(ordered([whole[i] for i in range(n)], a), 0))
    normed, scales = [], []
    for values in zs:
        mean = jnp.sum(values, 0) / batch
        scale = lax.rsqrt(jnp.sum(values * values, 0) / batch - mean * mean + bn_eps)
        normed.append((values - mean) * scale)
        scales.append(scale)
    diag = jnp.sum(normed[0] * normed[1], 0) / batch
    packed = [values.astype(BF16) for values in normed]
    dims = (((1,), (1,)), ((), ()))
    grams = []
    for values in packed:
        gram = lax.dot_general(values, values, dims, preferred_element_type=F32)
        grams.append(plain_gram(place, gram))
    frob = jnp.sum(grams[0].astype(F32) * grams[1].astype(F32)) / (batch * batch)
    coeff = 2.0 * ((1.0 - off_weight) * diag - 1.0)
    factor = 2.0 * off_weight / batch
    outs = []
    for view in range(2):
        grad = (
            factor * jnp.dot(grams[1 - view], packed[view], preferred_element_type=F32)
            + coeff * normed[1 - view]
        )
        first = jnp.sum(grad, 0) / batch
        second = jnp.sum(grad * normed[view], 0) / batch
        out = (scales[view] * (grad - first - normed[view] * second)).astype(BF16)
        parts = exchange(place, "z", out.reshape(n, rows, columns))
        outs.append(jnp.concatenate(ordered(parts, z), 1))
    share = jnp.sum((1.0 - diag) ** 2) - off_weight * jnp.sum(diag * diag)
    loss = (lax.psum(share, ("dp", "mp")) + off_weight * frob) / D
    return (outs[0], outs[1], loss)


def per_device(h_first, h_second, weight):
    place = Place()
    columns = weight.shape[1] // place.n
    fits = columns % 128 == 0 and place.n == SHARED and place.k == 2
    return (with_kernels if fits else plain)(place, h_first, h_second, weight)


def solution(mesh):
    in_specs = (P("dp", "mp"), P("dp", "mp"), P("dp", "mp"))
    out_specs = (P("dp", "mp"), P("dp", "mp"), P())
    return jax.shard_map(
        per_device, mesh=mesh, in_specs=in_specs, out_specs=out_specs, check_vma=False
    )
```

```python
import functools

import jax
import jax.numpy as jnp
from jax import lax
from jax.experimental import pallas as pl
from jax.experimental.pallas import tpu as pltpu
from jax.sharding import PartitionSpec as P

D = 8192


off_weight = 0.0051
bn_eps = 1e-05

F32 = jnp.float32
BF16 = jnp.bfloat16
VMEM_BYTES = 16 * 1024 * 1024
POWERS = 240
HIGHEST = 128 * POWERS - 1
SCALE_ROWS = 16


class Place:
    def __init__(self):
        self.n = lax.axis_size("dp")
        self.k = lax.axis_size("mp") // self.n
        self.z = lax.axis_index("dp")
        self.a = lax.axis_index("mp") // self.k
        self.b = lax.axis_index("mp") % self.k

    def send(self, value, target):
        n, k = self.n, self.k
        pairs = []
        for z in range(n):
            for a in range(n):
                for b in range(k):
                    to_z, to_a, to_b = target(z, a, b)
                    pairs.append(((z * n + a) * k + b, (to_z * n + to_a) * k + to_b))
        return lax.ppermute(value, ("dp", "mp"), pairs)

    def along(self, axis):
        if axis == "z":
            return self.n, self.z, lambda step: lambda z, a, b: (z ^ step, a, b)
        if axis == "a":
            return self.n, self.a, lambda step: lambda z, a, b: (z, a ^ step, b)
        return self.k, self.b, lambda step: lambda z, a, b: (z, a, b ^ step)


def ordered(parts, place):
    bit = 1
    while bit < len(parts):
        odd = (place & bit) != 0
        parts = [jnp.where(odd, parts[i ^ bit], parts[i]) for i in range(len(parts))]
        bit *= 2
    return parts


def tree_sum(parts):
    while len(parts) > 1:
        parts = [parts[i] + parts[i + 1] for i in range(0, len(parts), 2)]
    return parts[0]


def pick(value, index):
    return lax.dynamic_index_in_dim(value, index, 0, keepdims=False)


def exchange(place, axis, value, few=False):
    size, here, toward = place.along(axis)
    return sends(place, axis, [pick(value, here ^ step) for step in range(size)], few)


def sends(place, axis, parts, few=False):
    size, here, toward = place.along(axis)
    met = [parts[0]]
    for step in range(1, size):
        part = parts[step]
        if few and step > 2:
            met[step - 2], part = lax.optimization_barrier((met[step - 2], part))
        met.append(place.send(part, toward(step)))
    return met


def reduce_scatter(place, axis, value, few=False):
    size, here, toward = place.along(axis)
    value = value.reshape((size, value.shape[0] // size) + value.shape[1:])
    return tree_sum(exchange(place, axis, value, few))


def gather(place, axis, value, few=False):
    size, here, toward = place.along(axis)
    parts = sends(place, axis, [value] * size, few)
    return jnp.concatenate(ordered(parts, here), 0)


def halve_kernel(place_ref, kept_ref, met_ref, *outs, axis):
    height = outs[0].shape[0]
    for step, out in enumerate(outs):
        at = pl.ds(pl.multiple_of((place_ref[axis] ^ step) * height, height), height)
        out[...] = kept_ref[at, :] + met_ref[at, :]


def plane_kernel(place_ref, *refs, n):
    met, outs, whole_ref = refs[:n], refs[n:-1], refs[-1]
    whole_ref[...] = tree_sum([ref[...] for ref in met])
    height = outs[0].shape[0]
    for step, out in enumerate(outs):
        at = pl.ds(pl.multiple_of((place_ref[0] ^ step) * height, height), height)
        out[...] = whole_ref[at, :]


def rows_kernel(place_ref, *refs):
    refs[-1][...] = tree_sum([ref[...] for ref in refs[:-1]]).astype(BF16)


def code_kernel(place_ref, *refs, n):
    met, rows_ref, out_ref = refs[:n], refs[n], refs[n + 1]
    total = tree_sum([ref[...] for ref in met])
    coded = total.shape[0] + SCALE_ROWS
    encode(total, out_ref.at[:coded])
    out_ref[coded:] = rows_ref[...]


def finish_kernel(place_ref, *refs, n, k):
    out_ref = refs[-1]
    height = out_ref.shape[0] // 2
    coded, few = height + SCALE_ROWS, height // n
    met = []
    for step in range(n):
        at = pl.ds(pl.multiple_of((place_ref[0] ^ step) * few, few), few)
        out_ref[at, :] = refs[step][coded:]
        met += decode(refs[step].at[:coded], 1)
    total = tree_sum(met)
    last = (place_ref[1] == n - 1) & (place_ref[2] == k - 1)
    edge = total[-8:, :128]
    row = lax.broadcasted_iota(jnp.int32, edge.shape, 0)
    column = lax.broadcasted_iota(jnp.int32, edge.shape, 1)
    taken = (row == 7) & last
    whole = jnp.sum(jnp.where(taken & (column == 0), edge, 0.0), keepdims=True)
    high = whole.astype(BF16).astype(F32)
    middle = (whole - high).astype(BF16).astype(F32)
    three = jnp.where(column == 0, high, jnp.where(column == 1, middle, whole - high - middle))
    edge = jnp.where(taken & (column < 3), three, edge)
    edge = jnp.concatenate([edge, total[-8:, 128:]], 1)
    out_ref[height:] = jnp.concatenate([total[:-8], edge], 0).astype(BF16)


def local(kernel, place_array, args, shapes, name, **more):
    space = pl.BlockSpec(memory_space=pltpu.VMEM)
    return pl.pallas_call(
        kernel,
        in_specs=[pl.BlockSpec(memory_space=pltpu.SMEM)] + [space] * len(args),
        out_specs=[space] * len(shapes),
        out_shape=[jax.ShapeDtypeStruct(shape, dtype) for shape, dtype in shapes],
        compiler_params=pltpu.CompilerParams(vmem_limit_bytes=VMEM_BYTES // 2),
        name=name,
        **more,
    )(place_array, *args)


def plane_rows(place, place_array, grams, few=False):
    half, batch = grams[0].shape
    kept, other = grams
    other = place.send(other, lambda z, a, b: (z, a, b ^ 1))
    parts = local(
        functools.partial(halve_kernel, axis=1),
        place_array,
        (kept, other),
        [((half // place.n, batch), F32)] * place.n,
        "halve",
    )
    return sends(place, "a", parts, few)


def first_rows(place, place_array, grams):
    parts = plane_rows(place, place_array, grams, True)
    height, batch = parts[0].shape
    return local(
        functools.partial(plane_kernel, n=place.n),
        place_array,
        parts,
        [((height // place.n, batch), F32)] * place.n,
        "plane",
        scratch_shapes=[pltpu.VMEM((height, batch), F32)],
    )


def in_one(place, run, args):
    shapes = jax.eval_shape(run, *args)
    return lax.cond(
        place.z < place.n,
        run,
        lambda *args: jax.tree.map(lambda leaf: jnp.zeros(leaf.shape, leaf.dtype), shapes),
        *args,
    )


def plain_gram(place, part):
    for axis in ("b", "a", "z"):
        part = reduce_scatter(place, axis, part)
    part = part.astype(BF16)
    for axis in ("z", "a", "b"):
        part = gather(place, axis, part)
    return part


def lay_kernel(place_ref, *refs, n):
    parts, outs = refs[:n], refs[n:]
    few = parts[0].shape[0] // len(outs)
    for step in range(n):
        at = pl.ds(pl.multiple_of((place_ref[0] ^ step) * few, few), few)
        for i, out in enumerate(outs):
            out[at, :] = parts[step][i * few : (i + 1) * few, :]


def fetch_kernel(weight_ref, held_ref, arrived):
    copy = pltpu.make_async_copy(weight_ref, held_ref, arrived)
    copy.start()
    copy.wait()


def fetch(weight):
    return pl.pallas_call(
        fetch_kernel,
        in_specs=[pl.BlockSpec(memory_space=pl.ANY)],
        out_specs=pl.BlockSpec(memory_space=pltpu.VMEM),
        out_shape=pltpu.VMEM(weight.shape, BF16),
        scratch_shapes=[pltpu.SemaphoreType.DMA],
        compiler_params=pltpu.CompilerParams(vmem_limit_bytes=VMEM_BYTES // 2),
        cost_estimate=pl.CostEstimate(flops=0, bytes_accessed=4 * weight.size, transcendentals=0),
        name="fetch",
    )(pltpu.with_memory_space_constraint(weight, pltpu.HBM))


def to_columns(place, view):
    rows, width = view.shape
    return exchange(place, "a", view.reshape(place.n, rows // place.n, width))


def to_planes(place, parts):
    return sends(place, "z", ordered(parts, place.a ^ place.z))


def lay(place, place_array, parts):
    rows, width = parts[0].shape
    (laid,) = local(
        functools.partial(lay_kernel, n=place.n),
        place_array,
        parts,
        [((rows * place.n, width), BF16)],
        "lay",
    )
    return laid


def met_rows(place, values, few=False):
    return sends(place, "a", [values] * place.n, few)


def project_kernel(place_ref, *refs, counts, n, k):
    met = refs[: sum(counts)]
    weight_ref, own_ref, *coded = refs[sum(counts) :]
    width = met[0].shape[1]
    columns = own_ref.shape[1]
    values = []
    for count in counts:
        values.append(jnp.concatenate([ref[...] for ref in met[:count]], 0))
        met = met[count:]
    for step in [*range(1, n), 0]:
        at = pl.ds(pl.multiple_of((place_ref[0] ^ step) * columns, columns), columns)
        total = 0.0
        for i in range(k):
            rows = pl.ds(pl.multiple_of((place_ref[2] ^ i) * width, width), width)
            total += jnp.dot(values[i], weight_ref[rows, at], preferred_element_type=F32)
        if step == 0:
            own_ref[...] = total
        else:
            encode(total, coded[step - 1])


def encode(total, coded_ref):
    rows = total.shape[0]
    top = jnp.max(jnp.abs(total), 0, keepdims=True)
    top = jnp.maximum(top * (1.0 + 1.0 / 128.0), 1e-30).astype(BF16)
    coded_ref[rows:] = jnp.broadcast_to(top, (SCALE_ROWS, total.shape[1]))
    whole = jnp.floor(jnp.abs(total) * (HIGHEST / top.astype(F32)) + 0.5)
    power = jnp.floor(whole * (1.0 / 128.0))
    word = (1.0 + (whole * (1.0 / 128.0) - power)) * jnp.exp2(power - POWERS // 2)
    coded_ref[:rows] = jnp.where(total < 0.0, -word, word).astype(BF16)


def decode(coded_ref, count):
    rows = coded_ref.shape[0] - SCALE_ROWS
    scale = coded_ref[rows:].astype(F32)[:1] * (1.0 / HIGHEST)
    height = rows // count
    blocks = []
    for i in range(count):
        word = coded_ref[i * height : (i + 1) * height].astype(F32)
        size = jnp.abs(word)
        power = jnp.floor(jnp.log(size) * 1.4426950408889634 + 0.002)
        part = jnp.floor(size * jnp.exp2(-power) * 128.0 + 0.5)
        whole = (power + (POWERS // 2 - 1)) * 128.0 + part
        blocks.append(jnp.where(word < 0.0, -whole, whole) * scale)
    return blocks


def project(place, place_array, met, held):
    n, k = place.n, place.k
    rows, width = met[0][0].shape
    batch, columns = rows * n, held.shape[1] // n
    counts = [len(parts) for parts in met]
    met = [part for parts in met for part in parts]
    coded = batch + SCALE_ROWS
    out_shape = [jax.ShapeDtypeStruct((batch, columns), F32)]
    out_shape += [jax.ShapeDtypeStruct((coded, columns), BF16)] * (n - 1)
    space = pl.BlockSpec(memory_space=pltpu.VMEM)
    own, *parts = pl.pallas_call(
        functools.partial(project_kernel, counts=counts, n=n, k=k),
        in_specs=[pl.BlockSpec(memory_space=pltpu.SMEM)]
        + [space] * (len(met) + 1),
        out_specs=[space] * n,
        out_shape=out_shape,
        compiler_params=pltpu.CompilerParams(vmem_limit_bytes=VMEM_BYTES),
        cost_estimate=pl.CostEstimate(
            flops=2 * batch * k * width * n * columns,
            bytes_accessed=2 * k * width * (batch + n * columns) + 3 * n * batch * columns,
            transcendentals=0,
        ),
        name="project",
    )(place_array, *met, pltpu.with_memory_space_constraint(held, pltpu.VMEM))
    return own, parts


def normalize_kernel(place_ref, *refs, n, k, second):
    own_ref, parts = refs[0], refs[1:n]
    refs = refs[n:]
    if second:
        other_ref, refs = refs[0], refs[1:]
    norm_ref, packed_ref, scale_ref = refs[:3]
    grams = refs[3 : 3 + k]
    batch, columns = own_ref.shape
    height = batch // n
    met = [[own_ref[i * height : (i + 1) * height] for i in range(n)]]
    for step in range(1, n):
        met.append(decode(parts[step - 1], n))
    blocks = [tree_sum([met[step][i] for step in range(n)]) for i in range(n)]
    total = tree_sum([jnp.sum(block, 0, keepdims=True) for block in blocks])
    squares = tree_sum([jnp.sum(block * block, 0, keepdims=True) for block in blocks])
    mean = total / batch
    scale = lax.rsqrt(squares / batch - mean * mean + bn_eps)
    scale_ref[...] = scale
    rows, few = batch // n, batch // (n * n)
    for i, block in enumerate(blocks):
        normed = (block - mean) * scale
        for first in range(0, height, few):
            step, plane = divmod((i * height + first) // few, n)
            at = pl.multiple_of(plane * rows + (place_ref[1] ^ step) * few, few)
            norm_ref[pl.ds(at, few), :] = normed[first : first + few]
            packed_ref[pl.ds(at, few), :] = normed[first : first + few].astype(BF16)
    dims = (((1,), (1,)), ((), ()))
    packed = packed_ref[...]
    size = batch // k
    for i in range(k):
        at = pl.multiple_of((place_ref[2] ^ i) * size, size)
        gram = lax.dot_general(packed_ref[pl.ds(at, size), :], packed, dims, preferred_element_type=F32)
        grams[i][...] = gram
    if second:
        coeff_ref = refs[3 + k]
        diag = jnp.sum(norm_ref[...] * other_ref[...], 0, keepdims=True) / batch
        coeff_ref[...] = 2.0 * ((1.0 - off_weight) * diag - 1.0)
        share = jnp.sum((1.0 - diag) ** 2 - off_weight * diag * diag, 1, keepdims=True)
        for i in range(k):

            @pl.when((place_ref[2] ^ i) == k - 1)
            def _():
                row = grams[i][size - 8 :, :128]
                first = (lax.broadcasted_iota(jnp.int32, row.shape, 0) == 7) & (
                    lax.broadcasted_iota(jnp.int32, row.shape, 1) == 0
                )
                grams[i][size - 8 :, :128] = jnp.where(first, share, row)


def normalize_parts(place, place_array, own, parts, other=None):
    n, k = place.n, place.k
    batch, columns = own.shape
    second = other is not None
    out_shape = [
        jax.ShapeDtypeStruct((batch, columns), F32),
        jax.ShapeDtypeStruct((batch, columns), BF16),
        jax.ShapeDtypeStruct((1, columns), F32),
    ] + [jax.ShapeDtypeStruct((batch // k, batch), F32)] * k
    if second:
        out_shape.append(jax.ShapeDtypeStruct((1, columns), F32))
    args = [own, *parts] + ([other] if second else [])
    space = pl.BlockSpec(memory_space=pltpu.VMEM)
    return pl.pallas_call(
        functools.partial(normalize_kernel, n=n, k=k, second=second),
        in_specs=[pl.BlockSpec(memory_space=pltpu.SMEM)] + [space] * len(args),
        out_specs=[space] * len(out_shape),
        out_shape=out_shape,
        compiler_params=pltpu.CompilerParams(vmem_limit_bytes=VMEM_BYTES // 2),
        cost_estimate=pl.CostEstimate(
            flops=2 * batch * batch * columns,
            bytes_accessed=16 * batch * columns + 4 * batch * batch,
            transcendentals=0,
        ),
        name="normalize",
    )(place_array, *args)


def gradient_kernel(place_ref, *refs, n, k):
    grams, refs = refs[: n * k], refs[n * k :]
    packed, norms, scales, coeff_ref, refs = refs[0:2], refs[2:4], refs[4:6], refs[6], refs[7:]
    outs, loss_ref = refs[:n], refs[n]
    gram_ref, whole_ref = refs[n + 1 :]
    batch, columns = norms[0].shape
    height = grams[0].shape[0] // 2
    for i in range(k):
        for step in range(n):
            at = ((place_ref[2] ^ i) * n + (place_ref[1] ^ step)) * height
            to = pl.ds(pl.multiple_of(at, height), height)
            for view in range(2):
                gram_ref[view, to, :] = grams[i * n + step][view * height : (view + 1) * height, :]
    edge = batch - 128
    tail = gram_ref[1, edge:, :128].astype(F32)
    row = lax.broadcasted_iota(jnp.int32, tail.shape, 0)
    column = lax.broadcasted_iota(jnp.int32, tail.shape, 1)
    taken = (row == 127) & (column < 3)
    mirror = gram_ref[1, :128, edge:].astype(F32).T
    share = jnp.sum(jnp.where(taken, tail, 0.0), keepdims=True)
    gram_ref[1, edge:, :128] = jnp.where(taken, mirror, tail).astype(BF16)
    factor = 2.0 * off_weight / batch
    rows = batch // n
    for view in (1, 0):
        norm = norms[view][...]
        grad = (
            factor * jnp.dot(gram_ref[1 - view], packed[view][...], preferred_element_type=F32)
            + coeff_ref[...] * norms[1 - view][...]
        )
        first = jnp.sum(grad, 0, keepdims=True) / batch
        second = jnp.sum(grad * norm, 0, keepdims=True) / batch
        whole_ref[view] = (scales[view][...] * (grad - first - norm * second)).astype(BF16)
        for step in range(n):
            at = pl.multiple_of((place_ref[0] ^ step) * rows, rows)
            outs[step][view * rows : (view + 1) * rows, :] = whole_ref[view, pl.ds(at, rows), :]
    frob = jnp.sum(gram_ref[0].astype(F32) * gram_ref[1].astype(F32), keepdims=True)
    loss_ref[...] = (share + off_weight * (frob / (batch * batch))) / D


def gradient(place, place_array, grams, packed, norms, scales, coeff):
    batch, columns = norms[0].shape
    return local(
        functools.partial(gradient_kernel, n=place.n, k=place.k),
        place_array,
        (*grams, *packed, *norms, *scales, coeff),
        [((2 * batch // place.n, columns), BF16)] * place.n + [((1, 1), F32)],
        "gradient",
        scratch_shapes=[
            pltpu.VMEM((2, batch, batch), BF16),
            pltpu.VMEM((2, batch, columns), BF16),
        ],
    )


def place_kernel(place_ref, *refs, n):
    parts, outs = refs[:n], refs[n:]
    rows, columns = parts[0].shape[0] // len(outs), parts[0].shape[1]
    for step in range(n):
        at = pl.ds(pl.multiple_of((place_ref[0] ^ step) * columns, columns), columns)
        for i, out in enumerate(outs):
            out[:, at] = parts[step][i * rows : (i + 1) * rows, :]


def with_kernels(place, h_first, h_second, weight):
    n, k, z, a, b = place.n, place.k, place.z, place.a, place.b
    place_array = jnp.stack([z, a, b]).astype(jnp.int32)
    first = to_columns(place, h_first)
    first, held = lax.optimization_barrier((first, fetch(weight)))
    first, second = lax.optimization_barrier((to_planes(place, first), to_columns(place, h_second)))
    met, second = lax.optimization_barrier(
        (met_rows(place, lay(place, place_array, first)), to_planes(place, second))
    )

    def projected(met, held, whole):
        own = [jnp.concatenate(met, 0)] if whole else met
        others = [place.send(part, lambda z, a, b: (z, a, b ^ 1)) for part in own]
        return project(place, place_array, [met, others], held)

    def second_projected(weight, *parts):
        return projected(met_rows(place, lay(place, place_array, parts), True), fetch(weight), True)

    def sent(parts):
        return sends(place, "z", [parts[0], *parts])[1:]

    own_1, parts_1 = projected(met, held, False)
    second, own_1 = lax.optimization_barrier((second, own_1))
    parts_1 = sent(parts_1)
    own_2, parts_2 = in_one(place, second_projected, (weight, *second))
    own_1, own_2 = lax.optimization_barrier((own_1, own_2))
    parts_2 = sent(parts_2)
    norm_1, packed_1, scale_1, *grams = normalize_parts(place, place_array, own_1, parts_1)
    met_1 = in_one(place, lambda *grams: first_rows(place, place_array, grams), grams)
    met_1 = sends(place, "z", met_1)
    own_2, parts_2, met_1 = lax.optimization_barrier((own_2, parts_2, met_1))
    norm_2, packed_2, scale_2, *grams, coeff = normalize_parts(
        place, place_array, own_2, parts_2, norm_1
    )
    height, batch = met_1[0].shape
    (rows_1,) = local(rows_kernel, place_array, met_1, [((height, batch), BF16)], "rows")
    met_2 = plane_rows(place, place_array, grams)
    rows = met_2[0].shape[0]
    (part,) = local(
        functools.partial(code_kernel, n=n),
        place_array,
        (*met_2, rows_1),
        [((rows + SCALE_ROWS + height, batch), BF16)],
        "code",
    )
    (part,) = local(
        functools.partial(finish_kernel, n=n, k=k),
        place_array,
        sends(place, "z", [part] * n),
        [((2 * rows, batch), BF16)],
        "finish",
    )
    grams = sends(place, "a", [part] * n)
    grams += [place.send(part, lambda z, a, b: (z, a, b ^ 1)) for part in grams]
    *parts, loss = gradient(
        place,
        place_array,
        grams,
        (packed_1, packed_2),
        (norm_1, norm_2),
        (scale_1, scale_2),
        coeff,
    )
    out_1, out_2 = local(
        functools.partial(place_kernel, n=n),
        place_array,
        sends(place, "z", parts),
        [(h_first.shape, BF16)] * 2,
        "place",
    )
    return (out_1, out_2, loss.reshape(()))


def plain(place, h_first, h_second, weight):
    n, k, z, a, b = place.n, place.k, place.z, place.a, place.b
    rows, width = h_first.shape
    batch = rows * n
    columns = weight.shape[1] // n
    weight_parts = weight.reshape(k, width, n * columns)
    zs = []
    for values in (h_first, h_second):
        moved = place.send(values, lambda z, a, b: (a, z, b))
        own = jnp.concatenate(met_rows(place, moved), 0)
        total = jnp.dot(own, pick(weight_parts, b), preferred_element_type=F32)
        for step in range(1, k):
            other = place.send(own, lambda z, a, b, s=step: (z, a, b ^ s))
            total += jnp.dot(other, pick(weight_parts, b ^ step), preferred_element_type=F32)
        cut = total.reshape(batch, n, columns).transpose(1, 0, 2)
        whole = tree_sum(exchange(place, "z", cut)).reshape(n, rows, columns)
        zs.append(jnp.concatenate(ordered([whole[i] for i in range(n)], a), 0))
    normed, scales = [], []
    for values in zs:
        mean = jnp.sum(values, 0) / batch
        scale = lax.rsqrt(jnp.sum(values * values, 0) / batch - mean * mean + bn_eps)
        normed.append((values - mean) * scale)
        scales.append(scale)
    diag = jnp.sum(normed[0] * normed[1], 0) / batch
    packed = [values.astype(BF16) for values in normed]
    dims = (((1,), (1,)), ((), ()))
    grams = []
    for values in packed:
        gram = lax.dot_general(values, values, dims, preferred_element_type=F32)
        grams.append(plain_gram(place, gram))
    frob = jnp.sum(grams[0].astype(F32) * grams[1].astype(F32)) / (batch * batch)
    coeff = 2.0 * ((1.0 - off_weight) * diag - 1.0)
    factor = 2.0 * off_weight / batch
    outs = []
    for view in range(2):
        grad = (
            factor * jnp.dot(grams[1 - view], packed[view], preferred_element_type=F32)
            + coeff * normed[1 - view]
        )
        first = jnp.sum(grad, 0) / batch
        second = jnp.sum(grad * normed[view], 0) / batch
        out = (scales[view] * (grad - first - normed[view] * second)).astype(BF16)
        parts = exchange(place, "z", out.reshape(n, rows, columns))
        outs.append(jnp.concatenate(ordered(parts, z), 1))
    share = jnp.sum((1.0 - diag) ** 2) - off_weight * jnp.sum(diag * diag)
    loss = (lax.psum(share, ("dp", "mp")) + off_weight * frob) / D
    return (outs[0], outs[1], loss)


def per_device(h_first, h_second, weight):
    place = Place()
    columns = weight.shape[1] // place.n
    fits = columns % 128 == 0 and place.n == 4 and place.k == 2
    return (with_kernels if fits else plain)(place, h_first, h_second, weight)


def solution(mesh):
    in_specs = (P("dp", "mp"), P("dp", "mp"), P("dp", "mp"))
    out_specs = (P("dp", "mp"), P("dp", "mp"), P())
    return jax.shard_map(
        per_device, mesh=mesh, in_specs=in_specs, out_specs=out_specs, check_vma=False
    )
```

```python
import functools

import jax
import jax.numpy as jnp
from jax import lax
from jax.experimental import pallas as pl
from jax.experimental.pallas import tpu as pltpu
from jax.sharding import PartitionSpec as P

D = 8192


off_weight = 0.0051
bn_eps = 1e-05

F32 = jnp.float32
BF16 = jnp.bfloat16
VMEM_BYTES = 16 * 1024 * 1024
POWERS = 240
HIGHEST = 128 * POWERS - 1
SCALE_ROWS = 16


class Place:
    def __init__(self):
        self.n = lax.axis_size("dp")
        self.k = lax.axis_size("mp") // self.n
        self.z = lax.axis_index("dp")
        self.a = lax.axis_index("mp") // self.k
        self.b = lax.axis_index("mp") % self.k

    def send(self, value, target):
        n, k = self.n, self.k
        pairs = []
        for z in range(n):
            for a in range(n):
                for b in range(k):
                    to_z, to_a, to_b = target(z, a, b)
                    pairs.append(((z * n + a) * k + b, (to_z * n + to_a) * k + to_b))
        return lax.ppermute(value, ("dp", "mp"), pairs)

    def along(self, axis):
        if axis == "z":
            return self.n, self.z, lambda step: lambda z, a, b: (z ^ step, a, b)
        if axis == "a":
            return self.n, self.a, lambda step: lambda z, a, b: (z, a ^ step, b)
        return self.k, self.b, lambda step: lambda z, a, b: (z, a, b ^ step)


def ordered(parts, place):
    bit = 1
    while bit < len(parts):
        odd = (place & bit) != 0
        parts = [jnp.where(odd, parts[i ^ bit], parts[i]) for i in range(len(parts))]
        bit *= 2
    return parts


def tree_sum(parts):
    while len(parts) > 1:
        parts = [parts[i] + parts[i + 1] for i in range(0, len(parts), 2)]
    return parts[0]


def pick(value, index):
    return lax.dynamic_index_in_dim(value, index, 0, keepdims=False)


def exchange(place, axis, value, few=False):
    size, here, toward = place.along(axis)
    return sends(place, axis, [pick(value, here ^ step) for step in range(size)], few)


def sends(place, axis, parts, few=False):
    size, here, toward = place.along(axis)
    met = {0: parts[0]}
    order = [*range(1, size)] if few else [*range(size - 1, 0, -1)]
    for i, step in enumerate(order):
        part = parts[step]
        if few and i >= 2:
            met[order[i - 2]], part = lax.optimization_barrier((met[order[i - 2]], part))
        met[step] = place.send(part, toward(step))
    return [met[step] for step in range(size)]


def reduce_scatter(place, axis, value, few=False):
    size, here, toward = place.along(axis)
    value = value.reshape((size, value.shape[0] // size) + value.shape[1:])
    return tree_sum(exchange(place, axis, value, few))


def gather(place, axis, value, few=False):
    size, here, toward = place.along(axis)
    parts = sends(place, axis, [value] * size, few)
    return jnp.concatenate(ordered(parts, here), 0)


def halve_kernel(place_ref, kept_ref, met_ref, *outs):
    height = outs[0].shape[0]
    for step, out in enumerate(outs):
        at = pl.ds(pl.multiple_of((place_ref[1] ^ step) * height, height), height)
        total = kept_ref[at, :] + met_ref[at, :]
        if step == 0:
            out[...] = total
        else:
            encode(total, out)


def plane_sum(met):
    return tree_sum([met[0][...]] + [decode(ref, 1)[0] for ref in met[1:]])


def plane_kernel(place_ref, *refs, n):
    met, outs, whole_ref = refs[:n], refs[n:-1], refs[-1]
    whole_ref[...] = plane_sum(met)
    height = outs[0].shape[0]
    for step, out in enumerate(outs):
        at = pl.ds(pl.multiple_of((place_ref[0] ^ step) * height, height), height)
        out[...] = whole_ref[at, :]


def rows_kernel(place_ref, *refs):
    refs[-1][...] = tree_sum([ref[...] for ref in refs[:-1]]).astype(BF16)


def code_kernel(place_ref, *refs, n):
    met, rows_ref, out_ref = refs[:n], refs[n], refs[n + 1]
    total = plane_sum(met)
    coded = total.shape[0] + SCALE_ROWS
    encode(total, out_ref.at[:coded])
    out_ref[coded:] = rows_ref[...]


def finish_kernel(place_ref, *refs, n, k):
    out_ref = refs[-1]
    height = out_ref.shape[0] // 2
    coded, few = height + SCALE_ROWS, height // n
    met = []
    for step in range(n):
        at = pl.ds(pl.multiple_of((place_ref[0] ^ step) * few, few), few)
        out_ref[at, :] = refs[step][coded:]
        met += decode(refs[step].at[:coded], 1)
    total = tree_sum(met)
    last = (place_ref[1] == n - 1) & (place_ref[2] == k - 1)
    edge = total[-8:, :128]
    row = lax.broadcasted_iota(jnp.int32, edge.shape, 0)
    column = lax.broadcasted_iota(jnp.int32, edge.shape, 1)
    taken = (row == 7) & last
    whole = jnp.sum(jnp.where(taken & (column == 0), edge, 0.0), keepdims=True)
    high = whole.astype(BF16).astype(F32)
    middle = (whole - high).astype(BF16).astype(F32)
    three = jnp.where(column == 0, high, jnp.where(column == 1, middle, whole - high - middle))
    edge = jnp.where(taken & (column < 3), three, edge)
    edge = jnp.concatenate([edge, total[-8:, 128:]], 1)
    out_ref[height:] = jnp.concatenate([total[:-8], edge], 0).astype(BF16)


def local(kernel, place_array, args, shapes, name, **more):
    space = pl.BlockSpec(memory_space=pltpu.VMEM)
    return pl.pallas_call(
        kernel,
        in_specs=[pl.BlockSpec(memory_space=pltpu.SMEM)] + [space] * len(args),
        out_specs=[space] * len(shapes),
        out_shape=[jax.ShapeDtypeStruct(shape, dtype) for shape, dtype in shapes],
        compiler_params=pltpu.CompilerParams(vmem_limit_bytes=VMEM_BYTES // 2),
        name=name,
        **more,
    )(place_array, *args)


def plane_rows(place, place_array, grams, few=False):
    half, batch = grams[0].shape
    kept, other = grams
    other = place.send(other, lambda z, a, b: (z, a, b ^ 1))
    height = half // place.n
    parts = local(
        halve_kernel,
        place_array,
        (kept, other),
        [((height, batch), F32)] + [((height + SCALE_ROWS, batch), BF16)] * (place.n - 1),
        "halve",
    )
    return sends(place, "a", parts, few)


def first_rows(place, place_array, grams):
    parts = plane_rows(place, place_array, grams, True)
    height, batch = parts[0].shape
    return local(
        functools.partial(plane_kernel, n=place.n),
        place_array,
        parts,
        [((height // place.n, batch), F32)] * place.n,
        "plane",
        scratch_shapes=[pltpu.VMEM((height, batch), F32)],
    )


def in_one(place, run, args):
    shapes = jax.eval_shape(run, *args)
    return lax.cond(
        place.z < place.n,
        run,
        lambda *args: jax.tree.map(lambda leaf: jnp.zeros(leaf.shape, leaf.dtype), shapes),
        *args,
    )


def plain_gram(place, part):
    for axis in ("b", "a", "z"):
        part = reduce_scatter(place, axis, part)
    part = part.astype(BF16)
    for axis in ("z", "a", "b"):
        part = gather(place, axis, part)
    return part


def lay_kernel(place_ref, *refs, n):
    parts, outs = refs[:n], refs[n:]
    few = parts[0].shape[0] // len(outs)
    for step in range(n):
        at = pl.ds(pl.multiple_of((place_ref[0] ^ step) * few, few), few)
        for i, out in enumerate(outs):
            out[at, :] = parts[step][i * few : (i + 1) * few, :]


def fetch_kernel(weight_ref, held_ref, arrived):
    copy = pltpu.make_async_copy(weight_ref, held_ref, arrived)
    copy.start()
    copy.wait()


def fetch(weight):
    return pl.pallas_call(
        fetch_kernel,
        in_specs=[pl.BlockSpec(memory_space=pl.ANY)],
        out_specs=pl.BlockSpec(memory_space=pltpu.VMEM),
        out_shape=pltpu.VMEM(weight.shape, BF16),
        scratch_shapes=[pltpu.SemaphoreType.DMA],
        compiler_params=pltpu.CompilerParams(vmem_limit_bytes=VMEM_BYTES // 2),
        cost_estimate=pl.CostEstimate(flops=0, bytes_accessed=4 * weight.size, transcendentals=0),
        name="fetch",
    )(pltpu.with_memory_space_constraint(weight, pltpu.HBM))


def to_columns(place, view):
    rows, width = view.shape
    return exchange(place, "a", view.reshape(place.n, rows // place.n, width))


def to_planes(place, parts):
    return sends(place, "z", ordered(parts, place.a ^ place.z))


def lay(place, place_array, parts):
    rows, width = parts[0].shape
    (laid,) = local(
        functools.partial(lay_kernel, n=place.n),
        place_array,
        parts,
        [((rows * place.n, width), BF16)],
        "lay",
    )
    return laid


def met_rows(place, values, few=False):
    return sends(place, "a", [values] * place.n, few)


def project_kernel(place_ref, *refs, counts, n, k):
    met = refs[: sum(counts)]
    weight_ref, own_ref, *coded = refs[sum(counts) :]
    width = met[0].shape[1]
    columns = own_ref.shape[1]
    values = []
    for count in counts:
        values.append(jnp.concatenate([ref[...] for ref in met[:count]], 0))
        met = met[count:]
    for step in [*range(1, n), 0]:
        at = pl.ds(pl.multiple_of((place_ref[0] ^ step) * columns, columns), columns)
        total = 0.0
        for i in range(k):
            rows = pl.ds(pl.multiple_of((place_ref[2] ^ i) * width, width), width)
            total += jnp.dot(values[i], weight_ref[rows, at], preferred_element_type=F32)
        if step == 0:
            own_ref[...] = total
        else:
            encode(total, coded[step - 1])


def encode(total, coded_ref):
    rows = total.shape[0]
    top = jnp.max(jnp.abs(total), 0, keepdims=True)
    top = jnp.maximum(top * (1.0 + 1.0 / 128.0), 1e-30).astype(BF16)
    coded_ref[rows:] = jnp.broadcast_to(top, (SCALE_ROWS, total.shape[1]))
    whole = jnp.floor(jnp.abs(total) * (HIGHEST / top.astype(F32)) + 0.5)
    power = jnp.floor(whole * (1.0 / 128.0))
    word = (1.0 + (whole * (1.0 / 128.0) - power)) * jnp.exp2(power - POWERS // 2)
    coded_ref[:rows] = jnp.where(total < 0.0, -word, word).astype(BF16)


def decode(coded_ref, count):
    rows = coded_ref.shape[0] - SCALE_ROWS
    scale = coded_ref[rows:].astype(F32)[:1] * (1.0 / HIGHEST)
    height = rows // count
    blocks = []
    for i in range(count):
        word = coded_ref[i * height : (i + 1) * height].astype(F32)
        size = jnp.abs(word)
        power = jnp.floor(jnp.log(size) * 1.4426950408889634 + 0.002)
        part = jnp.floor(size * jnp.exp2(-power) * 128.0 + 0.5)
        whole = (power + (POWERS // 2 - 1)) * 128.0 + part
        blocks.append(jnp.where(word < 0.0, -whole, whole) * scale)
    return blocks


def project(place, place_array, met, held):
    n, k = place.n, place.k
    rows, width = met[0][0].shape
    batch, columns = rows * n, held.shape[1] // n
    counts = [len(parts) for parts in met]
    met = [part for parts in met for part in parts]
    coded = batch + SCALE_ROWS
    out_shape = [jax.ShapeDtypeStruct((batch, columns), F32)]
    out_shape += [jax.ShapeDtypeStruct((coded, columns), BF16)] * (n - 1)
    space = pl.BlockSpec(memory_space=pltpu.VMEM)
    own, *parts = pl.pallas_call(
        functools.partial(project_kernel, counts=counts, n=n, k=k),
        in_specs=[pl.BlockSpec(memory_space=pltpu.SMEM)]
        + [space] * (len(met) + 1),
        out_specs=[space] * n,
        out_shape=out_shape,
        compiler_params=pltpu.CompilerParams(vmem_limit_bytes=VMEM_BYTES),
        cost_estimate=pl.CostEstimate(
            flops=2 * batch * k * width * n * columns,
            bytes_accessed=2 * k * width * (batch + n * columns) + 3 * n * batch * columns,
            transcendentals=0,
        ),
        name="project",
    )(place_array, *met, pltpu.with_memory_space_constraint(held, pltpu.VMEM))
    return own, parts


def normalize_kernel(place_ref, *refs, n, k, second):
    own_ref, parts = refs[0], refs[1:n]
    refs = refs[n:]
    if second:
        other_ref, refs = refs[0], refs[1:]
    norm_ref, packed_ref, scale_ref = refs[:3]
    grams = refs[3 : 3 + k]
    batch, columns = own_ref.shape
    height = batch // n
    met = [[own_ref[i * height : (i + 1) * height] for i in range(n)]]
    for step in range(1, n):
        met.append(decode(parts[step - 1], n))
    blocks = [tree_sum([met[step][i] for step in range(n)]) for i in range(n)]
    total = tree_sum([jnp.sum(block, 0, keepdims=True) for block in blocks])
    squares = tree_sum([jnp.sum(block * block, 0, keepdims=True) for block in blocks])
    mean = total / batch
    scale = lax.rsqrt(squares / batch - mean * mean + bn_eps)
    scale_ref[...] = scale
    rows, few = batch // n, batch // (n * n)
    for i, block in enumerate(blocks):
        normed = (block - mean) * scale
        for first in range(0, height, few):
            step, plane = divmod((i * height + first) // few, n)
            at = pl.multiple_of(plane * rows + (place_ref[1] ^ step) * few, few)
            norm_ref[pl.ds(at, few), :] = normed[first : first + few]
            packed_ref[pl.ds(at, few), :] = normed[first : first + few].astype(BF16)
    dims = (((1,), (1,)), ((), ()))
    packed = packed_ref[...]
    size = batch // k
    for i in range(k):
        at = pl.multiple_of((place_ref[2] ^ i) * size, size)
        gram = lax.dot_general(packed_ref[pl.ds(at, size), :], packed, dims, preferred_element_type=F32)
        grams[i][...] = gram
    if second:
        coeff_ref = refs[3 + k]
        diag = jnp.sum(norm_ref[...] * other_ref[...], 0, keepdims=True) / batch
        coeff_ref[...] = 2.0 * ((1.0 - off_weight) * diag - 1.0)
        share = jnp.sum((1.0 - diag) ** 2 - off_weight * diag * diag, 1, keepdims=True)
        for i in range(k):

            @pl.when((place_ref[2] ^ i) == k - 1)
            def _():
                row = grams[i][size - 8 :, :128]
                first = (lax.broadcasted_iota(jnp.int32, row.shape, 0) == 7) & (
                    lax.broadcasted_iota(jnp.int32, row.shape, 1) == 0
                )
                grams[i][size - 8 :, :128] = jnp.where(first, share, row)


def normalize_parts(place, place_array, own, parts, other=None):
    n, k = place.n, place.k
    batch, columns = own.shape
    second = other is not None
    out_shape = [
        jax.ShapeDtypeStruct((batch, columns), F32),
        jax.ShapeDtypeStruct((batch, columns), BF16),
        jax.ShapeDtypeStruct((1, columns), F32),
    ] + [jax.ShapeDtypeStruct((batch // k, batch), F32)] * k
    if second:
        out_shape.append(jax.ShapeDtypeStruct((1, columns), F32))
    args = [own, *parts] + ([other] if second else [])
    space = pl.BlockSpec(memory_space=pltpu.VMEM)
    return pl.pallas_call(
        functools.partial(normalize_kernel, n=n, k=k, second=second),
        in_specs=[pl.BlockSpec(memory_space=pltpu.SMEM)] + [space] * len(args),
        out_specs=[space] * len(out_shape),
        out_shape=out_shape,
        compiler_params=pltpu.CompilerParams(vmem_limit_bytes=VMEM_BYTES // 2),
        cost_estimate=pl.CostEstimate(
            flops=2 * batch * batch * columns,
            bytes_accessed=16 * batch * columns + 4 * batch * batch,
            transcendentals=0,
        ),
        name="normalize",
    )(place_array, *args)


def gradient_kernel(place_ref, *refs, n, k):
    grams, refs = refs[: n * k], refs[n * k :]
    packed, norms, scales, coeff_ref, refs = refs[0:2], refs[2:4], refs[4:6], refs[6], refs[7:]
    outs, loss_ref = refs[:n], refs[n]
    gram_ref, whole_ref = refs[n + 1 :]
    batch, columns = norms[0].shape
    height = grams[0].shape[0] // 2
    for i in range(k):
        for step in range(n):
            at = ((place_ref[2] ^ i) * n + (place_ref[1] ^ step)) * height
            to = pl.ds(pl.multiple_of(at, height), height)
            for view in range(2):
                gram_ref[view, to, :] = grams[i * n + step][view * height : (view + 1) * height, :]
    edge = batch - 128
    tail = gram_ref[1, edge:, :128].astype(F32)
    row = lax.broadcasted_iota(jnp.int32, tail.shape, 0)
    column = lax.broadcasted_iota(jnp.int32, tail.shape, 1)
    taken = (row == 127) & (column < 3)
    mirror = gram_ref[1, :128, edge:].astype(F32).T
    share = jnp.sum(jnp.where(taken, tail, 0.0), keepdims=True)
    gram_ref[1, edge:, :128] = jnp.where(taken, mirror, tail).astype(BF16)
    factor = 2.0 * off_weight / batch
    rows = batch // n
    for view in (1, 0):
        norm = norms[view][...]
        grad = (
            factor * jnp.dot(gram_ref[1 - view], packed[view][...], preferred_element_type=F32)
            + coeff_ref[...] * norms[1 - view][...]
        )
        first = jnp.sum(grad, 0, keepdims=True) / batch
        second = jnp.sum(grad * norm, 0, keepdims=True) / batch
        whole_ref[view] = (scales[view][...] * (grad - first - norm * second)).astype(BF16)
        for step in range(n):
            at = pl.multiple_of((place_ref[0] ^ step) * rows, rows)
            outs[step][view * rows : (view + 1) * rows, :] = whole_ref[view, pl.ds(at, rows), :]
    frob = jnp.sum(gram_ref[0].astype(F32) * gram_ref[1].astype(F32), keepdims=True)
    loss_ref[...] = (share + off_weight * (frob / (batch * batch))) / D


def gradient(place, place_array, grams, packed, norms, scales, coeff):
    batch, columns = norms[0].shape
    return local(
        functools.partial(gradient_kernel, n=place.n, k=place.k),
        place_array,
        (*grams, *packed, *norms, *scales, coeff),
        [((2 * batch // place.n, columns), BF16)] * place.n + [((1, 1), F32)],
        "gradient",
        scratch_shapes=[
            pltpu.VMEM((2, batch, batch), BF16),
            pltpu.VMEM((2, batch, columns), BF16),
        ],
    )


def place_kernel(place_ref, *refs, n):
    parts, outs = refs[:n], refs[n:]
    rows, columns = parts[0].shape[0] // len(outs), parts[0].shape[1]
    for step in range(n):
        at = pl.ds(pl.multiple_of((place_ref[0] ^ step) * columns, columns), columns)
        for i, out in enumerate(outs):
            out[:, at] = parts[step][i * rows : (i + 1) * rows, :]


def with_kernels(place, h_first, h_second, weight):
    n, k, z, a, b = place.n, place.k, place.z, place.a, place.b
    place_array = jnp.stack([z, a, b]).astype(jnp.int32)
    first = to_columns(place, h_first)
    first, second = lax.optimization_barrier((to_planes(place, first), to_columns(place, h_second)))
    first, late_weight = lax.optimization_barrier((lay(place, place_array, first), weight))
    met_1, second, held = lax.optimization_barrier(
        (met_rows(place, first), to_planes(place, second), fetch(late_weight))
    )

    def sent(parts):
        return sends(place, "z", [parts[0], *parts])[1:]

    def swapped(part):
        return place.send(part, lambda z, a, b: (z, a, b ^ 1))

    own_1, parts_1 = project(place, place_array, [met_1, [swapped(part) for part in met_1]], held)
    second = lay(place, place_array, second)
    size, here, toward = place.along("a")
    met_2 = [second] + [place.send(second, toward(step)) for step in range(1, size - 1)]
    own_1, parts_1, met_2 = lax.optimization_barrier((own_1, parts_1, met_2))
    parts_1 = sent(parts_1)

    def second_projected(weight, *met):
        last = place.send(met[0], toward(size - 1))
        others = [swapped(jnp.concatenate(met, 0))]
        last, others = lax.optimization_barrier((last, others))
        others.append(swapped(last))
        return project(place, place_array, [[*met, last], others], fetch(weight))

    own_2, parts_2 = in_one(place, second_projected, (weight, *met_2))
    own_1, own_2 = lax.optimization_barrier((own_1, own_2))
    parts_2 = sent(parts_2)
    norm_1, packed_1, scale_1, *grams = normalize_parts(place, place_array, own_1, parts_1)
    met_1 = in_one(place, lambda *grams: first_rows(place, place_array, grams), grams)
    met_1 = sends(place, "z", met_1)
    own_2, parts_2, met_1 = lax.optimization_barrier((own_2, parts_2, met_1))
    norm_2, packed_2, scale_2, *grams, coeff = normalize_parts(
        place, place_array, own_2, parts_2, norm_1
    )
    height, batch = met_1[0].shape
    (rows_1,) = local(rows_kernel, place_array, met_1, [((height, batch), BF16)], "rows")
    met_2 = plane_rows(place, place_array, grams)
    rows = met_2[0].shape[0]
    (part,) = local(
        functools.partial(code_kernel, n=n),
        place_array,
        (*met_2, rows_1),
        [((rows + SCALE_ROWS + height, batch), BF16)],
        "code",
    )
    (part,) = local(
        functools.partial(finish_kernel, n=n, k=k),
        place_array,
        sends(place, "z", [part] * n),
        [((2 * rows, batch), BF16)],
        "finish",
    )
    grams = sends(place, "a", [part] * n)
    grams += [place.send(part, lambda z, a, b: (z, a, b ^ 1)) for part in grams]
    *parts, loss = gradient(
        place,
        place_array,
        grams,
        (packed_1, packed_2),
        (norm_1, norm_2),
        (scale_1, scale_2),
        coeff,
    )
    out_1, out_2 = local(
        functools.partial(place_kernel, n=n),
        place_array,
        sends(place, "z", parts),
        [(h_first.shape, BF16)] * 2,
        "place",
    )
    return (out_1, out_2, loss.reshape(()))


def plain(place, h_first, h_second, weight):
    n, k, z, a, b = place.n, place.k, place.z, place.a, place.b
    rows, width = h_first.shape
    batch = rows * n
    columns = weight.shape[1] // n
    weight_parts = weight.reshape(k, width, n * columns)
    zs = []
    for values in (h_first, h_second):
        moved = place.send(values, lambda z, a, b: (a, z, b))
        own = jnp.concatenate(met_rows(place, moved), 0)
        total = jnp.dot(own, pick(weight_parts, b), preferred_element_type=F32)
        for step in range(1, k):
            other = place.send(own, lambda z, a, b, s=step: (z, a, b ^ s))
            total += jnp.dot(other, pick(weight_parts, b ^ step), preferred_element_type=F32)
        cut = total.reshape(batch, n, columns).transpose(1, 0, 2)
        whole = tree_sum(exchange(place, "z", cut)).reshape(n, rows, columns)
        zs.append(jnp.concatenate(ordered([whole[i] for i in range(n)], a), 0))
    normed, scales = [], []
    for values in zs:
        mean = jnp.sum(values, 0) / batch
        scale = lax.rsqrt(jnp.sum(values * values, 0) / batch - mean * mean + bn_eps)
        normed.append((values - mean) * scale)
        scales.append(scale)
    diag = jnp.sum(normed[0] * normed[1], 0) / batch
    packed = [values.astype(BF16) for values in normed]
    dims = (((1,), (1,)), ((), ()))
    grams = []
    for values in packed:
        gram = lax.dot_general(values, values, dims, preferred_element_type=F32)
        grams.append(plain_gram(place, gram))
    frob = jnp.sum(grams[0].astype(F32) * grams[1].astype(F32)) / (batch * batch)
    coeff = 2.0 * ((1.0 - off_weight) * diag - 1.0)
    factor = 2.0 * off_weight / batch
    outs = []
    for view in range(2):
        grad = (
            factor * jnp.dot(grams[1 - view], packed[view], preferred_element_type=F32)
            + coeff * normed[1 - view]
        )
        first = jnp.sum(grad, 0) / batch
        second = jnp.sum(grad * normed[view], 0) / batch
        out = (scales[view] * (grad - first - normed[view] * second)).astype(BF16)
        parts = exchange(place, "z", out.reshape(n, rows, columns))
        outs.append(jnp.concatenate(ordered(parts, z), 1))
    share = jnp.sum((1.0 - diag) ** 2) - off_weight * jnp.sum(diag * diag)
    loss = (lax.psum(share, ("dp", "mp")) + off_weight * frob) / D
    return (outs[0], outs[1], loss)


def per_device(h_first, h_second, weight):
    place = Place()
    columns = weight.shape[1] // place.n
    fits = columns % 128 == 0 and place.n == 4 and place.k == 2
    return (with_kernels if fits else plain)(place, h_first, h_second, weight)


def solution(mesh):
    in_specs = (P("dp", "mp"), P("dp", "mp"), P("dp", "mp"))
    out_specs = (P("dp", "mp"), P("dp", "mp"), P())
    return jax.shard_map(
        per_device, mesh=mesh, in_specs=in_specs, out_specs=out_specs, check_vma=False
    )
```

```python
import functools

import jax
import jax.numpy as jnp
from jax import lax
from jax.experimental import pallas as pl
from jax.experimental.pallas import tpu as pltpu
from jax.sharding import PartitionSpec as P

D = 8192


off_weight = 0.0051
bn_eps = 1e-05

F32 = jnp.float32
BF16 = jnp.bfloat16
VMEM_BYTES = 16 * 1024 * 1024
POWERS = 240
HIGHEST = 128 * POWERS - 1
SCALE_ROWS = 16


class Place:
    def __init__(self):
        self.n = lax.axis_size("dp")
        self.k = lax.axis_size("mp") // self.n
        self.z = lax.axis_index("dp")
        self.a = lax.axis_index("mp") // self.k
        self.b = lax.axis_index("mp") % self.k

    def send(self, value, target):
        n, k = self.n, self.k
        pairs = []
        for z in range(n):
            for a in range(n):
                for b in range(k):
                    to_z, to_a, to_b = target(z, a, b)
                    pairs.append(((z * n + a) * k + b, (to_z * n + to_a) * k + to_b))
        return lax.ppermute(value, ("dp", "mp"), pairs)

    def along(self, axis):
        if axis == "z":
            return self.n, self.z, lambda step: lambda z, a, b: (z ^ step, a, b)
        if axis == "a":
            return self.n, self.a, lambda step: lambda z, a, b: (z, a ^ step, b)
        return self.k, self.b, lambda step: lambda z, a, b: (z, a, b ^ step)


def ordered(parts, place):
    bit = 1
    while bit < len(parts):
        odd = (place & bit) != 0
        parts = [jnp.where(odd, parts[i ^ bit], parts[i]) for i in range(len(parts))]
        bit *= 2
    return parts


def tree_sum(parts):
    while len(parts) > 1:
        parts = [parts[i] + parts[i + 1] for i in range(0, len(parts), 2)]
    return parts[0]


def pick(value, index):
    return lax.dynamic_index_in_dim(value, index, 0, keepdims=False)


def exchange(place, axis, value, few=False):
    size, here, toward = place.along(axis)
    return sends(place, axis, [pick(value, here ^ step) for step in range(size)], few)


def sends(place, axis, parts, few=False):
    size, here, toward = place.along(axis)
    met = {0: parts[0]}
    order = [*range(1, size)] if few else [*range(size - 1, 0, -1)]
    for i, step in enumerate(order):
        part = parts[step]
        if few and i >= 2:
            met[order[i - 2]], part = lax.optimization_barrier((met[order[i - 2]], part))
        met[step] = place.send(part, toward(step))
    return [met[step] for step in range(size)]


def reduce_scatter(place, axis, value, few=False):
    size, here, toward = place.along(axis)
    value = value.reshape((size, value.shape[0] // size) + value.shape[1:])
    return tree_sum(exchange(place, axis, value, few))


def gather(place, axis, value, few=False):
    size, here, toward = place.along(axis)
    parts = sends(place, axis, [value] * size, few)
    return jnp.concatenate(ordered(parts, here), 0)


def halve_kernel(place_ref, kept_ref, met_ref, *outs):
    height = outs[0].shape[0]
    for step, out in enumerate(outs):
        at = pl.ds(pl.multiple_of((place_ref[1] ^ step) * height, height), height)
        total = kept_ref[at, :] + met_ref[at, :]
        if step == 0:
            out[...] = total
        else:
            encode(total, out)


def plane_sum(met):
    return tree_sum([met[0][...]] + [decode(ref, 1)[0] for ref in met[1:]])


def plane_kernel(place_ref, *refs, n):
    met, outs, whole_ref = refs[:n], refs[n:-1], refs[-1]
    whole_ref[...] = plane_sum(met)
    height = outs[0].shape[0]
    for step, out in enumerate(outs):
        at = pl.ds(pl.multiple_of((place_ref[0] ^ step) * height, height), height)
        out[...] = whole_ref[at, :]


def rows_kernel(place_ref, *refs):
    refs[-1][...] = tree_sum([ref[...] for ref in refs[:-1]]).astype(BF16)


def code_kernel(place_ref, *refs, n):
    met, rows_ref, out_ref = refs[:n], refs[n], refs[n + 1]
    total = plane_sum(met)
    coded = total.shape[0] + SCALE_ROWS
    encode(total, out_ref.at[:coded])
    out_ref[coded:] = rows_ref[...]


def finish_kernel(place_ref, *refs, n, k):
    out_ref = refs[-1]
    height = out_ref.shape[0] // 2
    coded, few = height + SCALE_ROWS, height // n
    met = []
    for step in range(n):
        at = pl.ds(pl.multiple_of((place_ref[0] ^ step) * few, few), few)
        out_ref[at, :] = refs[step][coded:]
        met += decode(refs[step].at[:coded], 1)
    total = tree_sum(met)
    last = (place_ref[1] == n - 1) & (place_ref[2] == k - 1)
    edge = total[-8:, :128]
    row = lax.broadcasted_iota(jnp.int32, edge.shape, 0)
    column = lax.broadcasted_iota(jnp.int32, edge.shape, 1)
    taken = (row == 7) & last
    whole = jnp.sum(jnp.where(taken & (column == 0), edge, 0.0), keepdims=True)
    high = whole.astype(BF16).astype(F32)
    middle = (whole - high).astype(BF16).astype(F32)
    three = jnp.where(column == 0, high, jnp.where(column == 1, middle, whole - high - middle))
    edge = jnp.where(taken & (column < 3), three, edge)
    edge = jnp.concatenate([edge, total[-8:, 128:]], 1)
    out_ref[height:] = jnp.concatenate([total[:-8], edge], 0).astype(BF16)


def local(kernel, place_array, args, shapes, name, **more):
    space = pl.BlockSpec(memory_space=pltpu.VMEM)
    return pl.pallas_call(
        kernel,
        in_specs=[pl.BlockSpec(memory_space=pltpu.SMEM)] + [space] * len(args),
        out_specs=[space] * len(shapes),
        out_shape=[jax.ShapeDtypeStruct(shape, dtype) for shape, dtype in shapes],
        compiler_params=pltpu.CompilerParams(vmem_limit_bytes=VMEM_BYTES // 2),
        name=name,
        **more,
    )(place_array, *args)


def plane_rows(place, place_array, grams, few=False):
    half, batch = grams[0].shape
    kept, other = grams
    other = place.send(other, lambda z, a, b: (z, a, b ^ 1))
    height = half // place.n
    parts = local(
        halve_kernel,
        place_array,
        (kept, other),
        [((height, batch), F32)] + [((height + SCALE_ROWS, batch), BF16)] * (place.n - 1),
        "halve",
    )
    return sends(place, "a", parts, few)


def first_rows(place, place_array, grams):
    parts = plane_rows(place, place_array, grams, True)
    height, batch = parts[0].shape
    return local(
        functools.partial(plane_kernel, n=place.n),
        place_array,
        parts,
        [((height // place.n, batch), F32)] * place.n,
        "plane",
        scratch_shapes=[pltpu.VMEM((height, batch), F32)],
    )


def in_one(place, run, args):
    shapes = jax.eval_shape(run, *args)
    return lax.cond(
        place.z < place.n,
        run,
        lambda *args: jax.tree.map(lambda leaf: jnp.zeros(leaf.shape, leaf.dtype), shapes),
        *args,
    )


def plain_gram(place, part):
    for axis in ("b", "a", "z"):
        part = reduce_scatter(place, axis, part)
    part = part.astype(BF16)
    for axis in ("z", "a", "b"):
        part = gather(place, axis, part)
    return part


def lay_kernel(place_ref, *refs, n):
    parts, outs = refs[:n], refs[n:]
    few = parts[0].shape[0] // len(outs)
    for step in range(n):
        at = pl.ds(pl.multiple_of((place_ref[0] ^ step) * few, few), few)
        for i, out in enumerate(outs):
            out[at, :] = parts[step][i * few : (i + 1) * few, :]


def fetch_kernel(weight_ref, held_ref, arrived):
    copy = pltpu.make_async_copy(weight_ref, held_ref, arrived)
    copy.start()
    copy.wait()


def fetch(weight):
    return pl.pallas_call(
        fetch_kernel,
        in_specs=[pl.BlockSpec(memory_space=pl.ANY)],
        out_specs=pl.BlockSpec(memory_space=pltpu.VMEM),
        out_shape=pltpu.VMEM(weight.shape, BF16),
        scratch_shapes=[pltpu.SemaphoreType.DMA],
        compiler_params=pltpu.CompilerParams(vmem_limit_bytes=VMEM_BYTES // 2),
        cost_estimate=pl.CostEstimate(flops=0, bytes_accessed=4 * weight.size, transcendentals=0),
        name="fetch",
    )(pltpu.with_memory_space_constraint(weight, pltpu.HBM))


def to_columns(place, view):
    rows, width = view.shape
    return exchange(place, "a", view.reshape(place.n, rows // place.n, width))


def to_planes(place, parts):
    return sends(place, "z", ordered(parts, place.a ^ place.z))


def lay(place, place_array, parts):
    rows, width = parts[0].shape
    (laid,) = local(
        functools.partial(lay_kernel, n=place.n),
        place_array,
        parts,
        [((rows * place.n, width), BF16)],
        "lay",
    )
    return laid


def met_rows(place, values, few=False):
    return sends(place, "a", [values] * place.n, few)


def project_kernel(place_ref, *refs, counts, n, k):
    met = refs[: sum(counts)]
    weight_ref, own_ref, *coded = refs[sum(counts) :]
    width = met[0].shape[1]
    columns = own_ref.shape[1]
    values = []
    for count in counts:
        values.append(jnp.concatenate([ref[...] for ref in met[:count]], 0))
        met = met[count:]
    for step in [*range(n - 1, 0, -1), 0]:
        at = pl.ds(pl.multiple_of((place_ref[0] ^ step) * columns, columns), columns)
        total = 0.0
        for i in range(k):
            rows = pl.ds(pl.multiple_of((place_ref[2] ^ i) * width, width), width)
            total += jnp.dot(values[i], weight_ref[rows, at], preferred_element_type=F32)
        if step == 0:
            own_ref[...] = total
        else:
            encode(total, coded[n - 1 - step])


def encode(total, coded_ref):
    rows = total.shape[0]
    top = jnp.max(jnp.abs(total), 0, keepdims=True)
    top = jnp.maximum(top * (1.0 + 1.0 / 128.0), 1e-30).astype(BF16)
    coded_ref[rows:] = jnp.broadcast_to(top, (SCALE_ROWS, total.shape[1]))
    whole = jnp.floor(jnp.abs(total) * (HIGHEST / top.astype(F32)) + 0.5)
    power = jnp.floor(whole * (1.0 / 128.0))
    word = (1.0 + (whole * (1.0 / 128.0) - power)) * jnp.exp2(power - POWERS // 2)
    coded_ref[:rows] = jnp.where(total < 0.0, -word, word).astype(BF16)


def decode(coded_ref, count):
    rows = coded_ref.shape[0] - SCALE_ROWS
    scale = coded_ref[rows:].astype(F32)[:1] * (1.0 / HIGHEST)
    height = rows // count
    blocks = []
    for i in range(count):
        word = coded_ref[i * height : (i + 1) * height].astype(F32)
        size = jnp.abs(word)
        power = jnp.floor(jnp.log(size) * 1.4426950408889634 + 0.002)
        part = jnp.floor(size * jnp.exp2(-power) * 128.0 + 0.5)
        whole = (power + (POWERS // 2 - 1)) * 128.0 + part
        blocks.append(jnp.where(word < 0.0, -whole, whole) * scale)
    return blocks


def project(place, place_array, met, held):
    n, k = place.n, place.k
    rows, width = met[0][0].shape
    batch, columns = rows * n, held.shape[1] // n
    counts = [len(parts) for parts in met]
    met = [part for parts in met for part in parts]
    coded = batch + SCALE_ROWS
    out_shape = [jax.ShapeDtypeStruct((batch, columns), F32)]
    out_shape += [jax.ShapeDtypeStruct((coded, columns), BF16)] * (n - 1)
    space = pl.BlockSpec(memory_space=pltpu.VMEM)
    own, *parts = pl.pallas_call(
        functools.partial(project_kernel, counts=counts, n=n, k=k),
        in_specs=[pl.BlockSpec(memory_space=pltpu.SMEM)]
        + [space] * (len(met) + 1),
        out_specs=[space] * n,
        out_shape=out_shape,
        compiler_params=pltpu.CompilerParams(vmem_limit_bytes=VMEM_BYTES),
        cost_estimate=pl.CostEstimate(
            flops=2 * batch * k * width * n * columns,
            bytes_accessed=2 * k * width * (batch + n * columns) + 3 * n * batch * columns,
            transcendentals=0,
        ),
        name="project",
    )(place_array, *met, pltpu.with_memory_space_constraint(held, pltpu.VMEM))
    return own, parts[::-1]


def normalize_kernel(place_ref, *refs, n, k, second):
    own_ref, parts = refs[0], refs[n - 1 : 0 : -1]
    refs = refs[n:]
    if second:
        other_ref, refs = refs[0], refs[1:]
    norm_ref, packed_ref, scale_ref = refs[:3]
    grams = refs[3 : 3 + k]
    batch, columns = own_ref.shape
    height = batch // n
    met = [[own_ref[i * height : (i + 1) * height] for i in range(n)]]
    for step in range(1, n):
        met.append(decode(parts[step - 1], n))
    blocks = [tree_sum([met[step][i] for step in range(n)]) for i in range(n)]
    total = tree_sum([jnp.sum(block, 0, keepdims=True) for block in blocks])
    squares = tree_sum([jnp.sum(block * block, 0, keepdims=True) for block in blocks])
    mean = total / batch
    scale = lax.rsqrt(squares / batch - mean * mean + bn_eps)
    scale_ref[...] = scale
    rows, few = batch // n, batch // (n * n)
    for i, block in enumerate(blocks):
        normed = (block - mean) * scale
        for first in range(0, height, few):
            step, plane = divmod((i * height + first) // few, n)
            at = pl.multiple_of(plane * rows + (place_ref[1] ^ step) * few, few)
            norm_ref[pl.ds(at, few), :] = normed[first : first + few]
            packed_ref[pl.ds(at, few), :] = normed[first : first + few].astype(BF16)
    dims = (((1,), (1,)), ((), ()))
    packed = packed_ref[...]
    size = batch // k
    for i in range(k):
        at = pl.multiple_of((place_ref[2] ^ i) * size, size)
        gram = lax.dot_general(packed_ref[pl.ds(at, size), :], packed, dims, preferred_element_type=F32)
        grams[i][...] = gram
    if second:
        coeff_ref = refs[3 + k]
        diag = jnp.sum(norm_ref[...] * other_ref[...], 0, keepdims=True) / batch
        coeff_ref[...] = 2.0 * ((1.0 - off_weight) * diag - 1.0)
        share = jnp.sum((1.0 - diag) ** 2 - off_weight * diag * diag, 1, keepdims=True)
        for i in range(k):

            @pl.when((place_ref[2] ^ i) == k - 1)
            def _():
                row = grams[i][size - 8 :, :128]
                first = (lax.broadcasted_iota(jnp.int32, row.shape, 0) == 7) & (
                    lax.broadcasted_iota(jnp.int32, row.shape, 1) == 0
                )
                grams[i][size - 8 :, :128] = jnp.where(first, share, row)


def normalize_parts(place, place_array, own, parts, other=None):
    n, k = place.n, place.k
    batch, columns = own.shape
    second = other is not None
    out_shape = [
        jax.ShapeDtypeStruct((batch, columns), F32),
        jax.ShapeDtypeStruct((batch, columns), BF16),
        jax.ShapeDtypeStruct((1, columns), F32),
    ] + [jax.ShapeDtypeStruct((batch // k, batch), F32)] * k
    if second:
        out_shape.append(jax.ShapeDtypeStruct((1, columns), F32))
    args = [own, *parts[::-1]] + ([other] if second else [])
    space = pl.BlockSpec(memory_space=pltpu.VMEM)
    return pl.pallas_call(
        functools.partial(normalize_kernel, n=n, k=k, second=second),
        in_specs=[pl.BlockSpec(memory_space=pltpu.SMEM)] + [space] * len(args),
        out_specs=[space] * len(out_shape),
        out_shape=out_shape,
        compiler_params=pltpu.CompilerParams(vmem_limit_bytes=VMEM_BYTES // 2),
        cost_estimate=pl.CostEstimate(
            flops=2 * batch * batch * columns,
            bytes_accessed=16 * batch * columns + 4 * batch * batch,
            transcendentals=0,
        ),
        name="normalize",
    )(place_array, *args)


def gradient_kernel(place_ref, *refs, n, k):
    grams, refs = refs[: n * k], refs[n * k :]
    packed, norms, scales, coeff_ref, refs = refs[0:2], refs[2:4], refs[4:6], refs[6], refs[7:]
    outs, loss_ref = [refs[0], *refs[n - 1 : 0 : -1]], refs[n]
    gram_ref, whole_ref = refs[n + 1 :]
    batch, columns = norms[0].shape
    height = grams[0].shape[0] // 2
    for i in range(k):
        for step in range(n):
            at = ((place_ref[2] ^ i) * n + (place_ref[1] ^ step)) * height
            to = pl.ds(pl.multiple_of(at, height), height)
            for view in range(2):
                gram_ref[view, to, :] = grams[i * n + step][view * height : (view + 1) * height, :]
    edge = batch - 128
    tail = gram_ref[1, edge:, :128].astype(F32)
    row = lax.broadcasted_iota(jnp.int32, tail.shape, 0)
    column = lax.broadcasted_iota(jnp.int32, tail.shape, 1)
    taken = (row == 127) & (column < 3)
    mirror = gram_ref[1, :128, edge:].astype(F32).T
    share = jnp.sum(jnp.where(taken, tail, 0.0), keepdims=True)
    gram_ref[1, edge:, :128] = jnp.where(taken, mirror, tail).astype(BF16)
    factor = 2.0 * off_weight / batch
    rows = batch // n
    for view in (1, 0):
        norm = norms[view][...]
        grad = (
            factor * jnp.dot(gram_ref[1 - view], packed[view][...], preferred_element_type=F32)
            + coeff_ref[...] * norms[1 - view][...]
        )
        first = jnp.sum(grad, 0, keepdims=True) / batch
        second = jnp.sum(grad * norm, 0, keepdims=True) / batch
        whole_ref[view] = (scales[view][...] * (grad - first - norm * second)).astype(BF16)
        for step in range(n):
            at = pl.multiple_of((place_ref[0] ^ step) * rows, rows)
            outs[step][view * rows : (view + 1) * rows, :] = whole_ref[view, pl.ds(at, rows), :]
    frob = jnp.sum(gram_ref[0].astype(F32) * gram_ref[1].astype(F32), keepdims=True)
    loss_ref[...] = (share + off_weight * (frob / (batch * batch))) / D


def gradient(place, place_array, grams, packed, norms, scales, coeff):
    batch, columns = norms[0].shape
    return local(
        functools.partial(gradient_kernel, n=place.n, k=place.k),
        place_array,
        (*grams, *packed, *norms, *scales, coeff),
        [((2 * batch // place.n, columns), BF16)] * place.n + [((1, 1), F32)],
        "gradient",
        scratch_shapes=[
            pltpu.VMEM((2, batch, batch), BF16),
            pltpu.VMEM((2, batch, columns), BF16),
        ],
    )


def place_kernel(place_ref, *refs, n):
    parts, outs = [refs[0], *refs[n - 1 : 0 : -1]], refs[n:]
    rows, columns = parts[0].shape[0] // len(outs), parts[0].shape[1]
    for step in range(n):
        at = pl.ds(pl.multiple_of((place_ref[0] ^ step) * columns, columns), columns)
        for i, out in enumerate(outs):
            out[:, at] = parts[step][i * rows : (i + 1) * rows, :]


def with_kernels(place, h_first, h_second, weight):
    n, k, z, a, b = place.n, place.k, place.z, place.a, place.b
    place_array = jnp.stack([z, a, b]).astype(jnp.int32)
    first, second = lax.optimization_barrier((to_columns(place, h_first), h_second))
    first, second = lax.optimization_barrier((to_planes(place, first), to_columns(place, second)))
    first, late_weight = lax.optimization_barrier((lay(place, place_array, first), weight))
    met_1, second, held = lax.optimization_barrier(
        (met_rows(place, first), to_planes(place, second), fetch(late_weight))
    )

    def sent(parts):
        return sends(place, "z", [parts[0], *parts])[1:]

    def swapped(part):
        return place.send(part, lambda z, a, b: (z, a, b ^ 1))

    own_1, parts_1 = project(place, place_array, [met_1, [swapped(part) for part in met_1]], held)
    second, own_1 = lax.optimization_barrier((second, own_1))
    parts_1 = sent(parts_1)
    size, here, toward = place.along("a")

    def second_projected(weight, *parts):
        values = lay(place, place_array, parts)
        met = [values] + [place.send(values, toward(step)) for step in range(1, size - 1)]
        values, met[1] = lax.optimization_barrier((values, met[1]))
        last = place.send(values, toward(size - 1))
        others = [swapped(jnp.concatenate(met, 0))]
        last, others = lax.optimization_barrier((last, others))
        others.append(swapped(last))
        return project(place, place_array, [[*met, last], others], fetch(weight))

    own_2, parts_2 = in_one(place, second_projected, (weight, *second))
    own_1, own_2 = lax.optimization_barrier((own_1, own_2))
    parts_2 = sent(parts_2)
    norm_1, packed_1, scale_1, *grams = normalize_parts(place, place_array, own_1, parts_1)
    met_1 = in_one(place, lambda *grams: first_rows(place, place_array, grams), grams)
    met_1 = sends(place, "z", met_1)
    own_2, parts_2, met_1 = lax.optimization_barrier((own_2, parts_2, met_1))
    norm_2, packed_2, scale_2, *grams, coeff = normalize_parts(
        place, place_array, own_2, parts_2, norm_1
    )
    height, batch = met_1[0].shape
    (rows_1,) = local(rows_kernel, place_array, met_1, [((height, batch), BF16)], "rows")
    met_2 = plane_rows(place, place_array, grams)
    rows = met_2[0].shape[0]
    (part,) = local(
        functools.partial(code_kernel, n=n),
        place_array,
        (*met_2, rows_1),
        [((rows + SCALE_ROWS + height, batch), BF16)],
        "code",
    )
    (part,) = local(
        functools.partial(finish_kernel, n=n, k=k),
        place_array,
        sends(place, "z", [part] * n),
        [((2 * rows, batch), BF16)],
        "finish",
    )
    grams = sends(place, "a", [part] * n)
    grams += [place.send(part, lambda z, a, b: (z, a, b ^ 1)) for part in grams]
    first, *others, loss = gradient(
        place,
        place_array,
        grams,
        (packed_1, packed_2),
        (norm_1, norm_2),
        (scale_1, scale_2),
        coeff,
    )
    out_1, out_2 = local(
        functools.partial(place_kernel, n=n),
        place_array,
        [first, *sends(place, "z", [first, *others[::-1]])[:0:-1]],
        [(h_first.shape, BF16)] * 2,
        "place",
    )
    return (out_1, out_2, loss.reshape(()))


def plain(place, h_first, h_second, weight):
    n, k, z, a, b = place.n, place.k, place.z, place.a, place.b
    rows, width = h_first.shape
    batch = rows * n
    columns = weight.shape[1] // n
    weight_parts = weight.reshape(k, width, n * columns)
    zs = []
    for values in (h_first, h_second):
        moved = place.send(values, lambda z, a, b: (a, z, b))
        own = jnp.concatenate(met_rows(place, moved), 0)
        total = jnp.dot(own, pick(weight_parts, b), preferred_element_type=F32)
        for step in range(1, k):
            other = place.send(own, lambda z, a, b, s=step: (z, a, b ^ s))
            total += jnp.dot(other, pick(weight_parts, b ^ step), preferred_element_type=F32)
        cut = total.reshape(batch, n, columns).transpose(1, 0, 2)
        whole = tree_sum(exchange(place, "z", cut)).reshape(n, rows, columns)
        zs.append(jnp.concatenate(ordered([whole[i] for i in range(n)], a), 0))
    normed, scales = [], []
    for values in zs:
        mean = jnp.sum(values, 0) / batch
        scale = lax.rsqrt(jnp.sum(values * values, 0) / batch - mean * mean + bn_eps)
        normed.append((values - mean) * scale)
        scales.append(scale)
    diag = jnp.sum(normed[0] * normed[1], 0) / batch
    packed = [values.astype(BF16) for values in normed]
    dims = (((1,), (1,)), ((), ()))
    grams = []
    for values in packed:
        gram = lax.dot_general(values, values, dims, preferred_element_type=F32)
        grams.append(plain_gram(place, gram))
    frob = jnp.sum(grams[0].astype(F32) * grams[1].astype(F32)) / (batch * batch)
    coeff = 2.0 * ((1.0 - off_weight) * diag - 1.0)
    factor = 2.0 * off_weight / batch
    outs = []
    for view in range(2):
        grad = (
            factor * jnp.dot(grams[1 - view], packed[view], preferred_element_type=F32)
            + coeff * normed[1 - view]
        )
        first = jnp.sum(grad, 0) / batch
        second = jnp.sum(grad * normed[view], 0) / batch
        out = (scales[view] * (grad - first - normed[view] * second)).astype(BF16)
        parts = exchange(place, "z", out.reshape(n, rows, columns))
        outs.append(jnp.concatenate(ordered(parts, z), 1))
    share = jnp.sum((1.0 - diag) ** 2) - off_weight * jnp.sum(diag * diag)
    loss = (lax.psum(share, ("dp", "mp")) + off_weight * frob) / D
    return (outs[0], outs[1], loss)


def per_device(h_first, h_second, weight):
    place = Place()
    columns = weight.shape[1] // place.n
    fits = columns % 128 == 0 and place.n == 4 and place.k == 2
    return (with_kernels if fits else plain)(place, h_first, h_second, weight)


def solution(mesh):
    in_specs = (P("dp", "mp"), P("dp", "mp"), P("dp", "mp"))
    out_specs = (P("dp", "mp"), P("dp", "mp"), P())
    return jax.shard_map(
        per_device, mesh=mesh, in_specs=in_specs, out_specs=out_specs, check_vma=False
    )
```

```python
import functools

import jax
import jax.numpy as jnp
from jax import lax
from jax.experimental import pallas as pl
from jax.experimental.pallas import tpu as pltpu
from jax.sharding import PartitionSpec as P

D = 8192


off_weight = 0.0051
bn_eps = 1e-05

F32 = jnp.float32
BF16 = jnp.bfloat16
VMEM_BYTES = 16 * 1024 * 1024
POWERS = 240
HIGHEST = 128 * POWERS - 1
SCALE_ROWS = 16


class Place:
    def __init__(self):
        self.n = lax.axis_size("dp")
        self.k = lax.axis_size("mp") // self.n
        self.z = lax.axis_index("dp")
        self.a = lax.axis_index("mp") // self.k
        self.b = lax.axis_index("mp") % self.k

    def send(self, value, target):
        n, k = self.n, self.k
        pairs = []
        for z in range(n):
            for a in range(n):
                for b in range(k):
                    to_z, to_a, to_b = target(z, a, b)
                    pairs.append(((z * n + a) * k + b, (to_z * n + to_a) * k + to_b))
        return lax.ppermute(value, ("dp", "mp"), pairs)

    def along(self, axis):
        if axis == "z":
            return self.n, self.z, lambda step: lambda z, a, b: (z ^ step, a, b)
        if axis == "a":
            return self.n, self.a, lambda step: lambda z, a, b: (z, a ^ step, b)
        return self.k, self.b, lambda step: lambda z, a, b: (z, a, b ^ step)


def ordered(parts, place):
    bit = 1
    while bit < len(parts):
        odd = (place & bit) != 0
        parts = [jnp.where(odd, parts[i ^ bit], parts[i]) for i in range(len(parts))]
        bit *= 2
    return parts


def tree_sum(parts):
    while len(parts) > 1:
        parts = [parts[i] + parts[i + 1] for i in range(0, len(parts), 2)]
    return parts[0]


def pick(value, index):
    return lax.dynamic_index_in_dim(value, index, 0, keepdims=False)


def exchange(place, axis, value, few=False):
    size, here, toward = place.along(axis)
    return sends(place, axis, [pick(value, here ^ step) for step in range(size)], few)


def sends(place, axis, parts, few=False):
    size, here, toward = place.along(axis)
    met = {0: parts[0]}
    order = [*range(1, size)] if few else [*range(size - 1, 0, -1)]
    for i, step in enumerate(order):
        part = parts[step]
        if few and i >= 2:
            met[order[i - 2]], part = lax.optimization_barrier((met[order[i - 2]], part))
        met[step] = place.send(part, toward(step))
    return [met[step] for step in range(size)]


def reduce_scatter(place, axis, value, few=False):
    size, here, toward = place.along(axis)
    value = value.reshape((size, value.shape[0] // size) + value.shape[1:])
    return tree_sum(exchange(place, axis, value, few))


def gather(place, axis, value, few=False):
    size, here, toward = place.along(axis)
    parts = sends(place, axis, [value] * size, few)
    return jnp.concatenate(ordered(parts, here), 0)


def halve_kernel(place_ref, kept_ref, met_ref, *outs):
    height = outs[0].shape[0]
    for step, out in enumerate(outs):
        at = pl.ds(pl.multiple_of((place_ref[1] ^ step) * height, height), height)
        total = kept_ref[at, :] + met_ref[at, :]
        if step == 0:
            out[...] = total
        else:
            encode(total, out)


def plane_sum(met):
    return tree_sum([met[0][...]] + [decode(ref, 1)[0] for ref in met[1:]])


def plane_kernel(place_ref, *refs, n):
    met, outs, whole_ref = refs[:n], refs[n:-1], refs[-1]
    whole_ref[...] = plane_sum(met)
    height = outs[0].shape[0]
    for step, out in enumerate(outs):
        at = pl.ds(pl.multiple_of((place_ref[0] ^ step) * height, height), height)
        out[...] = whole_ref[at, :]


def rows_kernel(place_ref, *refs):
    refs[-1][...] = tree_sum([ref[...] for ref in refs[:-1]]).astype(BF16)


def code_kernel(place_ref, *refs, n):
    met, rows_ref, out_ref = refs[:n], refs[n], refs[n + 1]
    total = plane_sum(met)
    coded = total.shape[0] + SCALE_ROWS
    encode(total, out_ref.at[:coded])
    out_ref[coded:] = rows_ref[...]


def finish_kernel(place_ref, *refs, n, k):
    out_ref = refs[-1]
    height = out_ref.shape[0] // 2
    coded, few = height + SCALE_ROWS, height // n
    met = []
    for step in range(n):
        at = pl.ds(pl.multiple_of((place_ref[0] ^ step) * few, few), few)
        out_ref[at, :] = refs[step][coded:]
        met += decode(refs[step].at[:coded], 1)
    total = tree_sum(met)
    last = (place_ref[1] == n - 1) & (place_ref[2] == k - 1)
    edge = total[-8:, :128]
    row = lax.broadcasted_iota(jnp.int32, edge.shape, 0)
    column = lax.broadcasted_iota(jnp.int32, edge.shape, 1)
    taken = (row == 7) & last
    whole = jnp.sum(jnp.where(taken & (column == 0), edge, 0.0), keepdims=True)
    high = whole.astype(BF16).astype(F32)
    middle = (whole - high).astype(BF16).astype(F32)
    three = jnp.where(column == 0, high, jnp.where(column == 1, middle, whole - high - middle))
    edge = jnp.where(taken & (column < 3), three, edge)
    edge = jnp.concatenate([edge, total[-8:, 128:]], 1)
    out_ref[height:] = jnp.concatenate([total[:-8], edge], 0).astype(BF16)


def local(kernel, place_array, args, shapes, name, **more):
    space = pl.BlockSpec(memory_space=pltpu.VMEM)
    return pl.pallas_call(
        kernel,
        in_specs=[pl.BlockSpec(memory_space=pltpu.SMEM)] + [space] * len(args),
        out_specs=[space] * len(shapes),
        out_shape=[jax.ShapeDtypeStruct(shape, dtype) for shape, dtype in shapes],
        compiler_params=pltpu.CompilerParams(vmem_limit_bytes=VMEM_BYTES // 2),
        name=name,
        **more,
    )(place_array, *args)


def plane_rows(place, place_array, grams, few=False):
    half, batch = grams[0].shape
    kept, other = grams
    other = place.send(other, lambda z, a, b: (z, a, b ^ 1))
    height = half // place.n
    parts = local(
        halve_kernel,
        place_array,
        (kept, other),
        [((height, batch), F32)] + [((height + SCALE_ROWS, batch), BF16)] * (place.n - 1),
        "halve",
    )
    return sends(place, "a", parts, few)


def first_rows(place, place_array, grams):
    parts = plane_rows(place, place_array, grams, True)
    height, batch = parts[0].shape
    return local(
        functools.partial(plane_kernel, n=place.n),
        place_array,
        parts,
        [((height // place.n, batch), F32)] * place.n,
        "plane",
        scratch_shapes=[pltpu.VMEM((height, batch), F32)],
    )


def in_one(place, run, args):
    shapes = jax.eval_shape(run, *args)
    return lax.cond(
        place.z < place.n,
        run,
        lambda *args: jax.tree.map(lambda leaf: jnp.zeros(leaf.shape, leaf.dtype), shapes),
        *args,
    )


def plain_gram(place, part):
    for axis in ("b", "a", "z"):
        part = reduce_scatter(place, axis, part)
    part = part.astype(BF16)
    for axis in ("z", "a", "b"):
        part = gather(place, axis, part)
    return part


def lay_kernel(place_ref, *refs, n):
    parts, outs = refs[:n], refs[n:]
    few = parts[0].shape[0] // len(outs)
    for step in range(n):
        at = pl.ds(pl.multiple_of((place_ref[0] ^ step) * few, few), few)
        for i, out in enumerate(outs):
            out[at, :] = parts[step][i * few : (i + 1) * few, :]


def fetch_kernel(weight_ref, held_ref, arrived):
    copy = pltpu.make_async_copy(weight_ref, held_ref, arrived)
    copy.start()
    copy.wait()


def fetch(weight):
    return pl.pallas_call(
        fetch_kernel,
        in_specs=[pl.BlockSpec(memory_space=pl.ANY)],
        out_specs=pl.BlockSpec(memory_space=pltpu.VMEM),
        out_shape=pltpu.VMEM(weight.shape, BF16),
        scratch_shapes=[pltpu.SemaphoreType.DMA],
        compiler_params=pltpu.CompilerParams(vmem_limit_bytes=VMEM_BYTES // 2),
        cost_estimate=pl.CostEstimate(flops=0, bytes_accessed=4 * weight.size, transcendentals=0),
        name="fetch",
    )(pltpu.with_memory_space_constraint(weight, pltpu.HBM))


def to_columns(place, view):
    rows, width = view.shape
    return exchange(place, "a", view.reshape(place.n, rows // place.n, width))


def to_planes(place, parts):
    return sends(place, "z", ordered(parts, place.a ^ place.z))


def lay(place, place_array, parts):
    rows, width = parts[0].shape
    (laid,) = local(
        functools.partial(lay_kernel, n=place.n),
        place_array,
        parts,
        [((rows * place.n, width), BF16)],
        "lay",
    )
    return laid


def met_rows(place, values, few=False):
    return sends(place, "a", [values] * place.n, few)


def project_kernel(place_ref, *refs, counts, n, k):
    met = refs[: sum(counts)]
    weight_ref, own_ref, *coded = refs[sum(counts) :]
    width = met[0].shape[1]
    columns = own_ref.shape[1]
    values = []
    for count in counts:
        values.append(jnp.concatenate([ref[...] for ref in met[:count]], 0))
        met = met[count:]
    for step in [*range(n - 1, 0, -1), 0]:
        at = pl.ds(pl.multiple_of((place_ref[0] ^ step) * columns, columns), columns)
        total = 0.0
        for i in range(k):
            rows = pl.ds(pl.multiple_of((place_ref[2] ^ i) * width, width), width)
            total += jnp.dot(values[i], weight_ref[rows, at], preferred_element_type=F32)
        if step == 0:
            own_ref[...] = total
        else:
            encode(total, coded[n - 1 - step])


def encode(total, coded_ref):
    rows = total.shape[0]
    top = jnp.max(jnp.abs(total), 0, keepdims=True)
    top = jnp.maximum(top * (1.0 + 1.0 / 128.0), 1e-30).astype(BF16)
    coded_ref[rows:] = jnp.broadcast_to(top, (SCALE_ROWS, total.shape[1]))
    whole = jnp.floor(jnp.abs(total) * (HIGHEST / top.astype(F32)) + 0.5)
    power = jnp.floor(whole * (1.0 / 128.0))
    word = (1.0 + (whole * (1.0 / 128.0) - power)) * jnp.exp2(power - POWERS // 2)
    coded_ref[:rows] = jnp.where(total < 0.0, -word, word).astype(BF16)


def decode(coded_ref, count):
    rows = coded_ref.shape[0] - SCALE_ROWS
    scale = coded_ref[rows:].astype(F32)[:1] * (1.0 / HIGHEST)
    height = rows // count
    blocks = []
    for i in range(count):
        word = coded_ref[i * height : (i + 1) * height].astype(F32)
        size = jnp.abs(word)
        power = jnp.floor(jnp.log(size) * 1.4426950408889634 + 0.002)
        part = jnp.floor(size * jnp.exp2(-power) * 128.0 + 0.5)
        whole = (power + (POWERS // 2 - 1)) * 128.0 + part
        blocks.append(jnp.where(word < 0.0, -whole, whole) * scale)
    return blocks


def project(place, place_array, met, held):
    n, k = place.n, place.k
    rows, width = met[0][0].shape
    batch, columns = rows * n, held.shape[1] // n
    counts = [len(parts) for parts in met]
    met = [part for parts in met for part in parts]
    coded = batch + SCALE_ROWS
    out_shape = [jax.ShapeDtypeStruct((batch, columns), F32)]
    out_shape += [jax.ShapeDtypeStruct((coded, columns), BF16)] * (n - 1)
    space = pl.BlockSpec(memory_space=pltpu.VMEM)
    own, *parts = pl.pallas_call(
        functools.partial(project_kernel, counts=counts, n=n, k=k),
        in_specs=[pl.BlockSpec(memory_space=pltpu.SMEM)]
        + [space] * (len(met) + 1),
        out_specs=[space] * n,
        out_shape=out_shape,
        compiler_params=pltpu.CompilerParams(vmem_limit_bytes=VMEM_BYTES),
        cost_estimate=pl.CostEstimate(
            flops=2 * batch * k * width * n * columns,
            bytes_accessed=2 * k * width * (batch + n * columns) + 3 * n * batch * columns,
            transcendentals=0,
        ),
        name="project",
    )(place_array, *met, pltpu.with_memory_space_constraint(held, pltpu.VMEM))
    return own, parts[::-1]


def normalize_kernel(place_ref, *refs, n, k, second):
    own_ref, parts = refs[0], refs[n - 1 : 0 : -1]
    refs = refs[n:]
    if second:
        other_ref, refs = refs[0], refs[1:]
    norm_ref, packed_ref, scale_ref = refs[:3]
    grams = refs[3 : 3 + k]
    batch, columns = own_ref.shape
    height = batch // n
    met = [[own_ref[i * height : (i + 1) * height] for i in range(n)]]
    for step in range(1, n):
        met.append(decode(parts[step - 1], n))
    blocks = [tree_sum([met[step][i] for step in range(n)]) for i in range(n)]
    total = tree_sum([jnp.sum(block, 0, keepdims=True) for block in blocks])
    squares = tree_sum([jnp.sum(block * block, 0, keepdims=True) for block in blocks])
    mean = total / batch
    scale = lax.rsqrt(squares / batch - mean * mean + bn_eps)
    scale_ref[...] = scale
    rows, few = batch // n, batch // (n * n)
    for i, block in enumerate(blocks):
        normed = (block - mean) * scale
        for first in range(0, height, few):
            step, plane = divmod((i * height + first) // few, n)
            at = pl.multiple_of(plane * rows + (place_ref[1] ^ step) * few, few)
            norm_ref[pl.ds(at, few), :] = normed[first : first + few]
            packed_ref[pl.ds(at, few), :] = normed[first : first + few].astype(BF16)
    dims = (((1,), (1,)), ((), ()))
    packed = packed_ref[...]
    size = batch // k
    for i in range(k):
        at = pl.multiple_of((place_ref[2] ^ i) * size, size)
        gram = lax.dot_general(packed_ref[pl.ds(at, size), :], packed, dims, preferred_element_type=F32)
        grams[i][...] = gram
    if second:
        coeff_ref = refs[3 + k]
        diag = jnp.sum(norm_ref[...] * other_ref[...], 0, keepdims=True) / batch
        coeff_ref[...] = 2.0 * ((1.0 - off_weight) * diag - 1.0)
        share = jnp.sum((1.0 - diag) ** 2 - off_weight * diag * diag, 1, keepdims=True)
        for i in range(k):

            @pl.when((place_ref[2] ^ i) == k - 1)
            def _():
                row = grams[i][size - 8 :, :128]
                first = (lax.broadcasted_iota(jnp.int32, row.shape, 0) == 7) & (
                    lax.broadcasted_iota(jnp.int32, row.shape, 1) == 0
                )
                grams[i][size - 8 :, :128] = jnp.where(first, share, row)


def normalize_parts(place, place_array, own, parts, other=None):
    n, k = place.n, place.k
    batch, columns = own.shape
    second = other is not None
    out_shape = [
        jax.ShapeDtypeStruct((batch, columns), F32),
        jax.ShapeDtypeStruct((batch, columns), BF16),
        jax.ShapeDtypeStruct((1, columns), F32),
    ] + [jax.ShapeDtypeStruct((batch // k, batch), F32)] * k
    if second:
        out_shape.append(jax.ShapeDtypeStruct((1, columns), F32))
    args = [own, *parts[::-1]] + ([other] if second else [])
    space = pl.BlockSpec(memory_space=pltpu.VMEM)
    return pl.pallas_call(
        functools.partial(normalize_kernel, n=n, k=k, second=second),
        in_specs=[pl.BlockSpec(memory_space=pltpu.SMEM)] + [space] * len(args),
        out_specs=[space] * len(out_shape),
        out_shape=out_shape,
        compiler_params=pltpu.CompilerParams(vmem_limit_bytes=VMEM_BYTES // 2),
        cost_estimate=pl.CostEstimate(
            flops=2 * batch * batch * columns,
            bytes_accessed=16 * batch * columns + 4 * batch * batch,
            transcendentals=0,
        ),
        name="normalize",
    )(place_array, *args)


def gradient_kernel(place_ref, *refs, n, k):
    grams, refs = refs[: n * k], refs[n * k :]
    packed, norms, scales, coeff_ref, refs = refs[0:2], refs[2:4], refs[4:6], refs[6], refs[7:]
    outs, loss_ref = [refs[0], *refs[n - 1 : 0 : -1]], refs[n]
    gram_ref, whole_ref = refs[n + 1 :]
    batch, columns = norms[0].shape
    height = grams[0].shape[0] // 2
    for i in range(k):
        for step in range(n):
            at = ((place_ref[2] ^ i) * n + (place_ref[1] ^ step)) * height
            to = pl.ds(pl.multiple_of(at, height), height)
            for view in range(2):
                gram_ref[view, to, :] = grams[i * n + step][view * height : (view + 1) * height, :]
    edge = batch - 128
    tail = gram_ref[1, edge:, :128].astype(F32)
    row = lax.broadcasted_iota(jnp.int32, tail.shape, 0)
    column = lax.broadcasted_iota(jnp.int32, tail.shape, 1)
    taken = (row == 127) & (column < 3)
    mirror = gram_ref[1, :128, edge:].astype(F32).T
    share = jnp.sum(jnp.where(taken, tail, 0.0), keepdims=True)
    gram_ref[1, edge:, :128] = jnp.where(taken, mirror, tail).astype(BF16)
    factor = 2.0 * off_weight / batch
    rows = batch // n
    for view in (1, 0):
        norm = norms[view][...]
        grad = (
            factor * jnp.dot(gram_ref[1 - view], packed[view][...], preferred_element_type=F32)
            + coeff_ref[...] * norms[1 - view][...]
        )
        first = jnp.sum(grad, 0, keepdims=True) / batch
        second = jnp.sum(grad * norm, 0, keepdims=True) / batch
        whole_ref[view] = (scales[view][...] * (grad - first - norm * second)).astype(BF16)
        for step in range(n):
            at = pl.multiple_of((place_ref[0] ^ step) * rows, rows)
            outs[step][view * rows : (view + 1) * rows, :] = whole_ref[view, pl.ds(at, rows), :]
    frob = jnp.sum(gram_ref[0].astype(F32) * gram_ref[1].astype(F32), keepdims=True)
    loss_ref[...] = (share + off_weight * (frob / (batch * batch))) / D


def gradient(place, place_array, grams, packed, norms, scales, coeff):
    batch, columns = norms[0].shape
    return local(
        functools.partial(gradient_kernel, n=place.n, k=place.k),
        place_array,
        (*grams, *packed, *norms, *scales, coeff),
        [((2 * batch // place.n, columns), BF16)] * place.n + [((1, 1), F32)],
        "gradient",
        scratch_shapes=[
            pltpu.VMEM((2, batch, batch), BF16),
            pltpu.VMEM((2, batch, columns), BF16),
        ],
    )


def place_kernel(place_ref, *refs, n):
    parts, outs = [refs[0], *refs[n - 1 : 0 : -1]], refs[n:]
    rows, columns = parts[0].shape[0] // len(outs), parts[0].shape[1]
    for step in range(n):
        at = pl.ds(pl.multiple_of((place_ref[0] ^ step) * columns, columns), columns)
        for i, out in enumerate(outs):
            out[:, at] = parts[step][i * rows : (i + 1) * rows, :]


def with_kernels(place, h_first, h_second, weight):
    n, k, z, a, b = place.n, place.k, place.z, place.a, place.b
    place_array = jnp.stack([z, a, b]).astype(jnp.int32)
    first, second = lax.optimization_barrier((to_columns(place, h_first), h_second))
    first, second = lax.optimization_barrier((to_planes(place, first), to_columns(place, second)))
    first, late_weight = lax.optimization_barrier((lay(place, place_array, first), weight))
    met_1, second, held = lax.optimization_barrier(
        (met_rows(place, first), to_planes(place, second), fetch(late_weight))
    )

    def sent(parts):
        return sends(place, "z", [parts[0], *parts])[1:]

    def swapped(part):
        return place.send(part, lambda z, a, b: (z, a, b ^ 1))

    own_1, parts_1 = project(place, place_array, [met_1, [swapped(part) for part in met_1]], held)
    second = lay(place, place_array, second)
    size, here, toward = place.along("a")
    met_2 = [second] + [place.send(second, toward(step)) for step in range(1, size - 1)]
    own_1, parts_1, late_weight = lax.optimization_barrier((own_1, parts_1, weight))
    parts_1 = sent(parts_1)

    def second_projected(weight, *met):
        last = place.send(met[0], toward(size - 1))
        others = [swapped(jnp.concatenate(met, 0))]
        last, others = lax.optimization_barrier((last, others))
        others.append(swapped(last))
        return project(place, place_array, [[*met, last], others], fetch(weight))

    own_2, parts_2 = in_one(place, second_projected, (late_weight, *met_2))
    own_1, own_2 = lax.optimization_barrier((own_1, own_2))
    parts_2 = sent(parts_2)
    norm_1, packed_1, scale_1, *grams = normalize_parts(place, place_array, own_1, parts_1)
    met_1 = in_one(place, lambda *grams: first_rows(place, place_array, grams), grams)
    met_1 = sends(place, "z", met_1)
    own_2, parts_2, met_1 = lax.optimization_barrier((own_2, parts_2, met_1))
    norm_2, packed_2, scale_2, *grams, coeff = normalize_parts(
        place, place_array, own_2, parts_2, norm_1
    )
    height, batch = met_1[0].shape
    (rows_1,) = local(rows_kernel, place_array, met_1, [((height, batch), BF16)], "rows")
    met_2 = plane_rows(place, place_array, grams)
    rows = met_2[0].shape[0]
    (part,) = local(
        functools.partial(code_kernel, n=n),
        place_array,
        (*met_2, rows_1),
        [((rows + SCALE_ROWS + height, batch), BF16)],
        "code",
    )
    (part,) = local(
        functools.partial(finish_kernel, n=n, k=k),
        place_array,
        sends(place, "z", [part] * n),
        [((2 * rows, batch), BF16)],
        "finish",
    )
    grams = sends(place, "a", [part] * n)
    grams += [place.send(part, lambda z, a, b: (z, a, b ^ 1)) for part in grams]
    first, *others, loss = gradient(
        place,
        place_array,
        grams,
        (packed_1, packed_2),
        (norm_1, norm_2),
        (scale_1, scale_2),
        coeff,
    )
    out_1, out_2 = local(
        functools.partial(place_kernel, n=n),
        place_array,
        [first, *sends(place, "z", [first, *others[::-1]])[:0:-1]],
        [(h_first.shape, BF16)] * 2,
        "place",
    )
    return (out_1, out_2, loss.reshape(()))


def plain(place, h_first, h_second, weight):
    n, k, z, a, b = place.n, place.k, place.z, place.a, place.b
    rows, width = h_first.shape
    batch = rows * n
    columns = weight.shape[1] // n
    weight_parts = weight.reshape(k, width, n * columns)
    zs = []
    for values in (h_first, h_second):
        moved = place.send(values, lambda z, a, b: (a, z, b))
        own = jnp.concatenate(met_rows(place, moved), 0)
        total = jnp.dot(own, pick(weight_parts, b), preferred_element_type=F32)
        for step in range(1, k):
            other = place.send(own, lambda z, a, b, s=step: (z, a, b ^ s))
            total += jnp.dot(other, pick(weight_parts, b ^ step), preferred_element_type=F32)
        cut = total.reshape(batch, n, columns).transpose(1, 0, 2)
        whole = tree_sum(exchange(place, "z", cut)).reshape(n, rows, columns)
        zs.append(jnp.concatenate(ordered([whole[i] for i in range(n)], a), 0))
    normed, scales = [], []
    for values in zs:
        mean = jnp.sum(values, 0) / batch
        scale = lax.rsqrt(jnp.sum(values * values, 0) / batch - mean * mean + bn_eps)
        normed.append((values - mean) * scale)
        scales.append(scale)
    diag = jnp.sum(normed[0] * normed[1], 0) / batch
    packed = [values.astype(BF16) for values in normed]
    dims = (((1,), (1,)), ((), ()))
    grams = []
    for values in packed:
        gram = lax.dot_general(values, values, dims, preferred_element_type=F32)
        grams.append(plain_gram(place, gram))
    frob = jnp.sum(grams[0].astype(F32) * grams[1].astype(F32)) / (batch * batch)
    coeff = 2.0 * ((1.0 - off_weight) * diag - 1.0)
    factor = 2.0 * off_weight / batch
    outs = []
    for view in range(2):
        grad = (
            factor * jnp.dot(grams[1 - view], packed[view], preferred_element_type=F32)
            + coeff * normed[1 - view]
        )
        first = jnp.sum(grad, 0) / batch
        second = jnp.sum(grad * normed[view], 0) / batch
        out = (scales[view] * (grad - first - normed[view] * second)).astype(BF16)
        parts = exchange(place, "z", out.reshape(n, rows, columns))
        outs.append(jnp.concatenate(ordered(parts, z), 1))
    share = jnp.sum((1.0 - diag) ** 2) - off_weight * jnp.sum(diag * diag)
    loss = (lax.psum(share, ("dp", "mp")) + off_weight * frob) / D
    return (outs[0], outs[1], loss)


def per_device(h_first, h_second, weight):
    place = Place()
    columns = weight.shape[1] // place.n
    fits = columns % 128 == 0 and place.n == 4 and place.k == 2
    return (with_kernels if fits else plain)(place, h_first, h_second, weight)


def solution(mesh):
    in_specs = (P("dp", "mp"), P("dp", "mp"), P("dp", "mp"))
    out_specs = (P("dp", "mp"), P("dp", "mp"), P())
    return jax.shard_map(
        per_device, mesh=mesh, in_specs=in_specs, out_specs=out_specs, check_vma=False
    )
```

```python
import functools

import jax
import jax.numpy as jnp
from jax import lax
from jax.experimental import pallas as pl
from jax.experimental.pallas import tpu as pltpu
from jax.sharding import PartitionSpec as P

D = 8192


off_weight = 0.0051
bn_eps = 1e-05

F32 = jnp.float32
BF16 = jnp.bfloat16
VMEM_BYTES = 16 * 1024 * 1024
POWERS = 240
HIGHEST = 128 * POWERS - 1
SCALE_ROWS = 16


class Place:
    def __init__(self):
        self.n = lax.axis_size("dp")
        self.k = lax.axis_size("mp") // self.n
        self.z = lax.axis_index("dp")
        self.a = lax.axis_index("mp") // self.k
        self.b = lax.axis_index("mp") % self.k

    def send(self, value, target):
        n, k = self.n, self.k
        pairs = []
        for z in range(n):
            for a in range(n):
                for b in range(k):
                    to_z, to_a, to_b = target(z, a, b)
                    pairs.append(((z * n + a) * k + b, (to_z * n + to_a) * k + to_b))
        return lax.ppermute(value, ("dp", "mp"), pairs)

    def along(self, axis):
        if axis == "z":
            return self.n, self.z, lambda step: lambda z, a, b: (z ^ step, a, b)
        if axis == "a":
            return self.n, self.a, lambda step: lambda z, a, b: (z, a ^ step, b)
        return self.k, self.b, lambda step: lambda z, a, b: (z, a, b ^ step)


def ordered(parts, place):
    bit = 1
    while bit < len(parts):
        odd = (place & bit) != 0
        parts = [jnp.where(odd, parts[i ^ bit], parts[i]) for i in range(len(parts))]
        bit *= 2
    return parts


def tree_sum(parts):
    while len(parts) > 1:
        parts = [parts[i] + parts[i + 1] for i in range(0, len(parts), 2)]
    return parts[0]


def pick(value, index):
    return lax.dynamic_index_in_dim(value, index, 0, keepdims=False)


def exchange(place, axis, value, few=False):
    size, here, toward = place.along(axis)
    return sends(place, axis, [pick(value, here ^ step) for step in range(size)], few)


def sends(place, axis, parts, few=False):
    size, here, toward = place.along(axis)
    met = {0: parts[0]}
    order = [*range(1, size)] if few else [*range(size - 1, 0, -1)]
    for i, step in enumerate(order):
        part = parts[step]
        if few and i >= 2:
            met[order[i - 2]], part = lax.optimization_barrier((met[order[i - 2]], part))
        met[step] = place.send(part, toward(step))
    return [met[step] for step in range(size)]


def reduce_scatter(place, axis, value, few=False):
    size, here, toward = place.along(axis)
    value = value.reshape((size, value.shape[0] // size) + value.shape[1:])
    return tree_sum(exchange(place, axis, value, few))


def gather(place, axis, value, few=False):
    size, here, toward = place.along(axis)
    parts = sends(place, axis, [value] * size, few)
    return jnp.concatenate(ordered(parts, here), 0)


def halve_kernel(place_ref, kept_ref, met_ref, *outs):
    height = outs[0].shape[0]
    for step, out in enumerate(outs):
        at = pl.ds(pl.multiple_of((place_ref[1] ^ step) * height, height), height)
        total = kept_ref[at, :] + met_ref[at, :]
        if step == 0:
            out[...] = total
        else:
            encode(total, out)


def plane_sum(met):
    return tree_sum([met[0][...]] + [decode(ref, 1)[0] for ref in met[1:]])


def plane_kernel(place_ref, *refs, n):
    met, outs, whole_ref = refs[:n], refs[n:-1], refs[-1]
    whole_ref[...] = plane_sum(met)
    height = outs[0].shape[0]
    for step, out in enumerate(outs):
        at = pl.ds(pl.multiple_of((place_ref[0] ^ step) * height, height), height)
        out[...] = whole_ref[at, :]


def rows_kernel(place_ref, *refs):
    refs[-1][...] = tree_sum([ref[...] for ref in refs[:-1]]).astype(BF16)


def code_kernel(place_ref, *refs):
    encode(plane_sum(refs[:-1]), refs[-1])


def finish_kernel(place_ref, *refs, n, k):
    out_ref = refs[-1]
    total = tree_sum([decode(ref, 1)[0] for ref in refs[:n]])
    last = (place_ref[1] == n - 1) & (place_ref[2] == k - 1)
    edge = total[-8:, :128]
    row = lax.broadcasted_iota(jnp.int32, edge.shape, 0)
    column = lax.broadcasted_iota(jnp.int32, edge.shape, 1)
    taken = (row == 7) & last
    whole = jnp.sum(jnp.where(taken & (column == 0), edge, 0.0), keepdims=True)
    high = whole.astype(BF16).astype(F32)
    middle = (whole - high).astype(BF16).astype(F32)
    three = jnp.where(column == 0, high, jnp.where(column == 1, middle, whole - high - middle))
    edge = jnp.where(taken & (column < 3), three, edge)
    edge = jnp.concatenate([edge, total[-8:, 128:]], 1)
    out_ref[...] = jnp.concatenate([total[:-8], edge], 0).astype(BF16)


def local(kernel, place_array, args, shapes, name, **more):
    space = pl.BlockSpec(memory_space=pltpu.VMEM)
    return pl.pallas_call(
        kernel,
        in_specs=[pl.BlockSpec(memory_space=pltpu.SMEM)] + [space] * len(args),
        out_specs=[space] * len(shapes),
        out_shape=[jax.ShapeDtypeStruct(shape, dtype) for shape, dtype in shapes],
        compiler_params=pltpu.CompilerParams(vmem_limit_bytes=VMEM_BYTES // 2),
        name=name,
        **more,
    )(place_array, *args)


def plane_rows(place, place_array, grams, few=False):
    half, batch = grams[0].shape
    kept, other = grams
    other = place.send(other, lambda z, a, b: (z, a, b ^ 1))
    height = half // place.n
    parts = local(
        halve_kernel,
        place_array,
        (kept, other),
        [((height, batch), F32)] + [((height + SCALE_ROWS, batch), BF16)] * (place.n - 1),
        "halve",
    )
    return sends(place, "a", parts, few)


def first_rows(place, place_array, grams):
    parts = plane_rows(place, place_array, grams, True)
    height, batch = parts[0].shape
    return local(
        functools.partial(plane_kernel, n=place.n),
        place_array,
        parts,
        [((height // place.n, batch), F32)] * place.n,
        "plane",
        scratch_shapes=[pltpu.VMEM((height, batch), F32)],
    )


def in_one(place, run, args):
    shapes = jax.eval_shape(run, *args)
    return lax.cond(
        place.z < place.n,
        run,
        lambda *args: jax.tree.map(lambda leaf: jnp.zeros(leaf.shape, leaf.dtype), shapes),
        *args,
    )


def plain_gram(place, part):
    for axis in ("b", "a", "z"):
        part = reduce_scatter(place, axis, part)
    part = part.astype(BF16)
    for axis in ("z", "a", "b"):
        part = gather(place, axis, part)
    return part


def lay_kernel(place_ref, *refs, n):
    parts, outs = refs[:n], refs[n:]
    few = parts[0].shape[0] // len(outs)
    for step in range(n):
        at = pl.ds(pl.multiple_of((place_ref[0] ^ step) * few, few), few)
        for i, out in enumerate(outs):
            out[at, :] = parts[step][i * few : (i + 1) * few, :]


def fetch_kernel(weight_ref, held_ref, arrived):
    copy = pltpu.make_async_copy(weight_ref, held_ref, arrived)
    copy.start()
    copy.wait()


def fetch(weight):
    return pl.pallas_call(
        fetch_kernel,
        in_specs=[pl.BlockSpec(memory_space=pl.ANY)],
        out_specs=pl.BlockSpec(memory_space=pltpu.VMEM),
        out_shape=pltpu.VMEM(weight.shape, BF16),
        scratch_shapes=[pltpu.SemaphoreType.DMA],
        compiler_params=pltpu.CompilerParams(vmem_limit_bytes=VMEM_BYTES // 2),
        cost_estimate=pl.CostEstimate(flops=0, bytes_accessed=4 * weight.size, transcendentals=0),
        name="fetch",
    )(pltpu.with_memory_space_constraint(weight, pltpu.HBM))


def to_columns(place, view):
    rows, width = view.shape
    return exchange(place, "a", view.reshape(place.n, rows // place.n, width))


def to_planes(place, parts):
    return sends(place, "z", ordered(parts, place.a ^ place.z))


def lay(place, place_array, parts):
    rows, width = parts[0].shape
    (laid,) = local(
        functools.partial(lay_kernel, n=place.n),
        place_array,
        parts,
        [((rows * place.n, width), BF16)],
        "lay",
    )
    return laid


def met_rows(place, values, few=False):
    return sends(place, "a", [values] * place.n, few)


def project_kernel(place_ref, *refs, counts, n, k):
    met = refs[: sum(counts)]
    weight_ref, own_ref, *coded = refs[sum(counts) :]
    width = met[0].shape[1]
    columns = own_ref.shape[1]
    values = []
    for count in counts:
        values.append(jnp.concatenate([ref[...] for ref in met[:count]], 0))
        met = met[count:]
    for step in [*range(n - 1, 0, -1), 0]:
        at = pl.ds(pl.multiple_of((place_ref[0] ^ step) * columns, columns), columns)
        total = 0.0
        for i in range(k):
            rows = pl.ds(pl.multiple_of((place_ref[2] ^ i) * width, width), width)
            total += jnp.dot(values[i], weight_ref[rows, at], preferred_element_type=F32)
        if step == 0:
            own_ref[...] = total
        else:
            encode(total, coded[n - 1 - step])


def encode(total, coded_ref):
    rows = total.shape[0]
    top = jnp.max(jnp.abs(total), 0, keepdims=True)
    top = jnp.maximum(top * (1.0 + 1.0 / 128.0), 1e-30).astype(BF16)
    coded_ref[rows:] = jnp.broadcast_to(top, (SCALE_ROWS, total.shape[1]))
    whole = jnp.floor(jnp.abs(total) * (HIGHEST / top.astype(F32)) + 0.5)
    power = jnp.floor(whole * (1.0 / 128.0))
    word = (1.0 + (whole * (1.0 / 128.0) - power)) * jnp.exp2(power - POWERS // 2)
    coded_ref[:rows] = jnp.where(total < 0.0, -word, word).astype(BF16)


def decode(coded_ref, count):
    rows = coded_ref.shape[0] - SCALE_ROWS
    scale = coded_ref[rows:].astype(F32)[:1] * (1.0 / HIGHEST)
    height = rows // count
    blocks = []
    for i in range(count):
        word = coded_ref[i * height : (i + 1) * height].astype(F32)
        size = jnp.abs(word)
        power = jnp.floor(jnp.log(size) * 1.4426950408889634 + 0.002)
        part = jnp.floor(size * jnp.exp2(-power) * 128.0 + 0.5)
        whole = (power + (POWERS // 2 - 1)) * 128.0 + part
        blocks.append(jnp.where(word < 0.0, -whole, whole) * scale)
    return blocks


def project(place, place_array, met, held):
    n, k = place.n, place.k
    rows, width = met[0][0].shape
    batch, columns = rows * n, held.shape[1] // n
    counts = [len(parts) for parts in met]
    met = [part for parts in met for part in parts]
    coded = batch + SCALE_ROWS
    out_shape = [jax.ShapeDtypeStruct((batch, columns), F32)]
    out_shape += [jax.ShapeDtypeStruct((coded, columns), BF16)] * (n - 1)
    space = pl.BlockSpec(memory_space=pltpu.VMEM)
    own, *parts = pl.pallas_call(
        functools.partial(project_kernel, counts=counts, n=n, k=k),
        in_specs=[pl.BlockSpec(memory_space=pltpu.SMEM)]
        + [space] * (len(met) + 1),
        out_specs=[space] * n,
        out_shape=out_shape,
        compiler_params=pltpu.CompilerParams(vmem_limit_bytes=VMEM_BYTES),
        cost_estimate=pl.CostEstimate(
            flops=2 * batch * k * width * n * columns,
            bytes_accessed=2 * k * width * (batch + n * columns) + 3 * n * batch * columns,
            transcendentals=0,
        ),
        name="project",
    )(place_array, *met, pltpu.with_memory_space_constraint(held, pltpu.VMEM))
    return own, parts[::-1]


def normalize_kernel(place_ref, *refs, n, k, second):
    own_ref, parts = refs[0], refs[n - 1 : 0 : -1]
    refs = refs[n:]
    if second:
        other_ref, refs = refs[0], refs[1:]
    norm_ref, packed_ref, scale_ref = refs[:3]
    grams = refs[3 : 3 + k]
    batch, columns = own_ref.shape
    height = batch // n
    met = [[own_ref[i * height : (i + 1) * height] for i in range(n)]]
    for step in range(1, n):
        met.append(decode(parts[step - 1], n))
    blocks = [tree_sum([met[step][i] for step in range(n)]) for i in range(n)]
    total = tree_sum([jnp.sum(block, 0, keepdims=True) for block in blocks])
    squares = tree_sum([jnp.sum(block * block, 0, keepdims=True) for block in blocks])
    mean = total / batch
    scale = lax.rsqrt(squares / batch - mean * mean + bn_eps)
    scale_ref[...] = scale
    rows, few = batch // n, batch // (n * n)
    for i, block in enumerate(blocks):
        normed = (block - mean) * scale
        for first in range(0, height, few):
            step, plane = divmod((i * height + first) // few, n)
            at = pl.multiple_of(plane * rows + (place_ref[1] ^ step) * few, few)
            norm_ref[pl.ds(at, few), :] = normed[first : first + few]
            packed_ref[pl.ds(at, few), :] = normed[first : first + few].astype(BF16)
    dims = (((1,), (1,)), ((), ()))
    packed = packed_ref[...]
    size = batch // k
    for i in range(k):
        at = pl.multiple_of((place_ref[2] ^ i) * size, size)
        gram = lax.dot_general(packed_ref[pl.ds(at, size), :], packed, dims, preferred_element_type=F32)
        grams[i][...] = gram
    if second:
        coeff_ref = refs[3 + k]
        diag = jnp.sum(norm_ref[...] * other_ref[...], 0, keepdims=True) / batch
        coeff_ref[...] = 2.0 * ((1.0 - off_weight) * diag - 1.0)
        share = jnp.sum((1.0 - diag) ** 2 - off_weight * diag * diag, 1, keepdims=True)
        for i in range(k):

            @pl.when((place_ref[2] ^ i) == k - 1)
            def _():
                row = grams[i][size - 8 :, :128]
                first = (lax.broadcasted_iota(jnp.int32, row.shape, 0) == 7) & (
                    lax.broadcasted_iota(jnp.int32, row.shape, 1) == 0
                )
                grams[i][size - 8 :, :128] = jnp.where(first, share, row)


def normalize_parts(place, place_array, own, parts, other=None):
    n, k = place.n, place.k
    batch, columns = own.shape
    second = other is not None
    out_shape = [
        jax.ShapeDtypeStruct((batch, columns), F32),
        jax.ShapeDtypeStruct((batch, columns), BF16),
        jax.ShapeDtypeStruct((1, columns), F32),
    ] + [jax.ShapeDtypeStruct((batch // k, batch), F32)] * k
    if second:
        out_shape.append(jax.ShapeDtypeStruct((1, columns), F32))
    args = [own, *parts[::-1]] + ([other] if second else [])
    space = pl.BlockSpec(memory_space=pltpu.VMEM)
    return pl.pallas_call(
        functools.partial(normalize_kernel, n=n, k=k, second=second),
        in_specs=[pl.BlockSpec(memory_space=pltpu.SMEM)] + [space] * len(args),
        out_specs=[space] * len(out_shape),
        out_shape=out_shape,
        compiler_params=pltpu.CompilerParams(vmem_limit_bytes=VMEM_BYTES // 2),
        cost_estimate=pl.CostEstimate(
            flops=2 * batch * batch * columns,
            bytes_accessed=16 * batch * columns + 4 * batch * batch,
            transcendentals=0,
        ),
        name="normalize",
    )(place_array, *args)


def gradient_of(place_ref, gram, packed, norm, other, scale, coeff, whole_ref, outs):
    batch, n = norm.shape[0], len(outs)
    factor = 2.0 * off_weight / batch
    norm = norm[...]
    grad = factor * jnp.dot(gram, packed[...], preferred_element_type=F32) + coeff[...] * other[...]
    first = jnp.sum(grad, 0, keepdims=True) / batch
    second = jnp.sum(grad * norm, 0, keepdims=True) / batch
    whole_ref[...] = (scale[...] * (grad - first - norm * second)).astype(BF16)
    rows = batch // n
    for step in range(n):
        at = pl.ds(pl.multiple_of((place_ref[0] ^ step) * rows, rows), rows)
        outs[step][...] = whole_ref[at, :]


def second_gradient_kernel(place_ref, rows_ref, *refs, n, k):
    outs, gram_ref, whole_ref = [refs[5], *refs[n + 4 : 5 : -1]], refs[n + 5], refs[n + 6]
    few = rows_ref.shape[0] // (n * n * k)
    for z in range(n):
        for a in range(n):
            for b in range(k):
                to, at = ((b * n + a) * n + z) * few, ((z * n + a) * k + b) * few
                gram_ref[to : to + few, :] = rows_ref[at : at + few, :]
    gradient_of(place_ref, gram_ref[...], *refs[:5], whole_ref, outs)


def first_gradient_kernel(place_ref, *refs, n, k):
    grams, refs = refs[: n * k], refs[n * k :]
    first_ref, inputs, refs = refs[0], refs[1:6], refs[6:]
    outs, loss_ref, gram_ref, whole_ref = [refs[0], *refs[n - 1 : 0 : -1]], *refs[n:]
    batch = first_ref.shape[0]
    height = grams[0].shape[0]
    for i in range(k):
        for step in range(n):
            at = ((place_ref[2] ^ i) * n + (place_ref[1] ^ step)) * height
            gram_ref[pl.ds(pl.multiple_of(at, height), height), :] = grams[i * n + step][...]
    edge = batch - 128
    tail = gram_ref[edge:, :128].astype(F32)
    row = lax.broadcasted_iota(jnp.int32, tail.shape, 0)
    column = lax.broadcasted_iota(jnp.int32, tail.shape, 1)
    taken = (row == 127) & (column < 3)
    mirror = gram_ref[:128, edge:].astype(F32).T
    share = jnp.sum(jnp.where(taken, tail, 0.0), keepdims=True)
    gram_ref[edge:, :128] = jnp.where(taken, mirror, tail).astype(BF16)
    gram = gram_ref[...]
    gradient_of(place_ref, gram, *inputs, whole_ref, outs)
    frob = jnp.sum(gram.astype(F32) * first_ref[...].astype(F32), keepdims=True)
    loss_ref[...] = (share + off_weight * (frob / (batch * batch))) / D


def place_kernel(place_ref, *refs, n):
    parts, outs = [refs[0], *refs[n - 1 : 0 : -1]], refs[n:]
    rows, columns = parts[0].shape[0] // len(outs), parts[0].shape[1]
    for step in range(n):
        at = pl.ds(pl.multiple_of((place_ref[0] ^ step) * columns, columns), columns)
        for i, out in enumerate(outs):
            out[:, at] = parts[step][i * rows : (i + 1) * rows, :]


def with_kernels(place, h_first, h_second, weight):
    n, k, z, a, b = place.n, place.k, place.z, place.a, place.b
    place_array = jnp.stack([z, a, b]).astype(jnp.int32)
    first, second = lax.optimization_barrier((to_columns(place, h_first), h_second))
    first, second = lax.optimization_barrier((to_planes(place, first), to_columns(place, second)))
    first, late_weight = lax.optimization_barrier((lay(place, place_array, first), weight))
    met_1, second, held = lax.optimization_barrier(
        (
            met_rows(place, first),
            lay(place, place_array, to_planes(place, second)),
            fetch(late_weight),
        )
    )

    def sent(parts):
        return sends(place, "z", [parts[0], *parts])[1:]

    def swapped(part):
        return place.send(part, lambda z, a, b: (z, a, b ^ 1))

    own_1, parts_1 = project(place, place_array, [met_1, [swapped(part) for part in met_1]], held)
    size, here, toward = place.along("a")
    met_2 = [second] + [place.send(second, toward(step)) for step in range(1, size - 1)]
    own_1, parts_1, late_weight = lax.optimization_barrier((own_1, parts_1, weight))
    parts_1 = sent(parts_1)

    def second_projected(weight, *met):
        last = place.send(met[0], toward(size - 1))
        others = [swapped(jnp.concatenate(met, 0))]
        last, others = lax.optimization_barrier((last, others))
        others.append(swapped(last))
        return project(place, place_array, [[*met, last], others], fetch(weight))

    own_2, parts_2 = in_one(place, second_projected, (late_weight, *met_2))
    own_1, own_2 = lax.optimization_barrier((own_1, own_2))
    parts_2 = sent(parts_2)
    norm_1, packed_1, scale_1, *grams = normalize_parts(place, place_array, own_1, parts_1)
    met_1 = in_one(place, lambda *grams: first_rows(place, place_array, grams), grams)
    met_1 = sends(place, "z", met_1)
    height, batch = met_1[0].shape
    (rows_1,) = local(rows_kernel, place_array, met_1, [((height, batch), BF16)], "rows")
    own_2, parts_2, rows_1 = lax.optimization_barrier((own_2, parts_2, rows_1))
    rows_1 = lax.all_gather(rows_1, ("dp", "mp"), axis=0, tiled=True)
    norm_2, packed_2, scale_2, *grams, coeff = normalize_parts(
        place, place_array, own_2, parts_2, norm_1
    )
    met_2 = plane_rows(place, place_array, grams)
    rows, columns = met_2[0].shape[0], norm_1.shape[1]
    (part,) = local(
        code_kernel, place_array, met_2, [((rows + SCALE_ROWS, batch), BF16)], "code"
    )
    (part,) = local(
        functools.partial(finish_kernel, n=n, k=k),
        place_array,
        sends(place, "z", [part] * n),
        [((rows, batch), BF16)],
        "finish",
    )
    pieces = [((batch // n, columns), BF16)] * n
    held_rows = pltpu.VMEM((batch, columns), BF16)
    *grads_2, gram_1 = local(
        functools.partial(second_gradient_kernel, n=n, k=k),
        place_array,
        (rows_1, packed_2, norm_2, norm_1, scale_2, coeff),
        [*pieces, ((batch, batch), BF16)],
        "gradient",
        scratch_shapes=[held_rows],
    )
    part, grads_2 = lax.optimization_barrier((part, grads_2))

    def exchanged(first, *others):
        return sends(place, "z", [first, *others[::-1]])

    def placed(parts):
        (out,) = local(
            functools.partial(place_kernel, n=n),
            place_array,
            [parts[0], *parts[:0:-1]],
            [(h_first.shape, BF16)],
            "place",
        )
        return out

    grams = sends(place, "a", [part] * n)
    grams += [swapped(part) for part in grams]
    grams, met_1 = lax.optimization_barrier((grams, exchanged(*grads_2)))
    *grads_1, loss = local(
        functools.partial(first_gradient_kernel, n=n, k=k),
        place_array,
        (*grams, gram_1, packed_1, norm_1, norm_2, scale_1, coeff),
        [*pieces, ((1, 1), F32)],
        "gradient",
        scratch_shapes=[pltpu.VMEM((batch, batch), BF16), held_rows],
    )
    out_2 = placed(met_1)
    return (placed(exchanged(*grads_1)), out_2, loss.reshape(()))


def plain(place, h_first, h_second, weight):
    n, k, z, a, b = place.n, place.k, place.z, place.a, place.b
    rows, width = h_first.shape
    batch = rows * n
    columns = weight.shape[1] // n
    weight_parts = weight.reshape(k, width, n * columns)
    zs = []
    for values in (h_first, h_second):
        moved = place.send(values, lambda z, a, b: (a, z, b))
        own = jnp.concatenate(met_rows(place, moved), 0)
        total = jnp.dot(own, pick(weight_parts, b), preferred_element_type=F32)
        for step in range(1, k):
            other = place.send(own, lambda z, a, b, s=step: (z, a, b ^ s))
            total += jnp.dot(other, pick(weight_parts, b ^ step), preferred_element_type=F32)
        cut = total.reshape(batch, n, columns).transpose(1, 0, 2)
        whole = tree_sum(exchange(place, "z", cut)).reshape(n, rows, columns)
        zs.append(jnp.concatenate(ordered([whole[i] for i in range(n)], a), 0))
    normed, scales = [], []
    for values in zs:
        mean = jnp.sum(values, 0) / batch
        scale = lax.rsqrt(jnp.sum(values * values, 0) / batch - mean * mean + bn_eps)
        normed.append((values - mean) * scale)
        scales.append(scale)
    diag = jnp.sum(normed[0] * normed[1], 0) / batch
    packed = [values.astype(BF16) for values in normed]
    dims = (((1,), (1,)), ((), ()))
    grams = []
    for values in packed:
        gram = lax.dot_general(values, values, dims, preferred_element_type=F32)
        grams.append(plain_gram(place, gram))
    frob = jnp.sum(grams[0].astype(F32) * grams[1].astype(F32)) / (batch * batch)
    coeff = 2.0 * ((1.0 - off_weight) * diag - 1.0)
    factor = 2.0 * off_weight / batch
    outs = []
    for view in range(2):
        grad = (
            factor * jnp.dot(grams[1 - view], packed[view], preferred_element_type=F32)
            + coeff * normed[1 - view]
        )
        first = jnp.sum(grad, 0) / batch
        second = jnp.sum(grad * normed[view], 0) / batch
        out = (scales[view] * (grad - first - normed[view] * second)).astype(BF16)
        parts = exchange(place, "z", out.reshape(n, rows, columns))
        outs.append(jnp.concatenate(ordered(parts, z), 1))
    share = jnp.sum((1.0 - diag) ** 2) - off_weight * jnp.sum(diag * diag)
    loss = (lax.psum(share, ("dp", "mp")) + off_weight * frob) / D
    return (outs[0], outs[1], loss)


def per_device(h_first, h_second, weight):
    place = Place()
    columns = weight.shape[1] // place.n
    fits = columns % 128 == 0 and place.n == 4 and place.k == 2
    return (with_kernels if fits else plain)(place, h_first, h_second, weight)


def solution(mesh):
    in_specs = (P("dp", "mp"), P("dp", "mp"), P("dp", "mp"))
    out_specs = (P("dp", "mp"), P("dp", "mp"), P())
    return jax.shard_map(
        per_device, mesh=mesh, in_specs=in_specs, out_specs=out_specs, check_vma=False
    )
```

```python
import functools

import jax
import jax.numpy as jnp
from jax import lax
from jax.experimental import pallas as pl
from jax.experimental.pallas import tpu as pltpu
from jax.sharding import PartitionSpec as P

D = 8192


off_weight = 0.0051
bn_eps = 1e-05

F32 = jnp.float32
BF16 = jnp.bfloat16
VMEM_BYTES = 16 * 1024 * 1024
POWERS = 240
HIGHEST = 128 * POWERS - 1
SCALE_ROWS = 16


class Place:
    def __init__(self):
        self.n = lax.axis_size("dp")
        self.k = lax.axis_size("mp") // self.n
        self.z = lax.axis_index("dp")
        self.a = lax.axis_index("mp") // self.k
        self.b = lax.axis_index("mp") % self.k

    def send(self, value, target):
        n, k = self.n, self.k
        pairs = []
        for z in range(n):
            for a in range(n):
                for b in range(k):
                    to_z, to_a, to_b = target(z, a, b)
                    pairs.append(((z * n + a) * k + b, (to_z * n + to_a) * k + to_b))
        return lax.ppermute(value, ("dp", "mp"), pairs)

    def along(self, axis):
        if axis == "z":
            return self.n, self.z, lambda step: lambda z, a, b: (z ^ step, a, b)
        if axis == "a":
            return self.n, self.a, lambda step: lambda z, a, b: (z, a ^ step, b)
        return self.k, self.b, lambda step: lambda z, a, b: (z, a, b ^ step)


def ordered(parts, place):
    bit = 1
    while bit < len(parts):
        odd = (place & bit) != 0
        parts = [jnp.where(odd, parts[i ^ bit], parts[i]) for i in range(len(parts))]
        bit *= 2
    return parts


def tree_sum(parts):
    while len(parts) > 1:
        parts = [parts[i] + parts[i + 1] for i in range(0, len(parts), 2)]
    return parts[0]


def pick(value, index):
    return lax.dynamic_index_in_dim(value, index, 0, keepdims=False)


def exchange(place, axis, value, few=False):
    size, here, toward = place.along(axis)
    return sends(place, axis, [pick(value, here ^ step) for step in range(size)], few)


def sends(place, axis, parts, few=False):
    size, here, toward = place.along(axis)
    met = {0: parts[0]}
    order = [*range(1, size)] if few else [*range(size - 1, 0, -1)]
    for i, step in enumerate(order):
        part = parts[step]
        if few and i >= 2:
            met[order[i - 2]], part = lax.optimization_barrier((met[order[i - 2]], part))
        met[step] = place.send(part, toward(step))
    return [met[step] for step in range(size)]


def reduce_scatter(place, axis, value, few=False):
    size, here, toward = place.along(axis)
    value = value.reshape((size, value.shape[0] // size) + value.shape[1:])
    return tree_sum(exchange(place, axis, value, few))


def gather(place, axis, value, few=False):
    size, here, toward = place.along(axis)
    parts = sends(place, axis, [value] * size, few)
    return jnp.concatenate(ordered(parts, here), 0)


def gram_kernel(place_ref, own_ref, other_ref, *refs, n):
    share_ref = None
    if len(refs) > n:
        share_ref, refs = refs[0], refs[1:]
    height = refs[0].shape[0]
    dims = (((1,), (1,)), ((), ()))
    for step, out in enumerate(refs):
        at = place_ref[2] * (n * height) + (place_ref[1] ^ step) * height
        at = pl.ds(pl.multiple_of(at, height), height)
        total = 0.0
        for ref in (own_ref, other_ref):
            total += lax.dot_general(ref[at, :], ref[...], dims, preferred_element_type=F32)
        if share_ref is not None:
            row = lax.broadcasted_iota(jnp.int32, total.shape, 0)
            column = lax.broadcasted_iota(jnp.int32, total.shape, 1)
            first = (row == height - 1) & (column == 0) & ((place_ref[1] ^ step) == n - 1)
            total = jnp.where(first, share_ref[...], total)
        if step == 0:
            out[...] = total
        else:
            encode(total, out)


def plane_sum(met):
    return tree_sum([met[0][...]] + [decode(ref, 1)[0] for ref in met[1:]])


def plane_kernel(place_ref, *refs, n):
    met, outs, whole_ref = refs[:n], refs[n:-1], refs[-1]
    whole_ref[...] = plane_sum(met)
    height = outs[0].shape[0]
    for step, out in enumerate(outs):
        at = pl.ds(pl.multiple_of((place_ref[0] ^ step) * height, height), height)
        out[...] = whole_ref[at, :]


def rows_kernel(place_ref, *refs):
    refs[-1][...] = tree_sum([ref[...] for ref in refs[:-1]]).astype(BF16)


def code_kernel(place_ref, *refs, n):
    met, rows_ref, out_ref = refs[:n], refs[n], refs[n + 1]
    total = plane_sum(met)
    coded = total.shape[0] + SCALE_ROWS
    encode(total, out_ref.at[:coded])
    out_ref[coded:] = rows_ref[...]


def finish_kernel(place_ref, *refs, n, k):
    out_ref = refs[-1]
    height = out_ref.shape[0] // 2
    coded, few = height + SCALE_ROWS, height // n
    met = []
    for step in range(n):
        at = pl.ds(pl.multiple_of((place_ref[0] ^ step) * few, few), few)
        out_ref[at, :] = refs[step][coded:]
        met += decode(refs[step].at[:coded], 1)
    total = tree_sum(met)
    last = place_ref[1] == n - 1
    edge = total[-8:, :128]
    row = lax.broadcasted_iota(jnp.int32, edge.shape, 0)
    column = lax.broadcasted_iota(jnp.int32, edge.shape, 1)
    taken = (row == 7) & last
    whole = jnp.sum(jnp.where(taken & (column == 0), edge, 0.0), keepdims=True)
    high = whole.astype(BF16).astype(F32)
    middle = (whole - high).astype(BF16).astype(F32)
    three = jnp.where(column == 0, high, jnp.where(column == 1, middle, whole - high - middle))
    edge = jnp.where(taken & (column < 3), three, edge)
    edge = jnp.concatenate([edge, total[-8:, 128:]], 1)
    out_ref[height:] = jnp.concatenate([total[:-8], edge], 0).astype(BF16)


def local(kernel, place_array, args, shapes, name, out=None, **more):
    space = pl.BlockSpec(memory_space=pltpu.VMEM)
    return pl.pallas_call(
        kernel,
        in_specs=[pl.BlockSpec(memory_space=pltpu.SMEM)] + [space] * len(args),
        out_specs=[out or space] * len(shapes),
        out_shape=[jax.ShapeDtypeStruct(shape, dtype) for shape, dtype in shapes],
        compiler_params=pltpu.CompilerParams(vmem_limit_bytes=VMEM_BYTES // 2),
        name=name,
        **more,
    )(place_array, *args)


def plane_rows(place, place_array, packed, few=False, share=()):
    batch = packed.shape[0]
    height = batch // (place.n * place.k)
    other = place.send(packed, lambda z, a, b: (z, a, b ^ 1))
    parts = local(
        functools.partial(gram_kernel, n=place.n),
        place_array,
        (packed, other, *share),
        [((height, batch), F32)] + [((height + SCALE_ROWS, batch), BF16)] * (place.n - 1),
        "gram",
    )
    return sends(place, "a", parts, few)


def first_rows(place, place_array, packed):
    parts = plane_rows(place, place_array, packed, True)
    height, batch = parts[0].shape
    return local(
        functools.partial(plane_kernel, n=place.n),
        place_array,
        parts,
        [((height // place.n, batch), F32)] * place.n,
        "plane",
        scratch_shapes=[pltpu.VMEM((height, batch), F32)],
    )


def in_one(place, run, args):
    shapes = jax.eval_shape(run, *args)
    return lax.cond(
        place.z < place.n,
        run,
        lambda *args: jax.tree.map(lambda leaf: jnp.zeros(leaf.shape, leaf.dtype), shapes),
        *args,
    )


def plain_gram(place, part):
    for axis in ("b", "a", "z"):
        part = reduce_scatter(place, axis, part)
    part = part.astype(BF16)
    for axis in ("z", "a", "b"):
        part = gather(place, axis, part)
    return part


def lay_kernel(place_ref, *refs, n):
    parts, outs = refs[:n], refs[n:]
    few = parts[0].shape[0] // len(outs)
    for step in range(n):
        at = pl.ds(pl.multiple_of((place_ref[0] ^ step) * few, few), few)
        for i, out in enumerate(outs):
            out[at, :] = parts[step][i * few : (i + 1) * few, :]


def fetch_kernel(weight_ref, held_ref, arrived):
    copy = pltpu.make_async_copy(weight_ref, held_ref, arrived)
    copy.start()
    copy.wait()


def fetch(weight):
    return pl.pallas_call(
        fetch_kernel,
        in_specs=[pl.BlockSpec(memory_space=pl.ANY)],
        out_specs=pl.BlockSpec(memory_space=pltpu.VMEM),
        out_shape=pltpu.VMEM(weight.shape, BF16),
        scratch_shapes=[pltpu.SemaphoreType.DMA],
        compiler_params=pltpu.CompilerParams(vmem_limit_bytes=VMEM_BYTES // 2),
        cost_estimate=pl.CostEstimate(flops=0, bytes_accessed=4 * weight.size, transcendentals=0),
        name="fetch",
    )(pltpu.with_memory_space_constraint(weight, pltpu.HBM))


def to_columns(place, view):
    rows, width = view.shape
    return exchange(place, "a", view.reshape(place.n, rows // place.n, width))


def to_planes(place, parts):
    return sends(place, "z", ordered(parts, place.a ^ place.z))


def lay(place, place_array, parts):
    rows, width = parts[0].shape
    (laid,) = local(
        functools.partial(lay_kernel, n=place.n),
        place_array,
        parts,
        [((rows * place.n, width), BF16)],
        "lay",
    )
    return laid


def met_rows(place, values, few=False):
    return sends(place, "a", [values] * place.n, few)


def project_kernel(place_ref, *refs, counts, n, k):
    met = refs[: sum(counts)]
    weight_ref, own_ref, *coded = refs[sum(counts) :]
    width = met[0].shape[1]
    columns = own_ref.shape[1]
    values = []
    for count in counts:
        values.append(jnp.concatenate([ref[...] for ref in met[:count]], 0))
        met = met[count:]
    for step in [*range(n - 1, 0, -1), 0]:
        at = pl.ds(pl.multiple_of((place_ref[0] ^ step) * columns, columns), columns)
        total = 0.0
        for i in range(k):
            rows = pl.ds(pl.multiple_of((place_ref[2] ^ i) * width, width), width)
            total += jnp.dot(values[i], weight_ref[rows, at], preferred_element_type=F32)
        if step == 0:
            own_ref[...] = total
        else:
            encode(total, coded[n - 1 - step])


def encode(total, coded_ref):
    rows = total.shape[0]
    top = jnp.max(jnp.abs(total), 0, keepdims=True)
    top = jnp.maximum(top * (1.0 + 1.0 / 128.0), 1e-30).astype(BF16)
    coded_ref[rows:] = jnp.broadcast_to(top, (SCALE_ROWS, total.shape[1]))
    whole = jnp.floor(jnp.abs(total) * (HIGHEST / top.astype(F32)) + 0.5)
    power = jnp.floor(whole * (1.0 / 128.0))
    word = (1.0 + (whole * (1.0 / 128.0) - power)) * jnp.exp2(power - POWERS // 2)
    coded_ref[:rows] = jnp.where(total < 0.0, -word, word).astype(BF16)


def decode(coded_ref, count):
    rows = coded_ref.shape[0] - SCALE_ROWS
    scale = coded_ref[rows:].astype(F32)[:1] * (1.0 / HIGHEST)
    height = rows // count
    blocks = []
    for i in range(count):
        word = coded_ref[i * height : (i + 1) * height].astype(F32)
        size = jnp.abs(word)
        power = jnp.floor(jnp.log(size) * 1.4426950408889634 + 0.002)
        part = jnp.floor(size * jnp.exp2(-power) * 128.0 + 0.5)
        whole = (power + (POWERS // 2 - 1)) * 128.0 + part
        blocks.append(jnp.where(word < 0.0, -whole, whole) * scale)
    return blocks


def project(place, place_array, met, held):
    n, k = place.n, place.k
    rows, width = met[0][0].shape
    batch, columns = rows * n, held.shape[1] // n
    counts = [len(parts) for parts in met]
    met = [part for parts in met for part in parts]
    coded = batch + SCALE_ROWS
    out_shape = [jax.ShapeDtypeStruct((batch, columns), F32)]
    out_shape += [jax.ShapeDtypeStruct((coded, columns), BF16)] * (n - 1)
    space = pl.BlockSpec(memory_space=pltpu.VMEM)
    own, *parts = pl.pallas_call(
        functools.partial(project_kernel, counts=counts, n=n, k=k),
        in_specs=[pl.BlockSpec(memory_space=pltpu.SMEM)]
        + [space] * (len(met) + 1),
        out_specs=[space] * n,
        out_shape=out_shape,
        compiler_params=pltpu.CompilerParams(vmem_limit_bytes=VMEM_BYTES),
        cost_estimate=pl.CostEstimate(
            flops=2 * batch * k * width * n * columns,
            bytes_accessed=2 * k * width * (batch + n * columns) + 3 * n * batch * columns,
            transcendentals=0,
        ),
        name="project",
    )(place_array, *met, pltpu.with_memory_space_constraint(held, pltpu.VMEM))
    return own, parts[::-1]


def normalize_kernel(place_ref, *refs, n, second):
    own_ref, parts = refs[0], refs[n - 1 : 0 : -1]
    refs = refs[n:]
    if second:
        other_ref, refs = refs[0], refs[1:]
    norm_ref, packed_ref, scale_ref = refs[:3]
    batch, columns = own_ref.shape
    height = batch // n
    met = [[own_ref[i * height : (i + 1) * height] for i in range(n)]]
    for step in range(1, n):
        met.append(decode(parts[step - 1], n))
    blocks = [tree_sum([met[step][i] for step in range(n)]) for i in range(n)]
    total = tree_sum([jnp.sum(block, 0, keepdims=True) for block in blocks])
    squares = tree_sum([jnp.sum(block * block, 0, keepdims=True) for block in blocks])
    mean = total / batch
    scale = lax.rsqrt(squares / batch - mean * mean + bn_eps)
    scale_ref[...] = scale
    rows, few = batch // n, batch // (n * n)
    for i, block in enumerate(blocks):
        normed = (block - mean) * scale
        for first in range(0, height, few):
            step, plane = divmod((i * height + first) // few, n)
            at = pl.multiple_of(plane * rows + (place_ref[1] ^ step) * few, few)
            norm_ref[pl.ds(at, few), :] = normed[first : first + few]
            packed_ref[pl.ds(at, few), :] = normed[first : first + few].astype(BF16)
    if second:
        coeff_ref, share_ref = refs[3:]
        diag = jnp.sum(norm_ref[...] * other_ref[...], 0, keepdims=True) / batch
        coeff_ref[...] = 2.0 * ((1.0 - off_weight) * diag - 1.0)
        share_ref[...] = jnp.sum((1.0 - diag) ** 2 - off_weight * diag * diag, 1, keepdims=True)


def normalize_parts(place, place_array, own, parts, other=None):
    n, k = place.n, place.k
    batch, columns = own.shape
    second = other is not None
    out_shape = [
        jax.ShapeDtypeStruct((batch, columns), F32),
        jax.ShapeDtypeStruct((batch, columns), BF16),
        jax.ShapeDtypeStruct((1, columns), F32),
    ]
    if second:
        out_shape += [jax.ShapeDtypeStruct((1, columns), F32), jax.ShapeDtypeStruct((1, 1), F32)]
    args = [own, *parts[::-1]] + ([other] if second else [])
    space = pl.BlockSpec(memory_space=pltpu.VMEM)
    return pl.pallas_call(
        functools.partial(normalize_kernel, n=n, second=second),
        in_specs=[pl.BlockSpec(memory_space=pltpu.SMEM)] + [space] * len(args),
        out_specs=[space] * len(out_shape),
        out_shape=out_shape,
        compiler_params=pltpu.CompilerParams(vmem_limit_bytes=VMEM_BYTES // 2),
        cost_estimate=pl.CostEstimate(
            flops=40 * batch * columns,
            bytes_accessed=16 * batch * columns,
            transcendentals=0,
        ),
        name="normalize",
    )(place_array, *args)


def gradient_kernel(place_ref, *refs, n, k):
    grams, refs = refs[: n * k], refs[n * k :]
    packed, norms, scales, coeff_ref, refs = refs[0:2], refs[2:4], refs[4:6], refs[6], refs[7:]
    outs, loss_ref = [refs[0], *refs[n - 1 : 0 : -1]], refs[n]
    gram_ref, whole_ref = refs[n + 1 :]
    batch, columns = norms[0].shape
    height = grams[0].shape[0] // 2
    for i in range(k):
        for step in range(n):
            at = ((place_ref[2] ^ i) * n + (place_ref[1] ^ step)) * height
            to = pl.ds(pl.multiple_of(at, height), height)
            for view in range(2):
                gram_ref[view, to, :] = grams[i * n + step][view * height : (view + 1) * height, :]
    share = 0.0
    for edge in (batch // 2 - 128, batch - 128):
        tail = gram_ref[1, edge : edge + 128, :128].astype(F32)
        row = lax.broadcasted_iota(jnp.int32, tail.shape, 0)
        column = lax.broadcasted_iota(jnp.int32, tail.shape, 1)
        taken = (row == 127) & (column < 3)
        mirror = gram_ref[1, :128, edge : edge + 128].astype(F32).T
        share += jnp.sum(jnp.where(taken, tail, 0.0), keepdims=True)
        gram_ref[1, edge : edge + 128, :128] = jnp.where(taken, mirror, tail).astype(BF16)
    factor = 2.0 * off_weight / batch
    rows = batch // n
    for view in (1, 0):
        norm = norms[view][...]
        grad = (
            factor * jnp.dot(gram_ref[1 - view], packed[view][...], preferred_element_type=F32)
            + coeff_ref[...] * norms[1 - view][...]
        )
        first = jnp.sum(grad, 0, keepdims=True) / batch
        second = jnp.sum(grad * norm, 0, keepdims=True) / batch
        whole_ref[view] = (scales[view][...] * (grad - first - norm * second)).astype(BF16)
        for step in range(n):
            at = pl.multiple_of((place_ref[0] ^ step) * rows, rows)
            outs[step][view * rows : (view + 1) * rows, :] = whole_ref[view, pl.ds(at, rows), :]
    frob = jnp.sum(gram_ref[0].astype(F32) * gram_ref[1].astype(F32), keepdims=True)
    loss_ref[...] = (share + off_weight * (frob / (batch * batch))) / D


def gradient(place, place_array, grams, packed, norms, scales, coeff):
    batch, columns = norms[0].shape
    return local(
        functools.partial(gradient_kernel, n=place.n, k=place.k),
        place_array,
        (*grams, *packed, *norms, *scales, coeff),
        [((2 * batch // place.n, columns), BF16)] * place.n + [((1, 1), F32)],
        "gradient",
        scratch_shapes=[
            pltpu.VMEM((2, batch, batch), BF16),
            pltpu.VMEM((2, batch, columns), BF16),
        ],
    )


def place_kernel(place_ref, *refs, n):
    parts, outs, done = [refs[0], *refs[n - 1 : 0 : -1]], refs[n:-1], refs[-1]
    rows, columns = parts[0].shape[0] // len(outs), parts[0].shape[1]
    copies = []
    for step in range(n):
        at = pl.ds(pl.multiple_of((place_ref[0] ^ step) * columns, columns), columns)
        for i, out in enumerate(outs):
            part = parts[step].at[i * rows : (i + 1) * rows]
            copies.append(pltpu.make_async_copy(part, out.at[:, at], done.at[step, i]))
            copies[-1].start()
    for copy in copies:
        copy.wait()


def with_kernels(place, h_first, h_second, weight):
    n, k, z, a, b = place.n, place.k, place.z, place.a, place.b
    place_array = jnp.stack([z, a, b]).astype(jnp.int32)
    first, second = lax.optimization_barrier((to_columns(place, h_first), h_second))
    first, second = to_planes(place, first), to_columns(place, second)
    first, late_weight = lax.optimization_barrier((lay(place, place_array, first), weight))
    met_1, second, held = lax.optimization_barrier(
        (
            met_rows(place, first),
            lay(place, place_array, to_planes(place, second)),
            fetch(late_weight),
        )
    )

    def sent(parts):
        return sends(place, "z", [parts[0], *parts])[1:]

    def swapped(part):
        return place.send(part, lambda z, a, b: (z, a, b ^ 1))

    own_1, parts_1 = project(place, place_array, [met_1, [swapped(part) for part in met_1]], held)
    size, here, toward = place.along("a")
    met_2 = [second] + [place.send(second, toward(step)) for step in range(1, size - 1)]
    own_1, parts_1, late_weight = lax.optimization_barrier((own_1, parts_1, weight))
    parts_1 = sent(parts_1)

    def second_projected(weight, *met):
        last = place.send(met[0], toward(size - 1))
        others = [swapped(jnp.concatenate(met, 0))]
        last, others = lax.optimization_barrier((last, others))
        others.append(swapped(last))
        return project(place, place_array, [[*met, last], others], fetch(weight))

    own_2, parts_2 = in_one(place, second_projected, (late_weight, *met_2))
    own_1, own_2 = lax.optimization_barrier((own_1, own_2))
    parts_2 = sent(parts_2)
    norm_1, packed_1, scale_1 = normalize_parts(place, place_array, own_1, parts_1)
    met_1 = in_one(place, lambda packed: first_rows(place, place_array, packed), (packed_1,))
    met_1 = sends(place, "z", met_1)
    own_2, parts_2, met_1 = lax.optimization_barrier((own_2, parts_2, met_1))
    norm_2, packed_2, scale_2, coeff, share = normalize_parts(
        place, place_array, own_2, parts_2, norm_1
    )
    height, batch = met_1[0].shape
    (rows_1,) = local(rows_kernel, place_array, met_1, [((height, batch), BF16)], "rows")
    met_2 = plane_rows(place, place_array, packed_2, share=(share,))
    rows = met_2[0].shape[0]
    (part,) = local(
        functools.partial(code_kernel, n=n),
        place_array,
        (*met_2, rows_1),
        [((rows + SCALE_ROWS + height, batch), BF16)],
        "code",
    )
    (part,) = local(
        functools.partial(finish_kernel, n=n, k=k),
        place_array,
        sends(place, "z", [part] * n),
        [((2 * rows, batch), BF16)],
        "finish",
    )
    grams = sends(place, "a", [part] * n)
    grams += [place.send(part, lambda z, a, b: (z, a, b ^ 1)) for part in grams]
    first, *others, loss = gradient(
        place,
        place_array,
        grams,
        (packed_1, packed_2),
        (norm_1, norm_2),
        (scale_1, scale_2),
        coeff,
    )
    out_1, out_2 = local(
        functools.partial(place_kernel, n=n),
        place_array,
        [first, *sends(place, "z", [first, *others[::-1]])[:0:-1]],
        [(h_first.shape, BF16)] * 2,
        "place",
        pl.BlockSpec(memory_space=pltpu.HBM),
        scratch_shapes=[pltpu.SemaphoreType.DMA((n, 2))],
    )
    return (out_1, out_2, loss.reshape(()))


def plain(place, h_first, h_second, weight):
    n, k, z, a, b = place.n, place.k, place.z, place.a, place.b
    rows, width = h_first.shape
    batch = rows * n
    columns = weight.shape[1] // n
    weight_parts = weight.reshape(k, width, n * columns)
    zs = []
    for values in (h_first, h_second):
        moved = place.send(values, lambda z, a, b: (a, z, b))
        own = jnp.concatenate(met_rows(place, moved), 0)
        total = jnp.dot(own, pick(weight_parts, b), preferred_element_type=F32)
        for step in range(1, k):
            other = place.send(own, lambda z, a, b, s=step: (z, a, b ^ s))
            total += jnp.dot(other, pick(weight_parts, b ^ step), preferred_element_type=F32)
        cut = total.reshape(batch, n, columns).transpose(1, 0, 2)
        whole = tree_sum(exchange(place, "z", cut)).reshape(n, rows, columns)
        zs.append(jnp.concatenate(ordered([whole[i] for i in range(n)], a), 0))
    normed, scales = [], []
    for values in zs:
        mean = jnp.sum(values, 0) / batch
        scale = lax.rsqrt(jnp.sum(values * values, 0) / batch - mean * mean + bn_eps)
        normed.append((values - mean) * scale)
        scales.append(scale)
    diag = jnp.sum(normed[0] * normed[1], 0) / batch
    packed = [values.astype(BF16) for values in normed]
    dims = (((1,), (1,)), ((), ()))
    grams = []
    for values in packed:
        gram = lax.dot_general(values, values, dims, preferred_element_type=F32)
        grams.append(plain_gram(place, gram))
    frob = jnp.sum(grams[0].astype(F32) * grams[1].astype(F32)) / (batch * batch)
    coeff = 2.0 * ((1.0 - off_weight) * diag - 1.0)
    factor = 2.0 * off_weight / batch
    outs = []
    for view in range(2):
        grad = (
            factor * jnp.dot(grams[1 - view], packed[view], preferred_element_type=F32)
            + coeff * normed[1 - view]
        )
        first = jnp.sum(grad, 0) / batch
        second = jnp.sum(grad * normed[view], 0) / batch
        out = (scales[view] * (grad - first - normed[view] * second)).astype(BF16)
        parts = exchange(place, "z", out.reshape(n, rows, columns))
        outs.append(jnp.concatenate(ordered(parts, z), 1))
    share = jnp.sum((1.0 - diag) ** 2) - off_weight * jnp.sum(diag * diag)
    loss = (lax.psum(share, ("dp", "mp")) + off_weight * frob) / D
    return (outs[0], outs[1], loss)


def per_device(h_first, h_second, weight):
    place = Place()
    columns = weight.shape[1] // place.n
    fits = columns % 128 == 0 and place.n == 4 and place.k == 2
    return (with_kernels if fits else plain)(place, h_first, h_second, weight)


def solution(mesh):
    in_specs = (P("dp", "mp"), P("dp", "mp"), P("dp", "mp"))
    out_specs = (P("dp", "mp"), P("dp", "mp"), P())
    return jax.shard_map(
        per_device, mesh=mesh, in_specs=in_specs, out_specs=out_specs, check_vma=False
    )
```

```python
import functools

import jax
import jax.numpy as jnp
from jax import lax
from jax.experimental import pallas as pl
from jax.experimental.pallas import tpu as pltpu
from jax.sharding import PartitionSpec as P

D = 8192


off_weight = 0.0051
bn_eps = 1e-05

F32 = jnp.float32
BF16 = jnp.bfloat16
VMEM_BYTES = 16 * 1024 * 1024
POWERS = 240
HIGHEST = 128 * POWERS - 1
SCALE_ROWS = 16


class Place:
    def __init__(self):
        self.n = lax.axis_size("dp")
        self.k = lax.axis_size("mp") // self.n
        self.z = lax.axis_index("dp")
        self.a = lax.axis_index("mp") // self.k
        self.b = lax.axis_index("mp") % self.k

    def send(self, value, target):
        n, k = self.n, self.k
        pairs = []
        for z in range(n):
            for a in range(n):
                for b in range(k):
                    to_z, to_a, to_b = target(z, a, b)
                    pairs.append(((z * n + a) * k + b, (to_z * n + to_a) * k + to_b))
        return lax.ppermute(value, ("dp", "mp"), pairs)

    def along(self, axis):
        if axis == "z":
            return self.n, self.z, lambda step: lambda z, a, b: (z ^ step, a, b)
        if axis == "a":
            return self.n, self.a, lambda step: lambda z, a, b: (z, a ^ step, b)
        return self.k, self.b, lambda step: lambda z, a, b: (z, a, b ^ step)


def ordered(parts, place):
    bit = 1
    while bit < len(parts):
        odd = (place & bit) != 0
        parts = [jnp.where(odd, parts[i ^ bit], parts[i]) for i in range(len(parts))]
        bit *= 2
    return parts


def tree_sum(parts):
    while len(parts) > 1:
        parts = [parts[i] + parts[i + 1] for i in range(0, len(parts), 2)]
    return parts[0]


def pick(value, index):
    return lax.dynamic_index_in_dim(value, index, 0, keepdims=False)


def exchange(place, axis, value, few=False):
    size, here, toward = place.along(axis)
    return sends(place, axis, [pick(value, here ^ step) for step in range(size)], few)


def sends(place, axis, parts, few=False):
    size, here, toward = place.along(axis)
    met = {0: parts[0]}
    order = [*range(1, size)] if few else [*range(size - 1, 0, -1)]
    for i, step in enumerate(order):
        part = parts[step]
        if few and i >= 2:
            met[order[i - 2]], part = lax.optimization_barrier((met[order[i - 2]], part))
        met[step] = place.send(part, toward(step))
    return [met[step] for step in range(size)]


def reduce_scatter(place, axis, value, few=False):
    size, here, toward = place.along(axis)
    value = value.reshape((size, value.shape[0] // size) + value.shape[1:])
    return tree_sum(exchange(place, axis, value, few))


def gather(place, axis, value, few=False):
    size, here, toward = place.along(axis)
    parts = sends(place, axis, [value] * size, few)
    return jnp.concatenate(ordered(parts, here), 0)


BLOCKS = 4
KEPT = 3


def halve_kernel(place_ref, kept_ref, met_ref, *outs, n):
    height = kept_ref.shape[0] // n
    width = kept_ref.shape[1] // BLOCKS
    for step, out in enumerate(outs):
        block = place_ref[1] ^ step
        at = pl.ds(pl.multiple_of(block * height, height), height)
        block = (place_ref[2] * n + block) // (2 * n // BLOCKS)
        total = []
        for i in range(KEPT):
            cut = pl.ds(pl.multiple_of(lax.rem(block + i, BLOCKS) * width, width), width)
            total.append(kept_ref[at, cut] + met_ref[at, cut])
        total = jnp.concatenate(total, 1)
        if step == 0:
            out[...] = total
        else:
            encode(total, out)


def plane_sum(met):
    return tree_sum([met[0][...]] + [decode(ref, 1)[0] for ref in met[1:]])


def plane_kernel(place_ref, *refs, n):
    met, outs, whole_ref = refs[:n], refs[n:-1], refs[-1]
    whole_ref[...] = plane_sum(met)
    height = outs[0].shape[0]
    for step, out in enumerate(outs):
        at = pl.ds(pl.multiple_of((place_ref[0] ^ step) * height, height), height)
        out[...] = whole_ref[at, :]


def rows_kernel(place_ref, *refs):
    refs[-1][...] = tree_sum([ref[...] for ref in refs[:-1]]).astype(BF16)


def code_kernel(place_ref, *refs, n):
    met, rows_ref, out_ref = refs[:n], refs[n], refs[n + 1]
    total = plane_sum(met)
    coded = total.shape[0] + SCALE_ROWS
    encode(total, out_ref.at[:coded])
    out_ref[coded:] = rows_ref[...]


def finish_kernel(place_ref, *refs, n, k):
    out_ref = refs[-1]
    height = out_ref.shape[0] // 2
    coded, few = height + SCALE_ROWS, height // n
    met = []
    for step in range(n):
        at = pl.ds(pl.multiple_of((place_ref[0] ^ step) * few, few), few)
        out_ref[at, :] = refs[step][coded:]
        met += decode(refs[step].at[:coded], 1)
    total = tree_sum(met)
    last = (place_ref[1] == n - 1) & (place_ref[2] == k - 1)
    start = 2 * (total.shape[1] // KEPT)
    edge = total[-8:, start:]
    row = lax.broadcasted_iota(jnp.int32, edge.shape, 0)
    column = lax.broadcasted_iota(jnp.int32, edge.shape, 1)
    taken = (row == 7) & last
    whole = jnp.sum(jnp.where(taken & (column == 0), edge, 0.0), keepdims=True)
    high = whole.astype(BF16).astype(F32)
    middle = (whole - high).astype(BF16).astype(F32)
    three = jnp.where(column == 0, high, jnp.where(column == 1, middle, whole - high - middle))
    edge = jnp.where(taken & (column < 3), three, edge)
    edge = jnp.concatenate([total[-8:, :start], edge], 1)
    out_ref[height:] = jnp.concatenate([total[:-8], edge], 0).astype(BF16)


def local(kernel, place_array, args, shapes, name, **more):
    space = pl.BlockSpec(memory_space=pltpu.VMEM)
    return pl.pallas_call(
        kernel,
        in_specs=[pl.BlockSpec(memory_space=pltpu.SMEM)] + [space] * len(args),
        out_specs=[space] * len(shapes),
        out_shape=[jax.ShapeDtypeStruct(shape, dtype) for shape, dtype in shapes],
        compiler_params=pltpu.CompilerParams(vmem_limit_bytes=VMEM_BYTES // 2),
        name=name,
        **more,
    )(place_array, *args)


def plane_rows(place, place_array, grams, few=False):
    half, batch = grams[0].shape
    kept, other = grams
    other = place.send(other, lambda z, a, b: (z, a, b ^ 1))
    height, batch = half // place.n, batch * KEPT // BLOCKS
    parts = local(
        functools.partial(halve_kernel, n=place.n),
        place_array,
        (kept, other),
        [((height, batch), F32)] + [((height + SCALE_ROWS, batch), BF16)] * (place.n - 1),
        "halve",
    )
    return sends(place, "a", parts, few)


def first_rows(place, place_array, grams):
    parts = plane_rows(place, place_array, grams, True)
    height, batch = parts[0].shape
    return local(
        functools.partial(plane_kernel, n=place.n),
        place_array,
        parts,
        [((height // place.n, batch), F32)] * place.n,
        "plane",
        scratch_shapes=[pltpu.VMEM((height, batch), F32)],
    )


def in_one(place, run, args):
    shapes = jax.eval_shape(run, *args)
    return lax.cond(
        place.z < place.n,
        run,
        lambda *args: jax.tree.map(lambda leaf: jnp.zeros(leaf.shape, leaf.dtype), shapes),
        *args,
    )


def plain_gram(place, part):
    for axis in ("b", "a", "z"):
        part = reduce_scatter(place, axis, part)
    part = part.astype(BF16)
    for axis in ("z", "a", "b"):
        part = gather(place, axis, part)
    return part


def lay_kernel(place_ref, *refs, n):
    parts, outs = refs[:n], refs[n:]
    few = parts[0].shape[0] // len(outs)
    for step in range(n):
        at = pl.ds(pl.multiple_of((place_ref[0] ^ step) * few, few), few)
        for i, out in enumerate(outs):
            out[at, :] = parts[step][i * few : (i + 1) * few, :]


def fetch_kernel(weight_ref, held_ref, arrived):
    copy = pltpu.make_async_copy(weight_ref, held_ref, arrived)
    copy.start()
    copy.wait()


def fetch(weight):
    return pl.pallas_call(
        fetch_kernel,
        in_specs=[pl.BlockSpec(memory_space=pl.ANY)],
        out_specs=pl.BlockSpec(memory_space=pltpu.VMEM),
        out_shape=pltpu.VMEM(weight.shape, BF16),
        scratch_shapes=[pltpu.SemaphoreType.DMA],
        compiler_params=pltpu.CompilerParams(vmem_limit_bytes=VMEM_BYTES // 2),
        cost_estimate=pl.CostEstimate(flops=0, bytes_accessed=4 * weight.size, transcendentals=0),
        name="fetch",
    )(pltpu.with_memory_space_constraint(weight, pltpu.HBM))


def to_columns(place, view):
    rows, width = view.shape
    return exchange(place, "a", view.reshape(place.n, rows // place.n, width))


def to_planes(place, parts):
    return sends(place, "z", ordered(parts, place.a ^ place.z))


def lay(place, place_array, parts):
    rows, width = parts[0].shape
    (laid,) = local(
        functools.partial(lay_kernel, n=place.n),
        place_array,
        parts,
        [((rows * place.n, width), BF16)],
        "lay",
    )
    return laid


def met_rows(place, values, few=False):
    return sends(place, "a", [values] * place.n, few)


def project_kernel(place_ref, *refs, counts, n, k):
    met = refs[: sum(counts)]
    weight_ref, own_ref, *coded = refs[sum(counts) :]
    width = met[0].shape[1]
    columns = own_ref.shape[1]
    values = []
    for count in counts:
        values.append(jnp.concatenate([ref[...] for ref in met[:count]], 0))
        met = met[count:]
    for step in [*range(n - 1, 0, -1), 0]:
        at = pl.ds(pl.multiple_of((place_ref[0] ^ step) * columns, columns), columns)
        total = 0.0
        for i in range(k):
            rows = pl.ds(pl.multiple_of((place_ref[2] ^ i) * width, width), width)
            total += jnp.dot(values[i], weight_ref[rows, at], preferred_element_type=F32)
        if step == 0:
            own_ref[...] = total
        else:
            encode(total, coded[n - 1 - step])


def encode(total, coded_ref):
    rows = total.shape[0]
    top = jnp.max(jnp.abs(total), 0, keepdims=True)
    top = jnp.maximum(top * (1.0 + 1.0 / 128.0), 1e-30).astype(BF16)
    coded_ref[rows:] = jnp.broadcast_to(top, (SCALE_ROWS, total.shape[1]))
    whole = jnp.floor(jnp.abs(total) * (HIGHEST / top.astype(F32)) + 0.5)
    power = jnp.floor(whole * (1.0 / 128.0))
    word = (1.0 + (whole * (1.0 / 128.0) - power)) * jnp.exp2(power - POWERS // 2)
    coded_ref[:rows] = jnp.where(total < 0.0, -word, word).astype(BF16)


def decode(coded_ref, count):
    rows = coded_ref.shape[0] - SCALE_ROWS
    scale = coded_ref[rows:].astype(F32)[:1] * (1.0 / HIGHEST)
    height = rows // count
    blocks = []
    for i in range(count):
        word = coded_ref[i * height : (i + 1) * height].astype(F32)
        size = jnp.abs(word)
        power = jnp.floor(jnp.log(size) * 1.4426950408889634 + 0.002)
        part = jnp.floor(size * jnp.exp2(-power) * 128.0 + 0.5)
        whole = (power + (POWERS // 2 - 1)) * 128.0 + part
        blocks.append(jnp.where(word < 0.0, -whole, whole) * scale)
    return blocks


def project(place, place_array, met, held):
    n, k = place.n, place.k
    rows, width = met[0][0].shape
    batch, columns = rows * n, held.shape[1] // n
    counts = [len(parts) for parts in met]
    met = [part for parts in met for part in parts]
    coded = batch + SCALE_ROWS
    out_shape = [jax.ShapeDtypeStruct((batch, columns), F32)]
    out_shape += [jax.ShapeDtypeStruct((coded, columns), BF16)] * (n - 1)
    space = pl.BlockSpec(memory_space=pltpu.VMEM)
    own, *parts = pl.pallas_call(
        functools.partial(project_kernel, counts=counts, n=n, k=k),
        in_specs=[pl.BlockSpec(memory_space=pltpu.SMEM)]
        + [space] * (len(met) + 1),
        out_specs=[space] * n,
        out_shape=out_shape,
        compiler_params=pltpu.CompilerParams(vmem_limit_bytes=VMEM_BYTES),
        cost_estimate=pl.CostEstimate(
            flops=2 * batch * k * width * n * columns,
            bytes_accessed=2 * k * width * (batch + n * columns) + 3 * n * batch * columns,
            transcendentals=0,
        ),
        name="project",
    )(place_array, *met, pltpu.with_memory_space_constraint(held, pltpu.VMEM))
    return own, parts[::-1]


def normalize_kernel(place_ref, *refs, n, k, second):
    own_ref, parts = refs[0], refs[n - 1 : 0 : -1]
    refs = refs[n:]
    if second:
        other_ref, refs = refs[0], refs[1:]
    norm_ref, packed_ref, scale_ref = refs[:3]
    grams = refs[3 : 3 + k]
    batch, columns = own_ref.shape
    height = batch // n
    met = [[own_ref[i * height : (i + 1) * height] for i in range(n)]]
    for step in range(1, n):
        met.append(decode(parts[step - 1], n))
    blocks = [tree_sum([met[step][i] for step in range(n)]) for i in range(n)]
    total = tree_sum([jnp.sum(block, 0, keepdims=True) for block in blocks])
    squares = tree_sum([jnp.sum(block * block, 0, keepdims=True) for block in blocks])
    mean = total / batch
    scale = lax.rsqrt(squares / batch - mean * mean + bn_eps)
    scale_ref[...] = scale
    rows, few = batch // n, batch // (n * n)
    for i, block in enumerate(blocks):
        normed = (block - mean) * scale
        for first in range(0, height, few):
            step, plane = divmod((i * height + first) // few, n)
            at = pl.multiple_of(plane * rows + (place_ref[1] ^ step) * few, few)
            norm_ref[pl.ds(at, few), :] = normed[first : first + few]
            packed_ref[pl.ds(at, few), :] = normed[first : first + few].astype(BF16)
    dims = (((1,), (1,)), ((), ()))
    packed = packed_ref[...]
    size = batch // k
    for i in range(k):
        at = pl.multiple_of((place_ref[2] ^ i) * size, size)
        gram = lax.dot_general(packed_ref[pl.ds(at, size), :], packed, dims, preferred_element_type=F32)
        grams[i][...] = gram
    if second:
        coeff_ref = refs[3 + k]
        diag = jnp.sum(norm_ref[...] * other_ref[...], 0, keepdims=True) / batch
        coeff_ref[...] = 2.0 * ((1.0 - off_weight) * diag - 1.0)
        share = jnp.sum((1.0 - diag) ** 2 - off_weight * diag * diag, 1, keepdims=True)
        for i in range(k):

            @pl.when((place_ref[2] ^ i) == k - 1)
            def _():
                at = batch // BLOCKS
                row = grams[i][size - 8 :, at : at + 128]
                first = (lax.broadcasted_iota(jnp.int32, row.shape, 0) == 7) & (
                    lax.broadcasted_iota(jnp.int32, row.shape, 1) == 0
                )
                grams[i][size - 8 :, at : at + 128] = jnp.where(first, share, row)


def normalize_parts(place, place_array, own, parts, other=None):
    n, k = place.n, place.k
    batch, columns = own.shape
    second = other is not None
    out_shape = [
        jax.ShapeDtypeStruct((batch, columns), F32),
        jax.ShapeDtypeStruct((batch, columns), BF16),
        jax.ShapeDtypeStruct((1, columns), F32),
    ] + [jax.ShapeDtypeStruct((batch // k, batch), F32)] * k
    if second:
        out_shape.append(jax.ShapeDtypeStruct((1, columns), F32))
    args = [own, *parts[::-1]] + ([other] if second else [])
    space = pl.BlockSpec(memory_space=pltpu.VMEM)
    return pl.pallas_call(
        functools.partial(normalize_kernel, n=n, k=k, second=second),
        in_specs=[pl.BlockSpec(memory_space=pltpu.SMEM)] + [space] * len(args),
        out_specs=[space] * len(out_shape),
        out_shape=out_shape,
        compiler_params=pltpu.CompilerParams(vmem_limit_bytes=VMEM_BYTES // 2),
        cost_estimate=pl.CostEstimate(
            flops=2 * batch * batch * columns,
            bytes_accessed=16 * batch * columns + 4 * batch * batch,
            transcendentals=0,
        ),
        name="normalize",
    )(place_array, *args)


def gradient_kernel(place_ref, *refs, n, k):
    grams, refs = refs[: n * k], refs[n * k :]
    packed, norms, scales, coeff_ref, refs = refs[0:2], refs[2:4], refs[4:6], refs[6], refs[7:]
    outs, loss_ref = [refs[0], *refs[n - 1 : 0 : -1]], refs[n]
    gram_ref, whole_ref = refs[n + 1 :]
    batch, columns = norms[0].shape
    height = grams[0].shape[0] // 2
    width = batch // BLOCKS
    for i in range(k):
        for step in range(n):
            block = (place_ref[2] ^ i) * n + (place_ref[1] ^ step)
            at = pl.ds(pl.multiple_of(block * height, height), height)
            block = block // (2 * n // BLOCKS)
            for j in range(KEPT):
                to = pl.ds(pl.multiple_of(lax.rem(block + j, BLOCKS) * width, width), width)
                for view in range(2):
                    gram_ref[view, at, to] = grams[i * n + step][
                        view * height : (view + 1) * height, j * width : (j + 1) * width
                    ]
    blocks = [slice(i * width, (i + 1) * width) for i in range(BLOCKS)]
    for view in range(2):
        for i in range(BLOCKS):
            other = gram_ref[view, blocks[i - 1], blocks[i]].astype(F32).T
            gram_ref[view, blocks[i], blocks[i - 1]] = other.astype(BF16)
    tail = gram_ref[1, blocks[3], blocks[1]].astype(F32)
    row = lax.broadcasted_iota(jnp.int32, tail.shape, 0)
    column = lax.broadcasted_iota(jnp.int32, tail.shape, 1)
    taken = (row == width - 1) & (column < 3)
    mirror = gram_ref[1, blocks[1], blocks[3]].astype(F32).T
    share = jnp.sum(jnp.where(taken, tail, 0.0), keepdims=True)
    gram_ref[1, blocks[3], blocks[1]] = jnp.where(taken, mirror, tail).astype(BF16)
    factor = 2.0 * off_weight / batch
    rows = batch // n
    for view in (1, 0):
        norm = norms[view][...]
        grad = (
            factor * jnp.dot(gram_ref[1 - view], packed[view][...], preferred_element_type=F32)
            + coeff_ref[...] * norms[1 - view][...]
        )
        first = jnp.sum(grad, 0, keepdims=True) / batch
        second = jnp.sum(grad * norm, 0, keepdims=True) / batch
        whole_ref[view] = (scales[view][...] * (grad - first - norm * second)).astype(BF16)
        for step in range(n):
            at = pl.multiple_of((place_ref[0] ^ step) * rows, rows)
            outs[step][view * rows : (view + 1) * rows, :] = whole_ref[view, pl.ds(at, rows), :]
    frob = jnp.sum(gram_ref[0].astype(F32) * gram_ref[1].astype(F32), keepdims=True)
    loss_ref[...] = (share + off_weight * (frob / (batch * batch))) / D


def gradient(place, place_array, grams, packed, norms, scales, coeff):
    batch, columns = norms[0].shape
    return local(
        functools.partial(gradient_kernel, n=place.n, k=place.k),
        place_array,
        (*grams, *packed, *norms, *scales, coeff),
        [((2 * batch // place.n, columns), BF16)] * place.n + [((1, 1), F32)],
        "gradient",
        scratch_shapes=[
            pltpu.VMEM((2, batch, batch), BF16),
            pltpu.VMEM((2, batch, columns), BF16),
        ],
    )


def place_kernel(place_ref, *refs, n):
    parts, outs = [refs[0], *refs[n - 1 : 0 : -1]], refs[n:]
    rows, columns = parts[0].shape[0] // len(outs), parts[0].shape[1]
    for step in range(n):
        at = pl.ds(pl.multiple_of((place_ref[0] ^ step) * columns, columns), columns)
        for i, out in enumerate(outs):
            out[:, at] = parts[step][i * rows : (i + 1) * rows, :]


def with_kernels(place, h_first, h_second, weight):
    n, k, z, a, b = place.n, place.k, place.z, place.a, place.b
    place_array = jnp.stack([z, a, b]).astype(jnp.int32)
    first = to_columns(place, h_first)
    first, second = lax.optimization_barrier((to_planes(place, first), to_columns(place, h_second)))
    first, late_weight = lax.optimization_barrier((lay(place, place_array, first), weight))
    met_1, second, held = lax.optimization_barrier(
        (met_rows(place, first), to_planes(place, second), fetch(late_weight))
    )

    def sent(parts):
        return sends(place, "z", [parts[0], *parts])[1:]

    def swapped(part):
        return place.send(part, lambda z, a, b: (z, a, b ^ 1))

    own_1, parts_1 = project(place, place_array, [met_1, [swapped(part) for part in met_1]], held)
    second = lay(place, place_array, second)
    size, here, toward = place.along("a")
    met_2 = [second] + [place.send(second, toward(step)) for step in range(1, size - 1)]
    own_1, parts_1, late_weight = lax.optimization_barrier((own_1, parts_1, weight))
    parts_1 = sent(parts_1)

    def second_projected(weight, *met):
        last = place.send(met[0], toward(size - 1))
        others = [swapped(jnp.concatenate(met, 0))]
        last, others = lax.optimization_barrier((last, others))
        others.append(swapped(last))
        return project(place, place_array, [[*met, last], others], fetch(weight))

    own_2, parts_2 = in_one(place, second_projected, (late_weight, *met_2))
    own_1, own_2 = lax.optimization_barrier((own_1, own_2))
    parts_2 = sent(parts_2)
    norm_1, packed_1, scale_1, *grams = normalize_parts(place, place_array, own_1, parts_1)
    met_1 = in_one(place, lambda *grams: first_rows(place, place_array, grams), grams)
    met_1 = sends(place, "z", met_1)
    own_2, parts_2, met_1 = lax.optimization_barrier((own_2, parts_2, met_1))
    norm_2, packed_2, scale_2, *grams, coeff = normalize_parts(
        place, place_array, own_2, parts_2, norm_1
    )
    height, batch = met_1[0].shape
    (rows_1,) = local(rows_kernel, place_array, met_1, [((height, batch), BF16)], "rows")
    met_2 = plane_rows(place, place_array, grams)
    rows = met_2[0].shape[0]
    (part,) = local(
        functools.partial(code_kernel, n=n),
        place_array,
        (*met_2, rows_1),
        [((rows + SCALE_ROWS + height, batch), BF16)],
        "code",
    )
    (part,) = local(
        functools.partial(finish_kernel, n=n, k=k),
        place_array,
        sends(place, "z", [part] * n),
        [((2 * rows, batch), BF16)],
        "finish",
    )
    grams = sends(place, "a", [part] * n)
    grams += [place.send(part, lambda z, a, b: (z, a, b ^ 1)) for part in grams]
    first, *others, loss = gradient(
        place,
        place_array,
        grams,
        (packed_1, packed_2),
        (norm_1, norm_2),
        (scale_1, scale_2),
        coeff,
    )
    out_1, out_2 = local(
        functools.partial(place_kernel, n=n),
        place_array,
        [first, *sends(place, "z", [first, *others[::-1]])[:0:-1]],
        [(h_first.shape, BF16)] * 2,
        "place",
    )
    return (out_1, out_2, loss.reshape(()))


def plain(place, h_first, h_second, weight):
    n, k, z, a, b = place.n, place.k, place.z, place.a, place.b
    rows, width = h_first.shape
    batch = rows * n
    columns = weight.shape[1] // n
    weight_parts = weight.reshape(k, width, n * columns)
    zs = []
    for values in (h_first, h_second):
        moved = place.send(values, lambda z, a, b: (a, z, b))
        own = jnp.concatenate(met_rows(place, moved), 0)
        total = jnp.dot(own, pick(weight_parts, b), preferred_element_type=F32)
        for step in range(1, k):
            other = place.send(own, lambda z, a, b, s=step: (z, a, b ^ s))
            total += jnp.dot(other, pick(weight_parts, b ^ step), preferred_element_type=F32)
        cut = total.reshape(batch, n, columns).transpose(1, 0, 2)
        whole = tree_sum(exchange(place, "z", cut)).reshape(n, rows, columns)
        zs.append(jnp.concatenate(ordered([whole[i] for i in range(n)], a), 0))
    normed, scales = [], []
    for values in zs:
        mean = jnp.sum(values, 0) / batch
        scale = lax.rsqrt(jnp.sum(values * values, 0) / batch - mean * mean + bn_eps)
        normed.append((values - mean) * scale)
        scales.append(scale)
    diag = jnp.sum(normed[0] * normed[1], 0) / batch
    packed = [values.astype(BF16) for values in normed]
    dims = (((1,), (1,)), ((), ()))
    grams = []
    for values in packed:
        gram = lax.dot_general(values, values, dims, preferred_element_type=F32)
        grams.append(plain_gram(place, gram))
    frob = jnp.sum(grams[0].astype(F32) * grams[1].astype(F32)) / (batch * batch)
    coeff = 2.0 * ((1.0 - off_weight) * diag - 1.0)
    factor = 2.0 * off_weight / batch
    outs = []
    for view in range(2):
        grad = (
            factor * jnp.dot(grams[1 - view], packed[view], preferred_element_type=F32)
            + coeff * normed[1 - view]
        )
        first = jnp.sum(grad, 0) / batch
        second = jnp.sum(grad * normed[view], 0) / batch
        out = (scales[view] * (grad - first - normed[view] * second)).astype(BF16)
        parts = exchange(place, "z", out.reshape(n, rows, columns))
        outs.append(jnp.concatenate(ordered(parts, z), 1))
    share = jnp.sum((1.0 - diag) ** 2) - off_weight * jnp.sum(diag * diag)
    loss = (lax.psum(share, ("dp", "mp")) + off_weight * frob) / D
    return (outs[0], outs[1], loss)


def per_device(h_first, h_second, weight):
    place = Place()
    columns = weight.shape[1] // place.n
    fits = columns % 128 == 0 and place.n == 4 and place.k == 2
    return (with_kernels if fits else plain)(place, h_first, h_second, weight)


def solution(mesh):
    in_specs = (P("dp", "mp"), P("dp", "mp"), P("dp", "mp"))
    out_specs = (P("dp", "mp"), P("dp", "mp"), P())
    return jax.shard_map(
        per_device, mesh=mesh, in_specs=in_specs, out_specs=out_specs, check_vma=False
    )
```

```python
import functools

import jax
import jax.numpy as jnp
from jax import lax
from jax.experimental import pallas as pl
from jax.experimental.pallas import tpu as pltpu
from jax.sharding import PartitionSpec as P

D = 8192


off_weight = 0.0051
bn_eps = 1e-05

F32 = jnp.float32
BF16 = jnp.bfloat16
VMEM_BYTES = 16 * 1024 * 1024
POWERS = 240
HIGHEST = 128 * POWERS - 1
SCALE_ROWS = 16


class Place:
    def __init__(self):
        self.n = lax.axis_size("dp")
        self.k = lax.axis_size("mp") // self.n
        self.z = lax.axis_index("dp")
        self.a = lax.axis_index("mp") // self.k
        self.b = lax.axis_index("mp") % self.k

    def send(self, value, target):
        n, k = self.n, self.k
        pairs = []
        for z in range(n):
            for a in range(n):
                for b in range(k):
                    to_z, to_a, to_b = target(z, a, b)
                    pairs.append(((z * n + a) * k + b, (to_z * n + to_a) * k + to_b))
        return lax.ppermute(value, ("dp", "mp"), pairs)

    def along(self, axis):
        if axis == "z":
            return self.n, self.z, lambda step: lambda z, a, b: (z ^ step, a, b)
        if axis == "a":
            return self.n, self.a, lambda step: lambda z, a, b: (z, a ^ step, b)
        return self.k, self.b, lambda step: lambda z, a, b: (z, a, b ^ step)


def ordered(parts, place):
    bit = 1
    while bit < len(parts):
        odd = (place & bit) != 0
        parts = [jnp.where(odd, parts[i ^ bit], parts[i]) for i in range(len(parts))]
        bit *= 2
    return parts


def tree_sum(parts):
    while len(parts) > 1:
        parts = [parts[i] + parts[i + 1] for i in range(0, len(parts), 2)]
    return parts[0]


def pick(value, index):
    return lax.dynamic_index_in_dim(value, index, 0, keepdims=False)


def exchange(place, axis, value, few=False):
    size, here, toward = place.along(axis)
    return sends(place, axis, [pick(value, here ^ step) for step in range(size)], few)


def sends(place, axis, parts, few=False):
    size, here, toward = place.along(axis)
    met = {0: parts[0]}
    order = [*range(1, size)] if few else [*range(size - 1, 0, -1)]
    for i, step in enumerate(order):
        part = parts[step]
        if few and i >= 2:
            met[order[i - 2]], part = lax.optimization_barrier((met[order[i - 2]], part))
        met[step] = place.send(part, toward(step))
    return [met[step] for step in range(size)]


def reduce_scatter(place, axis, value, few=False):
    size, here, toward = place.along(axis)
    value = value.reshape((size, value.shape[0] // size) + value.shape[1:])
    return tree_sum(exchange(place, axis, value, few))


def gather(place, axis, value, few=False):
    size, here, toward = place.along(axis)
    parts = sends(place, axis, [value] * size, few)
    return jnp.concatenate(ordered(parts, here), 0)


BLOCKS = 4
KEPT = 3


def halve_kernel(place_ref, kept_ref, met_ref, *outs, n):
    height = kept_ref.shape[0] // n
    width = kept_ref.shape[1] // BLOCKS
    for step, out in enumerate(outs):
        block = place_ref[1] ^ step
        at = pl.ds(pl.multiple_of(block * height, height), height)
        block = (place_ref[2] * n + block) // (2 * n // BLOCKS)
        total = []
        for i in range(KEPT):
            cut = pl.ds(pl.multiple_of(lax.rem(block + i, BLOCKS) * width, width), width)
            total.append(kept_ref[at, cut] + met_ref[at, cut])
        total = jnp.concatenate(total, 1)
        if step == 0:
            out[...] = total
        else:
            encode(total, out)


def plane_sum(met):
    return tree_sum([met[0][...]] + [decode(ref, 1)[0] for ref in met[1:]])


def plane_kernel(place_ref, *refs, n):
    met, outs, whole_ref = refs[:n], refs[n:-1], refs[-1]
    whole_ref[...] = plane_sum(met)
    height = outs[0].shape[0]
    for step, out in enumerate(outs):
        at = pl.ds(pl.multiple_of((place_ref[0] ^ step) * height, height), height)
        out[...] = whole_ref[at, :]


def rows_kernel(place_ref, *refs):
    refs[-1][...] = tree_sum([ref[...] for ref in refs[:-1]]).astype(BF16)


def code_kernel(place_ref, *refs, n):
    met, rows_ref, out_ref = refs[:n], refs[n], refs[n + 1]
    total = plane_sum(met)
    coded = total.shape[0] + SCALE_ROWS
    encode(total, out_ref.at[:coded])
    out_ref[coded:] = rows_ref[...]


def finish_kernel(place_ref, *refs, n, k):
    out_ref = refs[-1]
    height = out_ref.shape[0] // 2
    coded, few = height + SCALE_ROWS, height // n
    met = []
    for step in range(n):
        at = pl.ds(pl.multiple_of((place_ref[0] ^ step) * few, few), few)
        out_ref[at, :] = refs[step][coded:]
        met += decode(refs[step].at[:coded], 1)
    total = tree_sum(met)
    last = (place_ref[1] == n - 1) & (place_ref[2] == k - 1)
    start = 2 * (total.shape[1] // KEPT)
    edge = total[-8:, start:]
    row = lax.broadcasted_iota(jnp.int32, edge.shape, 0)
    column = lax.broadcasted_iota(jnp.int32, edge.shape, 1)
    taken = (row == 7) & last
    whole = jnp.sum(jnp.where(taken & (column == 0), edge, 0.0), keepdims=True)
    high = whole.astype(BF16).astype(F32)
    middle = (whole - high).astype(BF16).astype(F32)
    three = jnp.where(column == 0, high, jnp.where(column == 1, middle, whole - high - middle))
    edge = jnp.where(taken & (column < 3), three, edge)
    edge = jnp.concatenate([total[-8:, :start], edge], 1)
    out_ref[height:] = jnp.concatenate([total[:-8], edge], 0).astype(BF16)


def local(kernel, place_array, args, shapes, name, **more):
    space = pl.BlockSpec(memory_space=pltpu.VMEM)
    return pl.pallas_call(
        kernel,
        in_specs=[pl.BlockSpec(memory_space=pltpu.SMEM)] + [space] * len(args),
        out_specs=[space] * len(shapes),
        out_shape=[jax.ShapeDtypeStruct(shape, dtype) for shape, dtype in shapes],
        compiler_params=pltpu.CompilerParams(vmem_limit_bytes=VMEM_BYTES // 2),
        name=name,
        **more,
    )(place_array, *args)


def plane_rows(place, place_array, grams, few=False):
    half, batch = grams[0].shape
    kept, other = grams
    other = place.send(other, lambda z, a, b: (z, a, b ^ 1))
    height, batch = half // place.n, batch * KEPT // BLOCKS
    parts = local(
        functools.partial(halve_kernel, n=place.n),
        place_array,
        (kept, other),
        [((height, batch), F32)] + [((height + SCALE_ROWS, batch), BF16)] * (place.n - 1),
        "halve",
    )
    return sends(place, "a", parts, few)


def first_rows(place, place_array, grams):
    parts = plane_rows(place, place_array, grams, True)
    height, batch = parts[0].shape
    return local(
        functools.partial(plane_kernel, n=place.n),
        place_array,
        parts,
        [((height // place.n, batch), F32)] * place.n,
        "plane",
        scratch_shapes=[pltpu.VMEM((height, batch), F32)],
    )


def in_one(place, run, args):
    shapes = jax.eval_shape(run, *args)
    return lax.cond(
        place.z < place.n,
        run,
        lambda *args: jax.tree.map(lambda leaf: jnp.zeros(leaf.shape, leaf.dtype), shapes),
        *args,
    )


def plain_gram(place, part):
    for axis in ("b", "a", "z"):
        part = reduce_scatter(place, axis, part)
    part = part.astype(BF16)
    for axis in ("z", "a", "b"):
        part = gather(place, axis, part)
    return part


def lay_kernel(place_ref, *refs, n):
    parts, outs = refs[:n], refs[n:]
    few = parts[0].shape[0] // len(outs)
    for step in range(n):
        at = pl.ds(pl.multiple_of((place_ref[0] ^ step) * few, few), few)
        for i, out in enumerate(outs):
            out[at, :] = parts[step][i * few : (i + 1) * few, :]


def fetch_kernel(weight_ref, held_ref, arrived):
    copy = pltpu.make_async_copy(weight_ref, held_ref, arrived)
    copy.start()
    copy.wait()


def fetch(weight):
    return pl.pallas_call(
        fetch_kernel,
        in_specs=[pl.BlockSpec(memory_space=pl.ANY)],
        out_specs=pl.BlockSpec(memory_space=pltpu.VMEM),
        out_shape=pltpu.VMEM(weight.shape, BF16),
        scratch_shapes=[pltpu.SemaphoreType.DMA],
        compiler_params=pltpu.CompilerParams(vmem_limit_bytes=VMEM_BYTES // 2),
        cost_estimate=pl.CostEstimate(flops=0, bytes_accessed=4 * weight.size, transcendentals=0),
        name="fetch",
    )(pltpu.with_memory_space_constraint(weight, pltpu.HBM))


def to_columns(place, view):
    rows, width = view.shape
    return exchange(place, "a", view.reshape(place.n, rows // place.n, width))


def to_planes(place, parts):
    return sends(place, "z", ordered(parts, place.a ^ place.z))


def lay(place, place_array, parts):
    rows, width = parts[0].shape
    (laid,) = local(
        functools.partial(lay_kernel, n=place.n),
        place_array,
        parts,
        [((rows * place.n, width), BF16)],
        "lay",
    )
    return laid


def met_rows(place, values, few=False):
    return sends(place, "a", [values] * place.n, few)


def project_kernel(place_ref, *refs, counts, n, k):
    met = refs[: sum(counts)]
    weight_ref, own_ref, *coded = refs[sum(counts) :]
    width = met[0].shape[1]
    columns = own_ref.shape[1]
    values = []
    for count in counts:
        values.append(jnp.concatenate([ref[...] for ref in met[:count]], 0))
        met = met[count:]
    for step in [*range(n - 1, 0, -1), 0]:
        at = pl.ds(pl.multiple_of((place_ref[0] ^ step) * columns, columns), columns)
        total = 0.0
        for i in range(k):
            rows = pl.ds(pl.multiple_of((place_ref[2] ^ i) * width, width), width)
            total += jnp.dot(values[i], weight_ref[rows, at], preferred_element_type=F32)
        if step == 0:
            own_ref[...] = total
        else:
            encode(total, coded[n - 1 - step])


def encode(total, coded_ref):
    rows = total.shape[0]
    top = jnp.max(jnp.abs(total), 0, keepdims=True)
    top = jnp.maximum(top * (1.0 + 1.0 / 128.0), 1e-30).astype(BF16)
    coded_ref[rows:] = jnp.broadcast_to(top, (SCALE_ROWS, total.shape[1]))
    whole = jnp.floor(jnp.abs(total) * (HIGHEST / top.astype(F32)) + 0.5)
    power = jnp.floor(whole * (1.0 / 128.0))
    word = (1.0 + (whole * (1.0 / 128.0) - power)) * jnp.exp2(power - POWERS // 2)
    coded_ref[:rows] = jnp.where(total < 0.0, -word, word).astype(BF16)


def decode(coded_ref, count):
    rows = coded_ref.shape[0] - SCALE_ROWS
    scale = coded_ref[rows:].astype(F32)[:1] * (1.0 / HIGHEST)
    height = rows // count
    blocks = []
    for i in range(count):
        word = coded_ref[i * height : (i + 1) * height].astype(F32)
        size = jnp.abs(word)
        power = jnp.floor(jnp.log(size) * 1.4426950408889634 + 0.002)
        part = jnp.floor(size * jnp.exp2(-power) * 128.0 + 0.5)
        whole = (power + (POWERS // 2 - 1)) * 128.0 + part
        blocks.append(jnp.where(word < 0.0, -whole, whole) * scale)
    return blocks


def project(place, place_array, met, held):
    n, k = place.n, place.k
    rows, width = met[0][0].shape
    batch, columns = rows * n, held.shape[1] // n
    counts = [len(parts) for parts in met]
    met = [part for parts in met for part in parts]
    coded = batch + SCALE_ROWS
    out_shape = [jax.ShapeDtypeStruct((batch, columns), F32)]
    out_shape += [jax.ShapeDtypeStruct((coded, columns), BF16)] * (n - 1)
    space = pl.BlockSpec(memory_space=pltpu.VMEM)
    own, *parts = pl.pallas_call(
        functools.partial(project_kernel, counts=counts, n=n, k=k),
        in_specs=[pl.BlockSpec(memory_space=pltpu.SMEM)]
        + [space] * (len(met) + 1),
        out_specs=[space] * n,
        out_shape=out_shape,
        compiler_params=pltpu.CompilerParams(vmem_limit_bytes=VMEM_BYTES),
        cost_estimate=pl.CostEstimate(
            flops=2 * batch * k * width * n * columns,
            bytes_accessed=2 * k * width * (batch + n * columns) + 3 * n * batch * columns,
            transcendentals=0,
        ),
        name="project",
    )(place_array, *met, pltpu.with_memory_space_constraint(held, pltpu.VMEM))
    return own, parts[::-1]


def normalize_kernel(place_ref, *refs, n, k, order, second):
    own_ref, parts = refs[0], refs[n - 1 : 0 : -1]
    refs = refs[n:]
    if second:
        other_ref, refs = refs[0], refs[1:]
    norm_ref, packed_ref, scale_ref = refs[:3]
    grams = refs[3 : 3 + k]
    batch, columns = own_ref.shape
    height = batch // n
    met = [[own_ref[i * height : (i + 1) * height] for i in range(n)]]
    for step in range(1, n):
        met.append(decode(parts[step - 1], n))
    blocks = [tree_sum([met[step][i] for step in range(n)]) for i in range(n)]
    total = tree_sum([jnp.sum(block, 0, keepdims=True) for block in blocks])
    squares = tree_sum([jnp.sum(block * block, 0, keepdims=True) for block in blocks])
    mean = total / batch
    scale = lax.rsqrt(squares / batch - mean * mean + bn_eps)
    scale_ref[...] = scale
    rows, few = batch // n, batch // (n * n)
    for i, block in enumerate(blocks):
        normed = (block - mean) * scale
        for first in range(0, height, few):
            step, plane = divmod((i * height + first) // few, n)
            at = pl.multiple_of(plane * rows + (place_ref[1] ^ order[step]) * few, few)
            norm_ref[pl.ds(at, few), :] = normed[first : first + few]
            packed_ref[pl.ds(at, few), :] = normed[first : first + few].astype(BF16)
    dims = (((1,), (1,)), ((), ()))
    packed = packed_ref[...]
    size = batch // k
    for i in range(k):
        at = pl.multiple_of((place_ref[2] ^ i) * size, size)
        gram = lax.dot_general(packed_ref[pl.ds(at, size), :], packed, dims, preferred_element_type=F32)
        grams[i][...] = gram
    if second:
        coeff_ref = refs[3 + k]
        diag = jnp.sum(norm_ref[...] * other_ref[...], 0, keepdims=True) / batch
        coeff_ref[...] = 2.0 * ((1.0 - off_weight) * diag - 1.0)
        share = jnp.sum((1.0 - diag) ** 2 - off_weight * diag * diag, 1, keepdims=True)
        for i in range(k):

            @pl.when((place_ref[2] ^ i) == k - 1)
            def _():
                at = batch // BLOCKS
                row = grams[i][size - 8 :, at : at + 128]
                first = (lax.broadcasted_iota(jnp.int32, row.shape, 0) == 7) & (
                    lax.broadcasted_iota(jnp.int32, row.shape, 1) == 0
                )
                grams[i][size - 8 :, at : at + 128] = jnp.where(first, share, row)


def normalize_parts(place, place_array, own, parts, order, other=None):
    n, k = place.n, place.k
    batch, columns = own.shape
    second = other is not None
    out_shape = [
        jax.ShapeDtypeStruct((batch, columns), F32),
        jax.ShapeDtypeStruct((batch, columns), BF16),
        jax.ShapeDtypeStruct((1, columns), F32),
    ] + [jax.ShapeDtypeStruct((batch // k, batch), F32)] * k
    if second:
        out_shape.append(jax.ShapeDtypeStruct((1, columns), F32))
    args = [own, *parts[::-1]] + ([other] if second else [])
    space = pl.BlockSpec(memory_space=pltpu.VMEM)
    return pl.pallas_call(
        functools.partial(normalize_kernel, n=n, k=k, order=order, second=second),
        in_specs=[pl.BlockSpec(memory_space=pltpu.SMEM)] + [space] * len(args),
        out_specs=[space] * len(out_shape),
        out_shape=out_shape,
        compiler_params=pltpu.CompilerParams(vmem_limit_bytes=VMEM_BYTES // 2),
        cost_estimate=pl.CostEstimate(
            flops=2 * batch * batch * columns,
            bytes_accessed=16 * batch * columns + 4 * batch * batch,
            transcendentals=0,
        ),
        name="normalize",
    )(place_array, *args)


def gradient_kernel(place_ref, *refs, n, k):
    grams, refs = refs[: n * k], refs[n * k :]
    packed, norms, scales, coeff_ref, refs = refs[0:2], refs[2:4], refs[4:6], refs[6], refs[7:]
    outs, loss_ref = [refs[0], *refs[n - 1 : 0 : -1]], refs[n]
    gram_ref, whole_ref = refs[n + 1 :]
    batch, columns = norms[0].shape
    height = grams[0].shape[0] // 2
    width = batch // BLOCKS
    for i in range(k):
        for step in range(n):
            block = (place_ref[2] ^ i) * n + (place_ref[1] ^ step)
            at = pl.ds(pl.multiple_of(block * height, height), height)
            block = block // (2 * n // BLOCKS)
            for j in range(KEPT):
                to = pl.ds(pl.multiple_of(lax.rem(block + j, BLOCKS) * width, width), width)
                for view in range(2):
                    gram_ref[view, at, to] = grams[i * n + step][
                        view * height : (view + 1) * height, j * width : (j + 1) * width
                    ]
    blocks = [slice(i * width, (i + 1) * width) for i in range(BLOCKS)]
    for view in range(2):
        for i in range(BLOCKS):
            other = gram_ref[view, blocks[i - 1], blocks[i]].astype(F32).T
            gram_ref[view, blocks[i], blocks[i - 1]] = other.astype(BF16)
    tail = gram_ref[1, blocks[3], blocks[1]].astype(F32)
    row = lax.broadcasted_iota(jnp.int32, tail.shape, 0)
    column = lax.broadcasted_iota(jnp.int32, tail.shape, 1)
    taken = (row == width - 1) & (column < 3)
    mirror = gram_ref[1, blocks[1], blocks[3]].astype(F32).T
    share = jnp.sum(jnp.where(taken, tail, 0.0), keepdims=True)
    gram_ref[1, blocks[3], blocks[1]] = jnp.where(taken, mirror, tail).astype(BF16)
    factor = 2.0 * off_weight / batch
    rows = batch // n
    for view in (1, 0):
        norm = norms[view][...]
        grad = (
            factor * jnp.dot(gram_ref[1 - view], packed[view][...], preferred_element_type=F32)
            + coeff_ref[...] * norms[1 - view][...]
        )
        first = jnp.sum(grad, 0, keepdims=True) / batch
        second = jnp.sum(grad * norm, 0, keepdims=True) / batch
        whole_ref[view] = (scales[view][...] * (grad - first - norm * second)).astype(BF16)
        for step in range(n):
            at = pl.multiple_of((place_ref[0] ^ step) * rows, rows)
            outs[step][view * rows : (view + 1) * rows, :] = whole_ref[view, pl.ds(at, rows), :]
    frob = jnp.sum(gram_ref[0].astype(F32) * gram_ref[1].astype(F32), keepdims=True)
    loss_ref[...] = (share + off_weight * (frob / (batch * batch))) / D


def gradient(place, place_array, grams, packed, norms, scales, coeff):
    batch, columns = norms[0].shape
    return local(
        functools.partial(gradient_kernel, n=place.n, k=place.k),
        place_array,
        (*grams, *packed, *norms, *scales, coeff),
        [((2 * batch // place.n, columns), BF16)] * place.n + [((1, 1), F32)],
        "gradient",
        scratch_shapes=[
            pltpu.VMEM((2, batch, batch), BF16),
            pltpu.VMEM((2, batch, columns), BF16),
        ],
    )


def place_kernel(place_ref, *refs, n):
    parts, outs = [refs[0], *refs[n - 1 : 0 : -1]], refs[n:]
    rows, columns = parts[0].shape[0] // len(outs), parts[0].shape[1]
    for step in range(n):
        at = pl.ds(pl.multiple_of((place_ref[0] ^ step) * columns, columns), columns)
        for i, out in enumerate(outs):
            out[:, at] = parts[step][i * rows : (i + 1) * rows, :]


def with_kernels(place, h_first, h_second, weight):
    n, k, z, a, b = place.n, place.k, place.z, place.a, place.b
    place_array = jnp.stack([z, a, b]).astype(jnp.int32)
    first = to_columns(place, h_first)
    first, second = lax.optimization_barrier((to_planes(place, first), to_columns(place, h_second)))
    first, late_weight = lax.optimization_barrier((lay(place, place_array, first), weight))
    met_1, second, held = lax.optimization_barrier(
        (met_rows(place, first), to_planes(place, second), fetch(late_weight))
    )

    def sent(parts):
        return sends(place, "z", [parts[0], *parts])[1:]

    def swapped(part):
        return place.send(part, lambda z, a, b: (z, a, b ^ 1))

    own_1, parts_1 = project(place, place_array, [met_1, [swapped(part) for part in met_1]], held)
    second = lay(place, place_array, second)
    size, here, toward = place.along("a")
    order_2 = [0, size - 1, *range(1, size - 1)]
    last = place.send(second, toward(size - 1))
    own_1, parts_1, late_weight = lax.optimization_barrier((own_1, parts_1, weight))
    parts_1 = sent(parts_1)

    def second_projected(weight, values, last):
        met = [place.send(values, toward(step)) for step in range(1, size - 1)]
        values, met[0] = lax.optimization_barrier((values, met[0]))
        early = swapped(jnp.concatenate([values, last], 0))
        late = swapped(jnp.concatenate(met, 0))
        return project(place, place_array, [[values, last, *met], [early, late]], fetch(weight))

    own_2, parts_2 = in_one(place, second_projected, (late_weight, second, last))
    own_1, own_2 = lax.optimization_barrier((own_1, own_2))
    parts_2 = sent(parts_2)
    norm_1, packed_1, scale_1, *grams = normalize_parts(
        place, place_array, own_1, parts_1, [*range(n)]
    )
    met_1 = in_one(place, lambda *grams: first_rows(place, place_array, grams), grams)
    met_1 = sends(place, "z", met_1)
    own_2, parts_2, met_1 = lax.optimization_barrier((own_2, parts_2, met_1))
    norm_2, packed_2, scale_2, *grams, coeff = normalize_parts(
        place, place_array, own_2, parts_2, order_2, norm_1
    )
    height, batch = met_1[0].shape
    (rows_1,) = local(rows_kernel, place_array, met_1, [((height, batch), BF16)], "rows")
    met_2 = plane_rows(place, place_array, grams)
    rows = met_2[0].shape[0]
    (part,) = local(
        functools.partial(code_kernel, n=n),
        place_array,
        (*met_2, rows_1),
        [((rows + SCALE_ROWS + height, batch), BF16)],
        "code",
    )
    (part,) = local(
        functools.partial(finish_kernel, n=n, k=k),
        place_array,
        sends(place, "z", [part] * n),
        [((2 * rows, batch), BF16)],
        "finish",
    )
    grams = sends(place, "a", [part] * n)
    grams += [place.send(part, lambda z, a, b: (z, a, b ^ 1)) for part in grams]
    first, *others, loss = gradient(
        place,
        place_array,
        grams,
        (packed_1, packed_2),
        (norm_1, norm_2),
        (scale_1, scale_2),
        coeff,
    )
    out_1, out_2 = local(
        functools.partial(place_kernel, n=n),
        place_array,
        [first, *sends(place, "z", [first, *others[::-1]])[:0:-1]],
        [(h_first.shape, BF16)] * 2,
        "place",
    )
    return (out_1, out_2, loss.reshape(()))


def plain(place, h_first, h_second, weight):
    n, k, z, a, b = place.n, place.k, place.z, place.a, place.b
    rows, width = h_first.shape
    batch = rows * n
    columns = weight.shape[1] // n
    weight_parts = weight.reshape(k, width, n * columns)
    zs = []
    for values in (h_first, h_second):
        moved = place.send(values, lambda z, a, b: (a, z, b))
        own = jnp.concatenate(met_rows(place, moved), 0)
        total = jnp.dot(own, pick(weight_parts, b), preferred_element_type=F32)
        for step in range(1, k):
            other = place.send(own, lambda z, a, b, s=step: (z, a, b ^ s))
            total += jnp.dot(other, pick(weight_parts, b ^ step), preferred_element_type=F32)
        cut = total.reshape(batch, n, columns).transpose(1, 0, 2)
        whole = tree_sum(exchange(place, "z", cut)).reshape(n, rows, columns)
        zs.append(jnp.concatenate(ordered([whole[i] for i in range(n)], a), 0))
    normed, scales = [], []
    for values in zs:
        mean = jnp.sum(values, 0) / batch
        scale = lax.rsqrt(jnp.sum(values * values, 0) / batch - mean * mean + bn_eps)
        normed.append((values - mean) * scale)
        scales.append(scale)
    diag = jnp.sum(normed[0] * normed[1], 0) / batch
    packed = [values.astype(BF16) for values in normed]
    dims = (((1,), (1,)), ((), ()))
    grams = []
    for values in packed:
        gram = lax.dot_general(values, values, dims, preferred_element_type=F32)
        grams.append(plain_gram(place, gram))
    frob = jnp.sum(grams[0].astype(F32) * grams[1].astype(F32)) / (batch * batch)
    coeff = 2.0 * ((1.0 - off_weight) * diag - 1.0)
    factor = 2.0 * off_weight / batch
    outs = []
    for view in range(2):
        grad = (
            factor * jnp.dot(grams[1 - view], packed[view], preferred_element_type=F32)
            + coeff * normed[1 - view]
        )
        first = jnp.sum(grad, 0) / batch
        second = jnp.sum(grad * normed[view], 0) / batch
        out = (scales[view] * (grad - first - normed[view] * second)).astype(BF16)
        parts = exchange(place, "z", out.reshape(n, rows, columns))
        outs.append(jnp.concatenate(ordered(parts, z), 1))
    share = jnp.sum((1.0 - diag) ** 2) - off_weight * jnp.sum(diag * diag)
    loss = (lax.psum(share, ("dp", "mp")) + off_weight * frob) / D
    return (outs[0], outs[1], loss)


def per_device(h_first, h_second, weight):
    place = Place()
    columns = weight.shape[1] // place.n
    fits = columns % 128 == 0 and place.n == 4 and place.k == 2
    return (with_kernels if fits else plain)(place, h_first, h_second, weight)


def solution(mesh):
    in_specs = (P("dp", "mp"), P("dp", "mp"), P("dp", "mp"))
    out_specs = (P("dp", "mp"), P("dp", "mp"), P())
    return jax.shard_map(
        per_device, mesh=mesh, in_specs=in_specs, out_specs=out_specs, check_vma=False
    )
```

```python
import functools

import jax
import jax.numpy as jnp
from jax import lax
from jax.experimental import pallas as pl
from jax.experimental.pallas import tpu as pltpu
from jax.sharding import PartitionSpec as P

D = 8192


off_weight = 0.0051
bn_eps = 1e-05

F32 = jnp.float32
BF16 = jnp.bfloat16
VMEM_BYTES = 16 * 1024 * 1024
POWERS = 240
HIGHEST = 128 * POWERS - 1
SCALE_ROWS = 16


class Place:
    def __init__(self):
        self.n = lax.axis_size("dp")
        self.k = lax.axis_size("mp") // self.n
        self.z = lax.axis_index("dp")
        self.a = lax.axis_index("mp") // self.k
        self.b = lax.axis_index("mp") % self.k

    def send(self, value, target):
        n, k = self.n, self.k
        pairs = []
        for z in range(n):
            for a in range(n):
                for b in range(k):
                    to_z, to_a, to_b = target(z, a, b)
                    pairs.append(((z * n + a) * k + b, (to_z * n + to_a) * k + to_b))
        return lax.ppermute(value, ("dp", "mp"), pairs)

    def along(self, axis):
        if axis == "z":
            return self.n, self.z, lambda step: lambda z, a, b: (z ^ step, a, b)
        if axis == "a":
            return self.n, self.a, lambda step: lambda z, a, b: (z, a ^ step, b)
        return self.k, self.b, lambda step: lambda z, a, b: (z, a, b ^ step)


def ordered(parts, place):
    bit = 1
    while bit < len(parts):
        odd = (place & bit) != 0
        parts = [jnp.where(odd, parts[i ^ bit], parts[i]) for i in range(len(parts))]
        bit *= 2
    return parts


def tree_sum(parts):
    while len(parts) > 1:
        parts = [parts[i] + parts[i + 1] for i in range(0, len(parts), 2)]
    return parts[0]


def pick(value, index):
    return lax.dynamic_index_in_dim(value, index, 0, keepdims=False)


def exchange(place, axis, value, few=False):
    size, here, toward = place.along(axis)
    return sends(place, axis, [pick(value, here ^ step) for step in range(size)], few)


def sends(place, axis, parts, few=False):
    size, here, toward = place.along(axis)
    met = {0: parts[0]}
    order = [*range(1, size)] if few else [*range(size - 1, 0, -1)]
    for i, step in enumerate(order):
        part = parts[step]
        if few and i >= 2:
            met[order[i - 2]], part = lax.optimization_barrier((met[order[i - 2]], part))
        met[step] = place.send(part, toward(step))
    return [met[step] for step in range(size)]


def reduce_scatter(place, axis, value, few=False):
    size, here, toward = place.along(axis)
    value = value.reshape((size, value.shape[0] // size) + value.shape[1:])
    return tree_sum(exchange(place, axis, value, few))


def gather(place, axis, value, few=False):
    size, here, toward = place.along(axis)
    parts = sends(place, axis, [value] * size, few)
    return jnp.concatenate(ordered(parts, here), 0)


BLOCKS = 4
KEPT = 3


def halve_kernel(place_ref, kept_ref, met_ref, *outs, n):
    height = kept_ref.shape[0] // n
    width = kept_ref.shape[1] // BLOCKS
    for step, out in enumerate(outs):
        block = place_ref[1] ^ step
        at = pl.ds(pl.multiple_of(block * height, height), height)
        block = (place_ref[2] * n + block) // (2 * n // BLOCKS)
        total = []
        for i in range(KEPT):
            cut = pl.ds(pl.multiple_of(lax.rem(block + i, BLOCKS) * width, width), width)
            total.append(kept_ref[at, cut] + met_ref[at, cut])
        total = jnp.concatenate(total, 1)
        if step == 0:
            out[...] = total
        else:
            encode(total, out)


def plane_sum(met):
    return tree_sum([met[0][...]] + [decode(ref, 1)[0] for ref in met[1:]])


def plane_kernel(place_ref, *refs, n):
    met, outs, whole_ref = refs[:n], refs[n:-1], refs[-1]
    whole_ref[...] = plane_sum(met)
    height = outs[0].shape[0]
    for step, out in enumerate(outs):
        at = pl.ds(pl.multiple_of((place_ref[0] ^ step) * height, height), height)
        out[...] = whole_ref[at, :]


def rows_kernel(place_ref, *refs):
    refs[-1][...] = tree_sum([ref[...] for ref in refs[:-1]]).astype(BF16)


def code_kernel(place_ref, *refs, n):
    met, rows_ref, out_ref = refs[:n], refs[n], refs[n + 1]
    total = plane_sum(met)
    coded = total.shape[0] + SCALE_ROWS
    encode(total, out_ref.at[:coded])
    out_ref[coded:] = rows_ref[...]


def finish_kernel(place_ref, *refs, n, k):
    out_ref = refs[-1]
    height = out_ref.shape[0] // 2
    coded, few = height + SCALE_ROWS, height // n
    met = []
    for step in range(n):
        at = pl.ds(pl.multiple_of((place_ref[0] ^ step) * few, few), few)
        out_ref[at, :] = refs[step][coded:]
        met += decode(refs[step].at[:coded], 1)
    total = tree_sum(met)
    last = (place_ref[1] == n - 1) & (place_ref[2] == k - 1)
    start = 2 * (total.shape[1] // KEPT)
    edge = total[-8:, start:]
    row = lax.broadcasted_iota(jnp.int32, edge.shape, 0)
    column = lax.broadcasted_iota(jnp.int32, edge.shape, 1)
    taken = (row == 7) & last
    whole = jnp.sum(jnp.where(taken & (column == 0), edge, 0.0), keepdims=True)
    high = whole.astype(BF16).astype(F32)
    middle = (whole - high).astype(BF16).astype(F32)
    three = jnp.where(column == 0, high, jnp.where(column == 1, middle, whole - high - middle))
    edge = jnp.where(taken & (column < 3), three, edge)
    edge = jnp.concatenate([total[-8:, :start], edge], 1)
    out_ref[height:] = jnp.concatenate([total[:-8], edge], 0).astype(BF16)


def local(kernel, place_array, args, shapes, name, **more):
    space = pl.BlockSpec(memory_space=pltpu.VMEM)
    return pl.pallas_call(
        kernel,
        in_specs=[pl.BlockSpec(memory_space=pltpu.SMEM)] + [space] * len(args),
        out_specs=[space] * len(shapes),
        out_shape=[jax.ShapeDtypeStruct(shape, dtype) for shape, dtype in shapes],
        compiler_params=pltpu.CompilerParams(vmem_limit_bytes=VMEM_BYTES // 2),
        name=name,
        **more,
    )(place_array, *args)


def plane_rows(place, place_array, grams, few=False):
    half, batch = grams[0].shape
    kept, other = grams
    other = place.send(other, lambda z, a, b: (z, a, b ^ 1))
    height, batch = half // place.n, batch * KEPT // BLOCKS
    parts = local(
        functools.partial(halve_kernel, n=place.n),
        place_array,
        (kept, other),
        [((height, batch), F32)] + [((height + SCALE_ROWS, batch), BF16)] * (place.n - 1),
        "halve",
    )
    return sends(place, "a", parts, few)


def first_rows(place, place_array, grams):
    parts = plane_rows(place, place_array, grams, True)
    height, batch = parts[0].shape
    return local(
        functools.partial(plane_kernel, n=place.n),
        place_array,
        parts,
        [((height // place.n, batch), F32)] * place.n,
        "plane",
        scratch_shapes=[pltpu.VMEM((height, batch), F32)],
    )


def in_one(place, run, args):
    shapes = jax.eval_shape(run, *args)
    return lax.cond(
        place.z < place.n,
        run,
        lambda *args: jax.tree.map(lambda leaf: jnp.zeros(leaf.shape, leaf.dtype), shapes),
        *args,
    )


def plain_gram(place, part):
    for axis in ("b", "a", "z"):
        part = reduce_scatter(place, axis, part)
    part = part.astype(BF16)
    for axis in ("z", "a", "b"):
        part = gather(place, axis, part)
    return part


def lay_kernel(place_ref, *refs, n):
    parts, outs = refs[:n], refs[n:]
    few = parts[0].shape[0] // len(outs)
    for step in range(n):
        at = pl.ds(pl.multiple_of((place_ref[0] ^ step) * few, few), few)
        for i, out in enumerate(outs):
            out[at, :] = parts[step][i * few : (i + 1) * few, :]


def fetch_kernel(weight_ref, held_ref, arrived):
    copy = pltpu.make_async_copy(weight_ref, held_ref, arrived)
    copy.start()
    copy.wait()


def fetch(weight):
    return pl.pallas_call(
        fetch_kernel,
        in_specs=[pl.BlockSpec(memory_space=pl.ANY)],
        out_specs=pl.BlockSpec(memory_space=pltpu.VMEM),
        out_shape=pltpu.VMEM(weight.shape, BF16),
        scratch_shapes=[pltpu.SemaphoreType.DMA],
        compiler_params=pltpu.CompilerParams(vmem_limit_bytes=VMEM_BYTES // 2),
        cost_estimate=pl.CostEstimate(flops=0, bytes_accessed=4 * weight.size, transcendentals=0),
        name="fetch",
    )(pltpu.with_memory_space_constraint(weight, pltpu.HBM))


def to_columns(place, view):
    rows, width = view.shape
    return exchange(place, "a", view.reshape(place.n, rows // place.n, width))


def to_planes(place, parts):
    return sends(place, "z", ordered(parts, place.a ^ place.z))


def lay(place, place_array, parts):
    rows, width = parts[0].shape
    (laid,) = local(
        functools.partial(lay_kernel, n=place.n),
        place_array,
        parts,
        [((rows * place.n, width), BF16)],
        "lay",
    )
    return laid


def met_rows(place, values, few=False):
    return sends(place, "a", [values] * place.n, few)


def project_kernel(place_ref, *refs, counts, n, k):
    met = refs[: sum(counts)]
    weight_ref, own_ref, *coded = refs[sum(counts) :]
    width = met[0].shape[1]
    columns = own_ref.shape[1]
    values = []
    for count in counts:
        values.append(jnp.concatenate([ref[...] for ref in met[:count]], 0))
        met = met[count:]
    for step in [*range(n - 1, 0, -1), 0]:
        at = pl.ds(pl.multiple_of((place_ref[0] ^ step) * columns, columns), columns)
        total = 0.0
        for i in range(k):
            rows = pl.ds(pl.multiple_of((place_ref[2] ^ i) * width, width), width)
            total += jnp.dot(values[i], weight_ref[rows, at], preferred_element_type=F32)
        if step == 0:
            own_ref[...] = total
        else:
            encode(total, coded[n - 1 - step])


def encode(total, coded_ref):
    rows = total.shape[0]
    top = jnp.max(jnp.abs(total), 0, keepdims=True)
    top = jnp.maximum(top * (1.0 + 1.0 / 128.0), 1e-30).astype(BF16)
    coded_ref[rows:] = jnp.broadcast_to(top, (SCALE_ROWS, total.shape[1]))
    whole = jnp.floor(jnp.abs(total) * (HIGHEST / top.astype(F32)) + 0.5)
    power = jnp.floor(whole * (1.0 / 128.0))
    word = (1.0 + (whole * (1.0 / 128.0) - power)) * jnp.exp2(power - POWERS // 2)
    coded_ref[:rows] = jnp.where(total < 0.0, -word, word).astype(BF16)


def decode(coded_ref, count):
    rows = coded_ref.shape[0] - SCALE_ROWS
    scale = coded_ref[rows:].astype(F32)[:1] * (1.0 / HIGHEST)
    height = rows // count
    blocks = []
    for i in range(count):
        word = coded_ref[i * height : (i + 1) * height].astype(F32)
        size = jnp.abs(word)
        power = jnp.floor(jnp.log(size) * 1.4426950408889634 + 0.002)
        part = jnp.floor(size * jnp.exp2(-power) * 128.0 + 0.5)
        whole = (power + (POWERS // 2 - 1)) * 128.0 + part
        blocks.append(jnp.where(word < 0.0, -whole, whole) * scale)
    return blocks


def project(place, place_array, met, held):
    n, k = place.n, place.k
    rows, width = met[0][0].shape
    batch, columns = rows * n, held.shape[1] // n
    counts = [len(parts) for parts in met]
    met = [part for parts in met for part in parts]
    coded = batch + SCALE_ROWS
    out_shape = [jax.ShapeDtypeStruct((batch, columns), F32)]
    out_shape += [jax.ShapeDtypeStruct((coded, columns), BF16)] * (n - 1)
    space = pl.BlockSpec(memory_space=pltpu.VMEM)
    own, *parts = pl.pallas_call(
        functools.partial(project_kernel, counts=counts, n=n, k=k),
        in_specs=[pl.BlockSpec(memory_space=pltpu.SMEM)]
        + [space] * (len(met) + 1),
        out_specs=[space] * n,
        out_shape=out_shape,
        compiler_params=pltpu.CompilerParams(vmem_limit_bytes=VMEM_BYTES),
        cost_estimate=pl.CostEstimate(
            flops=2 * batch * k * width * n * columns,
            bytes_accessed=2 * k * width * (batch + n * columns) + 3 * n * batch * columns,
            transcendentals=0,
        ),
        name="project",
    )(place_array, *met, pltpu.with_memory_space_constraint(held, pltpu.VMEM))
    return own, parts[::-1]


def normalize_kernel(place_ref, *refs, n, k, order, second):
    own_ref, parts = refs[0], refs[n - 1 : 0 : -1]
    refs = refs[n:]
    if second:
        other_ref, refs = refs[0], refs[1:]
    norm_ref, packed_ref, scale_ref = refs[:3]
    grams = refs[3 : 3 + k]
    batch, columns = own_ref.shape
    height = batch // n
    met = [[own_ref[i * height : (i + 1) * height] for i in range(n)]]
    for step in range(1, n):
        met.append(decode(parts[step - 1], n))
    blocks = [tree_sum([met[step][i] for step in range(n)]) for i in range(n)]
    total = tree_sum([jnp.sum(block, 0, keepdims=True) for block in blocks])
    squares = tree_sum([jnp.sum(block * block, 0, keepdims=True) for block in blocks])
    mean = total / batch
    scale = lax.rsqrt(squares / batch - mean * mean + bn_eps)
    scale_ref[...] = scale
    rows, few = batch // n, batch // (n * n)
    for i, block in enumerate(blocks):
        normed = (block - mean) * scale
        for first in range(0, height, few):
            step, plane = divmod((i * height + first) // few, n)
            at = pl.multiple_of(plane * rows + (place_ref[1] ^ order[step]) * few, few)
            norm_ref[pl.ds(at, few), :] = normed[first : first + few]
            packed_ref[pl.ds(at, few), :] = normed[first : first + few].astype(BF16)
    dims = (((1,), (1,)), ((), ()))
    packed = packed_ref[...]
    size = batch // k
    for i in range(k):
        at = pl.multiple_of((place_ref[2] ^ i) * size, size)
        gram = lax.dot_general(packed_ref[pl.ds(at, size), :], packed, dims, preferred_element_type=F32)
        grams[i][...] = gram
    if second:
        coeff_ref = refs[3 + k]
        diag = jnp.sum(norm_ref[...] * other_ref[...], 0, keepdims=True) / batch
        coeff_ref[...] = 2.0 * ((1.0 - off_weight) * diag - 1.0)
        share = jnp.sum((1.0 - diag) ** 2 - off_weight * diag * diag, 1, keepdims=True)
        for i in range(k):

            @pl.when((place_ref[2] ^ i) == k - 1)
            def _():
                at = batch // BLOCKS
                row = grams[i][size - 8 :, at : at + 128]
                first = (lax.broadcasted_iota(jnp.int32, row.shape, 0) == 7) & (
                    lax.broadcasted_iota(jnp.int32, row.shape, 1) == 0
                )
                grams[i][size - 8 :, at : at + 128] = jnp.where(first, share, row)


def normalize_parts(place, place_array, own, parts, order, other=None):
    n, k = place.n, place.k
    batch, columns = own.shape
    second = other is not None
    out_shape = [
        jax.ShapeDtypeStruct((batch, columns), F32),
        jax.ShapeDtypeStruct((batch, columns), BF16),
        jax.ShapeDtypeStruct((1, columns), F32),
    ] + [jax.ShapeDtypeStruct((batch // k, batch), F32)] * k
    if second:
        out_shape.append(jax.ShapeDtypeStruct((1, columns), F32))
    args = [own, *parts[::-1]] + ([other] if second else [])
    space = pl.BlockSpec(memory_space=pltpu.VMEM)
    return pl.pallas_call(
        functools.partial(normalize_kernel, n=n, k=k, order=order, second=second),
        in_specs=[pl.BlockSpec(memory_space=pltpu.SMEM)] + [space] * len(args),
        out_specs=[space] * len(out_shape),
        out_shape=out_shape,
        compiler_params=pltpu.CompilerParams(vmem_limit_bytes=VMEM_BYTES // 2),
        cost_estimate=pl.CostEstimate(
            flops=2 * batch * batch * columns,
            bytes_accessed=16 * batch * columns + 4 * batch * batch,
            transcendentals=0,
        ),
        name="normalize",
    )(place_array, *args)


def gradient_kernel(place_ref, *refs, n, k):
    grams, refs = refs[: n * k], refs[n * k :]
    packed, norms, scales, coeff_ref, refs = refs[0:2], refs[2:4], refs[4:6], refs[6], refs[7:]
    outs, loss_ref = [refs[0], *refs[n - 1 : 0 : -1]], refs[n]
    gram_ref, whole_ref = refs[n + 1 :]
    batch, columns = norms[0].shape
    height = grams[0].shape[0] // 2
    width = batch // BLOCKS
    for i in range(k):
        for step in range(n):
            block = (place_ref[2] ^ i) * n + (place_ref[1] ^ step)
            at = pl.ds(pl.multiple_of(block * height, height), height)
            block = block // (2 * n // BLOCKS)
            for j in range(KEPT):
                to = pl.ds(pl.multiple_of(lax.rem(block + j, BLOCKS) * width, width), width)
                for view in range(2):
                    gram_ref[view, at, to] = grams[i * n + step][
                        view * height : (view + 1) * height, j * width : (j + 1) * width
                    ]
    blocks = [slice(i * width, (i + 1) * width) for i in range(BLOCKS)]
    for view in range(2):
        for i in range(BLOCKS):
            other = gram_ref[view, blocks[i - 1], blocks[i]].astype(F32).T
            gram_ref[view, blocks[i], blocks[i - 1]] = other.astype(BF16)
    tail = gram_ref[1, blocks[3], blocks[1]].astype(F32)
    row = lax.broadcasted_iota(jnp.int32, tail.shape, 0)
    column = lax.broadcasted_iota(jnp.int32, tail.shape, 1)
    taken = (row == width - 1) & (column < 3)
    mirror = gram_ref[1, blocks[1], blocks[3]].astype(F32).T
    share = jnp.sum(jnp.where(taken, tail, 0.0), keepdims=True)
    gram_ref[1, blocks[3], blocks[1]] = jnp.where(taken, mirror, tail).astype(BF16)
    factor = 2.0 * off_weight / batch
    rows = batch // n
    for view in (1, 0):
        norm = norms[view][...]
        grad = (
            factor * jnp.dot(gram_ref[1 - view], packed[view][...], preferred_element_type=F32)
            + coeff_ref[...] * norms[1 - view][...]
        )
        first = jnp.sum(grad, 0, keepdims=True) / batch
        second = jnp.sum(grad * norm, 0, keepdims=True) / batch
        whole_ref[view] = (scales[view][...] * (grad - first - norm * second)).astype(BF16)
        for step in range(n):
            at = pl.multiple_of((place_ref[0] ^ step) * rows, rows)
            outs[step][view * rows : (view + 1) * rows, :] = whole_ref[view, pl.ds(at, rows), :]
    frob = jnp.sum(gram_ref[0].astype(F32) * gram_ref[1].astype(F32), keepdims=True)
    loss_ref[...] = (share + off_weight * (frob / (batch * batch))) / D


def gradient(place, place_array, grams, packed, norms, scales, coeff):
    batch, columns = norms[0].shape
    return local(
        functools.partial(gradient_kernel, n=place.n, k=place.k),
        place_array,
        (*grams, *packed, *norms, *scales, coeff),
        [((2 * batch // place.n, columns), BF16)] * place.n + [((1, 1), F32)],
        "gradient",
        scratch_shapes=[
            pltpu.VMEM((2, batch, batch), BF16),
            pltpu.VMEM((2, batch, columns), BF16),
        ],
    )


def place_kernel(place_ref, *refs, n):
    parts, outs = [refs[0], *refs[n - 1 : 0 : -1]], refs[n:]
    rows, columns = parts[0].shape[0] // len(outs), parts[0].shape[1]
    for step in range(n):
        at = pl.ds(pl.multiple_of((place_ref[0] ^ step) * columns, columns), columns)
        for i, out in enumerate(outs):
            out[:, at] = parts[step][i * rows : (i + 1) * rows, :]


def with_kernels(place, h_first, h_second, weight):
    n, k, z, a, b = place.n, place.k, place.z, place.a, place.b
    place_array = jnp.stack([z, a, b]).astype(jnp.int32)
    size, here, toward = place.along("a")
    first, second = lax.optimization_barrier((to_columns(place, h_first), h_second))
    first, second = to_planes(place, first), to_columns(place, second)
    first, late_weight = lax.optimization_barrier((lay(place, place_array, first), weight))
    met_1, second = met_rows(place, first), to_planes(place, second)
    met_1, second, held = lax.optimization_barrier((met_1, second, fetch(late_weight)))

    def sent(parts):
        return sends(place, "z", [parts[0], *parts])[1:]

    def swapped(part):
        return place.send(part, lambda z, a, b: (z, a, b ^ 1))

    others_1 = [swapped(part) for part in met_1]
    own_1, parts_1 = project(place, place_array, [met_1, others_1], held)
    own_1, parts_1, late_weight = lax.optimization_barrier((own_1, parts_1, weight))
    parts_1 = sent(parts_1)
    order_2 = [0, size - 1, *range(1, size - 1)]

    def second_projected(weight, *parts):
        values = lay(place, place_array, parts)
        last, met = [place.send(values, toward(step)) for step in (size - 1, 1)]
        again, met = lax.optimization_barrier((values, met))
        met = [met] + [place.send(again, toward(step)) for step in range(2, size - 1)]
        early = swapped(jnp.concatenate([values, last], 0))
        late = swapped(jnp.concatenate(met, 0))
        return project(place, place_array, [[values, last, *met], [early, late]], fetch(weight))

    own_2, parts_2 = in_one(place, second_projected, (late_weight, *second))
    own_1, own_2 = lax.optimization_barrier((own_1, own_2))
    parts_2 = sent(parts_2)
    norm_1, packed_1, scale_1, *grams = normalize_parts(
        place, place_array, own_1, parts_1, [*range(n)]
    )
    met_1 = in_one(place, lambda *grams: first_rows(place, place_array, grams), grams)
    met_1 = sends(place, "z", met_1)
    own_2, parts_2, met_1 = lax.optimization_barrier((own_2, parts_2, met_1))
    norm_2, packed_2, scale_2, *grams, coeff = normalize_parts(
        place, place_array, own_2, parts_2, order_2, norm_1
    )
    height, batch = met_1[0].shape
    (rows_1,) = local(rows_kernel, place_array, met_1, [((height, batch), BF16)], "rows")
    met_2 = plane_rows(place, place_array, grams)
    rows = met_2[0].shape[0]
    (part,) = local(
        functools.partial(code_kernel, n=n),
        place_array,
        (*met_2, rows_1),
        [((rows + SCALE_ROWS + height, batch), BF16)],
        "code",
    )
    (part,) = local(
        functools.partial(finish_kernel, n=n, k=k),
        place_array,
        sends(place, "z", [part] * n),
        [((2 * rows, batch), BF16)],
        "finish",
    )
    grams = sends(place, "a", [part] * n)
    grams += [place.send(part, lambda z, a, b: (z, a, b ^ 1)) for part in grams]
    first, *others, loss = gradient(
        place,
        place_array,
        grams,
        (packed_1, packed_2),
        (norm_1, norm_2),
        (scale_1, scale_2),
        coeff,
    )
    out_1, out_2 = local(
        functools.partial(place_kernel, n=n),
        place_array,
        [first, *sends(place, "z", [first, *others[::-1]])[:0:-1]],
        [(h_first.shape, BF16)] * 2,
        "place",
    )
    return (out_1, out_2, loss.reshape(()))


def plain(place, h_first, h_second, weight):
    n, k, z, a, b = place.n, place.k, place.z, place.a, place.b
    rows, width = h_first.shape
    batch = rows * n
    columns = weight.shape[1] // n
    weight_parts = weight.reshape(k, width, n * columns)
    zs = []
    for values in (h_first, h_second):
        moved = place.send(values, lambda z, a, b: (a, z, b))
        own = jnp.concatenate(met_rows(place, moved), 0)
        total = jnp.dot(own, pick(weight_parts, b), preferred_element_type=F32)
        for step in range(1, k):
            other = place.send(own, lambda z, a, b, s=step: (z, a, b ^ s))
            total += jnp.dot(other, pick(weight_parts, b ^ step), preferred_element_type=F32)
        cut = total.reshape(batch, n, columns).transpose(1, 0, 2)
        whole = tree_sum(exchange(place, "z", cut)).reshape(n, rows, columns)
        zs.append(jnp.concatenate(ordered([whole[i] for i in range(n)], a), 0))
    normed, scales = [], []
    for values in zs:
        mean = jnp.sum(values, 0) / batch
        scale = lax.rsqrt(jnp.sum(values * values, 0) / batch - mean * mean + bn_eps)
        normed.append((values - mean) * scale)
        scales.append(scale)
    diag = jnp.sum(normed[0] * normed[1], 0) / batch
    packed = [values.astype(BF16) for values in normed]
    dims = (((1,), (1,)), ((), ()))
    grams = []
    for values in packed:
        gram = lax.dot_general(values, values, dims, preferred_element_type=F32)
        grams.append(plain_gram(place, gram))
    frob = jnp.sum(grams[0].astype(F32) * grams[1].astype(F32)) / (batch * batch)
    coeff = 2.0 * ((1.0 - off_weight) * diag - 1.0)
    factor = 2.0 * off_weight / batch
    outs = []
    for view in range(2):
        grad = (
            factor * jnp.dot(grams[1 - view], packed[view], preferred_element_type=F32)
            + coeff * normed[1 - view]
        )
        first = jnp.sum(grad, 0) / batch
        second = jnp.sum(grad * normed[view], 0) / batch
        out = (scales[view] * (grad - first - normed[view] * second)).astype(BF16)
        parts = exchange(place, "z", out.reshape(n, rows, columns))
        outs.append(jnp.concatenate(ordered(parts, z), 1))
    share = jnp.sum((1.0 - diag) ** 2) - off_weight * jnp.sum(diag * diag)
    loss = (lax.psum(share, ("dp", "mp")) + off_weight * frob) / D
    return (outs[0], outs[1], loss)


def per_device(h_first, h_second, weight):
    place = Place()
    columns = weight.shape[1] // place.n
    fits = columns % 128 == 0 and place.n == 4 and place.k == 2
    return (with_kernels if fits else plain)(place, h_first, h_second, weight)


def solution(mesh):
    in_specs = (P("dp", "mp"), P("dp", "mp"), P("dp", "mp"))
    out_specs = (P("dp", "mp"), P("dp", "mp"), P())
    return jax.shard_map(
        per_device, mesh=mesh, in_specs=in_specs, out_specs=out_specs, check_vma=False
    )
```

```python
import functools

import jax
import jax.numpy as jnp
from jax import lax
from jax.experimental import pallas as pl
from jax.experimental.pallas import tpu as pltpu
from jax.sharding import PartitionSpec as P

D = 8192


off_weight = 0.0051
bn_eps = 1e-05

F32 = jnp.float32
BF16 = jnp.bfloat16
VMEM_BYTES = 16 * 1024 * 1024
POWERS = 240
HIGHEST = 128 * POWERS - 1
SCALE_ROWS = 16


class Place:
    def __init__(self):
        self.n = lax.axis_size("dp")
        self.k = lax.axis_size("mp") // self.n
        self.z = lax.axis_index("dp")
        self.a = lax.axis_index("mp") // self.k
        self.b = lax.axis_index("mp") % self.k

    def send(self, value, target):
        n, k = self.n, self.k
        pairs = []
        for z in range(n):
            for a in range(n):
                for b in range(k):
                    to_z, to_a, to_b = target(z, a, b)
                    pairs.append(((z * n + a) * k + b, (to_z * n + to_a) * k + to_b))
        return lax.ppermute(value, ("dp", "mp"), pairs)

    def along(self, axis):
        if axis == "z":
            return self.n, self.z, lambda step: lambda z, a, b: (z ^ step, a, b)
        if axis == "a":
            return self.n, self.a, lambda step: lambda z, a, b: (z, a ^ step, b)
        return self.k, self.b, lambda step: lambda z, a, b: (z, a, b ^ step)


def ordered(parts, place):
    bit = 1
    while bit < len(parts):
        odd = (place & bit) != 0
        parts = [jnp.where(odd, parts[i ^ bit], parts[i]) for i in range(len(parts))]
        bit *= 2
    return parts


def tree_sum(parts):
    while len(parts) > 1:
        parts = [parts[i] + parts[i + 1] for i in range(0, len(parts), 2)]
    return parts[0]


def pick(value, index):
    return lax.dynamic_index_in_dim(value, index, 0, keepdims=False)


def exchange(place, axis, value, few=False):
    size, here, toward = place.along(axis)
    return sends(place, axis, [pick(value, here ^ step) for step in range(size)], few)


def sends(place, axis, parts, few=False):
    size, here, toward = place.along(axis)
    met = {0: parts[0]}
    order = [*range(1, size)] if few else [*range(size - 1, 0, -1)]
    for i, step in enumerate(order):
        part = parts[step]
        if few and i >= 2:
            met[order[i - 2]], part = lax.optimization_barrier((met[order[i - 2]], part))
        met[step] = place.send(part, toward(step))
    return [met[step] for step in range(size)]


def reduce_scatter(place, axis, value, few=False):
    size, here, toward = place.along(axis)
    value = value.reshape((size, value.shape[0] // size) + value.shape[1:])
    return tree_sum(exchange(place, axis, value, few))


def gather(place, axis, value, few=False):
    size, here, toward = place.along(axis)
    parts = sends(place, axis, [value] * size, few)
    return jnp.concatenate(ordered(parts, here), 0)


BLOCKS = 4
KEPT = 3


def halve_kernel(place_ref, kept_ref, met_ref, *outs, n):
    height = kept_ref.shape[0] // n
    width = kept_ref.shape[1] // BLOCKS
    for step, out in enumerate(outs):
        block = place_ref[1] ^ step
        at = pl.ds(pl.multiple_of(block * height, height), height)
        block = (place_ref[2] * n + block) // (2 * n // BLOCKS)
        total = []
        for i in range(KEPT):
            cut = pl.ds(pl.multiple_of(lax.rem(block + i, BLOCKS) * width, width), width)
            total.append(kept_ref[at, cut] + met_ref[at, cut])
        total = jnp.concatenate(total, 1)
        if step == 0:
            out[...] = total
        else:
            encode(total, out)


def plane_sum(met):
    return tree_sum([met[0][...]] + [decode(ref, 1)[0] for ref in met[1:]])


def plane_kernel(place_ref, *refs, n):
    met, outs, whole_ref = refs[:n], refs[n:-1], refs[-1]
    whole_ref[...] = plane_sum(met)
    height = outs[0].shape[0]
    for step, out in enumerate(outs):
        at = pl.ds(pl.multiple_of((place_ref[0] ^ step) * height, height), height)
        out[...] = whole_ref[at, :]


def rows_kernel(place_ref, *refs):
    refs[-1][...] = tree_sum([ref[...] for ref in refs[:-1]]).astype(BF16)


def code_kernel(place_ref, *refs, n):
    met, rows_ref, out_ref = refs[:n], refs[n], refs[n + 1]
    total = plane_sum(met)
    coded = total.shape[0] + SCALE_ROWS
    encode(total, out_ref.at[:coded])
    out_ref[coded:] = rows_ref[...]


def finish_kernel(place_ref, *refs, n, k):
    out_ref = refs[-1]
    height = out_ref.shape[0] // 2
    coded, few = height + SCALE_ROWS, height // n
    met = []
    for step in range(n):
        at = pl.ds(pl.multiple_of((place_ref[0] ^ step) * few, few), few)
        out_ref[at, :] = refs[step][coded:]
        met += decode(refs[step].at[:coded], 1)
    total = tree_sum(met)
    last = (place_ref[1] == n - 1) & (place_ref[2] == k - 1)
    start = 2 * (total.shape[1] // KEPT)
    edge = total[-8:, start:]
    row = lax.broadcasted_iota(jnp.int32, edge.shape, 0)
    column = lax.broadcasted_iota(jnp.int32, edge.shape, 1)
    taken = (row == 7) & last
    whole = jnp.sum(jnp.where(taken & (column == 0), edge, 0.0), keepdims=True)
    high = whole.astype(BF16).astype(F32)
    middle = (whole - high).astype(BF16).astype(F32)
    three = jnp.where(column == 0, high, jnp.where(column == 1, middle, whole - high - middle))
    edge = jnp.where(taken & (column < 3), three, edge)
    edge = jnp.concatenate([total[-8:, :start], edge], 1)
    out_ref[height:] = jnp.concatenate([total[:-8], edge], 0).astype(BF16)


def local(kernel, place_array, args, shapes, name, **more):
    space = pl.BlockSpec(memory_space=pltpu.VMEM)
    return pl.pallas_call(
        kernel,
        in_specs=[pl.BlockSpec(memory_space=pltpu.SMEM)] + [space] * len(args),
        out_specs=[space] * len(shapes),
        out_shape=[jax.ShapeDtypeStruct(shape, dtype) for shape, dtype in shapes],
        compiler_params=pltpu.CompilerParams(vmem_limit_bytes=VMEM_BYTES // 2),
        name=name,
        **more,
    )(place_array, *args)


def plane_rows(place, place_array, grams, few=False):
    half, batch = grams[0].shape
    kept, other = grams
    other = place.send(other, lambda z, a, b: (z, a, b ^ 1))
    height, batch = half // place.n, batch * KEPT // BLOCKS
    parts = local(
        functools.partial(halve_kernel, n=place.n),
        place_array,
        (kept, other),
        [((height, batch), F32)] + [((height + SCALE_ROWS, batch), BF16)] * (place.n - 1),
        "halve",
    )
    return sends(place, "a", parts, few)


def first_rows(place, place_array, grams):
    parts = plane_rows(place, place_array, grams, True)
    height, batch = parts[0].shape
    return local(
        functools.partial(plane_kernel, n=place.n),
        place_array,
        parts,
        [((height // place.n, batch), F32)] * place.n,
        "plane",
        scratch_shapes=[pltpu.VMEM((height, batch), F32)],
    )


def in_one(place, run, args):
    shapes = jax.eval_shape(run, *args)
    return lax.cond(
        place.z < place.n,
        run,
        lambda *args: jax.tree.map(lambda leaf: jnp.zeros(leaf.shape, leaf.dtype), shapes),
        *args,
    )


def plain_gram(place, part):
    for axis in ("b", "a", "z"):
        part = reduce_scatter(place, axis, part)
    part = part.astype(BF16)
    for axis in ("z", "a", "b"):
        part = gather(place, axis, part)
    return part


def lay_kernel(place_ref, *refs, n):
    parts, outs = refs[:n], refs[n:]
    few = parts[0].shape[0] // len(outs)
    for step in range(n):
        at = pl.ds(pl.multiple_of((place_ref[0] ^ step) * few, few), few)
        for i, out in enumerate(outs):
            out[at, :] = parts[step][i * few : (i + 1) * few, :]


def fetch_kernel(weight_ref, held_ref, arrived):
    copy = pltpu.make_async_copy(weight_ref, held_ref, arrived)
    copy.start()
    copy.wait()


def fetch(weight):
    return pl.pallas_call(
        fetch_kernel,
        in_specs=[pl.BlockSpec(memory_space=pl.ANY)],
        out_specs=pl.BlockSpec(memory_space=pltpu.VMEM),
        out_shape=pltpu.VMEM(weight.shape, BF16),
        scratch_shapes=[pltpu.SemaphoreType.DMA],
        compiler_params=pltpu.CompilerParams(vmem_limit_bytes=VMEM_BYTES // 2),
        cost_estimate=pl.CostEstimate(flops=0, bytes_accessed=4 * weight.size, transcendentals=0),
        name="fetch",
    )(pltpu.with_memory_space_constraint(weight, pltpu.HBM))


def to_columns(place, view):
    rows, width = view.shape
    return exchange(place, "a", view.reshape(place.n, rows // place.n, width))


def to_planes(place, parts):
    return sends(place, "z", ordered(parts, place.a ^ place.z))


def lay(place, place_array, parts):
    rows, width = parts[0].shape
    (laid,) = local(
        functools.partial(lay_kernel, n=place.n),
        place_array,
        parts,
        [((rows * place.n, width), BF16)],
        "lay",
    )
    return laid


def met_rows(place, values, few=False):
    return sends(place, "a", [values] * place.n, few)


def project_kernel(place_ref, *refs, counts, n, k):
    met = refs[: sum(counts)]
    weight_ref, own_ref, *coded = refs[sum(counts) :]
    width = met[0].shape[1]
    columns = own_ref.shape[1]
    values = []
    for count in counts:
        values.append(jnp.concatenate([ref[...] for ref in met[:count]], 0))
        met = met[count:]
    for step in [*range(n - 1, 0, -1), 0]:
        at = pl.ds(pl.multiple_of((place_ref[0] ^ step) * columns, columns), columns)
        total = 0.0
        for i in range(k):
            rows = pl.ds(pl.multiple_of((place_ref[2] ^ i) * width, width), width)
            total += jnp.dot(values[i], weight_ref[rows, at], preferred_element_type=F32)
        if step == 0:
            own_ref[...] = total
        else:
            encode(total, coded[n - 1 - step])


def encode(total, coded_ref):
    rows = total.shape[0]
    top = jnp.max(jnp.abs(total), 0, keepdims=True)
    top = jnp.maximum(top * (1.0 + 1.0 / 128.0), 1e-30).astype(BF16)
    coded_ref[rows:] = jnp.broadcast_to(top, (SCALE_ROWS, total.shape[1]))
    whole = jnp.floor(jnp.abs(total) * (HIGHEST / top.astype(F32)) + 0.5)
    power = jnp.floor(whole * (1.0 / 128.0))
    word = (1.0 + (whole * (1.0 / 128.0) - power)) * jnp.exp2(power - POWERS // 2)
    coded_ref[:rows] = jnp.where(total < 0.0, -word, word).astype(BF16)


def decode(coded_ref, count):
    rows = coded_ref.shape[0] - SCALE_ROWS
    scale = coded_ref[rows:].astype(F32)[:1] * (1.0 / HIGHEST)
    height = rows // count
    blocks = []
    for i in range(count):
        word = coded_ref[i * height : (i + 1) * height].astype(F32)
        size = jnp.abs(word)
        power = jnp.floor(jnp.log(size) * 1.4426950408889634 + 0.002)
        part = jnp.floor(size * jnp.exp2(-power) * 128.0 + 0.5)
        whole = (power + (POWERS // 2 - 1)) * 128.0 + part
        blocks.append(jnp.where(word < 0.0, -whole, whole) * scale)
    return blocks


def project(place, place_array, met, held):
    n, k = place.n, place.k
    rows, width = met[0][0].shape
    batch, columns = rows * n, held.shape[1] // n
    counts = [len(parts) for parts in met]
    met = [part for parts in met for part in parts]
    coded = batch + SCALE_ROWS
    out_shape = [jax.ShapeDtypeStruct((batch, columns), F32)]
    out_shape += [jax.ShapeDtypeStruct((coded, columns), BF16)] * (n - 1)
    space = pl.BlockSpec(memory_space=pltpu.VMEM)
    own, *parts = pl.pallas_call(
        functools.partial(project_kernel, counts=counts, n=n, k=k),
        in_specs=[pl.BlockSpec(memory_space=pltpu.SMEM)]
        + [space] * (len(met) + 1),
        out_specs=[space] * n,
        out_shape=out_shape,
        compiler_params=pltpu.CompilerParams(vmem_limit_bytes=VMEM_BYTES),
        cost_estimate=pl.CostEstimate(
            flops=2 * batch * k * width * n * columns,
            bytes_accessed=2 * k * width * (batch + n * columns) + 3 * n * batch * columns,
            transcendentals=0,
        ),
        name="project",
    )(place_array, *met, pltpu.with_memory_space_constraint(held, pltpu.VMEM))
    return own, parts[::-1]


def normalize_kernel(place_ref, *refs, n, k, order, second):
    own_ref, parts = refs[0], refs[n - 1 : 0 : -1]
    refs = refs[n:]
    if second:
        other_ref, refs = refs[0], refs[1:]
    norm_ref, packed_ref, scale_ref = refs[:3]
    grams = refs[3 : 3 + k]
    batch, columns = own_ref.shape
    height = batch // n
    met = [[own_ref[i * height : (i + 1) * height] for i in range(n)]]
    for step in range(1, n):
        met.append(decode(parts[step - 1], n))
    blocks = [tree_sum([met[step][i] for step in range(n)]) for i in range(n)]
    total = tree_sum([jnp.sum(block, 0, keepdims=True) for block in blocks])
    squares = tree_sum([jnp.sum(block * block, 0, keepdims=True) for block in blocks])
    mean = total / batch
    scale = lax.rsqrt(squares / batch - mean * mean + bn_eps)
    scale_ref[...] = scale
    rows, few = batch // n, batch // (n * n)
    for i, block in enumerate(blocks):
        normed = (block - mean) * scale
        for first in range(0, height, few):
            step, plane = divmod((i * height + first) // few, n)
            at = pl.multiple_of(plane * rows + (place_ref[1] ^ order[step]) * few, few)
            norm_ref[pl.ds(at, few), :] = normed[first : first + few]
            packed_ref[pl.ds(at, few), :] = normed[first : first + few].astype(BF16)
    dims = (((1,), (1,)), ((), ()))
    packed = packed_ref[...]
    size = batch // k
    for i in range(k):
        at = pl.multiple_of((place_ref[2] ^ i) * size, size)
        gram = lax.dot_general(packed_ref[pl.ds(at, size), :], packed, dims, preferred_element_type=F32)
        grams[i][...] = gram
    if second:
        coeff_ref = refs[3 + k]
        diag = jnp.sum(norm_ref[...] * other_ref[...], 0, keepdims=True) / batch
        coeff_ref[...] = 2.0 * ((1.0 - off_weight) * diag - 1.0)
        share = jnp.sum((1.0 - diag) ** 2 - off_weight * diag * diag, 1, keepdims=True)
        for i in range(k):

            @pl.when((place_ref[2] ^ i) == k - 1)
            def _():
                at = batch // BLOCKS
                row = grams[i][size - 8 :, at : at + 128]
                first = (lax.broadcasted_iota(jnp.int32, row.shape, 0) == 7) & (
                    lax.broadcasted_iota(jnp.int32, row.shape, 1) == 0
                )
                grams[i][size - 8 :, at : at + 128] = jnp.where(first, share, row)


def normalize_parts(place, place_array, own, parts, order, other=None):
    n, k = place.n, place.k
    batch, columns = own.shape
    second = other is not None
    out_shape = [
        jax.ShapeDtypeStruct((batch, columns), F32),
        jax.ShapeDtypeStruct((batch, columns), BF16),
        jax.ShapeDtypeStruct((1, columns), F32),
    ] + [jax.ShapeDtypeStruct((batch // k, batch), F32)] * k
    if second:
        out_shape.append(jax.ShapeDtypeStruct((1, columns), F32))
    args = [own, *parts[::-1]] + ([other] if second else [])
    space = pl.BlockSpec(memory_space=pltpu.VMEM)
    return pl.pallas_call(
        functools.partial(normalize_kernel, n=n, k=k, order=order, second=second),
        in_specs=[pl.BlockSpec(memory_space=pltpu.SMEM)] + [space] * len(args),
        out_specs=[space] * len(out_shape),
        out_shape=out_shape,
        compiler_params=pltpu.CompilerParams(vmem_limit_bytes=VMEM_BYTES // 2),
        cost_estimate=pl.CostEstimate(
            flops=2 * batch * batch * columns,
            bytes_accessed=16 * batch * columns + 4 * batch * batch,
            transcendentals=0,
        ),
        name="normalize",
    )(place_array, *args)


def gradient_kernel(place_ref, *refs, n, k):
    grams, refs = refs[: n * k], refs[n * k :]
    packed, norms, scales, coeff_ref, refs = refs[0:2], refs[2:4], refs[4:6], refs[6], refs[7:]
    outs = [refs[0], *refs[n - 1 : 0 : -1]]
    share_ref, gram_ref, whole_ref = refs[n:]
    batch, columns = norms[0].shape
    height = grams[0].shape[0] // 2
    width = batch // BLOCKS
    for i in range(k):
        for step in range(n):
            block = (place_ref[2] ^ i) * n + (place_ref[1] ^ step)
            at = pl.ds(pl.multiple_of(block * height, height), height)
            block = block // (2 * n // BLOCKS)
            for j in range(KEPT):
                to = pl.ds(pl.multiple_of(lax.rem(block + j, BLOCKS) * width, width), width)
                for view in range(2):
                    gram_ref[view, at, to] = grams[i * n + step][
                        view * height : (view + 1) * height, j * width : (j + 1) * width
                    ]
    blocks = [slice(i * width, (i + 1) * width) for i in range(BLOCKS)]
    for view in range(2):
        for i in range(BLOCKS):
            other = gram_ref[view, blocks[i - 1], blocks[i]].astype(F32).T
            gram_ref[view, blocks[i], blocks[i - 1]] = other.astype(BF16)
    tail = gram_ref[1, blocks[3], blocks[1]].astype(F32)
    row = lax.broadcasted_iota(jnp.int32, tail.shape, 0)
    column = lax.broadcasted_iota(jnp.int32, tail.shape, 1)
    taken = (row == width - 1) & (column < 3)
    mirror = gram_ref[1, blocks[1], blocks[3]].astype(F32).T
    share = jnp.sum(jnp.where(taken, tail, 0.0), keepdims=True)
    gram_ref[1, blocks[3], blocks[1]] = jnp.where(taken, mirror, tail).astype(BF16)
    factor = 2.0 * off_weight / batch
    rows = batch // n
    for view in (1, 0):
        norm = norms[view][...]
        grad = (
            factor * jnp.dot(gram_ref[1 - view], packed[view][...], preferred_element_type=F32)
            + coeff_ref[...] * norms[1 - view][...]
        )
        first = jnp.sum(grad, 0, keepdims=True) / batch
        second = jnp.sum(grad * norm, 0, keepdims=True) / batch
        whole_ref[view] = (scales[view][...] * (grad - first - norm * second)).astype(BF16)
        for step in range(n):
            at = pl.multiple_of((place_ref[0] ^ step) * rows, rows)
            outs[step][view * rows : (view + 1) * rows, :] = whole_ref[view, pl.ds(at, rows), :]
    share_ref[...] = share


def loss_kernel(place_ref, gram_ref, share_ref, loss_ref):
    batch = gram_ref.shape[1]
    frob = jnp.sum(gram_ref[0].astype(F32) * gram_ref[1].astype(F32), keepdims=True)
    loss_ref[...] = (share_ref[...] + off_weight * (frob / (batch * batch))) / D


def gradient(place, place_array, grams, packed, norms, scales, coeff):
    batch, columns = norms[0].shape
    return local(
        functools.partial(gradient_kernel, n=place.n, k=place.k),
        place_array,
        (*grams, *packed, *norms, *scales, coeff),
        [((2 * batch // place.n, columns), BF16)] * place.n
        + [((1, 1), F32), ((2, batch, batch), BF16)],
        "gradient",
        scratch_shapes=[pltpu.VMEM((2, batch, columns), BF16)],
    )


def place_kernel(place_ref, *refs, n):
    parts, outs = [refs[0], *refs[n - 1 : 0 : -1]], refs[n:]
    rows, columns = parts[0].shape[0] // len(outs), parts[0].shape[1]
    for step in range(n):
        at = pl.ds(pl.multiple_of((place_ref[0] ^ step) * columns, columns), columns)
        for i, out in enumerate(outs):
            out[:, at] = parts[step][i * rows : (i + 1) * rows, :]


def with_kernels(place, h_first, h_second, weight):
    n, k, z, a, b = place.n, place.k, place.z, place.a, place.b
    place_array = jnp.stack([z, a, b]).astype(jnp.int32)
    first, second = lax.optimization_barrier((to_columns(place, h_first), h_second))
    first, second = to_planes(place, first), to_columns(place, second)
    first, late_weight = lax.optimization_barrier((lay(place, place_array, first), weight))
    met_1, second, held = lax.optimization_barrier(
        (met_rows(place, first), to_planes(place, second), fetch(late_weight))
    )

    def sent(parts):
        return sends(place, "z", [parts[0], *parts])[1:]

    def swapped(part):
        return place.send(part, lambda z, a, b: (z, a, b ^ 1))

    own_1, parts_1 = project(place, place_array, [met_1, [swapped(part) for part in met_1]], held)
    second = lay(place, place_array, second)
    size, here, toward = place.along("a")
    order_2 = [0, size - 1, *range(1, size - 1)]
    last = place.send(second, toward(size - 1))
    own_1, parts_1, late_weight = lax.optimization_barrier((own_1, parts_1, weight))
    parts_1 = sent(parts_1)

    def second_projected(weight, values, last):
        met = [place.send(values, toward(step)) for step in range(1, size - 1)]
        values, met[0] = lax.optimization_barrier((values, met[0]))
        early = swapped(jnp.concatenate([values, last], 0))
        late = swapped(jnp.concatenate(met, 0))
        return project(place, place_array, [[values, last, *met], [early, late]], fetch(weight))

    own_2, parts_2 = in_one(place, second_projected, (late_weight, second, last))
    own_1, own_2 = lax.optimization_barrier((own_1, own_2))
    parts_2 = sent(parts_2)
    norm_1, packed_1, scale_1, *grams = normalize_parts(
        place, place_array, own_1, parts_1, [*range(n)]
    )
    met_1 = in_one(place, lambda *grams: first_rows(place, place_array, grams), grams)
    met_1 = sends(place, "z", met_1)
    own_2, parts_2, met_1 = lax.optimization_barrier((own_2, parts_2, met_1))
    norm_2, packed_2, scale_2, *grams, coeff = normalize_parts(
        place, place_array, own_2, parts_2, order_2, norm_1
    )
    height, batch = met_1[0].shape
    (rows_1,) = local(rows_kernel, place_array, met_1, [((height, batch), BF16)], "rows")
    met_2 = plane_rows(place, place_array, grams)
    rows = met_2[0].shape[0]
    (part,) = local(
        functools.partial(code_kernel, n=n),
        place_array,
        (*met_2, rows_1),
        [((rows + SCALE_ROWS + height, batch), BF16)],
        "code",
    )
    (part,) = local(
        functools.partial(finish_kernel, n=n, k=k),
        place_array,
        sends(place, "z", [part] * n),
        [((2 * rows, batch), BF16)],
        "finish",
    )
    grams = sends(place, "a", [part] * n)
    grams += [place.send(part, lambda z, a, b: (z, a, b ^ 1)) for part in grams]
    first, *others, share, grams = gradient(
        place,
        place_array,
        grams,
        (packed_1, packed_2),
        (norm_1, norm_2),
        (scale_1, scale_2),
        coeff,
    )
    out_1, out_2 = local(
        functools.partial(place_kernel, n=n),
        place_array,
        [first, *sends(place, "z", [first, *others[::-1]])[:0:-1]],
        [(h_first.shape, BF16)] * 2,
        "place",
    )
    (loss,) = local(loss_kernel, place_array, (grams, share), [((1, 1), F32)], "loss")
    return (out_1, out_2, loss.reshape(()))


def plain(place, h_first, h_second, weight):
    n, k, z, a, b = place.n, place.k, place.z, place.a, place.b
    rows, width = h_first.shape
    batch = rows * n
    columns = weight.shape[1] // n
    weight_parts = weight.reshape(k, width, n * columns)
    zs = []
    for values in (h_first, h_second):
        moved = place.send(values, lambda z, a, b: (a, z, b))
        own = jnp.concatenate(met_rows(place, moved), 0)
        total = jnp.dot(own, pick(weight_parts, b), preferred_element_type=F32)
        for step in range(1, k):
            other = place.send(own, lambda z, a, b, s=step: (z, a, b ^ s))
            total += jnp.dot(other, pick(weight_parts, b ^ step), preferred_element_type=F32)
        cut = total.reshape(batch, n, columns).transpose(1, 0, 2)
        whole = tree_sum(exchange(place, "z", cut)).reshape(n, rows, columns)
        zs.append(jnp.concatenate(ordered([whole[i] for i in range(n)], a), 0))
    normed, scales = [], []
    for values in zs:
        mean = jnp.sum(values, 0) / batch
        scale = lax.rsqrt(jnp.sum(values * values, 0) / batch - mean * mean + bn_eps)
        normed.append((values - mean) * scale)
        scales.append(scale)
    diag = jnp.sum(normed[0] * normed[1], 0) / batch
    packed = [values.astype(BF16) for values in normed]
    dims = (((1,), (1,)), ((), ()))
    grams = []
    for values in packed:
        gram = lax.dot_general(values, values, dims, preferred_element_type=F32)
        grams.append(plain_gram(place, gram))
    frob = jnp.sum(grams[0].astype(F32) * grams[1].astype(F32)) / (batch * batch)
    coeff = 2.0 * ((1.0 - off_weight) * diag - 1.0)
    factor = 2.0 * off_weight / batch
    outs = []
    for view in range(2):
        grad = (
            factor * jnp.dot(grams[1 - view], packed[view], preferred_element_type=F32)
            + coeff * normed[1 - view]
        )
        first = jnp.sum(grad, 0) / batch
        second = jnp.sum(grad * normed[view], 0) / batch
        out = (scales[view] * (grad - first - normed[view] * second)).astype(BF16)
        parts = exchange(place, "z", out.reshape(n, rows, columns))
        outs.append(jnp.concatenate(ordered(parts, z), 1))
    share = jnp.sum((1.0 - diag) ** 2) - off_weight * jnp.sum(diag * diag)
    loss = (lax.psum(share, ("dp", "mp")) + off_weight * frob) / D
    return (outs[0], outs[1], loss)


def per_device(h_first, h_second, weight):
    place = Place()
    columns = weight.shape[1] // place.n
    fits = columns % 128 == 0 and place.n == 4 and place.k == 2
    return (with_kernels if fits else plain)(place, h_first, h_second, weight)


def solution(mesh):
    in_specs = (P("dp", "mp"), P("dp", "mp"), P("dp", "mp"))
    out_specs = (P("dp", "mp"), P("dp", "mp"), P())
    return jax.shard_map(
        per_device, mesh=mesh, in_specs=in_specs, out_specs=out_specs, check_vma=False
    )
```

```python
import functools

import jax
import jax.numpy as jnp
from jax import lax
from jax.experimental import pallas as pl
from jax.experimental.pallas import tpu as pltpu
from jax.sharding import PartitionSpec as P

D = 8192


off_weight = 0.0051
bn_eps = 1e-05

F32 = jnp.float32
BF16 = jnp.bfloat16
VMEM_BYTES = 16 * 1024 * 1024
POWERS = 240
HIGHEST = 128 * POWERS - 1
SCALE_ROWS = 16


class Place:
    def __init__(self):
        self.n = lax.axis_size("dp")
        self.k = lax.axis_size("mp") // self.n
        self.z = lax.axis_index("dp")
        self.a = lax.axis_index("mp") // self.k
        self.b = lax.axis_index("mp") % self.k

    def send(self, value, target):
        n, k = self.n, self.k
        pairs = []
        for z in range(n):
            for a in range(n):
                for b in range(k):
                    to_z, to_a, to_b = target(z, a, b)
                    pairs.append(((z * n + a) * k + b, (to_z * n + to_a) * k + to_b))
        return lax.ppermute(value, ("dp", "mp"), pairs)

    def along(self, axis):
        if axis == "z":
            return self.n, self.z, lambda step: lambda z, a, b: (z ^ step, a, b)
        if axis == "a":
            return self.n, self.a, lambda step: lambda z, a, b: (z, a ^ step, b)
        return self.k, self.b, lambda step: lambda z, a, b: (z, a, b ^ step)


def ordered(parts, place):
    bit = 1
    while bit < len(parts):
        odd = (place & bit) != 0
        parts = [jnp.where(odd, parts[i ^ bit], parts[i]) for i in range(len(parts))]
        bit *= 2
    return parts


def tree_sum(parts):
    while len(parts) > 1:
        parts = [parts[i] + parts[i + 1] for i in range(0, len(parts), 2)]
    return parts[0]


def pick(value, index):
    return lax.dynamic_index_in_dim(value, index, 0, keepdims=False)


def exchange(place, axis, value, few=False):
    size, here, toward = place.along(axis)
    return sends(place, axis, [pick(value, here ^ step) for step in range(size)], few)


def sends(place, axis, parts, few=False):
    size, here, toward = place.along(axis)
    met = {0: parts[0]}
    order = [*range(1, size)] if few else [*range(size - 1, 0, -1)]
    for i, step in enumerate(order):
        part = parts[step]
        if few and i >= 2:
            met[order[i - 2]], part = lax.optimization_barrier((met[order[i - 2]], part))
        met[step] = place.send(part, toward(step))
    return [met[step] for step in range(size)]


def reduce_scatter(place, axis, value, few=False):
    size, here, toward = place.along(axis)
    value = value.reshape((size, value.shape[0] // size) + value.shape[1:])
    return tree_sum(exchange(place, axis, value, few))


def gather(place, axis, value, few=False):
    size, here, toward = place.along(axis)
    parts = sends(place, axis, [value] * size, few)
    return jnp.concatenate(ordered(parts, here), 0)


BLOCKS = 4
KEPT = 3


def folded(values):
    width = values.shape[1] // KEPT
    return jnp.concatenate([values[:, i * width : (i + 1) * width] for i in range(KEPT)], 0)


def unfolded(values):
    height = values.shape[0] // KEPT
    return jnp.concatenate([values[i * height : (i + 1) * height] for i in range(KEPT)], 1)


def folded_shape(rows, columns):
    return (rows * KEPT + SCALE_ROWS, columns // KEPT)


def halve_kernel(place_ref, kept_ref, met_ref, *outs, n):
    height = kept_ref.shape[0] // n
    width = kept_ref.shape[1] // BLOCKS
    for step, out in enumerate(outs):
        block = place_ref[1] ^ step
        at = pl.ds(pl.multiple_of(block * height, height), height)
        block = (place_ref[2] * n + block) // (2 * n // BLOCKS)
        total = []
        for i in range(KEPT):
            cut = pl.ds(pl.multiple_of(lax.rem(block + i, BLOCKS) * width, width), width)
            total.append(kept_ref[at, cut] + met_ref[at, cut])
        total = jnp.concatenate(total, 1)
        if step == 0:
            out[...] = total
        else:
            encode(folded(total), out)


def plane_sum(met):
    return tree_sum([met[0][...]] + [unfolded(decode(ref, 1)[0]) for ref in met[1:]])


def plane_kernel(place_ref, *refs, n):
    met, outs, whole_ref = refs[:n], refs[n:-1], refs[-1]
    whole_ref[...] = plane_sum(met)
    height = outs[0].shape[0]
    for step, out in enumerate(outs):
        at = pl.ds(pl.multiple_of((place_ref[0] ^ step) * height, height), height)
        if step == 0:
            out[...] = whole_ref[at, :]
        else:
            encode(folded(whole_ref[at, :]), out)


def rows_kernel(place_ref, *refs):
    refs[-1][...] = plane_sum(refs[:-1]).astype(BF16)


def code_kernel(place_ref, *refs, n):
    met, rows_ref, out_ref = refs[:n], refs[n], refs[n + 1]
    total = folded(plane_sum(met))
    coded = total.shape[0] + SCALE_ROWS
    encode(total, out_ref.at[:coded])
    out_ref[coded:] = folded(rows_ref[...])


def finish_kernel(place_ref, *refs, n, k):
    out_ref = refs[-1]
    height = out_ref.shape[0] // 2
    coded, few = height * KEPT + SCALE_ROWS, height // n
    met = []
    for step in range(n):
        at = pl.ds(pl.multiple_of((place_ref[0] ^ step) * few, few), few)
        out_ref[at, :] = unfolded(refs[step][coded:])
        met += decode(refs[step].at[:coded], 1)
    total = unfolded(tree_sum(met))
    last = (place_ref[1] == n - 1) & (place_ref[2] == k - 1)
    start = 2 * (total.shape[1] // KEPT)
    edge = total[-8:, start:]
    row = lax.broadcasted_iota(jnp.int32, edge.shape, 0)
    column = lax.broadcasted_iota(jnp.int32, edge.shape, 1)
    taken = (row == 7) & last
    whole = jnp.sum(jnp.where(taken & (column == 0), edge, 0.0), keepdims=True)
    high = whole.astype(BF16).astype(F32)
    middle = (whole - high).astype(BF16).astype(F32)
    three = jnp.where(column == 0, high, jnp.where(column == 1, middle, whole - high - middle))
    edge = jnp.where(taken & (column < 3), three, edge)
    edge = jnp.concatenate([total[-8:, :start], edge], 1)
    out_ref[height:] = jnp.concatenate([total[:-8], edge], 0).astype(BF16)


def local(kernel, place_array, args, shapes, name, **more):
    space = pl.BlockSpec(memory_space=pltpu.VMEM)
    return pl.pallas_call(
        kernel,
        in_specs=[pl.BlockSpec(memory_space=pltpu.SMEM)] + [space] * len(args),
        out_specs=[space] * len(shapes),
        out_shape=[jax.ShapeDtypeStruct(shape, dtype) for shape, dtype in shapes],
        compiler_params=pltpu.CompilerParams(vmem_limit_bytes=VMEM_BYTES // 2),
        name=name,
        **more,
    )(place_array, *args)


def plane_rows(place, place_array, grams, few=False):
    half, batch = grams[0].shape
    kept, other = grams
    other = place.send(other, lambda z, a, b: (z, a, b ^ 1))
    height, batch = half // place.n, batch * KEPT // BLOCKS
    parts = local(
        functools.partial(halve_kernel, n=place.n),
        place_array,
        (kept, other),
        [((height, batch), F32)] + [(folded_shape(height, batch), BF16)] * (place.n - 1),
        "halve",
    )
    return sends(place, "a", parts, few)


def first_rows(place, place_array, grams):
    parts = plane_rows(place, place_array, grams, True)
    height, batch = parts[0].shape
    few = height // place.n
    return local(
        functools.partial(plane_kernel, n=place.n),
        place_array,
        parts,
        [((few, batch), F32)] + [(folded_shape(few, batch), BF16)] * (place.n - 1),
        "plane",
        scratch_shapes=[pltpu.VMEM((height, batch), F32)],
    )


def in_one(place, run, args):
    shapes = jax.eval_shape(run, *args)
    return lax.cond(
        place.z < place.n,
        run,
        lambda *args: jax.tree.map(lambda leaf: jnp.zeros(leaf.shape, leaf.dtype), shapes),
        *args,
    )


def plain_gram(place, part):
    for axis in ("b", "a", "z"):
        part = reduce_scatter(place, axis, part)
    part = part.astype(BF16)
    for axis in ("z", "a", "b"):
        part = gather(place, axis, part)
    return part


def lay_kernel(place_ref, *refs, n):
    parts, outs = refs[:n], refs[n:]
    few = parts[0].shape[0] // len(outs)
    for step in range(n):
        at = pl.ds(pl.multiple_of((place_ref[0] ^ step) * few, few), few)
        for i, out in enumerate(outs):
            out[at, :] = parts[step][i * few : (i + 1) * few, :]


def fetch_kernel(weight_ref, held_ref, arrived):
    copy = pltpu.make_async_copy(weight_ref, held_ref, arrived)
    copy.start()
    copy.wait()


def fetch(weight):
    return pl.pallas_call(
        fetch_kernel,
        in_specs=[pl.BlockSpec(memory_space=pl.ANY)],
        out_specs=pl.BlockSpec(memory_space=pltpu.VMEM),
        out_shape=pltpu.VMEM(weight.shape, BF16),
        scratch_shapes=[pltpu.SemaphoreType.DMA],
        compiler_params=pltpu.CompilerParams(vmem_limit_bytes=VMEM_BYTES // 2),
        cost_estimate=pl.CostEstimate(flops=0, bytes_accessed=4 * weight.size, transcendentals=0),
        name="fetch",
    )(pltpu.with_memory_space_constraint(weight, pltpu.HBM))


def to_columns(place, view):
    rows, width = view.shape
    return exchange(place, "a", view.reshape(place.n, rows // place.n, width))


def to_planes(place, parts):
    return sends(place, "z", ordered(parts, place.a ^ place.z))


def lay(place, place_array, parts):
    rows, width = parts[0].shape
    (laid,) = local(
        functools.partial(lay_kernel, n=place.n),
        place_array,
        parts,
        [((rows * place.n, width), BF16)],
        "lay",
    )
    return laid


def met_rows(place, values, few=False):
    return sends(place, "a", [values] * place.n, few)


def project_kernel(place_ref, *refs, counts, n, k):
    met = refs[: sum(counts)]
    weight_ref, own_ref, *coded = refs[sum(counts) :]
    width = met[0].shape[1]
    columns = own_ref.shape[1]
    values = []
    for count in counts:
        values.append(jnp.concatenate([ref[...] for ref in met[:count]], 0))
        met = met[count:]
    for step in [*range(n - 1, 0, -1), 0]:
        at = pl.ds(pl.multiple_of((place_ref[0] ^ step) * columns, columns), columns)
        total = 0.0
        for i in range(k):
            rows = pl.ds(pl.multiple_of((place_ref[2] ^ i) * width, width), width)
            total += jnp.dot(values[i], weight_ref[rows, at], preferred_element_type=F32)
        if step == 0:
            own_ref[...] = total
        else:
            encode(total, coded[n - 1 - step])


def encode(total, coded_ref):
    rows = total.shape[0]
    top = jnp.max(jnp.abs(total), 0, keepdims=True)
    top = jnp.maximum(top * (1.0 + 1.0 / 128.0), 1e-30).astype(BF16)
    coded_ref[rows:] = jnp.broadcast_to(top, (SCALE_ROWS, total.shape[1]))
    whole = jnp.floor(jnp.abs(total) * (HIGHEST / top.astype(F32)) + 0.5)
    power = jnp.floor(whole * (1.0 / 128.0))
    word = (1.0 + (whole * (1.0 / 128.0) - power)) * jnp.exp2(power - POWERS // 2)
    coded_ref[:rows] = jnp.where(total < 0.0, -word, word).astype(BF16)


def decode(coded_ref, count):
    rows = coded_ref.shape[0] - SCALE_ROWS
    scale = coded_ref[rows:].astype(F32)[:1] * (1.0 / HIGHEST)
    height = rows // count
    blocks = []
    for i in range(count):
        word = coded_ref[i * height : (i + 1) * height].astype(F32)
        size = jnp.abs(word)
        power = jnp.floor(jnp.log(size) * 1.4426950408889634 + 0.002)
        part = jnp.floor(size * jnp.exp2(-power) * 128.0 + 0.5)
        whole = (power + (POWERS // 2 - 1)) * 128.0 + part
        blocks.append(jnp.where(word < 0.0, -whole, whole) * scale)
    return blocks


def project(place, place_array, met, held):
    n, k = place.n, place.k
    rows, width = met[0][0].shape
    batch, columns = rows * n, held.shape[1] // n
    counts = [len(parts) for parts in met]
    met = [part for parts in met for part in parts]
    coded = batch + SCALE_ROWS
    out_shape = [jax.ShapeDtypeStruct((batch, columns), F32)]
    out_shape += [jax.ShapeDtypeStruct((coded, columns), BF16)] * (n - 1)
    space = pl.BlockSpec(memory_space=pltpu.VMEM)
    own, *parts = pl.pallas_call(
        functools.partial(project_kernel, counts=counts, n=n, k=k),
        in_specs=[pl.BlockSpec(memory_space=pltpu.SMEM)]
        + [space] * (len(met) + 1),
        out_specs=[space] * n,
        out_shape=out_shape,
        compiler_params=pltpu.CompilerParams(vmem_limit_bytes=VMEM_BYTES),
        cost_estimate=pl.CostEstimate(
            flops=2 * batch * k * width * n * columns,
            bytes_accessed=2 * k * width * (batch + n * columns) + 3 * n * batch * columns,
            transcendentals=0,
        ),
        name="project",
    )(place_array, *met, pltpu.with_memory_space_constraint(held, pltpu.VMEM))
    return own, parts[::-1]


def normalize_kernel(place_ref, *refs, n, k, order, second):
    own_ref, parts = refs[0], refs[n - 1 : 0 : -1]
    refs = refs[n:]
    if second:
        other_ref, refs = refs[0], refs[1:]
    norm_ref, packed_ref, scale_ref = refs[:3]
    grams = refs[3 : 3 + k]
    batch, columns = own_ref.shape
    height = batch // n
    met = [[own_ref[i * height : (i + 1) * height] for i in range(n)]]
    for step in range(1, n):
        met.append(decode(parts[step - 1], n))
    blocks = [tree_sum([met[step][i] for step in range(n)]) for i in range(n)]
    total = tree_sum([jnp.sum(block, 0, keepdims=True) for block in blocks])
    squares = tree_sum([jnp.sum(block * block, 0, keepdims=True) for block in blocks])
    mean = total / batch
    scale = lax.rsqrt(squares / batch - mean * mean + bn_eps)
    scale_ref[...] = scale
    rows, few = batch // n, batch // (n * n)
    for i, block in enumerate(blocks):
        normed = (block - mean) * scale
        for first in range(0, height, few):
            step, plane = divmod((i * height + first) // few, n)
            at = pl.multiple_of(plane * rows + (place_ref[1] ^ order[step]) * few, few)
            norm_ref[pl.ds(at, few), :] = normed[first : first + few]
            packed_ref[pl.ds(at, few), :] = normed[first : first + few].astype(BF16)
    dims = (((1,), (1,)), ((), ()))
    packed = packed_ref[...]
    size = batch // k
    for i in range(k):
        at = pl.multiple_of((place_ref[2] ^ i) * size, size)
        gram = lax.dot_general(packed_ref[pl.ds(at, size), :], packed, dims, preferred_element_type=F32)
        grams[i][...] = gram
    if second:
        coeff_ref = refs[3 + k]
        diag = jnp.sum(norm_ref[...] * other_ref[...], 0, keepdims=True) / batch
        coeff_ref[...] = 2.0 * ((1.0 - off_weight) * diag - 1.0)
        share = jnp.sum((1.0 - diag) ** 2 - off_weight * diag * diag, 1, keepdims=True)
        for i in range(k):

            @pl.when((place_ref[2] ^ i) == k - 1)
            def _():
                at = batch // BLOCKS
                row = grams[i][size - 8 :, at : at + 128]
                first = (lax.broadcasted_iota(jnp.int32, row.shape, 0) == 7) & (
                    lax.broadcasted_iota(jnp.int32, row.shape, 1) == 0
                )
                grams[i][size - 8 :, at : at + 128] = jnp.where(first, share, row)


def normalize_parts(place, place_array, own, parts, order, other=None):
    n, k = place.n, place.k
    batch, columns = own.shape
    second = other is not None
    out_shape = [
        jax.ShapeDtypeStruct((batch, columns), F32),
        jax.ShapeDtypeStruct((batch, columns), BF16),
        jax.ShapeDtypeStruct((1, columns), F32),
    ] + [jax.ShapeDtypeStruct((batch // k, batch), F32)] * k
    if second:
        out_shape.append(jax.ShapeDtypeStruct((1, columns), F32))
    args = [own, *parts[::-1]] + ([other] if second else [])
    space = pl.BlockSpec(memory_space=pltpu.VMEM)
    return pl.pallas_call(
        functools.partial(normalize_kernel, n=n, k=k, order=order, second=second),
        in_specs=[pl.BlockSpec(memory_space=pltpu.SMEM)] + [space] * len(args),
        out_specs=[space] * len(out_shape),
        out_shape=out_shape,
        compiler_params=pltpu.CompilerParams(vmem_limit_bytes=VMEM_BYTES // 2),
        cost_estimate=pl.CostEstimate(
            flops=2 * batch * batch * columns,
            bytes_accessed=16 * batch * columns + 4 * batch * batch,
            transcendentals=0,
        ),
        name="normalize",
    )(place_array, *args)


def gradient_kernel(place_ref, *refs, n, k):
    grams, refs = refs[: n * k], refs[n * k :]
    packed, norms, scales, coeff_ref, refs = refs[0:2], refs[2:4], refs[4:6], refs[6], refs[7:]
    outs = [refs[0], *refs[n - 1 : 0 : -1]]
    share_ref, gram_ref, whole_ref = refs[n:]
    batch, columns = norms[0].shape
    height = grams[0].shape[0] // 2
    width = batch // BLOCKS
    for i in range(k):
        for step in range(n):
            block = (place_ref[2] ^ i) * n + (place_ref[1] ^ step)
            at = pl.ds(pl.multiple_of(block * height, height), height)
            block = block // (2 * n // BLOCKS)
            for j in range(KEPT):
                to = pl.ds(pl.multiple_of(lax.rem(block + j, BLOCKS) * width, width), width)
                for view in range(2):
                    gram_ref[view, at, to] = grams[i * n + step][
                        view * height : (view + 1) * height, j * width : (j + 1) * width
                    ]
    blocks = [slice(i * width, (i + 1) * width) for i in range(BLOCKS)]
    for view in range(2):
        for i in range(BLOCKS):
            other = gram_ref[view, blocks[i - 1], blocks[i]].astype(F32).T
            gram_ref[view, blocks[i], blocks[i - 1]] = other.astype(BF16)
    tail = gram_ref[1, blocks[3], blocks[1]].astype(F32)
    row = lax.broadcasted_iota(jnp.int32, tail.shape, 0)
    column = lax.broadcasted_iota(jnp.int32, tail.shape, 1)
    taken = (row == width - 1) & (column < 3)
    mirror = gram_ref[1, blocks[1], blocks[3]].astype(F32).T
    share = jnp.sum(jnp.where(taken, tail, 0.0), keepdims=True)
    gram_ref[1, blocks[3], blocks[1]] = jnp.where(taken, mirror, tail).astype(BF16)
    factor = 2.0 * off_weight / batch
    rows = batch // n
    for view in (1, 0):
        norm = norms[view][...]
        grad = (
            factor * jnp.dot(gram_ref[1 - view], packed[view][...], preferred_element_type=F32)
            + coeff_ref[...] * norms[1 - view][...]
        )
        first = jnp.sum(grad, 0, keepdims=True) / batch
        second = jnp.sum(grad * norm, 0, keepdims=True) / batch
        whole_ref[view] = (scales[view][...] * (grad - first - norm * second)).astype(BF16)
        for step in range(n):
            at = pl.multiple_of((place_ref[0] ^ step) * rows, rows)
            outs[step][view * rows : (view + 1) * rows, :] = whole_ref[view, pl.ds(at, rows), :]
    share_ref[...] = share


def loss_kernel(place_ref, gram_ref, share_ref, loss_ref):
    batch = gram_ref.shape[1]
    frob = jnp.sum(gram_ref[0].astype(F32) * gram_ref[1].astype(F32), keepdims=True)
    loss_ref[...] = (share_ref[...] + off_weight * (frob / (batch * batch))) / D


def gradient(place, place_array, grams, packed, norms, scales, coeff):
    batch, columns = norms[0].shape
    return local(
        functools.partial(gradient_kernel, n=place.n, k=place.k),
        place_array,
        (*grams, *packed, *norms, *scales, coeff),
        [((2 * batch // place.n, columns), BF16)] * place.n
        + [((1, 1), F32), ((2, batch, batch), BF16)],
        "gradient",
        scratch_shapes=[pltpu.VMEM((2, batch, columns), BF16)],
    )


def place_kernel(place_ref, *refs, n):
    parts, outs = [refs[0], *refs[n - 1 : 0 : -1]], refs[n:]
    rows, columns = parts[0].shape[0] // len(outs), parts[0].shape[1]
    for step in range(n):
        at = pl.ds(pl.multiple_of((place_ref[0] ^ step) * columns, columns), columns)
        for i, out in enumerate(outs):
            out[:, at] = parts[step][i * rows : (i + 1) * rows, :]


def with_kernels(place, h_first, h_second, weight):
    n, k, z, a, b = place.n, place.k, place.z, place.a, place.b
    place_array = jnp.stack([z, a, b]).astype(jnp.int32)
    first = to_columns(place, h_first)
    first, second = lax.optimization_barrier((to_planes(place, first), to_columns(place, h_second)))
    first, late_weight = lax.optimization_barrier((lay(place, place_array, first), weight))
    met_1, second, held = lax.optimization_barrier(
        (met_rows(place, first), to_planes(place, second), fetch(late_weight))
    )

    def sent(parts):
        return sends(place, "z", [parts[0], *parts])[1:]

    def swapped(part):
        return place.send(part, lambda z, a, b: (z, a, b ^ 1))

    own_1, parts_1 = project(place, place_array, [met_1, [swapped(part) for part in met_1]], held)
    second = lay(place, place_array, second)
    size, here, toward = place.along("a")
    order_2 = [0, size - 1, *range(1, size - 1)]
    last = place.send(second, toward(size - 1))
    own_1, parts_1, late_weight = lax.optimization_barrier((own_1, parts_1, weight))
    parts_1 = sent(parts_1)

    def second_projected(weight, values, last):
        met = [place.send(values, toward(step)) for step in range(1, size - 1)]
        values, met[0] = lax.optimization_barrier((values, met[0]))
        early = swapped(jnp.concatenate([values, last], 0))
        late = swapped(jnp.concatenate(met, 0))
        return project(place, place_array, [[values, last, *met], [early, late]], fetch(weight))

    own_2, parts_2 = in_one(place, second_projected, (late_weight, second, last))
    own_1, own_2 = lax.optimization_barrier((own_1, own_2))
    parts_2 = sent(parts_2)
    norm_1, packed_1, scale_1, *grams = normalize_parts(
        place, place_array, own_1, parts_1, [*range(n)]
    )
    met_1 = in_one(place, lambda *grams: first_rows(place, place_array, grams), grams)
    met_1 = sends(place, "z", met_1)
    own_2, parts_2, met_1 = lax.optimization_barrier((own_2, parts_2, met_1))
    norm_2, packed_2, scale_2, *grams, coeff = normalize_parts(
        place, place_array, own_2, parts_2, order_2, norm_1
    )
    height, batch = met_1[0].shape
    (rows_1,) = local(rows_kernel, place_array, met_1, [((height, batch), BF16)], "rows")
    met_2 = plane_rows(place, place_array, grams)
    rows = met_2[0].shape[0]
    (part,) = local(
        functools.partial(code_kernel, n=n),
        place_array,
        (*met_2, rows_1),
        [((folded_shape(rows, batch)[0] + height * KEPT, batch // KEPT), BF16)],
        "code",
    )
    (part,) = local(
        functools.partial(finish_kernel, n=n, k=k),
        place_array,
        sends(place, "z", [part] * n),
        [((2 * rows, batch), BF16)],
        "finish",
    )
    grams = sends(place, "a", [part] * n)
    grams += [place.send(part, lambda z, a, b: (z, a, b ^ 1)) for part in grams]
    first, *others, share, grams = gradient(
        place,
        place_array,
        grams,
        (packed_1, packed_2),
        (norm_1, norm_2),
        (scale_1, scale_2),
        coeff,
    )
    out_1, out_2 = local(
        functools.partial(place_kernel, n=n),
        place_array,
        [first, *sends(place, "z", [first, *others[::-1]])[:0:-1]],
        [(h_first.shape, BF16)] * 2,
        "place",
    )
    (loss,) = local(loss_kernel, place_array, (grams, share), [((1, 1), F32)], "loss")
    return (out_1, out_2, loss.reshape(()))


def plain(place, h_first, h_second, weight):
    n, k, z, a, b = place.n, place.k, place.z, place.a, place.b
    rows, width = h_first.shape
    batch = rows * n
    columns = weight.shape[1] // n
    weight_parts = weight.reshape(k, width, n * columns)
    zs = []
    for values in (h_first, h_second):
        moved = place.send(values, lambda z, a, b: (a, z, b))
        own = jnp.concatenate(met_rows(place, moved), 0)
        total = jnp.dot(own, pick(weight_parts, b), preferred_element_type=F32)
        for step in range(1, k):
            other = place.send(own, lambda z, a, b, s=step: (z, a, b ^ s))
            total += jnp.dot(other, pick(weight_parts, b ^ step), preferred_element_type=F32)
        cut = total.reshape(batch, n, columns).transpose(1, 0, 2)
        whole = tree_sum(exchange(place, "z", cut)).reshape(n, rows, columns)
        zs.append(jnp.concatenate(ordered([whole[i] for i in range(n)], a), 0))
    normed, scales = [], []
    for values in zs:
        mean = jnp.sum(values, 0) / batch
        scale = lax.rsqrt(jnp.sum(values * values, 0) / batch - mean * mean + bn_eps)
        normed.append((values - mean) * scale)
        scales.append(scale)
    diag = jnp.sum(normed[0] * normed[1], 0) / batch
    packed = [values.astype(BF16) for values in normed]
    dims = (((1,), (1,)), ((), ()))
    grams = []
    for values in packed:
        gram = lax.dot_general(values, values, dims, preferred_element_type=F32)
        grams.append(plain_gram(place, gram))
    frob = jnp.sum(grams[0].astype(F32) * grams[1].astype(F32)) / (batch * batch)
    coeff = 2.0 * ((1.0 - off_weight) * diag - 1.0)
    factor = 2.0 * off_weight / batch
    outs = []
    for view in range(2):
        grad = (
            factor * jnp.dot(grams[1 - view], packed[view], preferred_element_type=F32)
            + coeff * normed[1 - view]
        )
        first = jnp.sum(grad, 0) / batch
        second = jnp.sum(grad * normed[view], 0) / batch
        out = (scales[view] * (grad - first - normed[view] * second)).astype(BF16)
        parts = exchange(place, "z", out.reshape(n, rows, columns))
        outs.append(jnp.concatenate(ordered(parts, z), 1))
    share = jnp.sum((1.0 - diag) ** 2) - off_weight * jnp.sum(diag * diag)
    loss = (lax.psum(share, ("dp", "mp")) + off_weight * frob) / D
    return (outs[0], outs[1], loss)


def per_device(h_first, h_second, weight):
    place = Place()
    columns = weight.shape[1] // place.n
    fits = columns % 128 == 0 and place.n == 4 and place.k == 2
    return (with_kernels if fits else plain)(place, h_first, h_second, weight)


def solution(mesh):
    in_specs = (P("dp", "mp"), P("dp", "mp"), P("dp", "mp"))
    out_specs = (P("dp", "mp"), P("dp", "mp"), P())
    return jax.shard_map(
        per_device, mesh=mesh, in_specs=in_specs, out_specs=out_specs, check_vma=False
    )
```

```python
import functools

import jax
import jax.numpy as jnp
from jax import lax
from jax.experimental import pallas as pl
from jax.experimental.pallas import tpu as pltpu
from jax.sharding import PartitionSpec as P

D = 8192


off_weight = 0.0051
bn_eps = 1e-05

F32 = jnp.float32
BF16 = jnp.bfloat16
VMEM_BYTES = 16 * 1024 * 1024
POWERS = 240
HIGHEST = 128 * POWERS - 1
SCALE_ROWS = 16


class Place:
    def __init__(self):
        self.n = lax.axis_size("dp")
        self.k = lax.axis_size("mp") // self.n
        self.z = lax.axis_index("dp")
        self.a = lax.axis_index("mp") // self.k
        self.b = lax.axis_index("mp") % self.k

    def send(self, value, target):
        n, k = self.n, self.k
        pairs = []
        for z in range(n):
            for a in range(n):
                for b in range(k):
                    to_z, to_a, to_b = target(z, a, b)
                    pairs.append(((z * n + a) * k + b, (to_z * n + to_a) * k + to_b))
        return lax.ppermute(value, ("dp", "mp"), pairs)

    def along(self, axis):
        if axis == "z":
            return self.n, self.z, lambda step: lambda z, a, b: (z ^ step, a, b)
        if axis == "a":
            return self.n, self.a, lambda step: lambda z, a, b: (z, a ^ step, b)
        return self.k, self.b, lambda step: lambda z, a, b: (z, a, b ^ step)


def ordered(parts, place):
    bit = 1
    while bit < len(parts):
        odd = (place & bit) != 0
        parts = [jnp.where(odd, parts[i ^ bit], parts[i]) for i in range(len(parts))]
        bit *= 2
    return parts


def tree_sum(parts):
    while len(parts) > 1:
        parts = [parts[i] + parts[i + 1] for i in range(0, len(parts), 2)]
    return parts[0]


def pick(value, index):
    return lax.dynamic_index_in_dim(value, index, 0, keepdims=False)


def exchange(place, axis, value, few=False):
    size, here, toward = place.along(axis)
    return sends(place, axis, [pick(value, here ^ step) for step in range(size)], few)


def sends(place, axis, parts, few=False):
    size, here, toward = place.along(axis)
    met = {0: parts[0]}
    order = [*range(1, size)] if few else [*range(size - 1, 0, -1)]
    for i, step in enumerate(order):
        part = parts[step]
        if few and i >= 2:
            met[order[i - 2]], part = lax.optimization_barrier((met[order[i - 2]], part))
        met[step] = place.send(part, toward(step))
    return [met[step] for step in range(size)]


def reduce_scatter(place, axis, value, few=False):
    size, here, toward = place.along(axis)
    value = value.reshape((size, value.shape[0] // size) + value.shape[1:])
    return tree_sum(exchange(place, axis, value, few))


def gather(place, axis, value, few=False):
    size, here, toward = place.along(axis)
    parts = sends(place, axis, [value] * size, few)
    return jnp.concatenate(ordered(parts, here), 0)


BLOCKS = 4
KEPT = 3


def folded(values):
    width = values.shape[1] // KEPT
    return jnp.concatenate([values[:, i * width : (i + 1) * width] for i in range(KEPT)], 0)


def unfolded(values):
    height = values.shape[0] // KEPT
    return jnp.concatenate([values[i * height : (i + 1) * height] for i in range(KEPT)], 1)


def folded_shape(rows, columns):
    return (rows * KEPT + SCALE_ROWS, columns // KEPT)


def halve_kernel(place_ref, kept_ref, met_ref, *outs, n):
    height = kept_ref.shape[0] // n
    width = kept_ref.shape[1] // BLOCKS
    for step, out in enumerate(outs):
        block = place_ref[1] ^ step
        at = pl.ds(pl.multiple_of(block * height, height), height)
        block = (place_ref[2] * n + block) // (2 * n // BLOCKS)
        total = []
        for i in range(KEPT):
            cut = pl.ds(pl.multiple_of(lax.rem(block + i, BLOCKS) * width, width), width)
            total.append(kept_ref[at, cut] + met_ref[at, cut])
        total = jnp.concatenate(total, 1)
        if step == 0:
            out[...] = total
        else:
            encode(folded(total), out)


def plane_sum(met):
    return tree_sum([met[0][...]] + [unfolded(decode(ref, 1)[0]) for ref in met[1:]])


def plane_kernel(place_ref, *refs, n):
    met, outs, whole_ref = refs[:n], refs[n:-1], refs[-1]
    whole_ref[...] = plane_sum(met)
    height = outs[0].shape[0]
    for step, out in enumerate(outs):
        at = pl.ds(pl.multiple_of((place_ref[0] ^ step) * height, height), height)
        if step == 0:
            out[...] = whole_ref[at, :]
        else:
            encode(folded(whole_ref[at, :]), out)


def rows_kernel(place_ref, *refs):
    refs[-1][...] = plane_sum(refs[:-1]).astype(BF16)


def code_kernel(place_ref, *refs, n):
    met, rows_ref, out_ref = refs[:n], refs[n], refs[n + 1]
    total = folded(plane_sum(met))
    coded = total.shape[0] + SCALE_ROWS
    encode(total, out_ref.at[:coded])
    out_ref[coded:] = folded(rows_ref[...])


def finish_kernel(place_ref, *refs, n, k):
    out_ref = refs[-1]
    height = out_ref.shape[0] // 2
    coded, few = height * KEPT + SCALE_ROWS, height // n
    met = []
    for step in range(n):
        at = pl.ds(pl.multiple_of((place_ref[0] ^ step) * few, few), few)
        out_ref[at, :] = unfolded(refs[step][coded:])
        met += decode(refs[step].at[:coded], 1)
    total = unfolded(tree_sum(met))
    last = (place_ref[1] == n - 1) & (place_ref[2] == k - 1)
    start = 2 * (total.shape[1] // KEPT)
    edge = total[-8:, start:]
    row = lax.broadcasted_iota(jnp.int32, edge.shape, 0)
    column = lax.broadcasted_iota(jnp.int32, edge.shape, 1)
    taken = (row == 7) & last
    whole = jnp.sum(jnp.where(taken & (column == 0), edge, 0.0), keepdims=True)
    high = whole.astype(BF16).astype(F32)
    middle = (whole - high).astype(BF16).astype(F32)
    three = jnp.where(column == 0, high, jnp.where(column == 1, middle, whole - high - middle))
    edge = jnp.where(taken & (column < 3), three, edge)
    edge = jnp.concatenate([total[-8:, :start], edge], 1)
    out_ref[height:] = jnp.concatenate([total[:-8], edge], 0).astype(BF16)


def local(kernel, place_array, args, shapes, name, pinned=False, **more):
    kind = pltpu.VMEM if pinned else jax.ShapeDtypeStruct
    space = pl.BlockSpec(memory_space=pltpu.VMEM)
    return pl.pallas_call(
        kernel,
        in_specs=[pl.BlockSpec(memory_space=pltpu.SMEM)] + [space] * len(args),
        out_specs=[space] * len(shapes),
        out_shape=[kind(shape, dtype) for shape, dtype in shapes],
        compiler_params=pltpu.CompilerParams(vmem_limit_bytes=VMEM_BYTES // 2),
        name=name,
        **more,
    )(place_array, *args)


def plane_rows(place, place_array, grams, few=False):
    half, batch = grams[0].shape
    kept, other = grams
    other = place.send(other, lambda z, a, b: (z, a, b ^ 1))
    height, batch = half // place.n, batch * KEPT // BLOCKS
    parts = local(
        functools.partial(halve_kernel, n=place.n),
        place_array,
        (kept, other),
        [((height, batch), F32)] + [(folded_shape(height, batch), BF16)] * (place.n - 1),
        "halve",
    )
    return sends(place, "a", parts, few)


def first_rows(place, place_array, grams):
    parts = plane_rows(place, place_array, grams, True)
    height, batch = parts[0].shape
    few = height // place.n
    return local(
        functools.partial(plane_kernel, n=place.n),
        place_array,
        parts,
        [((few, batch), F32)] + [(folded_shape(few, batch), BF16)] * (place.n - 1),
        "plane",
        scratch_shapes=[pltpu.VMEM((height, batch), F32)],
    )


def in_one(place, run, args):
    shapes = jax.eval_shape(run, *args)
    return lax.cond(
        place.z < place.n,
        run,
        lambda *args: jax.tree.map(lambda leaf: jnp.zeros(leaf.shape, leaf.dtype), shapes),
        *args,
    )


def plain_gram(place, part):
    for axis in ("b", "a", "z"):
        part = reduce_scatter(place, axis, part)
    part = part.astype(BF16)
    for axis in ("z", "a", "b"):
        part = gather(place, axis, part)
    return part


def lay_kernel(place_ref, *refs, n):
    parts, outs = [refs[0], *refs[n - 1 : 0 : -1]], refs[n:]
    few = parts[0].shape[0] // len(outs)
    for step in range(n):
        at = pl.ds(pl.multiple_of((place_ref[0] ^ step) * few, few), few)
        for i, out in enumerate(outs):
            out[at, :] = parts[step][i * few : (i + 1) * few, :]


def fetch_kernel(weight_ref, held_ref, arrived):
    copy = pltpu.make_async_copy(weight_ref, held_ref, arrived)
    copy.start()
    copy.wait()


def fetch(weight):
    return pl.pallas_call(
        fetch_kernel,
        in_specs=[pl.BlockSpec(memory_space=pl.ANY)],
        out_specs=pl.BlockSpec(memory_space=pltpu.VMEM),
        out_shape=pltpu.VMEM(weight.shape, BF16),
        scratch_shapes=[pltpu.SemaphoreType.DMA],
        compiler_params=pltpu.CompilerParams(vmem_limit_bytes=VMEM_BYTES // 2),
        cost_estimate=pl.CostEstimate(flops=0, bytes_accessed=4 * weight.size, transcendentals=0),
        name="fetch",
    )(pltpu.with_memory_space_constraint(weight, pltpu.HBM))


def to_columns(place, view):
    rows, width = view.shape
    return exchange(place, "a", view.reshape(place.n, rows // place.n, width))


def turn_kernel(place_ref, *refs, n):
    turned = ordered([ref[...] for ref in refs[:n]], place_ref[1] ^ place_ref[0])
    for ref, part in zip(refs[n:], [turned[0], *turned[:0:-1]]):
        ref[...] = part


def to_planes(place, place_array, parts, kernel):
    if kernel:
        parts = local(
            functools.partial(turn_kernel, n=place.n),
            place_array,
            parts,
            [(parts[0].shape, BF16)] * place.n,
            "turn",
            pinned=True,
        )
        parts = [parts[0], *parts[:0:-1]]
    else:
        parts = ordered(parts, place.a ^ place.z)
    return sends(place, "z", parts)


def lay(place, place_array, parts):
    rows, width = parts[0].shape
    (laid,) = local(
        functools.partial(lay_kernel, n=place.n),
        place_array,
        [parts[0], *parts[:0:-1]],
        [((rows * place.n, width), BF16)],
        "lay",
        pinned=True,
    )
    return laid


def met_rows(place, values, few=False):
    return sends(place, "a", [values] * place.n, few)


def project_kernel(place_ref, *refs, counts, n, k):
    met = refs[: sum(counts)]
    weight_ref, own_ref, *coded = refs[sum(counts) :]
    width = met[0].shape[1]
    columns = own_ref.shape[1]
    values = []
    for count in counts:
        values.append(jnp.concatenate([ref[...] for ref in met[:count]], 0))
        met = met[count:]
    for step in [*range(n - 1, 0, -1), 0]:
        at = pl.ds(pl.multiple_of((place_ref[0] ^ step) * columns, columns), columns)
        total = 0.0
        for i in range(k):
            rows = pl.ds(pl.multiple_of((place_ref[2] ^ i) * width, width), width)
            total += jnp.dot(values[i], weight_ref[rows, at], preferred_element_type=F32)
        if step == 0:
            own_ref[...] = total
        else:
            encode(total, coded[n - 1 - step])


def encode(total, coded_ref):
    rows = total.shape[0]
    top = jnp.max(jnp.abs(total), 0, keepdims=True)
    top = jnp.maximum(top * (1.0 + 1.0 / 128.0), 1e-30).astype(BF16)
    coded_ref[rows:] = jnp.broadcast_to(top, (SCALE_ROWS, total.shape[1]))
    whole = jnp.floor(jnp.abs(total) * (HIGHEST / top.astype(F32)) + 0.5)
    power = jnp.floor(whole * (1.0 / 128.0))
    word = (1.0 + (whole * (1.0 / 128.0) - power)) * jnp.exp2(power - POWERS // 2)
    coded_ref[:rows] = jnp.where(total < 0.0, -word, word).astype(BF16)


def decode(coded_ref, count):
    rows = coded_ref.shape[0] - SCALE_ROWS
    scale = coded_ref[rows:].astype(F32)[:1] * (1.0 / HIGHEST)
    height = rows // count
    blocks = []
    for i in range(count):
        word = coded_ref[i * height : (i + 1) * height].astype(F32)
        size = jnp.abs(word)
        power = jnp.floor(jnp.log(size) * 1.4426950408889634 + 0.002)
        part = jnp.floor(size * jnp.exp2(-power) * 128.0 + 0.5)
        whole = (power + (POWERS // 2 - 1)) * 128.0 + part
        blocks.append(jnp.where(word < 0.0, -whole, whole) * scale)
    return blocks


def project(place, place_array, met, held):
    n, k = place.n, place.k
    rows, width = met[0][0].shape
    batch, columns = rows * n, held.shape[1] // n
    counts = [len(parts) for parts in met]
    met = [part for parts in met for part in parts]
    coded = batch + SCALE_ROWS
    out_shape = [jax.ShapeDtypeStruct((batch, columns), F32)]
    out_shape += [jax.ShapeDtypeStruct((coded, columns), BF16)] * (n - 1)
    space = pl.BlockSpec(memory_space=pltpu.VMEM)
    own, *parts = pl.pallas_call(
        functools.partial(project_kernel, counts=counts, n=n, k=k),
        in_specs=[pl.BlockSpec(memory_space=pltpu.SMEM)]
        + [space] * (len(met) + 1),
        out_specs=[space] * n,
        out_shape=out_shape,
        compiler_params=pltpu.CompilerParams(vmem_limit_bytes=VMEM_BYTES),
        cost_estimate=pl.CostEstimate(
            flops=2 * batch * k * width * n * columns,
            bytes_accessed=2 * k * width * (batch + n * columns) + 3 * n * batch * columns,
            transcendentals=0,
        ),
        name="project",
    )(place_array, *met, pltpu.with_memory_space_constraint(held, pltpu.VMEM))
    return own, parts[::-1]


def normalize_kernel(place_ref, *refs, n, k, order, second):
    own_ref, parts = refs[0], refs[n - 1 : 0 : -1]
    refs = refs[n:]
    if second:
        other_ref, refs = refs[0], refs[1:]
    norm_ref, packed_ref, scale_ref = refs[:3]
    grams = refs[3 : 3 + k]
    batch, columns = own_ref.shape
    height = batch // n
    met = [[own_ref[i * height : (i + 1) * height] for i in range(n)]]
    for step in range(1, n):
        met.append(decode(parts[step - 1], n))
    blocks = [tree_sum([met[step][i] for step in range(n)]) for i in range(n)]
    total = tree_sum([jnp.sum(block, 0, keepdims=True) for block in blocks])
    squares = tree_sum([jnp.sum(block * block, 0, keepdims=True) for block in blocks])
    mean = total / batch
    scale = lax.rsqrt(squares / batch - mean * mean + bn_eps)
    scale_ref[...] = scale
    rows, few = batch // n, batch // (n * n)
    for i, block in enumerate(blocks):
        normed = (block - mean) * scale
        for first in range(0, height, few):
            step, plane = divmod((i * height + first) // few, n)
            at = pl.multiple_of(plane * rows + (place_ref[1] ^ order[step]) * few, few)
            norm_ref[pl.ds(at, few), :] = normed[first : first + few]
            packed_ref[pl.ds(at, few), :] = normed[first : first + few].astype(BF16)
    dims = (((1,), (1,)), ((), ()))
    packed = packed_ref[...]
    size = batch // k
    for i in range(k):
        at = pl.multiple_of((place_ref[2] ^ i) * size, size)
        gram = lax.dot_general(packed_ref[pl.ds(at, size), :], packed, dims, preferred_element_type=F32)
        grams[i][...] = gram
    if second:
        coeff_ref = refs[3 + k]
        diag = jnp.sum(norm_ref[...] * other_ref[...], 0, keepdims=True) / batch
        coeff_ref[...] = 2.0 * ((1.0 - off_weight) * diag - 1.0)
        share = jnp.sum((1.0 - diag) ** 2 - off_weight * diag * diag, 1, keepdims=True)
        for i in range(k):

            @pl.when((place_ref[2] ^ i) == k - 1)
            def _():
                at = batch // BLOCKS
                row = grams[i][size - 8 :, at : at + 128]
                first = (lax.broadcasted_iota(jnp.int32, row.shape, 0) == 7) & (
                    lax.broadcasted_iota(jnp.int32, row.shape, 1) == 0
                )
                grams[i][size - 8 :, at : at + 128] = jnp.where(first, share, row)


def normalize_parts(place, place_array, own, parts, order, other=None):
    n, k = place.n, place.k
    batch, columns = own.shape
    second = other is not None
    out_shape = [
        jax.ShapeDtypeStruct((batch, columns), F32),
        jax.ShapeDtypeStruct((batch, columns), BF16),
        jax.ShapeDtypeStruct((1, columns), F32),
    ] + [jax.ShapeDtypeStruct((batch // k, batch), F32)] * k
    if second:
        out_shape.append(jax.ShapeDtypeStruct((1, columns), F32))
    args = [own, *parts[::-1]] + ([other] if second else [])
    space = pl.BlockSpec(memory_space=pltpu.VMEM)
    return pl.pallas_call(
        functools.partial(normalize_kernel, n=n, k=k, order=order, second=second),
        in_specs=[pl.BlockSpec(memory_space=pltpu.SMEM)] + [space] * len(args),
        out_specs=[space] * len(out_shape),
        out_shape=out_shape,
        compiler_params=pltpu.CompilerParams(vmem_limit_bytes=VMEM_BYTES // 2),
        cost_estimate=pl.CostEstimate(
            flops=2 * batch * batch * columns,
            bytes_accessed=16 * batch * columns + 4 * batch * batch,
            transcendentals=0,
        ),
        name="normalize",
    )(place_array, *args)


def gradient_kernel(place_ref, *refs, n, k):
    grams, refs = refs[: n * k], refs[n * k :]
    packed, norms, scales, coeff_ref, refs = refs[0:2], refs[2:4], refs[4:6], refs[6], refs[7:]
    outs = [refs[0], *refs[n - 1 : 0 : -1]]
    share_ref, gram_ref, whole_ref = refs[n:]
    batch, columns = norms[0].shape
    height = grams[0].shape[0] // 2
    width = batch // BLOCKS
    for i in range(k):
        for step in range(n):
            block = (place_ref[2] ^ i) * n + (place_ref[1] ^ step)
            at = pl.ds(pl.multiple_of(block * height, height), height)
            block = block // (2 * n // BLOCKS)
            for j in range(KEPT):
                to = pl.ds(pl.multiple_of(lax.rem(block + j, BLOCKS) * width, width), width)
                for view in range(2):
                    gram_ref[view, at, to] = grams[i * n + step][
                        view * height : (view + 1) * height, j * width : (j + 1) * width
                    ]
    blocks = [slice(i * width, (i + 1) * width) for i in range(BLOCKS)]
    for view in range(2):
        for i in range(BLOCKS):
            other = gram_ref[view, blocks[i - 1], blocks[i]].astype(F32).T
            gram_ref[view, blocks[i], blocks[i - 1]] = other.astype(BF16)
    tail = gram_ref[1, blocks[3], blocks[1]].astype(F32)
    row = lax.broadcasted_iota(jnp.int32, tail.shape, 0)
    column = lax.broadcasted_iota(jnp.int32, tail.shape, 1)
    taken = (row == width - 1) & (column < 3)
    mirror = gram_ref[1, blocks[1], blocks[3]].astype(F32).T
    share = jnp.sum(jnp.where(taken, tail, 0.0), keepdims=True)
    gram_ref[1, blocks[3], blocks[1]] = jnp.where(taken, mirror, tail).astype(BF16)
    factor = 2.0 * off_weight / batch
    rows = batch // n
    for view in (1, 0):
        norm = norms[view][...]
        grad = (
            factor * jnp.dot(gram_ref[1 - view], packed[view][...], preferred_element_type=F32)
            + coeff_ref[...] * norms[1 - view][...]
        )
        first = jnp.sum(grad, 0, keepdims=True) / batch
        second = jnp.sum(grad * norm, 0, keepdims=True) / batch
        whole_ref[view] = (scales[view][...] * (grad - first - norm * second)).astype(BF16)
        for step in range(n):
            at = pl.multiple_of((place_ref[0] ^ step) * rows, rows)
            outs[step][view * rows : (view + 1) * rows, :] = whole_ref[view, pl.ds(at, rows), :]
    share_ref[...] = share


def loss_kernel(place_ref, gram_ref, share_ref, loss_ref):
    batch = gram_ref.shape[1]
    frob = jnp.sum(gram_ref[0].astype(F32) * gram_ref[1].astype(F32), keepdims=True)
    loss_ref[...] = (share_ref[...] + off_weight * (frob / (batch * batch))) / D


def gradient(place, place_array, grams, packed, norms, scales, coeff):
    batch, columns = norms[0].shape
    return local(
        functools.partial(gradient_kernel, n=place.n, k=place.k),
        place_array,
        (*grams, *packed, *norms, *scales, coeff),
        [((2 * batch // place.n, columns), BF16)] * place.n
        + [((1, 1), F32), ((2, batch, batch), BF16)],
        "gradient",
        scratch_shapes=[pltpu.VMEM((2, batch, columns), BF16)],
    )


def place_kernel(place_ref, *refs, n):
    parts, outs = [refs[0], *refs[n - 1 : 0 : -1]], refs[n:]
    rows, columns = parts[0].shape[0] // len(outs), parts[0].shape[1]
    for step in range(n):
        at = pl.ds(pl.multiple_of((place_ref[0] ^ step) * columns, columns), columns)
        for i, out in enumerate(outs):
            out[:, at] = parts[step][i * rows : (i + 1) * rows, :]


def with_kernels(place, h_first, h_second, weight):
    n, k, z, a, b = place.n, place.k, place.z, place.a, place.b
    place_array = jnp.stack([z, a, b]).astype(jnp.int32)
    first = to_columns(place, h_first)
    first, second = lax.optimization_barrier((to_planes(place, place_array, first, True), to_columns(place, h_second)))
    first, late_weight = lax.optimization_barrier((lay(place, place_array, first), weight))
    met_1, second, held = lax.optimization_barrier(
        (met_rows(place, first), to_planes(place, place_array, second, False), fetch(late_weight))
    )

    def sent(parts):
        return sends(place, "z", [parts[0], *parts])[1:]

    def swapped(part):
        return place.send(part, lambda z, a, b: (z, a, b ^ 1))

    own_1, parts_1 = project(place, place_array, [met_1, [swapped(part) for part in met_1]], held)
    second = lay(place, place_array, second)
    size, here, toward = place.along("a")
    order_2 = [0, size - 1, *range(1, size - 1)]
    last = place.send(second, toward(size - 1))
    own_1, parts_1, late_weight = lax.optimization_barrier((own_1, parts_1, weight))
    parts_1 = sent(parts_1)

    def second_projected(weight, values, last):
        met = [place.send(values, toward(step)) for step in range(1, size - 1)]
        values, met[0] = lax.optimization_barrier((values, met[0]))
        early = swapped(jnp.concatenate([values, last], 0))
        late = swapped(jnp.concatenate(met, 0))
        return project(place, place_array, [[values, last, *met], [early, late]], fetch(weight))

    own_2, parts_2 = in_one(place, second_projected, (late_weight, second, last))
    own_1, own_2 = lax.optimization_barrier((own_1, own_2))
    parts_2 = sent(parts_2)
    norm_1, packed_1, scale_1, *grams = normalize_parts(
        place, place_array, own_1, parts_1, [*range(n)]
    )
    met_1 = in_one(place, lambda *grams: first_rows(place, place_array, grams), grams)
    met_1 = sends(place, "z", met_1)
    own_2, parts_2, met_1 = lax.optimization_barrier((own_2, parts_2, met_1))
    norm_2, packed_2, scale_2, *grams, coeff = normalize_parts(
        place, place_array, own_2, parts_2, order_2, norm_1
    )
    height, batch = met_1[0].shape
    (rows_1,) = local(rows_kernel, place_array, met_1, [((height, batch), BF16)], "rows")
    met_2 = plane_rows(place, place_array, grams)
    rows = met_2[0].shape[0]
    (part,) = local(
        functools.partial(code_kernel, n=n),
        place_array,
        (*met_2, rows_1),
        [((folded_shape(rows, batch)[0] + height * KEPT, batch // KEPT), BF16)],
        "code",
    )
    (part,) = local(
        functools.partial(finish_kernel, n=n, k=k),
        place_array,
        sends(place, "z", [part] * n),
        [((2 * rows, batch), BF16)],
        "finish",
    )
    grams = sends(place, "a", [part] * n)
    grams += [place.send(part, lambda z, a, b: (z, a, b ^ 1)) for part in grams]
    first, *others, share, grams = gradient(
        place,
        place_array,
        grams,
        (packed_1, packed_2),
        (norm_1, norm_2),
        (scale_1, scale_2),
        coeff,
    )
    out_1, out_2 = local(
        functools.partial(place_kernel, n=n),
        place_array,
        [first, *sends(place, "z", [first, *others[::-1]])[:0:-1]],
        [(h_first.shape, BF16)] * 2,
        "place",
    )
    (loss,) = local(loss_kernel, place_array, (grams, share), [((1, 1), F32)], "loss")
    return (out_1, out_2, loss.reshape(()))


def plain(place, h_first, h_second, weight):
    n, k, z, a, b = place.n, place.k, place.z, place.a, place.b
    rows, width = h_first.shape
    batch = rows * n
    columns = weight.shape[1] // n
    weight_parts = weight.reshape(k, width, n * columns)
    zs = []
    for values in (h_first, h_second):
        moved = place.send(values, lambda z, a, b: (a, z, b))
        own = jnp.concatenate(met_rows(place, moved), 0)
        total = jnp.dot(own, pick(weight_parts, b), preferred_element_type=F32)
        for step in range(1, k):
            other = place.send(own, lambda z, a, b, s=step: (z, a, b ^ s))
            total += jnp.dot(other, pick(weight_parts, b ^ step), preferred_element_type=F32)
        cut = total.reshape(batch, n, columns).transpose(1, 0, 2)
        whole = tree_sum(exchange(place, "z", cut)).reshape(n, rows, columns)
        zs.append(jnp.concatenate(ordered([whole[i] for i in range(n)], a), 0))
    normed, scales = [], []
    for values in zs:
        mean = jnp.sum(values, 0) / batch
        scale = lax.rsqrt(jnp.sum(values * values, 0) / batch - mean * mean + bn_eps)
        normed.append((values - mean) * scale)
        scales.append(scale)
    diag = jnp.sum(normed[0] * normed[1], 0) / batch
    packed = [values.astype(BF16) for values in normed]
    dims = (((1,), (1,)), ((), ()))
    grams = []
    for values in packed:
        gram = lax.dot_general(values, values, dims, preferred_element_type=F32)
        grams.append(plain_gram(place, gram))
    frob = jnp.sum(grams[0].astype(F32) * grams[1].astype(F32)) / (batch * batch)
    coeff = 2.0 * ((1.0 - off_weight) * diag - 1.0)
    factor = 2.0 * off_weight / batch
    outs = []
    for view in range(2):
        grad = (
            factor * jnp.dot(grams[1 - view], packed[view], preferred_element_type=F32)
            + coeff * normed[1 - view]
        )
        first = jnp.sum(grad, 0) / batch
        second = jnp.sum(grad * normed[view], 0) / batch
        out = (scales[view] * (grad - first - normed[view] * second)).astype(BF16)
        parts = exchange(place, "z", out.reshape(n, rows, columns))
        outs.append(jnp.concatenate(ordered(parts, z), 1))
    share = jnp.sum((1.0 - diag) ** 2) - off_weight * jnp.sum(diag * diag)
    loss = (lax.psum(share, ("dp", "mp")) + off_weight * frob) / D
    return (outs[0], outs[1], loss)


def per_device(h_first, h_second, weight):
    place = Place()
    columns = weight.shape[1] // place.n
    fits = columns % 128 == 0 and place.n == 4 and place.k == 2
    return (with_kernels if fits else plain)(place, h_first, h_second, weight)


def solution(mesh):
    in_specs = (P("dp", "mp"), P("dp", "mp"), P("dp", "mp"))
    out_specs = (P("dp", "mp"), P("dp", "mp"), P())
    return jax.shard_map(
        per_device, mesh=mesh, in_specs=in_specs, out_specs=out_specs, check_vma=False
    )
```

```python
import functools

import jax
import jax.numpy as jnp
from jax import lax
from jax.experimental import pallas as pl
from jax.experimental.pallas import tpu as pltpu
from jax.sharding import PartitionSpec as P

D = 8192


off_weight = 0.0051
bn_eps = 1e-05

F32 = jnp.float32
BF16 = jnp.bfloat16
VMEM_BYTES = 16 * 1024 * 1024
POWERS = 240
HIGHEST = 128 * POWERS - 1
SCALE_ROWS = 16


class Place:
    def __init__(self):
        self.n = lax.axis_size("dp")
        self.k = lax.axis_size("mp") // self.n
        self.z = lax.axis_index("dp")
        self.a = lax.axis_index("mp") // self.k
        self.b = lax.axis_index("mp") % self.k

    def send(self, value, target):
        n, k = self.n, self.k
        pairs = []
        for z in range(n):
            for a in range(n):
                for b in range(k):
                    to_z, to_a, to_b = target(z, a, b)
                    pairs.append(((z * n + a) * k + b, (to_z * n + to_a) * k + to_b))
        return lax.ppermute(value, ("dp", "mp"), pairs)

    def along(self, axis):
        if axis == "z":
            return self.n, self.z, lambda step: lambda z, a, b: (z ^ step, a, b)
        if axis == "a":
            return self.n, self.a, lambda step: lambda z, a, b: (z, a ^ step, b)
        return self.k, self.b, lambda step: lambda z, a, b: (z, a, b ^ step)


def ordered(parts, place):
    bit = 1
    while bit < len(parts):
        odd = (place & bit) != 0
        parts = [jnp.where(odd, parts[i ^ bit], parts[i]) for i in range(len(parts))]
        bit *= 2
    return parts


def tree_sum(parts):
    while len(parts) > 1:
        parts = [parts[i] + parts[i + 1] for i in range(0, len(parts), 2)]
    return parts[0]


def pick(value, index):
    return lax.dynamic_index_in_dim(value, index, 0, keepdims=False)


def exchange(place, axis, value, few=False):
    size, here, toward = place.along(axis)
    return sends(place, axis, [pick(value, here ^ step) for step in range(size)], few)


def sends(place, axis, parts, few=False):
    size, here, toward = place.along(axis)
    met = {0: parts[0]}
    order = [size - 1, *range(1, size - 1)] if few else [*range(size - 1, 0, -1)]
    for i, step in enumerate(order):
        part = parts[step]
        if few and i >= 2:
            met[order[i - 2]], part = lax.optimization_barrier((met[order[i - 2]], part))
        met[step] = place.send(part, toward(step))
    return [met[step] for step in range(size)]


def reduce_scatter(place, axis, value, few=False):
    size, here, toward = place.along(axis)
    value = value.reshape((size, value.shape[0] // size) + value.shape[1:])
    return tree_sum(exchange(place, axis, value, few))


def gather(place, axis, value, few=False):
    size, here, toward = place.along(axis)
    parts = sends(place, axis, [value] * size, few)
    return jnp.concatenate(ordered(parts, here), 0)


BLOCKS = 4
KEPT = 3


def folded(values):
    width = values.shape[1] // KEPT
    return jnp.concatenate([values[:, i * width : (i + 1) * width] for i in range(KEPT)], 0)


def unfolded(values):
    height = values.shape[0] // KEPT
    return jnp.concatenate([values[i * height : (i + 1) * height] for i in range(KEPT)], 1)


def folded_shape(rows, columns):
    return (rows * KEPT + SCALE_ROWS, columns // KEPT)


def halve_kernel(place_ref, kept_ref, met_ref, *outs, n):
    height = kept_ref.shape[0] // n
    width = kept_ref.shape[1] // BLOCKS
    for step, out in enumerate(outs):
        block = place_ref[1] ^ step
        at = pl.ds(pl.multiple_of(block * height, height), height)
        block = (place_ref[2] * n + block) // (2 * n // BLOCKS)
        total = []
        for i in range(KEPT):
            cut = pl.ds(pl.multiple_of(lax.rem(block + i, BLOCKS) * width, width), width)
            total.append(kept_ref[at, cut] + met_ref[at, cut])
        total = jnp.concatenate(total, 1)
        if step == 0:
            out[...] = total
        else:
            encode(folded(total), out)


def plane_sum(met):
    return tree_sum([met[0][...]] + [unfolded(decode(ref, 1)[0]) for ref in met[1:]])


def plane_kernel(place_ref, *refs, n):
    met, outs, whole_ref = refs[:n], refs[n:-1], refs[-1]
    whole_ref[...] = plane_sum(met)
    height = outs[0].shape[0]
    for step, out in enumerate(outs):
        at = pl.ds(pl.multiple_of((place_ref[0] ^ step) * height, height), height)
        if step == 0:
            out[...] = whole_ref[at, :]
        else:
            encode(folded(whole_ref[at, :]), out)


def rows_kernel(place_ref, *refs):
    refs[-1][...] = plane_sum(refs[:-1]).astype(BF16)


def code_kernel(place_ref, *refs, n):
    met, rows_ref, out_ref = refs[:n], refs[n], refs[n + 1]
    total = folded(plane_sum(met))
    coded = total.shape[0] + SCALE_ROWS
    encode(total, out_ref.at[:coded])
    out_ref[coded:] = folded(rows_ref[...])


def finish_kernel(place_ref, *refs, n, k):
    out_ref = refs[-1]
    height = out_ref.shape[0] // 2
    coded, few = height * KEPT + SCALE_ROWS, height // n
    met = []
    for step in range(n):
        at = pl.ds(pl.multiple_of((place_ref[0] ^ step) * few, few), few)
        out_ref[at, :] = unfolded(refs[step][coded:])
        met += decode(refs[step].at[:coded], 1)
    total = unfolded(tree_sum(met))
    last = (place_ref[1] == n - 1) & (place_ref[2] == k - 1)
    start = 2 * (total.shape[1] // KEPT)
    edge = total[-8:, start:]
    row = lax.broadcasted_iota(jnp.int32, edge.shape, 0)
    column = lax.broadcasted_iota(jnp.int32, edge.shape, 1)
    taken = (row == 7) & last
    whole = jnp.sum(jnp.where(taken & (column == 0), edge, 0.0), keepdims=True)
    high = whole.astype(BF16).astype(F32)
    middle = (whole - high).astype(BF16).astype(F32)
    three = jnp.where(column == 0, high, jnp.where(column == 1, middle, whole - high - middle))
    edge = jnp.where(taken & (column < 3), three, edge)
    edge = jnp.concatenate([total[-8:, :start], edge], 1)
    out_ref[height:] = jnp.concatenate([total[:-8], edge], 0).astype(BF16)


def local(kernel, place_array, args, shapes, name, pinned=False, **more):
    kind = pltpu.VMEM if pinned else jax.ShapeDtypeStruct
    space = pl.BlockSpec(memory_space=pltpu.VMEM)
    return pl.pallas_call(
        kernel,
        in_specs=[pl.BlockSpec(memory_space=pltpu.SMEM)] + [space] * len(args),
        out_specs=[space] * len(shapes),
        out_shape=[kind(shape, dtype) for shape, dtype in shapes],
        compiler_params=pltpu.CompilerParams(vmem_limit_bytes=VMEM_BYTES // 2),
        name=name,
        **more,
    )(place_array, *args)


def plane_rows(place, place_array, grams, few=False):
    half, batch = grams[0].shape
    kept, other = grams
    other = place.send(other, lambda z, a, b: (z, a, b ^ 1))
    height, batch = half // place.n, batch * KEPT // BLOCKS
    parts = local(
        functools.partial(halve_kernel, n=place.n),
        place_array,
        (kept, other),
        [((height, batch), F32)] + [(folded_shape(height, batch), BF16)] * (place.n - 1),
        "halve",
    )
    return sends(place, "a", parts, few)


def first_rows(place, place_array, grams):
    parts = plane_rows(place, place_array, grams, True)
    height, batch = parts[0].shape
    few = height // place.n
    return local(
        functools.partial(plane_kernel, n=place.n),
        place_array,
        parts,
        [((few, batch), F32)] + [(folded_shape(few, batch), BF16)] * (place.n - 1),
        "plane",
        scratch_shapes=[pltpu.VMEM((height, batch), F32)],
    )


def in_one(place, run, args):
    shapes = jax.eval_shape(run, *args)
    return lax.cond(
        place.z < place.n,
        run,
        lambda *args: jax.tree.map(lambda leaf: jnp.zeros(leaf.shape, leaf.dtype), shapes),
        *args,
    )


def plain_gram(place, part):
    for axis in ("b", "a", "z"):
        part = reduce_scatter(place, axis, part)
    part = part.astype(BF16)
    for axis in ("z", "a", "b"):
        part = gather(place, axis, part)
    return part


def lay_kernel(place_ref, *refs, n):
    parts, outs = [refs[0], *refs[n - 1 : 0 : -1]], refs[n:]
    few = parts[0].shape[0] // len(outs)
    for step in range(n):
        at = pl.ds(pl.multiple_of((place_ref[0] ^ step) * few, few), few)
        for i, out in enumerate(outs):
            out[at, :] = parts[step][i * few : (i + 1) * few, :]


def fetch_kernel(weight_ref, held_ref, arrived):
    copy = pltpu.make_async_copy(weight_ref, held_ref, arrived)
    copy.start()
    copy.wait()


def fetch(weight):
    return pl.pallas_call(
        fetch_kernel,
        in_specs=[pl.BlockSpec(memory_space=pl.ANY)],
        out_specs=pl.BlockSpec(memory_space=pltpu.VMEM),
        out_shape=pltpu.VMEM(weight.shape, BF16),
        scratch_shapes=[pltpu.SemaphoreType.DMA],
        compiler_params=pltpu.CompilerParams(vmem_limit_bytes=VMEM_BYTES // 2),
        cost_estimate=pl.CostEstimate(flops=0, bytes_accessed=4 * weight.size, transcendentals=0),
        name="fetch",
    )(pltpu.with_memory_space_constraint(weight, pltpu.HBM))


def to_columns(place, view):
    rows, width = view.shape
    return exchange(place, "a", view.reshape(place.n, rows // place.n, width))


def turn_kernel(place_ref, *refs, n):
    turned = ordered([ref[...] for ref in refs[:n]], place_ref[1] ^ place_ref[0])
    for ref, part in zip(refs[n:], [turned[0], *turned[:0:-1]]):
        ref[...] = part


def to_planes(place, place_array, parts, kernel):
    if kernel:
        parts = local(
            functools.partial(turn_kernel, n=place.n),
            place_array,
            parts,
            [(parts[0].shape, BF16)] * place.n,
            "turn",
            pinned=True,
        )
        parts = [parts[0], *parts[:0:-1]]
    else:
        parts = ordered(parts, place.a ^ place.z)
    return sends(place, "z", parts)


def lay(place, place_array, parts):
    rows, width = parts[0].shape
    (laid,) = local(
        functools.partial(lay_kernel, n=place.n),
        place_array,
        [parts[0], *parts[:0:-1]],
        [((rows * place.n, width), BF16)],
        "lay",
        pinned=True,
    )
    return laid


def met_rows(place, values, few=False):
    return sends(place, "a", [values] * place.n, few)


def project_kernel(place_ref, *refs, counts, n, k):
    met = refs[: sum(counts)]
    weight_ref, own_ref, *coded = refs[sum(counts) :]
    width = met[0].shape[1]
    columns = own_ref.shape[1]
    values = []
    for count in counts:
        values.append(jnp.concatenate([ref[...] for ref in met[:count]], 0))
        met = met[count:]
    for step in [*range(n - 1, 0, -1), 0]:
        at = pl.ds(pl.multiple_of((place_ref[0] ^ step) * columns, columns), columns)
        total = 0.0
        for i in range(k):
            rows = pl.ds(pl.multiple_of((place_ref[2] ^ i) * width, width), width)
            total += jnp.dot(values[i], weight_ref[rows, at], preferred_element_type=F32)
        if step == 0:
            own_ref[...] = total
        else:
            encode(total, coded[n - 1 - step])


def encode(total, coded_ref):
    rows = total.shape[0]
    top = jnp.max(jnp.abs(total), 0, keepdims=True)
    top = jnp.maximum(top * (1.0 + 1.0 / 128.0), 1e-30).astype(BF16)
    coded_ref[rows:] = jnp.broadcast_to(top, (SCALE_ROWS, total.shape[1]))
    whole = jnp.floor(jnp.abs(total) * (HIGHEST / top.astype(F32)) + 0.5)
    power = jnp.floor(whole * (1.0 / 128.0))
    word = (1.0 + (whole * (1.0 / 128.0) - power)) * jnp.exp2(power - POWERS // 2)
    coded_ref[:rows] = jnp.where(total < 0.0, -word, word).astype(BF16)


def decode(coded_ref, count):
    rows = coded_ref.shape[0] - SCALE_ROWS
    scale = coded_ref[rows:].astype(F32)[:1] * (1.0 / HIGHEST)
    height = rows // count
    blocks = []
    for i in range(count):
        word = coded_ref[i * height : (i + 1) * height].astype(F32)
        size = jnp.abs(word)
        power = jnp.floor(jnp.log(size) * 1.4426950408889634 + 0.002)
        part = jnp.floor(size * jnp.exp2(-power) * 128.0 + 0.5)
        whole = (power + (POWERS // 2 - 1)) * 128.0 + part
        blocks.append(jnp.where(word < 0.0, -whole, whole) * scale)
    return blocks


def project(place, place_array, met, held):
    n, k = place.n, place.k
    rows, width = met[0][0].shape
    batch, columns = rows * n, held.shape[1] // n
    counts = [len(parts) for parts in met]
    met = [part for parts in met for part in parts]
    coded = batch + SCALE_ROWS
    out_shape = [jax.ShapeDtypeStruct((batch, columns), F32)]
    out_shape += [jax.ShapeDtypeStruct((coded, columns), BF16)] * (n - 1)
    space = pl.BlockSpec(memory_space=pltpu.VMEM)
    own, *parts = pl.pallas_call(
        functools.partial(project_kernel, counts=counts, n=n, k=k),
        in_specs=[pl.BlockSpec(memory_space=pltpu.SMEM)]
        + [space] * (len(met) + 1),
        out_specs=[space] * n,
        out_shape=out_shape,
        compiler_params=pltpu.CompilerParams(vmem_limit_bytes=VMEM_BYTES),
        cost_estimate=pl.CostEstimate(
            flops=2 * batch * k * width * n * columns,
            bytes_accessed=2 * k * width * (batch + n * columns) + 3 * n * batch * columns,
            transcendentals=0,
        ),
        name="project",
    )(place_array, *met, pltpu.with_memory_space_constraint(held, pltpu.VMEM))
    return own, parts[::-1]


def normalize_kernel(place_ref, *refs, n, k, order, second):
    own_ref, parts = refs[0], refs[n - 1 : 0 : -1]
    refs = refs[n:]
    if second:
        other_ref, refs = refs[0], refs[1:]
    norm_ref, packed_ref, scale_ref = refs[:3]
    grams = refs[3 : 3 + k]
    batch, columns = own_ref.shape
    height = batch // n
    met = [[own_ref[i * height : (i + 1) * height] for i in range(n)]]
    for step in range(1, n):
        met.append(decode(parts[step - 1], n))
    blocks = [tree_sum([met[step][i] for step in range(n)]) for i in range(n)]
    total = tree_sum([jnp.sum(block, 0, keepdims=True) for block in blocks])
    squares = tree_sum([jnp.sum(block * block, 0, keepdims=True) for block in blocks])
    mean = total / batch
    scale = lax.rsqrt(squares / batch - mean * mean + bn_eps)
    scale_ref[...] = scale
    rows, few = batch // n, batch // (n * n)
    for i, block in enumerate(blocks):
        normed = (block - mean) * scale
        for first in range(0, height, few):
            step, plane = divmod((i * height + first) // few, n)
            at = pl.multiple_of(plane * rows + (place_ref[1] ^ order[step]) * few, few)
            norm_ref[pl.ds(at, few), :] = normed[first : first + few]
            packed_ref[pl.ds(at, few), :] = normed[first : first + few].astype(BF16)
    dims = (((1,), (1,)), ((), ()))
    packed = packed_ref[...]
    size = batch // k
    for i in range(k):
        at = pl.multiple_of((place_ref[2] ^ i) * size, size)
        gram = lax.dot_general(packed_ref[pl.ds(at, size), :], packed, dims, preferred_element_type=F32)
        grams[i][...] = gram
    if second:
        coeff_ref = refs[3 + k]
        diag = jnp.sum(norm_ref[...] * other_ref[...], 0, keepdims=True) / batch
        coeff_ref[...] = 2.0 * ((1.0 - off_weight) * diag - 1.0)
        share = jnp.sum((1.0 - diag) ** 2 - off_weight * diag * diag, 1, keepdims=True)
        for i in range(k):

            @pl.when((place_ref[2] ^ i) == k - 1)
            def _():
                at = batch // BLOCKS
                row = grams[i][size - 8 :, at : at + 128]
                first = (lax.broadcasted_iota(jnp.int32, row.shape, 0) == 7) & (
                    lax.broadcasted_iota(jnp.int32, row.shape, 1) == 0
                )
                grams[i][size - 8 :, at : at + 128] = jnp.where(first, share, row)


def normalize_parts(place, place_array, own, parts, order, other=None):
    n, k = place.n, place.k
    batch, columns = own.shape
    second = other is not None
    out_shape = [
        jax.ShapeDtypeStruct((batch, columns), F32),
        jax.ShapeDtypeStruct((batch, columns), BF16),
        jax.ShapeDtypeStruct((1, columns), F32),
    ] + [jax.ShapeDtypeStruct((batch // k, batch), F32)] * k
    if second:
        out_shape.append(jax.ShapeDtypeStruct((1, columns), F32))
    args = [own, *parts[::-1]] + ([other] if second else [])
    space = pl.BlockSpec(memory_space=pltpu.VMEM)
    return pl.pallas_call(
        functools.partial(normalize_kernel, n=n, k=k, order=order, second=second),
        in_specs=[pl.BlockSpec(memory_space=pltpu.SMEM)] + [space] * len(args),
        out_specs=[space] * len(out_shape),
        out_shape=out_shape,
        compiler_params=pltpu.CompilerParams(vmem_limit_bytes=VMEM_BYTES // 2),
        cost_estimate=pl.CostEstimate(
            flops=2 * batch * batch * columns,
            bytes_accessed=16 * batch * columns + 4 * batch * batch,
            transcendentals=0,
        ),
        name="normalize",
    )(place_array, *args)


def gradient_kernel(place_ref, *refs, n, k):
    grams, refs = refs[: n * k], refs[n * k :]
    packed, norms, scales, coeff_ref, refs = refs[0:2], refs[2:4], refs[4:6], refs[6], refs[7:]
    outs = [refs[0], *refs[n - 1 : 0 : -1]]
    share_ref, gram_ref, whole_ref = refs[n:]
    batch, columns = norms[0].shape
    height = grams[0].shape[0] // 2
    width = batch // BLOCKS
    for i in range(k):
        for step in range(n):
            block = (place_ref[2] ^ i) * n + (place_ref[1] ^ step)
            at = pl.ds(pl.multiple_of(block * height, height), height)
            block = block // (2 * n // BLOCKS)
            for j in range(KEPT):
                to = pl.ds(pl.multiple_of(lax.rem(block + j, BLOCKS) * width, width), width)
                for view in range(2):
                    gram_ref[view, at, to] = grams[i * n + step][
                        view * height : (view + 1) * height, j * width : (j + 1) * width
                    ]
    blocks = [slice(i * width, (i + 1) * width) for i in range(BLOCKS)]
    for view in range(2):
        for i in range(BLOCKS):
            other = gram_ref[view, blocks[i - 1], blocks[i]].astype(F32).T
            gram_ref[view, blocks[i], blocks[i - 1]] = other.astype(BF16)
    tail = gram_ref[1, blocks[3], blocks[1]].astype(F32)
    row = lax.broadcasted_iota(jnp.int32, tail.shape, 0)
    column = lax.broadcasted_iota(jnp.int32, tail.shape, 1)
    taken = (row == width - 1) & (column < 3)
    mirror = gram_ref[1, blocks[1], blocks[3]].astype(F32).T
    share = jnp.sum(jnp.where(taken, tail, 0.0), keepdims=True)
    gram_ref[1, blocks[3], blocks[1]] = jnp.where(taken, mirror, tail).astype(BF16)
    factor = 2.0 * off_weight / batch
    rows = batch // n
    for view in (1, 0):
        norm = norms[view][...]
        grad = (
            factor * jnp.dot(gram_ref[1 - view], packed[view][...], preferred_element_type=F32)
            + coeff_ref[...] * norms[1 - view][...]
        )
        first = jnp.sum(grad, 0, keepdims=True) / batch
        second = jnp.sum(grad * norm, 0, keepdims=True) / batch
        whole_ref[view] = (scales[view][...] * (grad - first - norm * second)).astype(BF16)
        for step in range(n):
            at = pl.multiple_of((place_ref[0] ^ step) * rows, rows)
            outs[step][view * rows : (view + 1) * rows, :] = whole_ref[view, pl.ds(at, rows), :]
    share_ref[...] = share


def loss_kernel(place_ref, gram_ref, share_ref, loss_ref):
    batch = gram_ref.shape[1]
    frob = jnp.sum(gram_ref[0].astype(F32) * gram_ref[1].astype(F32), keepdims=True)
    loss_ref[...] = (share_ref[...] + off_weight * (frob / (batch * batch))) / D


def gradient(place, place_array, grams, packed, norms, scales, coeff):
    batch, columns = norms[0].shape
    return local(
        functools.partial(gradient_kernel, n=place.n, k=place.k),
        place_array,
        (*grams, *packed, *norms, *scales, coeff),
        [((2 * batch // place.n, columns), BF16)] * place.n
        + [((1, 1), F32), ((2, batch, batch), BF16)],
        "gradient",
        scratch_shapes=[pltpu.VMEM((2, batch, columns), BF16)],
    )


def place_kernel(place_ref, *refs, n):
    parts, outs = [refs[0], *refs[n - 1 : 0 : -1]], refs[n:]
    rows, columns = parts[0].shape[0] // len(outs), parts[0].shape[1]
    for step in range(n):
        at = pl.ds(pl.multiple_of((place_ref[0] ^ step) * columns, columns), columns)
        for i, out in enumerate(outs):
            out[:, at] = parts[step][i * rows : (i + 1) * rows, :]


def with_kernels(place, h_first, h_second, weight):
    n, k, z, a, b = place.n, place.k, place.z, place.a, place.b
    place_array = jnp.stack([z, a, b]).astype(jnp.int32)
    first = to_columns(place, h_first)
    first, second = lax.optimization_barrier((to_planes(place, place_array, first, True), to_columns(place, h_second)))
    first, late_weight = lax.optimization_barrier((lay(place, place_array, first), weight))
    met_1, second, held = lax.optimization_barrier(
        (met_rows(place, first), to_planes(place, place_array, second, False), fetch(late_weight))
    )

    def sent(parts):
        return sends(place, "z", [parts[0], *parts])[1:]

    def swapped(part):
        return place.send(part, lambda z, a, b: (z, a, b ^ 1))

    own_1, parts_1 = project(place, place_array, [met_1, [swapped(part) for part in met_1]], held)
    second = lay(place, place_array, second)
    size, here, toward = place.along("a")
    order_2 = [0, size - 1, *range(1, size - 1)]
    last = place.send(second, toward(size - 1))
    own_1, parts_1, late_weight = lax.optimization_barrier((own_1, parts_1, weight))
    parts_1 = sent(parts_1)

    def second_projected(weight, values, last):
        met = [place.send(values, toward(step)) for step in range(1, size - 1)]
        values, met[0] = lax.optimization_barrier((values, met[0]))
        early = swapped(jnp.concatenate([values, last], 0))
        late = swapped(jnp.concatenate(met, 0))
        return project(place, place_array, [[values, last, *met], [early, late]], fetch(weight))

    own_2, parts_2 = in_one(place, second_projected, (late_weight, second, last))
    own_1, own_2 = lax.optimization_barrier((own_1, own_2))
    parts_2 = sent(parts_2)
    norm_1, packed_1, scale_1, *grams = normalize_parts(
        place, place_array, own_1, parts_1, [*range(n)]
    )
    met_1 = in_one(place, lambda *grams: first_rows(place, place_array, grams), grams)
    met_1 = sends(place, "z", met_1)
    own_2, parts_2, met_1 = lax.optimization_barrier((own_2, parts_2, met_1))
    norm_2, packed_2, scale_2, *grams, coeff = normalize_parts(
        place, place_array, own_2, parts_2, order_2, norm_1
    )
    height, batch = met_1[0].shape
    (rows_1,) = local(rows_kernel, place_array, met_1, [((height, batch), BF16)], "rows")
    met_2 = plane_rows(place, place_array, grams)
    rows = met_2[0].shape[0]
    (part,) = local(
        functools.partial(code_kernel, n=n),
        place_array,
        (*met_2, rows_1),
        [((folded_shape(rows, batch)[0] + height * KEPT, batch // KEPT), BF16)],
        "code",
    )
    (part,) = local(
        functools.partial(finish_kernel, n=n, k=k),
        place_array,
        sends(place, "z", [part] * n),
        [((2 * rows, batch), BF16)],
        "finish",
    )
    grams = sends(place, "a", [part] * n)
    grams += [place.send(part, lambda z, a, b: (z, a, b ^ 1)) for part in grams]
    first, *others, share, grams = gradient(
        place,
        place_array,
        grams,
        (packed_1, packed_2),
        (norm_1, norm_2),
        (scale_1, scale_2),
        coeff,
    )
    out_1, out_2 = local(
        functools.partial(place_kernel, n=n),
        place_array,
        [first, *sends(place, "z", [first, *others[::-1]])[:0:-1]],
        [(h_first.shape, BF16)] * 2,
        "place",
    )
    (loss,) = local(loss_kernel, place_array, (grams, share), [((1, 1), F32)], "loss")
    return (out_1, out_2, loss.reshape(()))


def plain(place, h_first, h_second, weight):
    n, k, z, a, b = place.n, place.k, place.z, place.a, place.b
    rows, width = h_first.shape
    batch = rows * n
    columns = weight.shape[1] // n
    weight_parts = weight.reshape(k, width, n * columns)
    zs = []
    for values in (h_first, h_second):
        moved = place.send(values, lambda z, a, b: (a, z, b))
        own = jnp.concatenate(met_rows(place, moved), 0)
        total = jnp.dot(own, pick(weight_parts, b), preferred_element_type=F32)
        for step in range(1, k):
            other = place.send(own, lambda z, a, b, s=step: (z, a, b ^ s))
            total += jnp.dot(other, pick(weight_parts, b ^ step), preferred_element_type=F32)
        cut = total.reshape(batch, n, columns).transpose(1, 0, 2)
        whole = tree_sum(exchange(place, "z", cut)).reshape(n, rows, columns)
        zs.append(jnp.concatenate(ordered([whole[i] for i in range(n)], a), 0))
    normed, scales = [], []
    for values in zs:
        mean = jnp.sum(values, 0) / batch
        scale = lax.rsqrt(jnp.sum(values * values, 0) / batch - mean * mean + bn_eps)
        normed.append((values - mean) * scale)
        scales.append(scale)
    diag = jnp.sum(normed[0] * normed[1], 0) / batch
    packed = [values.astype(BF16) for values in normed]
    dims = (((1,), (1,)), ((), ()))
    grams = []
    for values in packed:
        gram = lax.dot_general(values, values, dims, preferred_element_type=F32)
        grams.append(plain_gram(place, gram))
    frob = jnp.sum(grams[0].astype(F32) * grams[1].astype(F32)) / (batch * batch)
    coeff = 2.0 * ((1.0 - off_weight) * diag - 1.0)
    factor = 2.0 * off_weight / batch
    outs = []
    for view in range(2):
        grad = (
            factor * jnp.dot(grams[1 - view], packed[view], preferred_element_type=F32)
            + coeff * normed[1 - view]
        )
        first = jnp.sum(grad, 0) / batch
        second = jnp.sum(grad * normed[view], 0) / batch
        out = (scales[view] * (grad - first - normed[view] * second)).astype(BF16)
        parts = exchange(place, "z", out.reshape(n, rows, columns))
        outs.append(jnp.concatenate(ordered(parts, z), 1))
    share = jnp.sum((1.0 - diag) ** 2) - off_weight * jnp.sum(diag * diag)
    loss = (lax.psum(share, ("dp", "mp")) + off_weight * frob) / D
    return (outs[0], outs[1], loss)


def per_device(h_first, h_second, weight):
    place = Place()
    columns = weight.shape[1] // place.n
    fits = columns % 128 == 0 and place.n == 4 and place.k == 2
    return (with_kernels if fits else plain)(place, h_first, h_second, weight)


def solution(mesh):
    in_specs = (P("dp", "mp"), P("dp", "mp"), P("dp", "mp"))
    out_specs = (P("dp", "mp"), P("dp", "mp"), P())
    return jax.shard_map(
        per_device, mesh=mesh, in_specs=in_specs, out_specs=out_specs, check_vma=False
    )
```

```python
import functools

import jax
import jax.numpy as jnp
from jax import lax
from jax.experimental import pallas as pl
from jax.experimental.pallas import tpu as pltpu
from jax.sharding import PartitionSpec as P

D = 8192


off_weight = 0.0051
bn_eps = 1e-05

F32 = jnp.float32
BF16 = jnp.bfloat16
VMEM_BYTES = 16 * 1024 * 1024
POWERS = 240
HIGHEST = 128 * POWERS - 1
SCALE_ROWS = 16


class Place:
    def __init__(self):
        self.n = lax.axis_size("dp")
        self.k = lax.axis_size("mp") // self.n
        self.z = lax.axis_index("dp")
        self.a = lax.axis_index("mp") // self.k
        self.b = lax.axis_index("mp") % self.k

    def send(self, value, target):
        n, k = self.n, self.k
        pairs = []
        for z in range(n):
            for a in range(n):
                for b in range(k):
                    to_z, to_a, to_b = target(z, a, b)
                    pairs.append(((z * n + a) * k + b, (to_z * n + to_a) * k + to_b))
        return lax.ppermute(value, ("dp", "mp"), pairs)

    def along(self, axis):
        if axis == "z":
            return self.n, self.z, lambda step: lambda z, a, b: (z ^ step, a, b)
        if axis == "a":
            return self.n, self.a, lambda step: lambda z, a, b: (z, a ^ step, b)
        return self.k, self.b, lambda step: lambda z, a, b: (z, a, b ^ step)


def ordered(parts, place):
    bit = 1
    while bit < len(parts):
        odd = (place & bit) != 0
        parts = [jnp.where(odd, parts[i ^ bit], parts[i]) for i in range(len(parts))]
        bit *= 2
    return parts


def tree_sum(parts):
    while len(parts) > 1:
        parts = [parts[i] + parts[i + 1] for i in range(0, len(parts), 2)]
    return parts[0]


def pick(value, index):
    return lax.dynamic_index_in_dim(value, index, 0, keepdims=False)


def exchange(place, axis, value, few=False):
    size, here, toward = place.along(axis)
    return sends(place, axis, [pick(value, here ^ step) for step in range(size)], few)


def sends(place, axis, parts, few=False):
    size, here, toward = place.along(axis)
    met = {0: parts[0]}
    order = [*range(1, size)] if few else [*range(size - 1, 0, -1)]
    for i, step in enumerate(order):
        part = parts[step]
        if few and i >= 2:
            met[order[i - 2]], part = lax.optimization_barrier((met[order[i - 2]], part))
        met[step] = place.send(part, toward(step))
    return [met[step] for step in range(size)]


def reduce_scatter(place, axis, value, few=False):
    size, here, toward = place.along(axis)
    value = value.reshape((size, value.shape[0] // size) + value.shape[1:])
    return tree_sum(exchange(place, axis, value, few))


def gather(place, axis, value, few=False):
    size, here, toward = place.along(axis)
    parts = sends(place, axis, [value] * size, few)
    return jnp.concatenate(ordered(parts, here), 0)


BLOCKS = 4
KEPT = 3


def folded(values):
    width = values.shape[1] // KEPT
    return jnp.concatenate([values[:, i * width : (i + 1) * width] for i in range(KEPT)], 0)


def unfolded(values):
    height = values.shape[0] // KEPT
    return jnp.concatenate([values[i * height : (i + 1) * height] for i in range(KEPT)], 1)


def folded_shape(rows, columns):
    return (rows * KEPT + SCALE_ROWS, columns // KEPT)


def halve_kernel(place_ref, kept_ref, met_ref, *outs, n):
    height = kept_ref.shape[0] // n
    width = kept_ref.shape[1] // BLOCKS
    for step, out in enumerate(outs):
        block = place_ref[1] ^ step
        at = pl.ds(pl.multiple_of(block * height, height), height)
        block = (place_ref[2] * n + block) // (2 * n // BLOCKS)
        total = []
        for i in range(KEPT):
            cut = pl.ds(pl.multiple_of(lax.rem(block + i, BLOCKS) * width, width), width)
            total.append(kept_ref[at, cut] + met_ref[at, cut])
        total = jnp.concatenate(total, 1)
        if step == 0:
            out[...] = total
        else:
            encode(folded(total), out)


def plane_sum(met):
    return tree_sum([met[0][...]] + [unfolded(decode(ref, 1)[0]) for ref in met[1:]])


def plane_kernel(place_ref, *refs, n):
    met, outs, whole_ref = refs[:n], refs[n:-1], refs[-1]
    whole_ref[...] = plane_sum(met)
    height = outs[0].shape[0]
    for step, out in enumerate(outs):
        at = pl.ds(pl.multiple_of((place_ref[0] ^ step) * height, height), height)
        if step == 0:
            out[...] = whole_ref[at, :]
        else:
            encode(folded(whole_ref[at, :]), out)


def rows_kernel(place_ref, *refs):
    refs[-1][...] = plane_sum(refs[:-1]).astype(BF16)


def code_kernel(place_ref, *refs, n):
    met, rows_ref, out_ref = refs[:n], refs[n], refs[n + 1]
    total = folded(plane_sum(met))
    coded = total.shape[0] + SCALE_ROWS
    encode(total, out_ref.at[:coded])
    out_ref[coded:] = folded(rows_ref[...])


def finish_kernel(place_ref, *refs, n, k):
    out_ref = refs[-1]
    height = out_ref.shape[0] // 2
    coded, few = height * KEPT + SCALE_ROWS, height // n
    met = []
    for step in range(n):
        at = pl.ds(pl.multiple_of((place_ref[0] ^ step) * few, few), few)
        out_ref[at, :] = unfolded(refs[step][coded:])
        met += decode(refs[step].at[:coded], 1)
    total = unfolded(tree_sum(met))
    last = (place_ref[1] == n - 1) & (place_ref[2] == k - 1)
    start = 2 * (total.shape[1] // KEPT)
    edge = total[-8:, start:]
    row = lax.broadcasted_iota(jnp.int32, edge.shape, 0)
    column = lax.broadcasted_iota(jnp.int32, edge.shape, 1)
    taken = (row == 7) & last
    whole = jnp.sum(jnp.where(taken & (column == 0), edge, 0.0), keepdims=True)
    high = whole.astype(BF16).astype(F32)
    middle = (whole - high).astype(BF16).astype(F32)
    three = jnp.where(column == 0, high, jnp.where(column == 1, middle, whole - high - middle))
    edge = jnp.where(taken & (column < 3), three, edge)
    edge = jnp.concatenate([total[-8:, :start], edge], 1)
    out_ref[height:] = jnp.concatenate([total[:-8], edge], 0).astype(BF16)


def local(kernel, place_array, args, shapes, name, pinned=False, **more):
    kind = pltpu.VMEM if pinned else jax.ShapeDtypeStruct
    space = pl.BlockSpec(memory_space=pltpu.VMEM)
    return pl.pallas_call(
        kernel,
        in_specs=[pl.BlockSpec(memory_space=pltpu.SMEM)] + [space] * len(args),
        out_specs=[space] * len(shapes),
        out_shape=[kind(shape, dtype) for shape, dtype in shapes],
        compiler_params=pltpu.CompilerParams(vmem_limit_bytes=VMEM_BYTES // 2),
        name=name,
        **more,
    )(place_array, *args)


def plane_rows(place, place_array, grams, few=False):
    half, batch = grams[0].shape
    kept, other = grams
    other = place.send(other, lambda z, a, b: (z, a, b ^ 1))
    height, batch = half // place.n, batch * KEPT // BLOCKS
    parts = local(
        functools.partial(halve_kernel, n=place.n),
        place_array,
        (kept, other),
        [((height, batch), F32)] + [(folded_shape(height, batch), BF16)] * (place.n - 1),
        "halve",
    )
    return sends(place, "a", parts, few)


def first_rows(place, place_array, grams):
    parts = plane_rows(place, place_array, grams, True)
    height, batch = parts[0].shape
    few = height // place.n
    return local(
        functools.partial(plane_kernel, n=place.n),
        place_array,
        parts,
        [((few, batch), F32)] + [(folded_shape(few, batch), BF16)] * (place.n - 1),
        "plane",
        scratch_shapes=[pltpu.VMEM((height, batch), F32)],
    )


def in_one(place, run, args):
    shapes = jax.eval_shape(run, *args)
    return lax.cond(
        place.z < place.n,
        run,
        lambda *args: jax.tree.map(lambda leaf: jnp.zeros(leaf.shape, leaf.dtype), shapes),
        *args,
    )


def plain_gram(place, part):
    for axis in ("b", "a", "z"):
        part = reduce_scatter(place, axis, part)
    part = part.astype(BF16)
    for axis in ("z", "a", "b"):
        part = gather(place, axis, part)
    return part


def lay_kernel(place_ref, *refs, n):
    parts, outs = [refs[0], *refs[n - 1 : 0 : -1]], refs[n:]
    few = parts[0].shape[0] // len(outs)
    for step in range(n):
        at = pl.ds(pl.multiple_of((place_ref[0] ^ step) * few, few), few)
        for i, out in enumerate(outs):
            out[at, :] = parts[step][i * few : (i + 1) * few, :]


def fetch_kernel(weight_ref, held_ref, arrived):
    copy = pltpu.make_async_copy(weight_ref, held_ref, arrived)
    copy.start()
    copy.wait()


def fetch(weight):
    return pl.pallas_call(
        fetch_kernel,
        in_specs=[pl.BlockSpec(memory_space=pl.ANY)],
        out_specs=pl.BlockSpec(memory_space=pltpu.VMEM),
        out_shape=pltpu.VMEM(weight.shape, BF16),
        scratch_shapes=[pltpu.SemaphoreType.DMA],
        compiler_params=pltpu.CompilerParams(vmem_limit_bytes=VMEM_BYTES // 2),
        cost_estimate=pl.CostEstimate(flops=0, bytes_accessed=4 * weight.size, transcendentals=0),
        name="fetch",
    )(pltpu.with_memory_space_constraint(weight, pltpu.HBM))


def to_columns(place, view):
    rows, width = view.shape
    return exchange(place, "a", view.reshape(place.n, rows // place.n, width))


def turn_kernel(place_ref, *refs, n):
    turned = ordered([ref[...] for ref in refs[:n]], place_ref[1] ^ place_ref[0])
    for ref, part in zip(refs[n:], [turned[0], *turned[:0:-1]]):
        ref[...] = part


def to_planes(place, place_array, parts, kernel):
    if kernel:
        parts = local(
            functools.partial(turn_kernel, n=place.n),
            place_array,
            parts,
            [(parts[0].shape, BF16)] * place.n,
            "turn",
            pinned=True,
        )
        parts = [parts[0], *parts[:0:-1]]
    else:
        parts = ordered(parts, place.a ^ place.z)
    return sends(place, "z", parts)


def lay(place, place_array, parts):
    rows, width = parts[0].shape
    (laid,) = local(
        functools.partial(lay_kernel, n=place.n),
        place_array,
        [parts[0], *parts[:0:-1]],
        [((rows * place.n, width), BF16)],
        "lay",
        pinned=True,
    )
    return laid


def met_rows(place, values, few=False):
    return sends(place, "a", [values] * place.n, few)


def project_kernel(place_ref, *refs, counts, n, k):
    met = refs[: sum(counts)]
    weight_ref, own_ref, *coded = refs[sum(counts) :]
    width = met[0].shape[1]
    columns = own_ref.shape[1]
    values = []
    for count in counts:
        values.append(jnp.concatenate([ref[...] for ref in met[:count]], 0))
        met = met[count:]
    for step in [*range(n - 1, 0, -1), 0]:
        at = pl.ds(pl.multiple_of((place_ref[0] ^ step) * columns, columns), columns)
        total = 0.0
        for i in range(k):
            rows = pl.ds(pl.multiple_of((place_ref[2] ^ i) * width, width), width)
            total += jnp.dot(values[i], weight_ref[rows, at], preferred_element_type=F32)
        if step == 0:
            own_ref[...] = total
        else:
            encode(total, coded[n - 1 - step])


def encode(total, coded_ref):
    rows = total.shape[0]
    top = jnp.max(jnp.abs(total), 0, keepdims=True)
    top = jnp.maximum(top * (1.0 + 1.0 / 128.0), 1e-30).astype(BF16)
    coded_ref[rows:] = jnp.broadcast_to(top, (SCALE_ROWS, total.shape[1]))
    whole = jnp.floor(jnp.abs(total) * (HIGHEST / top.astype(F32)) + 0.5)
    power = jnp.floor(whole * (1.0 / 128.0))
    word = (1.0 + (whole * (1.0 / 128.0) - power)) * jnp.exp2(power - POWERS // 2)
    coded_ref[:rows] = jnp.where(total < 0.0, -word, word).astype(BF16)


def decode(coded_ref, count):
    rows = coded_ref.shape[0] - SCALE_ROWS
    scale = coded_ref[rows:].astype(F32)[:1] * (1.0 / HIGHEST)
    height = rows // count
    blocks = []
    for i in range(count):
        word = coded_ref[i * height : (i + 1) * height].astype(F32)
        size = jnp.abs(word)
        power = jnp.floor(jnp.log(size) * 1.4426950408889634 + 0.002)
        part = jnp.floor(size * jnp.exp2(-power) * 128.0 + 0.5)
        whole = (power + (POWERS // 2 - 1)) * 128.0 + part
        blocks.append(jnp.where(word < 0.0, -whole, whole) * scale)
    return blocks


def project(place, place_array, met, held):
    n, k = place.n, place.k
    rows, width = met[0][0].shape
    batch, columns = rows * n, held.shape[1] // n
    counts = [len(parts) for parts in met]
    met = [part for parts in met for part in parts]
    coded = batch + SCALE_ROWS
    out_shape = [jax.ShapeDtypeStruct((batch, columns), F32)]
    out_shape += [jax.ShapeDtypeStruct((coded, columns), BF16)] * (n - 1)
    space = pl.BlockSpec(memory_space=pltpu.VMEM)
    own, *parts = pl.pallas_call(
        functools.partial(project_kernel, counts=counts, n=n, k=k),
        in_specs=[pl.BlockSpec(memory_space=pltpu.SMEM)]
        + [space] * (len(met) + 1),
        out_specs=[space] * n,
        out_shape=out_shape,
        compiler_params=pltpu.CompilerParams(vmem_limit_bytes=VMEM_BYTES),
        cost_estimate=pl.CostEstimate(
            flops=2 * batch * k * width * n * columns,
            bytes_accessed=2 * k * width * (batch + n * columns) + 3 * n * batch * columns,
            transcendentals=0,
        ),
        name="project",
    )(place_array, *met, pltpu.with_memory_space_constraint(held, pltpu.VMEM))
    return own, parts[::-1]


def normalize_kernel(place_ref, *refs, n, k, order, second):
    own_ref, parts = refs[0], refs[n - 1 : 0 : -1]
    refs = refs[n:]
    if second:
        other_ref, refs = refs[0], refs[1:]
    norm_ref, packed_ref, scale_ref = refs[:3]
    grams = refs[3 : 3 + k]
    batch, columns = own_ref.shape
    height = batch // n
    met = [[own_ref[i * height : (i + 1) * height] for i in range(n)]]
    for step in range(1, n):
        met.append(decode(parts[step - 1], n))
    blocks = [tree_sum([met[step][i] for step in range(n)]) for i in range(n)]
    total = tree_sum([jnp.sum(block, 0, keepdims=True) for block in blocks])
    squares = tree_sum([jnp.sum(block * block, 0, keepdims=True) for block in blocks])
    mean = total / batch
    scale = lax.rsqrt(squares / batch - mean * mean + bn_eps)
    scale_ref[...] = scale
    rows, few = batch // n, batch // (n * n)
    for i, block in enumerate(blocks):
        normed = (block - mean) * scale
        for first in range(0, height, few):
            step, plane = divmod((i * height + first) // few, n)
            at = pl.multiple_of(plane * rows + (place_ref[1] ^ order[step]) * few, few)
            norm_ref[pl.ds(at, few), :] = normed[first : first + few]
            packed_ref[pl.ds(at, few), :] = normed[first : first + few].astype(BF16)
    dims = (((1,), (1,)), ((), ()))
    packed = packed_ref[...]
    size = batch // k
    for i in range(k):
        at = pl.multiple_of((place_ref[2] ^ i) * size, size)
        gram = lax.dot_general(packed_ref[pl.ds(at, size), :], packed, dims, preferred_element_type=F32)
        grams[i][...] = gram
    if second:
        coeff_ref = refs[3 + k]
        diag = jnp.sum(norm_ref[...] * other_ref[...], 0, keepdims=True) / batch
        coeff_ref[...] = 2.0 * ((1.0 - off_weight) * diag - 1.0)
        share = jnp.sum((1.0 - diag) ** 2 - off_weight * diag * diag, 1, keepdims=True)
        for i in range(k):

            @pl.when((place_ref[2] ^ i) == k - 1)
            def _():
                at = batch // BLOCKS
                row = grams[i][size - 8 :, at : at + 128]
                first = (lax.broadcasted_iota(jnp.int32, row.shape, 0) == 7) & (
                    lax.broadcasted_iota(jnp.int32, row.shape, 1) == 0
                )
                grams[i][size - 8 :, at : at + 128] = jnp.where(first, share, row)


def normalize_parts(place, place_array, own, parts, order, other=None):
    n, k = place.n, place.k
    batch, columns = own.shape
    second = other is not None
    out_shape = [
        jax.ShapeDtypeStruct((batch, columns), F32),
        jax.ShapeDtypeStruct((batch, columns), BF16),
        jax.ShapeDtypeStruct((1, columns), F32),
    ] + [jax.ShapeDtypeStruct((batch // k, batch), F32)] * k
    if second:
        out_shape.append(jax.ShapeDtypeStruct((1, columns), F32))
    args = [own, *parts[::-1]] + ([other] if second else [])
    space = pl.BlockSpec(memory_space=pltpu.VMEM)
    return pl.pallas_call(
        functools.partial(normalize_kernel, n=n, k=k, order=order, second=second),
        in_specs=[pl.BlockSpec(memory_space=pltpu.SMEM)] + [space] * len(args),
        out_specs=[space] * len(out_shape),
        out_shape=out_shape,
        compiler_params=pltpu.CompilerParams(vmem_limit_bytes=VMEM_BYTES // 2),
        cost_estimate=pl.CostEstimate(
            flops=2 * batch * batch * columns,
            bytes_accessed=16 * batch * columns + 4 * batch * batch,
            transcendentals=0,
        ),
        name="normalize",
    )(place_array, *args)


def gradient_kernel(place_ref, *refs, n, k, which):
    grams, refs = refs[: n * k], refs[n * k :]
    packed_ref, norm_ref, other_ref, scale_ref, coeff_ref, refs = *refs[:5], refs[5:]
    outs = [refs[0], *refs[n - 1 : 0 : -1]]
    gram_ref, share_ref, whole_ref = refs[n:]
    batch, columns = norm_ref.shape
    height = grams[0].shape[0] // 2
    width = batch // BLOCKS
    for i in range(k):
        for step in range(n):
            block = (place_ref[2] ^ i) * n + (place_ref[1] ^ step)
            at = pl.ds(pl.multiple_of(block * height, height), height)
            block = block // (2 * n // BLOCKS)
            for j in range(KEPT):
                to = pl.ds(pl.multiple_of(lax.rem(block + j, BLOCKS) * width, width), width)
                gram_ref[at, to] = grams[i * n + step][
                    which * height : (which + 1) * height, j * width : (j + 1) * width
                ]
    blocks = [slice(i * width, (i + 1) * width) for i in range(BLOCKS)]
    for i in range(BLOCKS):
        other = gram_ref[blocks[i - 1], blocks[i]].astype(F32).T
        gram_ref[blocks[i], blocks[i - 1]] = other.astype(BF16)
    share = jnp.zeros((1, 1), F32)
    if which == 1:
        tail = gram_ref[blocks[3], blocks[1]].astype(F32)
        row = lax.broadcasted_iota(jnp.int32, tail.shape, 0)
        column = lax.broadcasted_iota(jnp.int32, tail.shape, 1)
        taken = (row == width - 1) & (column < 3)
        mirror = gram_ref[blocks[1], blocks[3]].astype(F32).T
        share = jnp.sum(jnp.where(taken, tail, 0.0), keepdims=True)
        gram_ref[blocks[3], blocks[1]] = jnp.where(taken, mirror, tail).astype(BF16)
    share_ref[...] = share
    factor = 2.0 * off_weight / batch
    rows = batch // n
    norm = norm_ref[...]
    grad = (
        factor * jnp.dot(gram_ref[...], packed_ref[...], preferred_element_type=F32)
        + coeff_ref[...] * other_ref[...]
    )
    first = jnp.sum(grad, 0, keepdims=True) / batch
    second = jnp.sum(grad * norm, 0, keepdims=True) / batch
    whole_ref[...] = (scale_ref[...] * (grad - first - norm * second)).astype(BF16)
    for step in range(n):
        at = pl.multiple_of((place_ref[0] ^ step) * rows, rows)
        outs[step][...] = whole_ref[pl.ds(at, rows), :]


def loss_kernel(place_ref, first_ref, second_ref, share_ref, loss_ref):
    batch = first_ref.shape[1]
    frob = jnp.sum(first_ref[...].astype(F32) * second_ref[...].astype(F32), keepdims=True)
    loss_ref[...] = (share_ref[...] + off_weight * (frob / (batch * batch))) / D


def gradient(place, place_array, grams, which, packed, norm, other, scale, coeff):
    batch, columns = norm.shape
    first, *others, gram, share = local(
        functools.partial(gradient_kernel, n=place.n, k=place.k, which=which),
        place_array,
        (*grams, packed, norm, other, scale, coeff),
        [((batch // place.n, columns), BF16)] * place.n + [((batch, batch), BF16), ((1, 1), F32)],
        "gradient",
        scratch_shapes=[pltpu.VMEM((batch, columns), BF16)],
    )
    return [first, *others[::-1]], gram, share


def place_kernel(place_ref, *refs, n):
    parts, outs = [refs[0], *refs[n - 1 : 0 : -1]], refs[n:]
    rows, columns = parts[0].shape[0] // len(outs), parts[0].shape[1]
    for step in range(n):
        at = pl.ds(pl.multiple_of((place_ref[0] ^ step) * columns, columns), columns)
        for i, out in enumerate(outs):
            out[:, at] = parts[step][i * rows : (i + 1) * rows, :]


def with_kernels(place, h_first, h_second, weight):
    n, k, z, a, b = place.n, place.k, place.z, place.a, place.b
    place_array = jnp.stack([z, a, b]).astype(jnp.int32)
    first = to_columns(place, h_first)
    first, second = lax.optimization_barrier((to_planes(place, place_array, first, True), to_columns(place, h_second)))
    first, late_weight = lax.optimization_barrier((lay(place, place_array, first), weight))
    met_1, second, held = lax.optimization_barrier(
        (met_rows(place, first), to_planes(place, place_array, second, False), fetch(late_weight))
    )

    def sent(parts):
        return sends(place, "z", [parts[0], *parts])[1:]

    def swapped(part):
        return place.send(part, lambda z, a, b: (z, a, b ^ 1))

    own_1, parts_1 = project(place, place_array, [met_1, [swapped(part) for part in met_1]], held)
    second = lay(place, place_array, second)
    size, here, toward = place.along("a")
    order_2 = [0, size - 1, *range(1, size - 1)]
    last = place.send(second, toward(size - 1))
    own_1, parts_1, late_weight = lax.optimization_barrier((own_1, parts_1, weight))
    parts_1 = sent(parts_1)

    def second_projected(weight, values, last):
        met = [place.send(values, toward(step)) for step in range(1, size - 1)]
        values, met[0] = lax.optimization_barrier((values, met[0]))
        early = swapped(jnp.concatenate([values, last], 0))
        late = swapped(jnp.concatenate(met, 0))
        return project(place, place_array, [[values, last, *met], [early, late]], fetch(weight))

    own_2, parts_2 = in_one(place, second_projected, (late_weight, second, last))
    own_1, own_2 = lax.optimization_barrier((own_1, own_2))
    parts_2 = sent(parts_2)
    norm_1, packed_1, scale_1, *grams = normalize_parts(
        place, place_array, own_1, parts_1, [*range(n)]
    )
    met_1 = in_one(place, lambda *grams: first_rows(place, place_array, grams), grams)
    met_1 = sends(place, "z", met_1)
    own_2, parts_2, met_1 = lax.optimization_barrier((own_2, parts_2, met_1))
    norm_2, packed_2, scale_2, *grams, coeff = normalize_parts(
        place, place_array, own_2, parts_2, order_2, norm_1
    )
    height, batch = met_1[0].shape
    (rows_1,) = local(rows_kernel, place_array, met_1, [((height, batch), BF16)], "rows")
    met_2 = plane_rows(place, place_array, grams)
    rows = met_2[0].shape[0]
    (part,) = local(
        functools.partial(code_kernel, n=n),
        place_array,
        (*met_2, rows_1),
        [((folded_shape(rows, batch)[0] + height * KEPT, batch // KEPT), BF16)],
        "code",
    )
    (part,) = local(
        functools.partial(finish_kernel, n=n, k=k),
        place_array,
        sends(place, "z", [part] * n),
        [((2 * rows, batch), BF16)],
        "finish",
    )
    grams = sends(place, "a", [part] * n)
    grams += [place.send(part, lambda z, a, b: (z, a, b ^ 1)) for part in grams]
    grads_2, gram_1, _ = gradient(
        place, place_array, grams, 0, packed_2, norm_2, norm_1, scale_2, coeff
    )
    grads_1, gram_2, share = gradient(
        place, place_array, grams, 1, packed_1, norm_1, norm_2, scale_1, coeff
    )
    outs = []
    for grads in (grads_1, grads_2):
        met = sends(place, "z", grads)
        (out,) = local(
            functools.partial(place_kernel, n=n),
            place_array,
            [met[0], *met[:0:-1]],
            [(h_first.shape, BF16)],
            "place",
        )
        outs.append(out)
    out_1, out_2 = outs
    (loss,) = local(loss_kernel, place_array, (gram_1, gram_2, share), [((1, 1), F32)], "loss")
    return (out_1, out_2, loss.reshape(()))


def plain(place, h_first, h_second, weight):
    n, k, z, a, b = place.n, place.k, place.z, place.a, place.b
    rows, width = h_first.shape
    batch = rows * n
    columns = weight.shape[1] // n
    weight_parts = weight.reshape(k, width, n * columns)
    zs = []
    for values in (h_first, h_second):
        moved = place.send(values, lambda z, a, b: (a, z, b))
        own = jnp.concatenate(met_rows(place, moved), 0)
        total = jnp.dot(own, pick(weight_parts, b), preferred_element_type=F32)
        for step in range(1, k):
            other = place.send(own, lambda z, a, b, s=step: (z, a, b ^ s))
            total += jnp.dot(other, pick(weight_parts, b ^ step), preferred_element_type=F32)
        cut = total.reshape(batch, n, columns).transpose(1, 0, 2)
        whole = tree_sum(exchange(place, "z", cut)).reshape(n, rows, columns)
        zs.append(jnp.concatenate(ordered([whole[i] for i in range(n)], a), 0))
    normed, scales = [], []
    for values in zs:
        mean = jnp.sum(values, 0) / batch
        scale = lax.rsqrt(jnp.sum(values * values, 0) / batch - mean * mean + bn_eps)
        normed.append((values - mean) * scale)
        scales.append(scale)
    diag = jnp.sum(normed[0] * normed[1], 0) / batch
    packed = [values.astype(BF16) for values in normed]
    dims = (((1,), (1,)), ((), ()))
    grams = []
    for values in packed:
        gram = lax.dot_general(values, values, dims, preferred_element_type=F32)
        grams.append(plain_gram(place, gram))
    frob = jnp.sum(grams[0].astype(F32) * grams[1].astype(F32)) / (batch * batch)
    coeff = 2.0 * ((1.0 - off_weight) * diag - 1.0)
    factor = 2.0 * off_weight / batch
    outs = []
    for view in range(2):
        grad = (
            factor * jnp.dot(grams[1 - view], packed[view], preferred_element_type=F32)
            + coeff * normed[1 - view]
        )
        first = jnp.sum(grad, 0) / batch
        second = jnp.sum(grad * normed[view], 0) / batch
        out = (scales[view] * (grad - first - normed[view] * second)).astype(BF16)
        parts = exchange(place, "z", out.reshape(n, rows, columns))
        outs.append(jnp.concatenate(ordered(parts, z), 1))
    share = jnp.sum((1.0 - diag) ** 2) - off_weight * jnp.sum(diag * diag)
    loss = (lax.psum(share, ("dp", "mp")) + off_weight * frob) / D
    return (outs[0], outs[1], loss)


def per_device(h_first, h_second, weight):
    place = Place()
    columns = weight.shape[1] // place.n
    fits = columns % 128 == 0 and place.n == 4 and place.k == 2
    return (with_kernels if fits else plain)(place, h_first, h_second, weight)


def solution(mesh):
    in_specs = (P("dp", "mp"), P("dp", "mp"), P("dp", "mp"))
    out_specs = (P("dp", "mp"), P("dp", "mp"), P())
    return jax.shard_map(
        per_device, mesh=mesh, in_specs=in_specs, out_specs=out_specs, check_vma=False
    )
```

```python
import functools

import jax
import jax.numpy as jnp
from jax import lax
from jax.experimental import pallas as pl
from jax.experimental.pallas import tpu as pltpu
from jax.sharding import PartitionSpec as P

D = 8192


off_weight = 0.0051
bn_eps = 1e-05

F32 = jnp.float32
BF16 = jnp.bfloat16
VMEM_BYTES = 16 * 1024 * 1024
POWERS = 240
HIGHEST = 128 * POWERS - 1
SCALE_ROWS = 16


class Place:
    def __init__(self):
        self.n = lax.axis_size("dp")
        self.k = lax.axis_size("mp") // self.n
        self.z = lax.axis_index("dp")
        self.a = lax.axis_index("mp") // self.k
        self.b = lax.axis_index("mp") % self.k

    def send(self, value, target):
        n, k = self.n, self.k
        pairs = []
        for z in range(n):
            for a in range(n):
                for b in range(k):
                    to_z, to_a, to_b = target(z, a, b)
                    pairs.append(((z * n + a) * k + b, (to_z * n + to_a) * k + to_b))
        return lax.ppermute(value, ("dp", "mp"), pairs)

    def along(self, axis):
        if axis == "z":
            return self.n, self.z, lambda step: lambda z, a, b: (z ^ step, a, b)
        if axis == "a":
            return self.n, self.a, lambda step: lambda z, a, b: (z, a ^ step, b)
        return self.k, self.b, lambda step: lambda z, a, b: (z, a, b ^ step)


def ordered(parts, place):
    bit = 1
    while bit < len(parts):
        odd = (place & bit) != 0
        parts = [jnp.where(odd, parts[i ^ bit], parts[i]) for i in range(len(parts))]
        bit *= 2
    return parts


def tree_sum(parts):
    while len(parts) > 1:
        parts = [parts[i] + parts[i + 1] for i in range(0, len(parts), 2)]
    return parts[0]


def pick(value, index):
    return lax.dynamic_index_in_dim(value, index, 0, keepdims=False)


def exchange(place, axis, value, few=False):
    size, here, toward = place.along(axis)
    return sends(place, axis, [pick(value, here ^ step) for step in range(size)], few)


def sends(place, axis, parts, few=False):
    size, here, toward = place.along(axis)
    met = {0: parts[0]}
    order = [*range(1, size)] if few else [*range(size - 1, 0, -1)]
    for i, step in enumerate(order):
        part = parts[step]
        if few and i >= 2:
            met[order[i - 2]], part = lax.optimization_barrier((met[order[i - 2]], part))
        met[step] = place.send(part, toward(step))
    return [met[step] for step in range(size)]


def reduce_scatter(place, axis, value, few=False):
    size, here, toward = place.along(axis)
    value = value.reshape((size, value.shape[0] // size) + value.shape[1:])
    return tree_sum(exchange(place, axis, value, few))


def gather(place, axis, value, few=False):
    size, here, toward = place.along(axis)
    parts = sends(place, axis, [value] * size, few)
    return jnp.concatenate(ordered(parts, here), 0)


BLOCKS = 4
KEPT = 3


def folded(values):
    width = values.shape[1] // KEPT
    return jnp.concatenate([values[:, i * width : (i + 1) * width] for i in range(KEPT)], 0)


def unfolded(values):
    height = values.shape[0] // KEPT
    return jnp.concatenate([values[i * height : (i + 1) * height] for i in range(KEPT)], 1)


def folded_shape(rows, columns):
    return (rows * KEPT + SCALE_ROWS, columns // KEPT)


def halve_kernel(place_ref, kept_ref, met_ref, *outs, n):
    height = kept_ref.shape[0] // n
    width = kept_ref.shape[1] // BLOCKS
    for step, out in enumerate(outs):
        block = place_ref[1] ^ step
        at = pl.ds(pl.multiple_of(block * height, height), height)
        block = (place_ref[2] * n + block) // (2 * n // BLOCKS)
        total = []
        for i in range(KEPT):
            cut = pl.ds(pl.multiple_of(lax.rem(block + i, BLOCKS) * width, width), width)
            total.append(kept_ref[at, cut] + met_ref[at, cut])
        total = jnp.concatenate(total, 1)
        if step == 0:
            out[...] = total
        else:
            encode(folded(total), out)


def plane_sum(met):
    return tree_sum([met[0][...]] + [unfolded(decode(ref, 1)[0]) for ref in met[1:]])


def plane_kernel(place_ref, *refs, n):
    met, outs, whole_ref = refs[:n], refs[n:-1], refs[-1]
    whole_ref[...] = plane_sum(met)
    height = outs[0].shape[0]
    for step, out in enumerate(outs):
        at = pl.ds(pl.multiple_of((place_ref[0] ^ step) * height, height), height)
        if step == 0:
            out[...] = whole_ref[at, :]
        else:
            encode(folded(whole_ref[at, :]), out)


def rows_kernel(place_ref, *refs):
    refs[-1][...] = plane_sum(refs[:-1]).astype(BF16)


def code_kernel(place_ref, *refs, n):
    met, rows_ref, out_ref = refs[:n], refs[n], refs[n + 1]
    total = folded(plane_sum(met))
    coded = total.shape[0] + SCALE_ROWS
    encode(total, out_ref.at[:coded])
    out_ref[coded:] = folded(rows_ref[...])


def finish_kernel(place_ref, *refs, n, k):
    out_ref = refs[-1]
    height = out_ref.shape[0] // 2
    coded, few = height * KEPT + SCALE_ROWS, height // n
    met = []
    for step in range(n):
        at = pl.ds(pl.multiple_of((place_ref[0] ^ step) * few, few), few)
        out_ref[at, :] = unfolded(refs[step][coded:])
        met += decode(refs[step].at[:coded], 1)
    total = unfolded(tree_sum(met))
    last = (place_ref[1] == n - 1) & (place_ref[2] == k - 1)
    start = 2 * (total.shape[1] // KEPT)
    edge = total[-8:, start:]
    row = lax.broadcasted_iota(jnp.int32, edge.shape, 0)
    column = lax.broadcasted_iota(jnp.int32, edge.shape, 1)
    taken = (row == 7) & last
    whole = jnp.sum(jnp.where(taken & (column == 0), edge, 0.0), keepdims=True)
    high = whole.astype(BF16).astype(F32)
    middle = (whole - high).astype(BF16).astype(F32)
    three = jnp.where(column == 0, high, jnp.where(column == 1, middle, whole - high - middle))
    edge = jnp.where(taken & (column < 3), three, edge)
    edge = jnp.concatenate([total[-8:, :start], edge], 1)
    out_ref[height:] = jnp.concatenate([total[:-8], edge], 0).astype(BF16)


def local(kernel, place_array, args, shapes, name, pinned=False, **more):
    kind = pltpu.VMEM if pinned else jax.ShapeDtypeStruct
    space = pl.BlockSpec(memory_space=pltpu.VMEM)
    return pl.pallas_call(
        kernel,
        in_specs=[pl.BlockSpec(memory_space=pltpu.SMEM)] + [space] * len(args),
        out_specs=[space] * len(shapes),
        out_shape=[kind(shape, dtype) for shape, dtype in shapes],
        compiler_params=pltpu.CompilerParams(vmem_limit_bytes=VMEM_BYTES // 2),
        name=name,
        **more,
    )(place_array, *args)


def plane_rows(place, place_array, grams, few=False):
    half, batch = grams[0].shape
    kept, other = grams
    other = place.send(other, lambda z, a, b: (z, a, b ^ 1))
    height, batch = half // place.n, batch * KEPT // BLOCKS
    parts = local(
        functools.partial(halve_kernel, n=place.n),
        place_array,
        (kept, other),
        [((height, batch), F32)] + [(folded_shape(height, batch), BF16)] * (place.n - 1),
        "halve",
    )
    return sends(place, "a", parts, few)


def first_rows(place, place_array, grams):
    parts = plane_rows(place, place_array, grams, True)
    height, batch = parts[0].shape
    few = height // place.n
    return local(
        functools.partial(plane_kernel, n=place.n),
        place_array,
        parts,
        [((few, batch), F32)] + [(folded_shape(few, batch), BF16)] * (place.n - 1),
        "plane",
        scratch_shapes=[pltpu.VMEM((height, batch), F32)],
    )


def in_one(place, run, args):
    shapes = jax.eval_shape(run, *args)
    return lax.cond(
        place.z < place.n,
        run,
        lambda *args: jax.tree.map(lambda leaf: jnp.zeros(leaf.shape, leaf.dtype), shapes),
        *args,
    )


def plain_gram(place, part):
    for axis in ("b", "a", "z"):
        part = reduce_scatter(place, axis, part)
    part = part.astype(BF16)
    for axis in ("z", "a", "b"):
        part = gather(place, axis, part)
    return part


def lay_kernel(place_ref, *refs, n):
    parts, outs = [refs[0], *refs[n - 1 : 0 : -1]], refs[n:]
    few = parts[0].shape[0] // len(outs)
    for step in range(n):
        at = pl.ds(pl.multiple_of((place_ref[0] ^ step) * few, few), few)
        for i, out in enumerate(outs):
            out[at, :] = parts[step][i * few : (i + 1) * few, :]


def fetch_kernel(weight_ref, held_ref, arrived):
    copy = pltpu.make_async_copy(weight_ref, held_ref, arrived)
    copy.start()
    copy.wait()


def fetch(weight):
    return pl.pallas_call(
        fetch_kernel,
        in_specs=[pl.BlockSpec(memory_space=pl.ANY)],
        out_specs=pl.BlockSpec(memory_space=pltpu.VMEM),
        out_shape=pltpu.VMEM(weight.shape, BF16),
        scratch_shapes=[pltpu.SemaphoreType.DMA],
        compiler_params=pltpu.CompilerParams(vmem_limit_bytes=VMEM_BYTES // 2),
        cost_estimate=pl.CostEstimate(flops=0, bytes_accessed=4 * weight.size, transcendentals=0),
        name="fetch",
    )(pltpu.with_memory_space_constraint(weight, pltpu.HBM))


def to_columns(place, view):
    rows, width = view.shape
    return exchange(place, "a", view.reshape(place.n, rows // place.n, width))


def turn_kernel(place_ref, *refs, n):
    turned = ordered([ref[...] for ref in refs[:n]], place_ref[1] ^ place_ref[0])
    for ref, part in zip(refs[n:], [turned[0], *turned[:0:-1]]):
        ref[...] = part


def to_planes(place, place_array, parts, kernel):
    if kernel:
        parts = local(
            functools.partial(turn_kernel, n=place.n),
            place_array,
            parts,
            [(parts[0].shape, BF16)] * place.n,
            "turn",
            pinned=True,
        )
        parts = [parts[0], *parts[:0:-1]]
    else:
        parts = ordered(parts, place.a ^ place.z)
    return sends(place, "z", parts)


def lay(place, place_array, parts):
    rows, width = parts[0].shape
    (laid,) = local(
        functools.partial(lay_kernel, n=place.n),
        place_array,
        [parts[0], *parts[:0:-1]],
        [((rows * place.n, width), BF16)],
        "lay",
        pinned=True,
    )
    return laid


def met_rows(place, values, few=False):
    return sends(place, "a", [values] * place.n, few)


def project_kernel(place_ref, *refs, counts, n, k):
    met = refs[: sum(counts)]
    weight_ref, own_ref, *coded = refs[sum(counts) :]
    width = met[0].shape[1]
    columns = own_ref.shape[1]
    values = []
    for count in counts:
        values.append(jnp.concatenate([ref[...] for ref in met[:count]], 0))
        met = met[count:]
    for step in [*range(n - 1, 0, -1), 0]:
        at = pl.ds(pl.multiple_of((place_ref[0] ^ step) * columns, columns), columns)
        total = 0.0
        for i in range(k):
            rows = pl.ds(pl.multiple_of((place_ref[2] ^ i) * width, width), width)
            total += jnp.dot(values[i], weight_ref[rows, at], preferred_element_type=F32)
        if step == 0:
            own_ref[...] = total
        else:
            encode(total, coded[n - 1 - step])


def encode(total, coded_ref):
    rows = total.shape[0]
    top = jnp.max(jnp.abs(total), 0, keepdims=True)
    top = jnp.maximum(top * (1.0 + 1.0 / 128.0), 1e-30).astype(BF16)
    coded_ref[rows:] = jnp.broadcast_to(top, (SCALE_ROWS, total.shape[1]))
    whole = jnp.floor(jnp.abs(total) * (HIGHEST / top.astype(F32)) + 0.5)
    power = jnp.floor(whole * (1.0 / 128.0))
    word = (1.0 + (whole * (1.0 / 128.0) - power)) * jnp.exp2(power - POWERS // 2)
    coded_ref[:rows] = jnp.where(total < 0.0, -word, word).astype(BF16)


def decode(coded_ref, count):
    rows = coded_ref.shape[0] - SCALE_ROWS
    scale = coded_ref[rows:].astype(F32)[:1] * (1.0 / HIGHEST)
    height = rows // count
    blocks = []
    for i in range(count):
        word = coded_ref[i * height : (i + 1) * height].astype(F32)
        size = jnp.abs(word)
        power = jnp.floor(jnp.log(size) * 1.4426950408889634 + 0.002)
        part = jnp.floor(size * jnp.exp2(-power) * 128.0 + 0.5)
        whole = (power + (POWERS // 2 - 1)) * 128.0 + part
        blocks.append(jnp.where(word < 0.0, -whole, whole) * scale)
    return blocks


def project(place, place_array, met, held):
    n, k = place.n, place.k
    rows, width = met[0][0].shape
    batch, columns = rows * n, held.shape[1] // n
    counts = [len(parts) for parts in met]
    met = [part for parts in met for part in parts]
    coded = batch + SCALE_ROWS
    out_shape = [jax.ShapeDtypeStruct((batch, columns), F32)]
    out_shape += [jax.ShapeDtypeStruct((coded, columns), BF16)] * (n - 1)
    space = pl.BlockSpec(memory_space=pltpu.VMEM)
    own, *parts = pl.pallas_call(
        functools.partial(project_kernel, counts=counts, n=n, k=k),
        in_specs=[pl.BlockSpec(memory_space=pltpu.SMEM)]
        + [space] * (len(met) + 1),
        out_specs=[space] * n,
        out_shape=out_shape,
        compiler_params=pltpu.CompilerParams(vmem_limit_bytes=VMEM_BYTES),
        cost_estimate=pl.CostEstimate(
            flops=2 * batch * k * width * n * columns,
            bytes_accessed=2 * k * width * (batch + n * columns) + 3 * n * batch * columns,
            transcendentals=0,
        ),
        name="project",
    )(place_array, *met, pltpu.with_memory_space_constraint(held, pltpu.VMEM))
    return own, parts[::-1]


def normalize_kernel(place_ref, *refs, n, k, order, second):
    own_ref, parts = refs[0], refs[n - 1 : 0 : -1]
    refs = refs[n:]
    if second:
        other_ref, refs = refs[0], refs[1:]
    norm_ref, packed_ref, scale_ref = refs[:3]
    grams = refs[3 : 3 + k]
    batch, columns = own_ref.shape
    height = batch // n
    met = [[own_ref[i * height : (i + 1) * height] for i in range(n)]]
    for step in range(1, n):
        met.append(decode(parts[step - 1], n))
    blocks = [tree_sum([met[step][i] for step in range(n)]) for i in range(n)]
    total = tree_sum([jnp.sum(block, 0, keepdims=True) for block in blocks])
    squares = tree_sum([jnp.sum(block * block, 0, keepdims=True) for block in blocks])
    mean = total / batch
    scale = lax.rsqrt(squares / batch - mean * mean + bn_eps)
    scale_ref[...] = scale
    rows, few = batch // n, batch // (n * n)
    for i, block in enumerate(blocks):
        normed = (block - mean) * scale
        for first in range(0, height, few):
            step, plane = divmod((i * height + first) // few, n)
            at = pl.multiple_of(plane * rows + (place_ref[1] ^ order[step]) * few, few)
            norm_ref[pl.ds(at, few), :] = normed[first : first + few]
            packed_ref[pl.ds(at, few), :] = normed[first : first + few].astype(BF16)
    dims = (((1,), (1,)), ((), ()))
    packed = packed_ref[...]
    size = batch // k
    for i in range(k):
        at = pl.multiple_of((place_ref[2] ^ i) * size, size)
        gram = lax.dot_general(packed_ref[pl.ds(at, size), :], packed, dims, preferred_element_type=F32)
        grams[i][...] = gram
    if second:
        coeff_ref = refs[3 + k]
        diag = jnp.sum(norm_ref[...] * other_ref[...], 0, keepdims=True) / batch
        coeff_ref[...] = 2.0 * ((1.0 - off_weight) * diag - 1.0)
        share = jnp.sum((1.0 - diag) ** 2 - off_weight * diag * diag, 1, keepdims=True)
        for i in range(k):

            @pl.when((place_ref[2] ^ i) == k - 1)
            def _():
                at = batch // BLOCKS
                row = grams[i][size - 8 :, at : at + 128]
                first = (lax.broadcasted_iota(jnp.int32, row.shape, 0) == 7) & (
                    lax.broadcasted_iota(jnp.int32, row.shape, 1) == 0
                )
                grams[i][size - 8 :, at : at + 128] = jnp.where(first, share, row)


def normalize_parts(place, place_array, own, parts, order, other=None):
    n, k = place.n, place.k
    batch, columns = own.shape
    second = other is not None
    out_shape = [
        jax.ShapeDtypeStruct((batch, columns), F32),
        jax.ShapeDtypeStruct((batch, columns), BF16),
        jax.ShapeDtypeStruct((1, columns), F32),
    ] + [jax.ShapeDtypeStruct((batch // k, batch), F32)] * k
    if second:
        out_shape.append(jax.ShapeDtypeStruct((1, columns), F32))
    args = [own, *parts[::-1]] + ([other] if second else [])
    space = pl.BlockSpec(memory_space=pltpu.VMEM)
    return pl.pallas_call(
        functools.partial(normalize_kernel, n=n, k=k, order=order, second=second),
        in_specs=[pl.BlockSpec(memory_space=pltpu.SMEM)] + [space] * len(args),
        out_specs=[space] * len(out_shape),
        out_shape=out_shape,
        compiler_params=pltpu.CompilerParams(vmem_limit_bytes=VMEM_BYTES // 2),
        cost_estimate=pl.CostEstimate(
            flops=2 * batch * batch * columns,
            bytes_accessed=16 * batch * columns + 4 * batch * batch,
            transcendentals=0,
        ),
        name="normalize",
    )(place_array, *args)


def gradient_kernel(place_ref, *refs, n, k, which):
    grams, refs = refs[: n * k], refs[n * k :]
    packed_ref, norm_ref, other_ref, scale_ref, coeff_ref, refs = *refs[:5], refs[5:]
    outs = [refs[0], *refs[n - 1 : 0 : -1]]
    gram_ref, share_ref, whole_ref = refs[n:]
    batch, columns = norm_ref.shape
    height = grams[0].shape[0] // 2
    width = batch // BLOCKS
    for i in range(k):
        for step in range(n):
            block = (place_ref[2] ^ i) * n + (place_ref[1] ^ step)
            at = pl.ds(pl.multiple_of(block * height, height), height)
            block = block // (2 * n // BLOCKS)
            for j in range(KEPT):
                to = pl.ds(pl.multiple_of(lax.rem(block + j, BLOCKS) * width, width), width)
                gram_ref[at, to] = grams[i * n + step][
                    which * height : (which + 1) * height, j * width : (j + 1) * width
                ]
    blocks = [slice(i * width, (i + 1) * width) for i in range(BLOCKS)]
    for i in range(BLOCKS):
        gram_ref[blocks[i], blocks[i - 1]] = gram_ref[blocks[i - 1], blocks[i]].T
    share = jnp.zeros((1, 1), F32)
    if which == 1:
        tail = gram_ref[blocks[3], blocks[1]].astype(F32)
        row = lax.broadcasted_iota(jnp.int32, tail.shape, 0)
        column = lax.broadcasted_iota(jnp.int32, tail.shape, 1)
        taken = (row == width - 1) & (column < 3)
        mirror = gram_ref[blocks[1], blocks[3]].astype(F32).T
        share = jnp.sum(jnp.where(taken, tail, 0.0), keepdims=True)
        gram_ref[blocks[3], blocks[1]] = jnp.where(taken, mirror, tail).astype(BF16)
    share_ref[...] = share
    factor = 2.0 * off_weight / batch
    rows = batch // n
    norm = norm_ref[...]
    grad = (
        factor * jnp.dot(gram_ref[...], packed_ref[...], preferred_element_type=F32)
        + coeff_ref[...] * other_ref[...]
    )
    first = jnp.sum(grad, 0, keepdims=True) / batch
    second = jnp.sum(grad * norm, 0, keepdims=True) / batch
    whole_ref[...] = (scale_ref[...] * (grad - first - norm * second)).astype(BF16)
    for step in range(n):
        at = pl.multiple_of((place_ref[0] ^ step) * rows, rows)
        outs[step][...] = whole_ref[pl.ds(at, rows), :]


def loss_kernel(place_ref, first_ref, second_ref, share_ref, loss_ref):
    batch = first_ref.shape[1]
    frob = jnp.sum(first_ref[...].astype(F32) * second_ref[...].astype(F32), keepdims=True)
    loss_ref[...] = (share_ref[...] + off_weight * (frob / (batch * batch))) / D


def gradient(place, place_array, grams, which, packed, norm, other, scale, coeff):
    batch, columns = norm.shape
    first, *others, gram, share = local(
        functools.partial(gradient_kernel, n=place.n, k=place.k, which=which),
        place_array,
        (*grams, packed, norm, other, scale, coeff),
        [((batch // place.n, columns), BF16)] * place.n + [((batch, batch), BF16), ((1, 1), F32)],
        "gradient",
        scratch_shapes=[pltpu.VMEM((batch, columns), BF16)],
    )
    return [first, *others[::-1]], gram, share


def place_kernel(place_ref, *refs, n):
    parts, outs = [refs[0], *refs[n - 1 : 0 : -1]], refs[n:]
    rows, columns = parts[0].shape[0] // len(outs), parts[0].shape[1]
    for step in range(n):
        at = pl.ds(pl.multiple_of((place_ref[0] ^ step) * columns, columns), columns)
        for i, out in enumerate(outs):
            out[:, at] = parts[step][i * rows : (i + 1) * rows, :]


def with_kernels(place, h_first, h_second, weight):
    n, k, z, a, b = place.n, place.k, place.z, place.a, place.b
    place_array = jnp.stack([z, a, b]).astype(jnp.int32)
    first = to_columns(place, h_first)
    first, second = lax.optimization_barrier((to_planes(place, place_array, first, True), to_columns(place, h_second)))
    first, late_weight = lax.optimization_barrier((lay(place, place_array, first), weight))
    met_1, second, held = lax.optimization_barrier(
        (met_rows(place, first), to_planes(place, place_array, second, False), fetch(late_weight))
    )

    def sent(parts):
        return sends(place, "z", [parts[0], *parts])[1:]

    def swapped(part):
        return place.send(part, lambda z, a, b: (z, a, b ^ 1))

    own_1, parts_1 = project(place, place_array, [met_1, [swapped(part) for part in met_1]], held)
    second = lay(place, place_array, second)
    size, here, toward = place.along("a")
    order_2 = [0, size - 1, *range(1, size - 1)]
    last = place.send(second, toward(size - 1))
    own_1, parts_1, late_weight = lax.optimization_barrier((own_1, parts_1, weight))
    parts_1 = sent(parts_1)

    def second_projected(weight, values, last):
        met = [place.send(values, toward(step)) for step in range(1, size - 1)]
        values, met[0] = lax.optimization_barrier((values, met[0]))
        early = swapped(jnp.concatenate([values, last], 0))
        late = swapped(jnp.concatenate(met, 0))
        return project(place, place_array, [[values, last, *met], [early, late]], fetch(weight))

    own_2, parts_2 = in_one(place, second_projected, (late_weight, second, last))
    own_1, own_2 = lax.optimization_barrier((own_1, own_2))
    parts_2 = sent(parts_2)
    norm_1, packed_1, scale_1, *grams = normalize_parts(
        place, place_array, own_1, parts_1, [*range(n)]
    )
    met_1 = in_one(place, lambda *grams: first_rows(place, place_array, grams), grams)
    met_1 = sends(place, "z", met_1)
    own_2, parts_2, met_1 = lax.optimization_barrier((own_2, parts_2, met_1))
    norm_2, packed_2, scale_2, *grams, coeff = normalize_parts(
        place, place_array, own_2, parts_2, order_2, norm_1
    )
    height, batch = met_1[0].shape
    (rows_1,) = local(rows_kernel, place_array, met_1, [((height, batch), BF16)], "rows")
    met_2 = plane_rows(place, place_array, grams)
    rows = met_2[0].shape[0]
    (part,) = local(
        functools.partial(code_kernel, n=n),
        place_array,
        (*met_2, rows_1),
        [((folded_shape(rows, batch)[0] + height * KEPT, batch // KEPT), BF16)],
        "code",
    )
    (part,) = local(
        functools.partial(finish_kernel, n=n, k=k),
        place_array,
        sends(place, "z", [part] * n),
        [((2 * rows, batch), BF16)],
        "finish",
    )
    grams = sends(place, "a", [part] * n)
    grams += [place.send(part, lambda z, a, b: (z, a, b ^ 1)) for part in grams]
    grads_2, gram_1, _ = gradient(
        place, place_array, grams, 0, packed_2, norm_2, norm_1, scale_2, coeff
    )
    grads_1, gram_2, share = gradient(
        place, place_array, grams, 1, packed_1, norm_1, norm_2, scale_1, coeff
    )
    outs = []
    for grads in (grads_1, grads_2):
        met = sends(place, "z", grads)
        (out,) = local(
            functools.partial(place_kernel, n=n),
            place_array,
            [met[0], *met[:0:-1]],
            [(h_first.shape, BF16)],
            "place",
        )
        outs.append(out)
    out_1, out_2 = outs
    (loss,) = local(loss_kernel, place_array, (gram_1, gram_2, share), [((1, 1), F32)], "loss")
    return (out_1, out_2, loss.reshape(()))


def plain(place, h_first, h_second, weight):
    n, k, z, a, b = place.n, place.k, place.z, place.a, place.b
    rows, width = h_first.shape
    batch = rows * n
    columns = weight.shape[1] // n
    weight_parts = weight.reshape(k, width, n * columns)
    zs = []
    for values in (h_first, h_second):
        moved = place.send(values, lambda z, a, b: (a, z, b))
        own = jnp.concatenate(met_rows(place, moved), 0)
        total = jnp.dot(own, pick(weight_parts, b), preferred_element_type=F32)
        for step in range(1, k):
            other = place.send(own, lambda z, a, b, s=step: (z, a, b ^ s))
            total += jnp.dot(other, pick(weight_parts, b ^ step), preferred_element_type=F32)
        cut = total.reshape(batch, n, columns).transpose(1, 0, 2)
        whole = tree_sum(exchange(place, "z", cut)).reshape(n, rows, columns)
        zs.append(jnp.concatenate(ordered([whole[i] for i in range(n)], a), 0))
    normed, scales = [], []
    for values in zs:
        mean = jnp.sum(values, 0) / batch
        scale = lax.rsqrt(jnp.sum(values * values, 0) / batch - mean * mean + bn_eps)
        normed.append((values - mean) * scale)
        scales.append(scale)
    diag = jnp.sum(normed[0] * normed[1], 0) / batch
    packed = [values.astype(BF16) for values in normed]
    dims = (((1,), (1,)), ((), ()))
    grams = []
    for values in packed:
        gram = lax.dot_general(values, values, dims, preferred_element_type=F32)
        grams.append(plain_gram(place, gram))
    frob = jnp.sum(grams[0].astype(F32) * grams[1].astype(F32)) / (batch * batch)
    coeff = 2.0 * ((1.0 - off_weight) * diag - 1.0)
    factor = 2.0 * off_weight / batch
    outs = []
    for view in range(2):
        grad = (
            factor * jnp.dot(grams[1 - view], packed[view], preferred_element_type=F32)
            + coeff * normed[1 - view]
        )
        first = jnp.sum(grad, 0) / batch
        second = jnp.sum(grad * normed[view], 0) / batch
        out = (scales[view] * (grad - first - normed[view] * second)).astype(BF16)
        parts = exchange(place, "z", out.reshape(n, rows, columns))
        outs.append(jnp.concatenate(ordered(parts, z), 1))
    share = jnp.sum((1.0 - diag) ** 2) - off_weight * jnp.sum(diag * diag)
    loss = (lax.psum(share, ("dp", "mp")) + off_weight * frob) / D
    return (outs[0], outs[1], loss)


def per_device(h_first, h_second, weight):
    place = Place()
    columns = weight.shape[1] // place.n
    fits = columns % 128 == 0 and place.n == 4 and place.k == 2
    return (with_kernels if fits else plain)(place, h_first, h_second, weight)


def solution(mesh):
    in_specs = (P("dp", "mp"), P("dp", "mp"), P("dp", "mp"))
    out_specs = (P("dp", "mp"), P("dp", "mp"), P())
    return jax.shard_map(
        per_device, mesh=mesh, in_specs=in_specs, out_specs=out_specs, check_vma=False
    )
```

```python
import functools

import jax
import jax.numpy as jnp
from jax import lax
from jax.experimental import pallas as pl
from jax.experimental.pallas import tpu as pltpu
from jax.sharding import PartitionSpec as P

D = 8192


off_weight = 0.0051
bn_eps = 1e-05

F32 = jnp.float32
BF16 = jnp.bfloat16
VMEM_BYTES = 16 * 1024 * 1024
POWERS = 240
HIGHEST = 128 * POWERS - 1
SCALE_ROWS = 16


class Place:
    def __init__(self):
        self.n = lax.axis_size("dp")
        self.k = lax.axis_size("mp") // self.n
        self.z = lax.axis_index("dp")
        self.a = lax.axis_index("mp") // self.k
        self.b = lax.axis_index("mp") % self.k

    def send(self, value, target):
        n, k = self.n, self.k
        pairs = []
        for z in range(n):
            for a in range(n):
                for b in range(k):
                    to_z, to_a, to_b = target(z, a, b)
                    pairs.append(((z * n + a) * k + b, (to_z * n + to_a) * k + to_b))
        return lax.ppermute(value, ("dp", "mp"), pairs)

    def along(self, axis):
        if axis == "z":
            return self.n, self.z, lambda step: lambda z, a, b: (z ^ step, a, b)
        if axis == "a":
            return self.n, self.a, lambda step: lambda z, a, b: (z, a ^ step, b)
        return self.k, self.b, lambda step: lambda z, a, b: (z, a, b ^ step)


def ordered(parts, place):
    bit = 1
    while bit < len(parts):
        odd = (place & bit) != 0
        parts = [jnp.where(odd, parts[i ^ bit], parts[i]) for i in range(len(parts))]
        bit *= 2
    return parts


def tree_sum(parts):
    while len(parts) > 1:
        parts = [parts[i] + parts[i + 1] for i in range(0, len(parts), 2)]
    return parts[0]


def pick(value, index):
    return lax.dynamic_index_in_dim(value, index, 0, keepdims=False)


def exchange(place, axis, value, few=False):
    size, here, toward = place.along(axis)
    return sends(place, axis, [pick(value, here ^ step) for step in range(size)], few)


def sends(place, axis, parts, few=False):
    size, here, toward = place.along(axis)
    met = {0: parts[0]}
    order = [*range(1, size)] if few else [*range(size - 1, 0, -1)]
    for i, step in enumerate(order):
        part = parts[step]
        if few and i >= 2:
            met[order[i - 2]], part = lax.optimization_barrier((met[order[i - 2]], part))
        met[step] = place.send(part, toward(step))
    return [met[step] for step in range(size)]


def reduce_scatter(place, axis, value, few=False):
    size, here, toward = place.along(axis)
    value = value.reshape((size, value.shape[0] // size) + value.shape[1:])
    return tree_sum(exchange(place, axis, value, few))


def gather(place, axis, value, few=False):
    size, here, toward = place.along(axis)
    parts = sends(place, axis, [value] * size, few)
    return jnp.concatenate(ordered(parts, here), 0)


BLOCKS = 4
KEPT = 3


def folded(values):
    width = values.shape[1] // KEPT
    return jnp.concatenate([values[:, i * width : (i + 1) * width] for i in range(KEPT)], 0)


def unfolded(values):
    height = values.shape[0] // KEPT
    return jnp.concatenate([values[i * height : (i + 1) * height] for i in range(KEPT)], 1)


def folded_shape(rows, columns):
    return (rows * KEPT + SCALE_ROWS, columns // KEPT)


def halve_kernel(place_ref, kept_ref, met_ref, *outs, n):
    height = kept_ref.shape[0] // n
    width = kept_ref.shape[1] // BLOCKS
    for step, out in enumerate(outs):
        block = place_ref[1] ^ step
        at = pl.ds(pl.multiple_of(block * height, height), height)
        block = (place_ref[2] * n + block) // (2 * n // BLOCKS)
        total = []
        for i in range(KEPT):
            cut = pl.ds(pl.multiple_of(lax.rem(block + i, BLOCKS) * width, width), width)
            total.append(kept_ref[at, cut] + met_ref[at, cut])
        total = jnp.concatenate(total, 1)
        if step == 0:
            out[...] = total
        else:
            encode(folded(total), out)


def plane_sum(met):
    return tree_sum([met[0][...]] + [unfolded(decode(ref, 1)[0]) for ref in met[1:]])


def plane_kernel(place_ref, *refs, n):
    met, outs, whole_ref = refs[:n], refs[n:-1], refs[-1]
    whole_ref[...] = plane_sum(met)
    height = outs[0].shape[0]
    for step, out in enumerate(outs):
        at = pl.ds(pl.multiple_of((place_ref[0] ^ step) * height, height), height)
        if step == 0:
            out[...] = whole_ref[at, :]
        else:
            encode(folded(whole_ref[at, :]), out)


def rows_kernel(place_ref, *refs):
    refs[-1][...] = plane_sum(refs[:-1]).astype(BF16)


def code_kernel(place_ref, *refs, n):
    met, rows_ref, out_ref = refs[:n], refs[n], refs[n + 1]
    total = folded(plane_sum(met))
    coded = total.shape[0] + SCALE_ROWS
    encode(total, out_ref.at[:coded])
    out_ref[coded:] = folded(rows_ref[...])


def finish_kernel(place_ref, *refs, n, k):
    out_ref = refs[-1]
    height = out_ref.shape[0] // 2
    coded, few = height * KEPT + SCALE_ROWS, height // n
    met = []
    for step in range(n):
        at = pl.ds(pl.multiple_of((place_ref[0] ^ step) * few, few), few)
        out_ref[at, :] = unfolded(refs[step][coded:])
        met += decode(refs[step].at[:coded], 1)
    total = unfolded(tree_sum(met))
    last = (place_ref[1] == n - 1) & (place_ref[2] == k - 1)
    start = 2 * (total.shape[1] // KEPT)
    edge = total[-8:, start:]
    row = lax.broadcasted_iota(jnp.int32, edge.shape, 0)
    column = lax.broadcasted_iota(jnp.int32, edge.shape, 1)
    taken = (row == 7) & last
    whole = jnp.sum(jnp.where(taken & (column == 0), edge, 0.0), keepdims=True)
    high = whole.astype(BF16).astype(F32)
    middle = (whole - high).astype(BF16).astype(F32)
    three = jnp.where(column == 0, high, jnp.where(column == 1, middle, whole - high - middle))
    edge = jnp.where(taken & (column < 3), three, edge)
    edge = jnp.concatenate([total[-8:, :start], edge], 1)
    out_ref[height:] = jnp.concatenate([total[:-8], edge], 0).astype(BF16)


def local(kernel, place_array, args, shapes, name, pinned=False, **more):
    kind = pltpu.VMEM if pinned else jax.ShapeDtypeStruct
    space = pl.BlockSpec(memory_space=pltpu.VMEM)
    return pl.pallas_call(
        kernel,
        in_specs=[pl.BlockSpec(memory_space=pltpu.SMEM)] + [space] * len(args),
        out_specs=[space] * len(shapes),
        out_shape=[kind(shape, dtype) for shape, dtype in shapes],
        compiler_params=pltpu.CompilerParams(vmem_limit_bytes=VMEM_BYTES // 2),
        name=name,
        **more,
    )(place_array, *args)


def plane_rows(place, place_array, grams, few=False):
    half, batch = grams[0].shape
    kept, other = grams
    other = place.send(other, lambda z, a, b: (z, a, b ^ 1))
    height, batch = half // place.n, batch * KEPT // BLOCKS
    parts = local(
        functools.partial(halve_kernel, n=place.n),
        place_array,
        (kept, other),
        [((height, batch), F32)] + [(folded_shape(height, batch), BF16)] * (place.n - 1),
        "halve",
    )
    return sends(place, "a", parts, few)


def first_rows(place, place_array, grams):
    parts = plane_rows(place, place_array, grams, True)
    height, batch = parts[0].shape
    few = height // place.n
    return local(
        functools.partial(plane_kernel, n=place.n),
        place_array,
        parts,
        [((few, batch), F32)] + [(folded_shape(few, batch), BF16)] * (place.n - 1),
        "plane",
        scratch_shapes=[pltpu.VMEM((height, batch), F32)],
    )


def in_one(place, run, args):
    shapes = jax.eval_shape(run, *args)
    return lax.cond(
        place.z < place.n,
        run,
        lambda *args: jax.tree.map(lambda leaf: jnp.zeros(leaf.shape, leaf.dtype), shapes),
        *args,
    )


def plain_gram(place, part):
    for axis in ("b", "a", "z"):
        part = reduce_scatter(place, axis, part)
    part = part.astype(BF16)
    for axis in ("z", "a", "b"):
        part = gather(place, axis, part)
    return part


def lay_kernel(place_ref, *refs, n):
    parts, outs = refs[:n], refs[n:]
    few = parts[0].shape[0] // len(outs)
    for step in range(n):
        at = pl.ds(pl.multiple_of((place_ref[0] ^ step) * few, few), few)
        for i, out in enumerate(outs):
            out[at, :] = parts[step][i * few : (i + 1) * few, :]


def fetch_kernel(weight_ref, held_ref, arrived):
    copy = pltpu.make_async_copy(weight_ref, held_ref, arrived)
    copy.start()
    copy.wait()


def fetch(weight):
    return pl.pallas_call(
        fetch_kernel,
        in_specs=[pl.BlockSpec(memory_space=pl.ANY)],
        out_specs=pl.BlockSpec(memory_space=pltpu.VMEM),
        out_shape=pltpu.VMEM(weight.shape, BF16),
        scratch_shapes=[pltpu.SemaphoreType.DMA],
        compiler_params=pltpu.CompilerParams(vmem_limit_bytes=VMEM_BYTES // 2),
        cost_estimate=pl.CostEstimate(flops=0, bytes_accessed=4 * weight.size, transcendentals=0),
        name="fetch",
    )(pltpu.with_memory_space_constraint(weight, pltpu.HBM))


def to_columns(place, view):
    rows, width = view.shape
    return exchange(place, "a", view.reshape(place.n, rows // place.n, width))


def turn_kernel(place_ref, *refs, n):
    turned = ordered([ref[...] for ref in refs[:n]], place_ref[1] ^ place_ref[0])
    for ref, part in zip(refs[n:], [turned[0], *turned[:0:-1]]):
        ref[...] = part


def to_planes(place, place_array, parts, kernel):
    if kernel:
        parts = local(
            functools.partial(turn_kernel, n=place.n),
            place_array,
            parts,
            [(parts[0].shape, BF16)] * place.n,
            "turn",
            pinned=True,
        )
        parts = [parts[0], *parts[:0:-1]]
    else:
        parts = ordered(parts, place.a ^ place.z)
    return sends(place, "z", parts)


def lay(place, place_array, parts):
    rows, width = parts[0].shape
    (laid,) = local(
        functools.partial(lay_kernel, n=place.n),
        place_array,
        parts,
        [((rows * place.n, width), BF16)],
        "lay",
        pinned=True,
    )
    return laid


def met_rows(place, values, few=False):
    return sends(place, "a", [values] * place.n, few)


def project_kernel(place_ref, *refs, counts, n, k):
    met = refs[: sum(counts)]
    weight_ref, own_ref, *coded = refs[sum(counts) :]
    width = met[0].shape[1]
    columns = own_ref.shape[1]
    values = []
    for count in counts:
        values.append(jnp.concatenate([ref[...] for ref in met[:count]], 0))
        met = met[count:]
    for step in [*range(n - 1, 0, -1), 0]:
        at = pl.ds(pl.multiple_of((place_ref[0] ^ step) * columns, columns), columns)
        total = 0.0
        for i in range(k):
            rows = pl.ds(pl.multiple_of((place_ref[2] ^ i) * width, width), width)
            total += jnp.dot(values[i], weight_ref[rows, at], preferred_element_type=F32)
        if step == 0:
            own_ref[...] = total
        else:
            encode(total, coded[n - 1 - step])


def encode(total, coded_ref):
    rows = total.shape[0]
    top = jnp.max(jnp.abs(total), 0, keepdims=True)
    top = jnp.maximum(top * (1.0 + 1.0 / 128.0), 1e-30).astype(BF16)
    coded_ref[rows:] = jnp.broadcast_to(top, (SCALE_ROWS, total.shape[1]))
    whole = jnp.floor(jnp.abs(total) * (HIGHEST / top.astype(F32)) + 0.5)
    power = jnp.floor(whole * (1.0 / 128.0))
    word = (1.0 + (whole * (1.0 / 128.0) - power)) * jnp.exp2(power - POWERS // 2)
    coded_ref[:rows] = jnp.where(total < 0.0, -word, word).astype(BF16)


def decode(coded_ref, count):
    rows = coded_ref.shape[0] - SCALE_ROWS
    scale = coded_ref[rows:].astype(F32)[:1] * (1.0 / HIGHEST)
    height = rows // count
    blocks = []
    for i in range(count):
        word = coded_ref[i * height : (i + 1) * height].astype(F32)
        size = jnp.abs(word)
        power = jnp.floor(jnp.log(size) * 1.4426950408889634 + 0.002)
        part = jnp.floor(size * jnp.exp2(-power) * 128.0 + 0.5)
        whole = (power + (POWERS // 2 - 1)) * 128.0 + part
        blocks.append(jnp.where(word < 0.0, -whole, whole) * scale)
    return blocks


def project(place, place_array, met, held):
    n, k = place.n, place.k
    rows, width = met[0][0].shape
    batch, columns = rows * n, held.shape[1] // n
    counts = [len(parts) for parts in met]
    met = [part for parts in met for part in parts]
    coded = batch + SCALE_ROWS
    out_shape = [jax.ShapeDtypeStruct((batch, columns), F32)]
    out_shape += [jax.ShapeDtypeStruct((coded, columns), BF16)] * (n - 1)
    space = pl.BlockSpec(memory_space=pltpu.VMEM)
    own, *parts = pl.pallas_call(
        functools.partial(project_kernel, counts=counts, n=n, k=k),
        in_specs=[pl.BlockSpec(memory_space=pltpu.SMEM)]
        + [space] * (len(met) + 1),
        out_specs=[space] * n,
        out_shape=out_shape,
        compiler_params=pltpu.CompilerParams(vmem_limit_bytes=VMEM_BYTES),
        cost_estimate=pl.CostEstimate(
            flops=2 * batch * k * width * n * columns,
            bytes_accessed=2 * k * width * (batch + n * columns) + 3 * n * batch * columns,
            transcendentals=0,
        ),
        name="project",
    )(place_array, *met, pltpu.with_memory_space_constraint(held, pltpu.VMEM))
    return own, parts[::-1]


def normalize_kernel(place_ref, *refs, n, k, order, second):
    own_ref, parts = refs[0], refs[n - 1 : 0 : -1]
    refs = refs[n:]
    if second:
        other_ref, refs = refs[0], refs[1:]
    norm_ref, packed_ref, scale_ref = refs[:3]
    grams = refs[3 : 3 + k]
    batch, columns = own_ref.shape
    height = batch // n
    met = [[own_ref[i * height : (i + 1) * height] for i in range(n)]]
    for step in range(1, n):
        met.append(decode(parts[step - 1], n))
    blocks = [tree_sum([met[step][i] for step in range(n)]) for i in range(n)]
    total = tree_sum([jnp.sum(block, 0, keepdims=True) for block in blocks])
    squares = tree_sum([jnp.sum(block * block, 0, keepdims=True) for block in blocks])
    mean = total / batch
    scale = lax.rsqrt(squares / batch - mean * mean + bn_eps)
    scale_ref[...] = scale
    rows, few = batch // n, batch // (n * n)
    for i, block in enumerate(blocks):
        normed = (block - mean) * scale
        for first in range(0, height, few):
            step, plane = divmod((i * height + first) // few, n)
            at = pl.multiple_of(plane * rows + (place_ref[1] ^ order[step]) * few, few)
            norm_ref[pl.ds(at, few), :] = normed[first : first + few]
            packed_ref[pl.ds(at, few), :] = normed[first : first + few].astype(BF16)
    dims = (((1,), (1,)), ((), ()))
    packed = packed_ref[...]
    size = batch // k
    for i in range(k):
        at = pl.multiple_of((place_ref[2] ^ i) * size, size)
        gram = lax.dot_general(packed_ref[pl.ds(at, size), :], packed, dims, preferred_element_type=F32)
        grams[i][...] = gram
    if second:
        coeff_ref = refs[3 + k]
        diag = jnp.sum(norm_ref[...] * other_ref[...], 0, keepdims=True) / batch
        coeff_ref[...] = 2.0 * ((1.0 - off_weight) * diag - 1.0)
        share = jnp.sum((1.0 - diag) ** 2 - off_weight * diag * diag, 1, keepdims=True)
        for i in range(k):

            @pl.when((place_ref[2] ^ i) == k - 1)
            def _():
                at = batch // BLOCKS
                row = grams[i][size - 8 :, at : at + 128]
                first = (lax.broadcasted_iota(jnp.int32, row.shape, 0) == 7) & (
                    lax.broadcasted_iota(jnp.int32, row.shape, 1) == 0
                )
                grams[i][size - 8 :, at : at + 128] = jnp.where(first, share, row)


def normalize_parts(place, place_array, own, parts, order, other=None):
    n, k = place.n, place.k
    batch, columns = own.shape
    second = other is not None
    out_shape = [
        jax.ShapeDtypeStruct((batch, columns), F32),
        jax.ShapeDtypeStruct((batch, columns), BF16),
        jax.ShapeDtypeStruct((1, columns), F32),
    ] + [jax.ShapeDtypeStruct((batch // k, batch), F32)] * k
    if second:
        out_shape.append(jax.ShapeDtypeStruct((1, columns), F32))
    args = [own, *parts[::-1]] + ([other] if second else [])
    space = pl.BlockSpec(memory_space=pltpu.VMEM)
    return pl.pallas_call(
        functools.partial(normalize_kernel, n=n, k=k, order=order, second=second),
        in_specs=[pl.BlockSpec(memory_space=pltpu.SMEM)] + [space] * len(args),
        out_specs=[space] * len(out_shape),
        out_shape=out_shape,
        compiler_params=pltpu.CompilerParams(vmem_limit_bytes=VMEM_BYTES // 2),
        cost_estimate=pl.CostEstimate(
            flops=2 * batch * batch * columns,
            bytes_accessed=16 * batch * columns + 4 * batch * batch,
            transcendentals=0,
        ),
        name="normalize",
    )(place_array, *args)


def gradient_kernel(place_ref, *refs, n, k, which):
    grams, refs = refs[: n * k], refs[n * k :]
    packed_ref, norm_ref, other_ref, scale_ref, coeff_ref, refs = *refs[:5], refs[5:]
    outs = [refs[0], *refs[n - 1 : 0 : -1]]
    gram_ref, share_ref, whole_ref = refs[n:]
    batch, columns = norm_ref.shape
    height = grams[0].shape[0] // 2
    width = batch // BLOCKS
    for i in range(k):
        for step in range(n):
            block = (place_ref[2] ^ i) * n + (place_ref[1] ^ step)
            at = pl.ds(pl.multiple_of(block * height, height), height)
            block = block // (2 * n // BLOCKS)
            for j in range(KEPT):
                to = pl.ds(pl.multiple_of(lax.rem(block + j, BLOCKS) * width, width), width)
                gram_ref[at, to] = grams[i * n + step][
                    which * height : (which + 1) * height, j * width : (j + 1) * width
                ]
    blocks = [slice(i * width, (i + 1) * width) for i in range(BLOCKS)]
    for i in range(BLOCKS):
        gram_ref[blocks[i], blocks[i - 1]] = gram_ref[blocks[i - 1], blocks[i]].T
    share = jnp.zeros((1, 1), F32)
    if which == 1:
        tail = gram_ref[blocks[3], blocks[1]].astype(F32)
        row = lax.broadcasted_iota(jnp.int32, tail.shape, 0)
        column = lax.broadcasted_iota(jnp.int32, tail.shape, 1)
        taken = (row == width - 1) & (column < 3)
        mirror = gram_ref[blocks[1], blocks[3]].astype(F32).T
        share = jnp.sum(jnp.where(taken, tail, 0.0), keepdims=True)
        gram_ref[blocks[3], blocks[1]] = jnp.where(taken, mirror, tail).astype(BF16)
    share_ref[...] = share
    factor = 2.0 * off_weight / batch
    rows = batch // n
    norm = norm_ref[...]
    grad = (
        factor * jnp.dot(gram_ref[...], packed_ref[...], preferred_element_type=F32)
        + coeff_ref[...] * other_ref[...]
    )
    first = jnp.sum(grad, 0, keepdims=True) / batch
    second = jnp.sum(grad * norm, 0, keepdims=True) / batch
    whole_ref[...] = (scale_ref[...] * (grad - first - norm * second)).astype(BF16)
    for step in range(n):
        at = pl.multiple_of((place_ref[0] ^ step) * rows, rows)
        outs[step][...] = whole_ref[pl.ds(at, rows), :]


def loss_kernel(place_ref, first_ref, second_ref, share_ref, loss_ref):
    batch = first_ref.shape[1]
    frob = jnp.sum(first_ref[...].astype(F32) * second_ref[...].astype(F32), keepdims=True)
    loss_ref[...] = (share_ref[...] + off_weight * (frob / (batch * batch))) / D


def gradient(place, place_array, grams, which, packed, norm, other, scale, coeff):
    batch, columns = norm.shape
    first, *others, gram, share = local(
        functools.partial(gradient_kernel, n=place.n, k=place.k, which=which),
        place_array,
        (*grams, packed, norm, other, scale, coeff),
        [((batch // place.n, columns), BF16)] * place.n + [((batch, batch), BF16), ((1, 1), F32)],
        "gradient",
        scratch_shapes=[pltpu.VMEM((batch, columns), BF16)],
    )
    return [first, *others[::-1]], gram, share


def place_kernel(place_ref, *refs, n):
    parts, outs = [refs[0], *refs[n - 1 : 0 : -1]], refs[n:]
    rows, columns = parts[0].shape[0] // len(outs), parts[0].shape[1]
    for step in range(n):
        at = pl.ds(pl.multiple_of((place_ref[0] ^ step) * columns, columns), columns)
        for i, out in enumerate(outs):
            out[:, at] = parts[step][i * rows : (i + 1) * rows, :]


def with_kernels(place, h_first, h_second, weight):
    n, k, z, a, b = place.n, place.k, place.z, place.a, place.b
    place_array = jnp.stack([z, a, b]).astype(jnp.int32)
    first = to_columns(place, h_first)
    first, second = lax.optimization_barrier((to_planes(place, place_array, first, True), to_columns(place, h_second)))
    first, late_weight = lax.optimization_barrier((lay(place, place_array, first), weight))
    met_1, second, held = lax.optimization_barrier(
        (met_rows(place, first), to_planes(place, place_array, second, False), fetch(late_weight))
    )

    def sent(parts):
        return sends(place, "z", [parts[0], *parts])[1:]

    def swapped(part):
        return place.send(part, lambda z, a, b: (z, a, b ^ 1))

    own_1, parts_1 = project(place, place_array, [met_1, [swapped(part) for part in met_1]], held)
    second = lay(place, place_array, second)
    size, here, toward = place.along("a")
    order_2 = [0, size - 1, *range(1, size - 1)]
    last = place.send(second, toward(size - 1))
    own_1, parts_1, late_weight = lax.optimization_barrier((own_1, parts_1, weight))
    parts_1 = sent(parts_1)

    def second_projected(weight, values, last):
        met = [place.send(values, toward(step)) for step in range(1, size - 1)]
        values, met[0] = lax.optimization_barrier((values, met[0]))
        early = swapped(jnp.concatenate([values, last], 0))
        late = swapped(jnp.concatenate(met, 0))
        return project(place, place_array, [[values, last, *met], [early, late]], fetch(weight))

    own_2, parts_2 = in_one(place, second_projected, (late_weight, second, last))
    own_1, own_2 = lax.optimization_barrier((own_1, own_2))
    parts_2 = sent(parts_2)
    norm_1, packed_1, scale_1, *grams = normalize_parts(
        place, place_array, own_1, parts_1, [*range(n)]
    )
    met_1 = in_one(place, lambda *grams: first_rows(place, place_array, grams), grams)
    met_1 = sends(place, "z", met_1)
    own_2, parts_2, met_1 = lax.optimization_barrier((own_2, parts_2, met_1))
    norm_2, packed_2, scale_2, *grams, coeff = normalize_parts(
        place, place_array, own_2, parts_2, order_2, norm_1
    )
    height, batch = met_1[0].shape
    (rows_1,) = local(rows_kernel, place_array, met_1, [((height, batch), BF16)], "rows")
    met_2 = plane_rows(place, place_array, grams)
    rows = met_2[0].shape[0]
    (part,) = local(
        functools.partial(code_kernel, n=n),
        place_array,
        (*met_2, rows_1),
        [((folded_shape(rows, batch)[0] + height * KEPT, batch // KEPT), BF16)],
        "code",
    )
    (part,) = local(
        functools.partial(finish_kernel, n=n, k=k),
        place_array,
        sends(place, "z", [part] * n),
        [((2 * rows, batch), BF16)],
        "finish",
    )
    grams = sends(place, "a", [part] * n)
    grams += [place.send(part, lambda z, a, b: (z, a, b ^ 1)) for part in grams]
    grads_2, gram_1, _ = gradient(
        place, place_array, grams, 0, packed_2, norm_2, norm_1, scale_2, coeff
    )
    grads_1, gram_2, share = gradient(
        place, place_array, grams, 1, packed_1, norm_1, norm_2, scale_1, coeff
    )
    outs = []
    for grads in (grads_1, grads_2):
        met = sends(place, "z", grads)
        (out,) = local(
            functools.partial(place_kernel, n=n),
            place_array,
            [met[0], *met[:0:-1]],
            [(h_first.shape, BF16)],
            "place",
        )
        outs.append(out)
    out_1, out_2 = outs
    (loss,) = local(loss_kernel, place_array, (gram_1, gram_2, share), [((1, 1), F32)], "loss")
    return (out_1, out_2, loss.reshape(()))


def plain(place, h_first, h_second, weight):
    n, k, z, a, b = place.n, place.k, place.z, place.a, place.b
    rows, width = h_first.shape
    batch = rows * n
    columns = weight.shape[1] // n
    weight_parts = weight.reshape(k, width, n * columns)
    zs = []
    for values in (h_first, h_second):
        moved = place.send(values, lambda z, a, b: (a, z, b))
        own = jnp.concatenate(met_rows(place, moved), 0)
        total = jnp.dot(own, pick(weight_parts, b), preferred_element_type=F32)
        for step in range(1, k):
            other = place.send(own, lambda z, a, b, s=step: (z, a, b ^ s))
            total += jnp.dot(other, pick(weight_parts, b ^ step), preferred_element_type=F32)
        cut = total.reshape(batch, n, columns).transpose(1, 0, 2)
        whole = tree_sum(exchange(place, "z", cut)).reshape(n, rows, columns)
        zs.append(jnp.concatenate(ordered([whole[i] for i in range(n)], a), 0))
    normed, scales = [], []
    for values in zs:
        mean = jnp.sum(values, 0) / batch
        scale = lax.rsqrt(jnp.sum(values * values, 0) / batch - mean * mean + bn_eps)
        normed.append((values - mean) * scale)
        scales.append(scale)
    diag = jnp.sum(normed[0] * normed[1], 0) / batch
    packed = [values.astype(BF16) for values in normed]
    dims = (((1,), (1,)), ((), ()))
    grams = []
    for values in packed:
        gram = lax.dot_general(values, values, dims, preferred_element_type=F32)
        grams.append(plain_gram(place, gram))
    frob = jnp.sum(grams[0].astype(F32) * grams[1].astype(F32)) / (batch * batch)
    coeff = 2.0 * ((1.0 - off_weight) * diag - 1.0)
    factor = 2.0 * off_weight / batch
    outs = []
    for view in range(2):
        grad = (
            factor * jnp.dot(grams[1 - view], packed[view], preferred_element_type=F32)
            + coeff * normed[1 - view]
        )
        first = jnp.sum(grad, 0) / batch
        second = jnp.sum(grad * normed[view], 0) / batch
        out = (scales[view] * (grad - first - normed[view] * second)).astype(BF16)
        parts = exchange(place, "z", out.reshape(n, rows, columns))
        outs.append(jnp.concatenate(ordered(parts, z), 1))
    share = jnp.sum((1.0 - diag) ** 2) - off_weight * jnp.sum(diag * diag)
    loss = (lax.psum(share, ("dp", "mp")) + off_weight * frob) / D
    return (outs[0], outs[1], loss)


def per_device(h_first, h_second, weight):
    place = Place()
    columns = weight.shape[1] // place.n
    fits = columns % 128 == 0 and place.n == 4 and place.k == 2
    return (with_kernels if fits else plain)(place, h_first, h_second, weight)


def solution(mesh):
    in_specs = (P("dp", "mp"), P("dp", "mp"), P("dp", "mp"))
    out_specs = (P("dp", "mp"), P("dp", "mp"), P())
    return jax.shard_map(
        per_device, mesh=mesh, in_specs=in_specs, out_specs=out_specs, check_vma=False
    )
```
